512 devices in a mesh: img: 32 (over y, x_hi, core), patch: 16 (over z, x_lo).
Axes of the slice: x: 4 (x_hi: 2, x_lo: 2; x = x_hi * 2 + x_lo), y: 8, z: 8, core: 2. Of those that a mesh axis runs over, the one named last changes fastest.
Arguments:
- fresh: bfloat16 [32, 16, 4, 16, 4608], P('img', 'patch'), may hold values from -9 to 9
- stale_keys: bfloat16 [32, 16, 4, 16, 1536], P('img', 'patch'), may hold values from -6 to 6
- stale_values: bfloat16 [32, 16, 4, 16, 1536], P('img', 'patch'), may hold values from -6 to 6
- text_kv: bfloat16 [32, 128, 3072], P('img'), may hold values from -6 to 6
- group_slots: int32 [32], replicated, may hold values from 1 to 3, as said below
- text_len: int32 [32], replicated, may hold values from 1 to 128, as said below
Outputs:
- attended: bfloat16 [32, 16, 4, 16, 1536], P('img', 'patch')
The draws below stay inside these ranges and needn't reach their ends.
Inputs may be any that keep to these rules, and one draw needn't show every extreme that they name: The groups hold 2 on average; the running sums over g of group_slots[g] - 2 differ by at most 1 between any two groups. `text_len`: some group has 128.
All inputs are finite; a program needn't handle non-finite values.
Results may differ from the reference program's by a relative error of at most 0.0046.
Values may be sent and summed in bfloat16 or wider, within the bound.
A program may use at most 64 MiB of HBM per device.

```python
import jax
import jax.numpy as jnp
from jax import lax

HDIM = 128
HD = 1536
BLK = 16
SLOTS = 4
TXT = 128
N_IMG = 32
N_PATCH = 16


def draw_fresh(key, part):
    key = jax.random.fold_in(key, 1)
    shape = (N_IMG, N_PATCH, SLOTS, BLK, 3 * HD)
    values = jax.random.truncated_normal(key, -6.0, 6.0, shape)
    return values.astype(jnp.bfloat16)


def draw_stale_keys(key, part):
    key = jax.random.fold_in(key, 2)
    shape = (N_IMG, N_PATCH, SLOTS, BLK, HD)
    values = jax.random.truncated_normal(key, -6.0, 6.0, shape)
    return values.astype(jnp.bfloat16)


def draw_group_slots(key, part):
    key = jax.random.fold_in(key, 3)
    half_slots = SLOTS // 2
    passing = jax.random.randint(jax.random.fold_in(key, 1), (N_IMG,), 1, half_slots + 1).astype(jnp.int32)
    pivot = jax.random.randint(jax.random.fold_in(key, 2), (), 0, N_IMG).astype(jnp.int32)
    groups = jnp.arange(N_IMG, dtype=jnp.int32)
    before = ((pivot + N_IMG - 1) % N_IMG).astype(jnp.int32)
    after = ((pivot + 1) % N_IMG).astype(jnp.int32)
    passing = jnp.where(groups == before, 1, jnp.where(groups == pivot, half_slots, jnp.where(groups == after, 1, passing))).astype(jnp.int32)
    return (half_slots + passing - jnp.roll(passing, 1)).astype(jnp.int32)


def draw_text_len(key, part):
    key = jax.random.fold_in(key, 4)
    lengths = jax.random.randint(jax.random.fold_in(key, 1), (N_IMG,), 1, TXT + 1)
    chosen = jax.random.randint(jax.random.fold_in(key, 2), (), 0, N_IMG)
    return jnp.where(jnp.arange(N_IMG) == chosen, TXT, lengths).astype(jnp.int32)


def levels(stream_key, shape, shards, least, top_value):
    loudness = 1.0
    for axis_at, shards_of in shards:
        draws = jax.random.uniform(jax.random.fold_in(jax.random.fold_in(stream_key, 6), axis_at), (shards_of,), jnp.float32, least / len(shards), top_value / len(shards))
        loudness = loudness * jnp.repeat(jnp.exp(draws), shape[axis_at] // shards_of).reshape((-1,) + (1,) * (len(shape) - 1 - axis_at))
    return loudness


def centred(key, dims, width, most, split=(), held_as=jnp.bfloat16):
    loudness = levels(key, dims, split, -0.22, 0.18) if split else 1.0
    result = jax.random.normal(key, dims, jnp.float32) * width * loudness
    return jnp.minimum(jnp.maximum(result, -most), most).astype(held_as)


def setup_inputs(seed: int = 0) -> dict:
    seeds = jax.random.split(jax.random.key(seed), 7)
    return {
        "fresh": draw_fresh(jax.random.fold_in(seeds[6], 71), 0),
        "stale_keys": draw_stale_keys(jax.random.fold_in(seeds[6], 71), 0),
        "stale_values": centred(seeds[2], (N_IMG, N_PATCH, SLOTS, BLK, HD), 1.0, 6.0, ((0, 32), (1, 16))),
        "text_kv": centred(seeds[3], (N_IMG, TXT, 2 * HD), 1.0, 6.0, ((0, 32),)),
        "group_slots": draw_group_slots(jax.random.fold_in(seeds[6], 71), 0),
        "text_len": draw_text_len(jax.random.fold_in(seeds[6], 71), 0),
    }


negative = -1.0e30


def attend(queries, query_ids, fresh_keys, fresh_values, keys, values, key_ids, key_live, text_keys, text_values, text_live):
    count_of_rows = queries.shape[0]
    blocks = fresh_keys.shape[0]
    rows_per_block = fresh_keys.shape[1]
    logit_scale = 1.0 / (HDIM ** 0.5)
    visible = key_live[None, :] & (key_ids[None, :] != query_ids[:, None])

    def per_head(head_index):
        offset = head_index * HDIM

        def head_slice(array):
            return lax.dynamic_slice_in_dim(array, offset, HDIM, array.ndim - 1)

        query_head = head_slice(queries)
        cache_keys = head_slice(keys)
        cache_values = head_slice(values)
        text_k = head_slice(text_keys)
        text_v = head_slice(text_values)
        local_image_keys = head_slice(fresh_keys)
        local_image_values = head_slice(fresh_values)
        text_scores = jnp.dot(query_head, text_k.T, preferred_element_type=jnp.float32) * logit_scale
        text_scores = jnp.where(text_live[None, :], text_scores, negative)
        cache_scores = jnp.dot(query_head, cache_keys.T, preferred_element_type=jnp.float32) * logit_scale
        cache_scores = jnp.where(visible, cache_scores, negative)
        query_block_list = query_head.reshape(blocks, rows_per_block, HDIM)
        local_image_scores = jnp.einsum("rin,rzn->riz", query_block_list.astype(jnp.float32), local_image_keys.astype(jnp.float32)).reshape(count_of_rows, rows_per_block) * logit_scale
        row_max = jnp.maximum(jnp.maximum(text_scores.max(axis=1), cache_scores.max(axis=1)), local_image_scores.max(axis=1))[:, None]
        text_weights = jnp.exp(text_scores - row_max)
        cache_weights = jnp.exp(cache_scores - row_max)
        own_weights = jnp.exp(local_image_scores - row_max)
        denominator = text_weights.sum(axis=1) + cache_weights.sum(axis=1) + own_weights.sum(axis=1)
        text_rounded = text_weights.astype(jnp.bfloat16)
        cache_rounded = cache_weights.astype(jnp.bfloat16)
        local_rounded_scores = own_weights.astype(jnp.bfloat16).reshape(blocks, rows_per_block, rows_per_block)
        summed = jnp.dot(text_rounded, text_v, preferred_element_type=jnp.float32)
        summed = summed + jnp.dot(cache_rounded, cache_values, preferred_element_type=jnp.float32)
        local_partial = jnp.einsum("tcj,tje->tce", local_rounded_scores.astype(jnp.float32), local_image_values.astype(jnp.float32))
        summed = summed + local_partial.reshape(count_of_rows, HDIM)
        return summed / denominator[:, None]

    head_count = queries.shape[1] // HDIM
    outputs = lax.map(per_head, jnp.arange(head_count, dtype=jnp.int32))
    return jnp.transpose(outputs, (1, 0, 2)).reshape(count_of_rows, head_count * HDIM)


def reference(fresh, stale_keys, stale_values, text_kv, group_slots, text_len):
    blocks = N_PATCH * SLOTS
    block_ids = (jnp.arange(blocks * BLK, dtype=jnp.int32) // BLK).astype(jnp.int32)

    def one_group(items):
        current, cache_keys, cache_values, text_pairs, live_slots, length = items
        queries = current[..., :HD].reshape(blocks * BLK, HD)
        local_image_keys = current[..., HD:2 * HD].reshape(blocks, BLK, HD)
        local_image_values = current[..., 2 * HD:].reshape(blocks, BLK, HD)
        live = (block_ids % SLOTS) < live_slots
        text_live = jnp.arange(TXT, dtype=jnp.int32) < length
        attended = attend(queries, block_ids, local_image_keys, local_image_values, cache_keys.reshape(blocks * BLK, HD), cache_values.reshape(blocks * BLK, HD), block_ids, live, text_pairs[:, :HD], text_pairs[:, HD:], text_live)
        attended = jnp.where(live[:, None], attended, jnp.float32(0.0)).astype(jnp.bfloat16)
        return attended.reshape(N_PATCH, SLOTS, BLK, HD)

    return lax.map(one_group, (fresh, stale_keys, stale_values, text_kv, group_slots, text_len))
```

```python
import functools

import jax
import jax.numpy as jnp
from jax import lax
from jax.experimental import pallas as pl
from jax.experimental.pallas import tpu as pltpu
from jax.sharding import PartitionSpec as P

MESH = pl.DeviceIdType.MESH
F32 = jnp.float32
BF16 = jnp.bfloat16

HDIM = 128
HEADS = 12
HD = HDIM * HEADS
BLK = 16
LIVE = 3
TXT = 128
PEERS = 16
ROWS = LIVE * BLK
BLOCKS = PEERS * LIVE
TBLOCKS = TXT // BLK
KBLOCKS = BLOCKS + TBLOCKS
CHUNKS = 4
CPEERS = PEERS // CHUNKS
CBLOCKS = BLOCKS // CHUNKS
CROWS = CBLOCKS * BLK
SCALE = 1.4426950408889634 / HDIM**0.5
MASKED = -1e30


def nt(a, b):
    return lax.dot_general(a, b, (((1,), (1,)), ((), ())), preferred_element_type=F32)


def owner_rank(peer, core):
    z, x = peer // 2, peer % 2
    return lax.rem(z + 15 - 2 * core - x, 4)


def owned_head(peer, core):
    z, x = peer // 2, peer % 2
    return (z // 4) * 6 + x * 3 + owner_rank(peer, core)


def partner(me, k):
    half = (k + 1) // 2
    odd = lax.rem(k, 2)
    offset = odd * half + (1 - odd) * (PEERS - half)
    return lax.rem(me + offset, PEERS)


def kernel(
    fresh, keys, values, text, slots, lengths, out,
    own, qbuf, kbuf, vbuf, qmask, kmask, pbuf, linv, osend, lsend, orecv, lrecv, ownout, ownlse, coef,
    own_sem, q_sem, k_sem, v_sem, o_sem, l_sem, send_sem, back_sem,
):
    image = lax.axis_index("img")
    me = lax.axis_index("patch")
    core = lax.rem(image, 2)
    my_rank = owner_rank(me, core)
    is_owner = my_rank < 3
    my_head = owned_head(me, core)

    barrier = pltpu.get_barrier_semaphore()

    def greet(k, carry):
        pl.semaphore_signal(barrier, inc=1, device_id=(image, partner(me, k)), device_id_type=MESH)
        return carry

    lax.fori_loop(1, PEERS, greet, 0)

    mine = pltpu.make_async_copy(fresh.at[pl.ds(0, LIVE)], own, own_sem)
    mine.start()

    def head_columns(head, third=0):
        return pl.ds(pl.multiple_of(third * HD + head * HDIM, HDIM), HDIM)

    def text_copies():
        where = pl.ds(BLOCKS, TBLOCKS)
        return (
            pltpu.make_async_copy(text.at[:, :, head_columns(my_head)], kbuf.at[where], k_sem),
            pltpu.make_async_copy(text.at[:, :, head_columns(my_head, 1)], vbuf.at[where], v_sem),
        )

    def own_copies():
        where = pl.ds(me * LIVE, LIVE)
        head = head_columns(my_head)
        return (
            pltpu.make_async_copy(keys.at[pl.ds(0, LIVE), :, head], kbuf.at[where], k_sem),
            pltpu.make_async_copy(fresh.at[pl.ds(0, LIVE), :, head], qbuf.at[where], q_sem),
            pltpu.make_async_copy(values.at[pl.ds(0, LIVE), :, head], vbuf.at[where], v_sem),
        )

    @pl.when(is_owner)
    def _():
        for copy in text_copies() + own_copies():
            copy.start()
        n = slots[image]
        length = lengths[image]
        shape = (KBLOCKS, BLK, HDIM)
        block = lax.broadcasted_iota(jnp.int32, shape, 0)
        row = lax.broadcasted_iota(jnp.int32, shape, 1)
        lane = lax.broadcasted_iota(jnp.int32, shape, 2)
        slot = block - 3 * ((block * 171) >> 9)
        dead = jnp.where(block < BLOCKS, slot - n, (block - BLOCKS) * BLK + row - length) >= 0
        hit = ((lane == block) & (block < BLOCKS)) | ((lane == HDIM - 1) & dead)
        kmask[...] = jnp.where(hit, MASKED, 0.0).astype(BF16)
        shape = (BLOCKS, BLK, HDIM)
        block = lax.broadcasted_iota(jnp.int32, shape, 0)
        lane = lax.broadcasted_iota(jnp.int32, shape, 2)
        qmask[...] = jnp.where((lane == block) | (lane == HDIM - 1), 1.0, 0.0).astype(BF16)

    pl.semaphore_wait(barrier, PEERS - 1)

    def outgoing(peer, which):
        head = head_columns(owned_head(peer, core))
        source = (keys, fresh, values)[which].at[pl.ds(0, LIVE), :, head]
        target = (kbuf, qbuf, vbuf)[which].at[pl.ds(me * LIVE, LIVE)]
        return pltpu.make_async_remote_copy(
            src_ref=source,
            dst_ref=target,
            send_sem=send_sem.at[peer, which],
            recv_sem=(k_sem, q_sem, v_sem)[which],
            device_id=(image, peer),
            device_id_type=MESH,
        )

    def each_owner(action):
        def body(k, carry):
            peer = partner(me, k)

            @pl.when(owner_rank(peer, core) < 3)
            def _():
                action(peer)

            return carry

        lax.fori_loop(1, PEERS, body, 0)

    def send_keys_queries(peer):
        outgoing(peer, 0).start()
        outgoing(peer, 1).start()

    def send_values(peer):
        outgoing(peer, 2).start()

    each_owner(send_keys_queries)
    each_owner(send_values)

    mine.wait()
    diagonal = (
        lax.broadcasted_iota(jnp.int32, (ROWS, ROWS), 0) // BLK
        == lax.broadcasted_iota(jnp.int32, (ROWS, ROWS), 1) // BLK
    )
    for head in range(HEADS):
        parts = [
            own[:, :, third * HD + head * HDIM : third * HD + (head + 1) * HDIM].reshape(ROWS, HDIM)
            for third in range(3)
        ]
        scores = jnp.where(diagonal, nt(parts[0], parts[1]), MASKED)
        top = jnp.max(scores, axis=1, keepdims=True)
        weights = jnp.exp2((scores - top) * SCALE)
        total = jnp.sum(weights, axis=1, keepdims=True)
        attended = jnp.dot(weights.astype(BF16), parts[2], preferred_element_type=F32)
        ownout[head] = attended / total
        ownlse[head] = jnp.broadcast_to(top * SCALE + jnp.log2(total), (ROWS, HDIM))

    def returning(peer, which):
        source = (osend.at[pl.ds(peer * LIVE, LIVE)], lsend.at[peer])[which]
        target = (orecv.at[my_head], lrecv.at[my_head])[which]
        return pltpu.make_async_remote_copy(
            src_ref=source,
            dst_ref=target,
            send_sem=back_sem.at[peer, which],
            recv_sem=(o_sem, l_sem)[which].at[my_head],
            device_id=(image, peer),
            device_id_type=MESH,
        )

    def staying(which):
        source = (osend.at[pl.ds(me * LIVE, LIVE)], lsend.at[me])[which]
        target = (orecv.at[my_head], lrecv.at[my_head])[which]
        return pltpu.make_async_copy(source, target, (o_sem, l_sem)[which].at[my_head])

    def send_back(first, count, which):
        def body(peer, carry):
            @pl.when(peer != me)
            def _():
                returning(peer, which).start()

            @pl.when(peer == me)
            def _():
                staying(which).start()

            return carry

        lax.fori_loop(first, first + count, body, 0)

    @pl.when(is_owner)
    def _():
        pltpu.make_async_copy(kbuf, kbuf, k_sem).wait()
        pltpu.make_async_copy(qbuf, qbuf, q_sem).wait()
        lane = lax.broadcasted_iota(jnp.int32, (ROWS, HDIM), 1)

        def score(chunk, stats):
            blocks = pl.ds(chunk * CBLOCKS, CBLOCKS)
            q = jnp.concatenate([qbuf[blocks].reshape(CROWS, HDIM), qmask[blocks].reshape(CROWS, HDIM)], axis=1)
            k = jnp.concatenate(
                [kbuf[...].reshape(KBLOCKS * BLK, HDIM), kmask[...].reshape(KBLOCKS * BLK, HDIM)], axis=1
            )
            scores = nt(q, k)
            top = jnp.max(scores, axis=1, keepdims=True)
            weights = jnp.exp2((scores - top) * SCALE)
            total = jnp.sum(weights, axis=1, keepdims=True)
            pbuf[chunk] = weights.astype(BF16)
            linv[chunk] = jnp.broadcast_to(1.0 / total, (CROWS, HDIM))
            lse = jnp.broadcast_to(top * SCALE + jnp.log2(total), (CROWS, HDIM))
            for i in range(CPEERS):
                stats = jnp.where(lane == chunk * CPEERS + i, lse[i * ROWS : (i + 1) * ROWS], stats)
            return stats

        stats = lax.fori_loop(0, CHUNKS, score, jnp.zeros((ROWS, HDIM), F32))
        turned = jnp.concatenate([stats, jnp.zeros((HDIM - ROWS, HDIM), F32)], axis=0).T
        for peer in range(PEERS):
            lsend[peer] = turned[peer : peer + 1]
        send_back(0, PEERS, 1)

        pltpu.make_async_copy(vbuf, vbuf, v_sem).wait()

        def attend(chunk, carry):
            v = vbuf[...].reshape(KBLOCKS * BLK, HDIM)
            attended = jnp.dot(pbuf[chunk], v, preferred_element_type=F32) * linv[chunk]
            osend[pl.ds(chunk * CBLOCKS, CBLOCKS)] = attended.astype(BF16).reshape(CBLOCKS, BLK, HDIM)
            send_back(chunk * CPEERS, CPEERS, 0)
            return carry

        lax.fori_loop(0, CHUNKS, attend, 0)

    for head in range(HEADS):
        pltpu.make_async_copy(lrecv.at[head], lrecv.at[head], l_sem.at[head]).wait()
    stacked = jnp.concatenate([lrecv[head] for head in range(HEADS)] + [jnp.zeros((HDIM - HEADS, HDIM), F32)], axis=0)
    columns = stacked.T
    for head in range(HEADS):
        sibling = jnp.broadcast_to(columns[:ROWS, head : head + 1], (ROWS, HDIM))
        local = ownlse[head]
        top = jnp.maximum(sibling, local)
        a = jnp.exp2(sibling - top)
        b = jnp.exp2(local - top)
        inverse = 1.0 / (a + b)
        coef[head] = a * inverse
        ownout[head] = ownout[head] * (b * inverse)
    for head in range(HEADS):
        pltpu.make_async_copy(orecv.at[head], orecv.at[head], o_sem.at[head]).wait()
        merged = orecv[head].reshape(ROWS, HDIM).astype(F32) * coef[head] + ownout[head]
        out[:, :, head * HDIM : (head + 1) * HDIM] = merged.astype(BF16).reshape(LIVE, BLK, HDIM)

    def finish_sends(peer):
        for which in range(3):
            outgoing(peer, which).wait_send()

    each_owner(finish_sends)

    @pl.when(is_owner)
    def _():
        def body(k, carry):
            peer = partner(me, k)
            returning(peer, 0).wait_send()
            returning(peer, 1).wait_send()
            return carry

        lax.fori_loop(1, PEERS, body, 0)


def attention(fresh, keys, values, text, slots, lengths):
    anywhere = pl.BlockSpec(memory_space=pl.ANY)
    scalars = pl.BlockSpec(memory_space=pltpu.SMEM)
    return pl.pallas_call(
        kernel,
        out_shape=jax.ShapeDtypeStruct((LIVE, BLK, HD), BF16),
        in_specs=[anywhere] * 4 + [scalars] * 2,
        out_specs=pl.BlockSpec(memory_space=pltpu.VMEM),
        scratch_shapes=[
            pltpu.VMEM((LIVE, BLK, 3 * HD), BF16),
            pltpu.VMEM((BLOCKS, BLK, HDIM), BF16),
            pltpu.VMEM((KBLOCKS, BLK, HDIM), BF16),
            pltpu.VMEM((KBLOCKS, BLK, HDIM), BF16),
            pltpu.VMEM((BLOCKS, BLK, HDIM), BF16),
            pltpu.VMEM((KBLOCKS, BLK, HDIM), BF16),
            pltpu.VMEM((CHUNKS, CROWS, KBLOCKS * BLK), BF16),
            pltpu.VMEM((CHUNKS, CROWS, HDIM), F32),
            pltpu.VMEM((BLOCKS, BLK, HDIM), BF16),
            pltpu.VMEM((PEERS, 1, HDIM), F32),
            pltpu.VMEM((HEADS, LIVE, BLK, HDIM), BF16),
            pltpu.VMEM((HEADS, 1, HDIM), F32),
            pltpu.VMEM((HEADS, ROWS, HDIM), F32),
            pltpu.VMEM((HEADS, ROWS, HDIM), F32),
            pltpu.VMEM((HEADS, ROWS, HDIM), F32),
            pltpu.SemaphoreType.DMA,
            pltpu.SemaphoreType.DMA,
            pltpu.SemaphoreType.DMA,
            pltpu.SemaphoreType.DMA,
            pltpu.SemaphoreType.DMA((HEADS,)),
            pltpu.SemaphoreType.DMA((HEADS,)),
            pltpu.SemaphoreType.DMA((PEERS, 3)),
            pltpu.SemaphoreType.DMA((PEERS, 2)),
        ],
        compiler_params=pltpu.CompilerParams(
            collective_id=0, has_side_effects=True, vmem_limit_bytes=40 * 1024 * 1024
        ),
    )(fresh, keys, values, text, slots, lengths)


def body(fresh, stale_keys, stale_values, text_kv, group_slots, text_len):
    slot_count = fresh.shape[2]
    text = text_kv[0].reshape(TBLOCKS, BLK, 2 * HD)
    merged = attention(fresh[0, 0], stale_keys[0, 0], stale_values[0, 0], text, group_slots, text_len)
    live = group_slots[lax.axis_index("img")]
    slot = lax.broadcasted_iota(jnp.int32, (slot_count, BLK, HD), 0)
    padded = jnp.pad(merged, ((0, slot_count - LIVE), (0, 0), (0, 0)))
    return jnp.where(slot < live, padded, jnp.zeros_like(padded))[None, None]


def solution(mesh):
    placed = (
        P("img", "patch", None, None, None),
        P("img", "patch", None, None, None),
        P("img", "patch", None, None, None),
        P("img", None, None),
        P(),
        P(),
    )
    return jax.shard_map(
        body,
        mesh=mesh,
        in_specs=placed,
        out_specs=P("img", "patch", None, None, None),
        check_vma=False,
    )
```

```python
import functools

import jax
import jax.numpy as jnp
from jax import lax
from jax.experimental import pallas as pl
from jax.experimental.pallas import tpu as pltpu
from jax.sharding import PartitionSpec as P

MESH = pl.DeviceIdType.MESH
F32 = jnp.float32
BF16 = jnp.bfloat16

HDIM = 128
HEADS = 12
HD = HDIM * HEADS
BLK = 16
LIVE = 3
TXT = 128
PEERS = 16
IMAGES = 32
ROWS = LIVE * BLK
BLOCKS = PEERS * LIVE
TBLOCKS = TXT // BLK
KBLOCKS = BLOCKS + TBLOCKS
CHUNKS = 4
CPEERS = PEERS // CHUNKS
CBLOCKS = BLOCKS // CHUNKS
CROWS = CBLOCKS * BLK
SCALE = 1.4426950408889634 / HDIM**0.5
MASKED = -1e30


def nt(a, b):
    return lax.dot_general(a, b, (((1,), (1,)), ((), ())), preferred_element_type=F32)


def owner_rank(peer, core):
    z, x = peer // 2, peer % 2
    return lax.rem(z + 15 - 2 * core - x, 4)


def owned_head(peer, core):
    z, x = peer // 2, peer % 2
    return (z // 4) * 6 + x * 3 + owner_rank(peer, core)


def partner(me, k):
    half = (k + 1) // 2
    odd = lax.rem(k, 2)
    offset = odd * half + (1 - odd) * (PEERS - half)
    return lax.rem(me + offset, PEERS)


def kernel(
    fresh, keys, values, text, slots_in, lengths_in, out,
    own, qbuf, kbuf, vbuf, qmask, kmask, pbuf, linv, osend, lsend, orecv, lrecv, ownout, ownlse, coef,
    counts, count_sem, own_sem, q_sem, k_sem, v_sem, o_sem, l_sem, send_sem, back_sem,
):
    image = lax.axis_index("img")
    me = lax.axis_index("patch")
    core = lax.rem(image, 2)
    my_rank = owner_rank(me, core)
    is_owner = my_rank < 3
    my_head = owned_head(me, core)

    barrier = pltpu.get_barrier_semaphore()

    def greet(k, carry):
        pl.semaphore_signal(barrier, inc=1, device_id=(image, partner(me, k)), device_id_type=MESH)
        return carry

    lax.fori_loop(1, PEERS, greet, 0)

    scalars = [
        pltpu.make_async_copy(source, counts.at[i], count_sem.at[i]) for i, source in enumerate((slots_in, lengths_in))
    ]
    for copy in scalars:
        copy.start()
    mine = pltpu.make_async_copy(fresh.at[pl.ds(0, LIVE)], own, own_sem)
    mine.start()

    def head_columns(head, third=0):
        return pl.ds(pl.multiple_of(third * HD + head * HDIM, HDIM), HDIM)

    def text_copies():
        where = pl.ds(BLOCKS, TBLOCKS)
        return (
            pltpu.make_async_copy(text.at[:, :, head_columns(my_head)], kbuf.at[where], k_sem),
            pltpu.make_async_copy(text.at[:, :, head_columns(my_head, 1)], vbuf.at[where], v_sem),
        )

    def own_copies():
        where = pl.ds(me * LIVE, LIVE)
        head = head_columns(my_head)
        return (
            pltpu.make_async_copy(keys.at[pl.ds(0, LIVE), :, head], kbuf.at[where], k_sem),
            pltpu.make_async_copy(fresh.at[pl.ds(0, LIVE), :, head], qbuf.at[where], q_sem),
            pltpu.make_async_copy(values.at[pl.ds(0, LIVE), :, head], vbuf.at[where], v_sem),
        )

    @pl.when(is_owner)
    def _():
        for copy in text_copies() + own_copies():
            copy.start()

    for copy in scalars:
        copy.wait()
    n = counts[0, image]
    length = counts[1, image]

    @pl.when(is_owner)
    def _():
        shape = (KBLOCKS, BLK, HDIM)
        block = lax.broadcasted_iota(jnp.int32, shape, 0)
        row = lax.broadcasted_iota(jnp.int32, shape, 1)
        lane = lax.broadcasted_iota(jnp.int32, shape, 2)
        slot = block - 3 * ((block * 171) >> 9)
        dead = jnp.where(block < BLOCKS, slot - n, (block - BLOCKS) * BLK + row - length) >= 0
        hit = ((lane == block) & (block < BLOCKS)) | ((lane == HDIM - 1) & dead)
        kmask[...] = jnp.where(hit, MASKED, 0.0).astype(BF16)
        shape = (BLOCKS, BLK, HDIM)
        block = lax.broadcasted_iota(jnp.int32, shape, 0)
        lane = lax.broadcasted_iota(jnp.int32, shape, 2)
        qmask[...] = jnp.where((lane == block) | (lane == HDIM - 1), 1.0, 0.0).astype(BF16)

    pl.semaphore_wait(barrier, PEERS - 1)

    def outgoing(peer, which):
        head = head_columns(owned_head(peer, core))
        source = (keys, fresh, values)[which].at[pl.ds(0, LIVE), :, head]
        target = (kbuf, qbuf, vbuf)[which].at[pl.ds(me * LIVE, LIVE)]
        return pltpu.make_async_remote_copy(
            src_ref=source,
            dst_ref=target,
            send_sem=send_sem.at[peer, which],
            recv_sem=(k_sem, q_sem, v_sem)[which],
            device_id=(image, peer),
            device_id_type=MESH,
        )

    def each_owner(action):
        def body(k, carry):
            peer = partner(me, k)

            @pl.when(owner_rank(peer, core) < 3)
            def _():
                action(peer)

            return carry

        lax.fori_loop(1, PEERS, body, 0)

    def send_keys_queries(peer):
        outgoing(peer, 0).start()
        outgoing(peer, 1).start()

    def send_values(peer):
        outgoing(peer, 2).start()

    each_owner(send_keys_queries)
    each_owner(send_values)

    mine.wait()
    diagonal = (
        lax.broadcasted_iota(jnp.int32, (ROWS, ROWS), 0) // BLK
        == lax.broadcasted_iota(jnp.int32, (ROWS, ROWS), 1) // BLK
    )
    for head in range(HEADS):
        parts = [
            own[:, :, third * HD + head * HDIM : third * HD + (head + 1) * HDIM].reshape(ROWS, HDIM)
            for third in range(3)
        ]
        scores = jnp.where(diagonal, nt(parts[0], parts[1]), MASKED)
        top = jnp.max(scores, axis=1, keepdims=True)
        weights = jnp.exp2((scores - top) * SCALE)
        total = jnp.sum(weights, axis=1, keepdims=True)
        attended = jnp.dot(weights.astype(BF16), parts[2], preferred_element_type=F32)
        ownout[head] = attended / total
        ownlse[head] = jnp.broadcast_to(top * SCALE + jnp.log2(total), (ROWS, HDIM))

    def returning(peer, which):
        source = (osend.at[pl.ds(peer * LIVE, LIVE)], lsend.at[peer])[which]
        target = (orecv.at[my_head], lrecv.at[my_head])[which]
        return pltpu.make_async_remote_copy(
            src_ref=source,
            dst_ref=target,
            send_sem=back_sem.at[peer, which],
            recv_sem=(o_sem, l_sem)[which].at[my_head],
            device_id=(image, peer),
            device_id_type=MESH,
        )

    def staying(which):
        source = (osend.at[pl.ds(me * LIVE, LIVE)], lsend.at[me])[which]
        target = (orecv.at[my_head], lrecv.at[my_head])[which]
        return pltpu.make_async_copy(source, target, (o_sem, l_sem)[which].at[my_head])

    def send_back(first, count, which):
        def body(peer, carry):
            @pl.when(peer != me)
            def _():
                returning(peer, which).start()

            @pl.when(peer == me)
            def _():
                staying(which).start()

            return carry

        lax.fori_loop(first, first + count, body, 0)

    @pl.when(is_owner)
    def _():
        pltpu.make_async_copy(kbuf, kbuf, k_sem).wait()
        pltpu.make_async_copy(qbuf, qbuf, q_sem).wait()
        lane = lax.broadcasted_iota(jnp.int32, (ROWS, HDIM), 1)

        def score(chunk, stats):
            blocks = pl.ds(chunk * CBLOCKS, CBLOCKS)
            q = jnp.concatenate([qbuf[blocks].reshape(CROWS, HDIM), qmask[blocks].reshape(CROWS, HDIM)], axis=1)
            k = jnp.concatenate(
                [kbuf[...].reshape(KBLOCKS * BLK, HDIM), kmask[...].reshape(KBLOCKS * BLK, HDIM)], axis=1
            )
            scores = nt(q, k)
            top = jnp.max(scores, axis=1, keepdims=True)
            weights = jnp.exp2((scores - top) * SCALE)
            total = jnp.sum(weights, axis=1, keepdims=True)
            pbuf[chunk] = weights.astype(BF16)
            linv[chunk] = jnp.broadcast_to(1.0 / total, (CROWS, HDIM))
            lse = jnp.broadcast_to(top * SCALE + jnp.log2(total), (CROWS, HDIM))
            for i in range(CPEERS):
                stats = jnp.where(lane == chunk * CPEERS + i, lse[i * ROWS : (i + 1) * ROWS], stats)
            return stats

        stats = lax.fori_loop(0, CHUNKS, score, jnp.zeros((ROWS, HDIM), F32))
        turned = jnp.concatenate([stats, jnp.zeros((HDIM - ROWS, HDIM), F32)], axis=0).T
        for peer in range(PEERS):
            lsend[peer] = turned[peer : peer + 1]
        send_back(0, PEERS, 1)

        pltpu.make_async_copy(vbuf, vbuf, v_sem).wait()

        def attend(chunk, carry):
            v = vbuf[...].reshape(KBLOCKS * BLK, HDIM)
            attended = jnp.dot(pbuf[chunk], v, preferred_element_type=F32) * linv[chunk]
            osend[pl.ds(chunk * CBLOCKS, CBLOCKS)] = attended.astype(BF16).reshape(CBLOCKS, BLK, HDIM)
            send_back(chunk * CPEERS, CPEERS, 0)
            return carry

        lax.fori_loop(0, CHUNKS, attend, 0)

    for head in range(HEADS):
        pltpu.make_async_copy(lrecv.at[head], lrecv.at[head], l_sem.at[head]).wait()
    stacked = jnp.concatenate([lrecv[head] for head in range(HEADS)] + [jnp.zeros((HDIM - HEADS, HDIM), F32)], axis=0)
    columns = stacked.T
    live = lax.broadcasted_iota(jnp.int32, (LIVE, BLK, HDIM), 0) < n
    for head in range(HEADS):
        sibling = jnp.broadcast_to(columns[:ROWS, head : head + 1], (ROWS, HDIM))
        local = ownlse[head]
        top = jnp.maximum(sibling, local)
        a = jnp.exp2(sibling - top)
        b = jnp.exp2(local - top)
        inverse = 1.0 / (a + b)
        coef[head] = a * inverse
        ownout[head] = ownout[head] * (b * inverse)
    for head in range(HEADS):
        pltpu.make_async_copy(orecv.at[head], orecv.at[head], o_sem.at[head]).wait()
        merged = orecv[head].reshape(ROWS, HDIM).astype(F32) * coef[head] + ownout[head]
        merged = jnp.where(live, merged.reshape(LIVE, BLK, HDIM), 0.0)
        out[:, :, head * HDIM : (head + 1) * HDIM] = merged.astype(BF16)

    def finish_sends(peer):
        for which in range(3):
            outgoing(peer, which).wait_send()

    each_owner(finish_sends)

    @pl.when(is_owner)
    def _():
        def body(k, carry):
            peer = partner(me, k)
            returning(peer, 0).wait_send()
            returning(peer, 1).wait_send()
            return carry

        lax.fori_loop(1, PEERS, body, 0)


def attention(fresh, keys, values, text, slots, lengths):
    anywhere = pl.BlockSpec(memory_space=pltpu.HBM)
    return pl.pallas_call(
        kernel,
        out_shape=jax.ShapeDtypeStruct((LIVE, BLK, HD), BF16),
        in_specs=[anywhere] * 6,
        out_specs=pl.BlockSpec(memory_space=pltpu.VMEM),
        scratch_shapes=[
            pltpu.VMEM((LIVE, BLK, 3 * HD), BF16),
            pltpu.VMEM((BLOCKS, BLK, HDIM), BF16),
            pltpu.VMEM((KBLOCKS, BLK, HDIM), BF16),
            pltpu.VMEM((KBLOCKS, BLK, HDIM), BF16),
            pltpu.VMEM((BLOCKS, BLK, HDIM), BF16),
            pltpu.VMEM((KBLOCKS, BLK, HDIM), BF16),
            pltpu.VMEM((CHUNKS, CROWS, KBLOCKS * BLK), BF16),
            pltpu.VMEM((CHUNKS, CROWS, HDIM), F32),
            pltpu.VMEM((BLOCKS, BLK, HDIM), BF16),
            pltpu.VMEM((PEERS, 1, HDIM), F32),
            pltpu.VMEM((HEADS, LIVE, BLK, HDIM), BF16),
            pltpu.VMEM((HEADS, 1, HDIM), F32),
            pltpu.VMEM((HEADS, ROWS, HDIM), F32),
            pltpu.VMEM((HEADS, ROWS, HDIM), F32),
            pltpu.VMEM((HEADS, ROWS, HDIM), F32),
            pltpu.SMEM((2, IMAGES), jnp.int32),
            pltpu.SemaphoreType.DMA((2,)),
            pltpu.SemaphoreType.DMA,
            pltpu.SemaphoreType.DMA,
            pltpu.SemaphoreType.DMA,
            pltpu.SemaphoreType.DMA,
            pltpu.SemaphoreType.DMA((HEADS,)),
            pltpu.SemaphoreType.DMA((HEADS,)),
            pltpu.SemaphoreType.DMA((PEERS, 3)),
            pltpu.SemaphoreType.DMA((PEERS, 2)),
        ],
        compiler_params=pltpu.CompilerParams(
            collective_id=0, has_side_effects=True, vmem_limit_bytes=60 * 1024 * 1024
        ),
    )(fresh, keys, values, text, slots, lengths)


def body(fresh, stale_keys, stale_values, text_kv, group_slots, text_len):
    slot_count = fresh.shape[2]
    text = text_kv[0].reshape(TBLOCKS, BLK, 2 * HD)
    merged = attention(fresh[0, 0], stale_keys[0, 0], stale_values[0, 0], text, group_slots, text_len)
    return jnp.pad(merged, ((0, slot_count - LIVE), (0, 0), (0, 0)))[None, None]


def solution(mesh):
    placed = (
        P("img", "patch", None, None, None),
        P("img", "patch", None, None, None),
        P("img", "patch", None, None, None),
        P("img", None, None),
        P(),
        P(),
    )
    return jax.shard_map(
        body,
        mesh=mesh,
        in_specs=placed,
        out_specs=P("img", "patch", None, None, None),
        check_vma=False,
    )
```

```python
import functools

import jax
import jax.numpy as jnp
from jax import lax
from jax.experimental import pallas as pl
from jax.experimental.pallas import tpu as pltpu
from jax.sharding import PartitionSpec as P

MESH = pl.DeviceIdType.MESH
F32 = jnp.float32
BF16 = jnp.bfloat16

HDIM = 128
HEADS = 12
HD = HDIM * HEADS
BLK = 16
LIVE = 3
TXT = 128
PEERS = 16
IMAGES = 32
ROWS = LIVE * BLK
BLOCKS = PEERS * LIVE
TBLOCKS = TXT // BLK
KBLOCKS = BLOCKS + TBLOCKS
CHUNKS = 4
CPEERS = PEERS // CHUNKS
CBLOCKS = BLOCKS // CHUNKS
CROWS = CBLOCKS * BLK
SCALE = 1.4426950408889634 / HDIM**0.5
MASKED = -1e30


def nt(a, b):
    return lax.dot_general(a, b, (((1,), (1,)), ((), ())), preferred_element_type=F32)


def owner_rank(peer, core):
    z, x = peer // 2, peer % 2
    return lax.rem(z + 15 - 2 * core - x, 4)


def owned_head(peer, core):
    z, x = peer // 2, peer % 2
    return (z // 4) * 6 + x * 3 + owner_rank(peer, core)


def partner(me, k):
    half = (k + 1) // 2
    odd = lax.rem(k, 2)
    offset = odd * half + (1 - odd) * (PEERS - half)
    return lax.rem(me + offset, PEERS)


def kernel(
    fresh, keys, values, text, slots_in, lengths_in, out,
    own, qbuf, kbuf, vbuf, qmask, kmask, pbuf, linv, osend, lsend, orecv, lrecv, ownout, ownlse, coef,
    counts, count_sem, own_sem, q_sem, k_sem, v_sem, o_sem, l_sem, send_sem, back_sem,
):
    image = lax.axis_index("img")
    me = lax.axis_index("patch")
    core = lax.rem(image, 2)
    my_rank = owner_rank(me, core)
    is_owner = my_rank < 3
    my_head = owned_head(me, core)

    barrier = pltpu.get_barrier_semaphore()

    def greet(k, carry):
        pl.semaphore_signal(barrier, inc=1, device_id=(image, partner(me, k)), device_id_type=MESH)
        return carry

    lax.fori_loop(1, PEERS, greet, 0)

    scalars = [
        pltpu.make_async_copy(source, counts.at[i], count_sem.at[i]) for i, source in enumerate((slots_in, lengths_in))
    ]
    for copy in scalars:
        copy.start()
    mine = pltpu.make_async_copy(fresh.at[pl.ds(0, LIVE)], own, own_sem)
    mine.start()

    def head_columns(head, third=0):
        return pl.ds(pl.multiple_of(third * HD + head * HDIM, HDIM), HDIM)

    def text_copies():
        where = pl.ds(BLOCKS, TBLOCKS)
        return (
            pltpu.make_async_copy(text.at[:, :, head_columns(my_head)], kbuf.at[where], k_sem),
            pltpu.make_async_copy(text.at[:, :, head_columns(my_head, 1)], vbuf.at[where], v_sem),
        )

    def own_copies():
        where = pl.ds(me * LIVE, LIVE)
        head = head_columns(my_head)
        return (
            pltpu.make_async_copy(keys.at[pl.ds(0, LIVE), :, head], kbuf.at[where], k_sem),
            pltpu.make_async_copy(fresh.at[pl.ds(0, LIVE), :, head], qbuf.at[where], q_sem),
            pltpu.make_async_copy(values.at[pl.ds(0, LIVE), :, head], vbuf.at[where], v_sem),
        )

    pl.semaphore_wait(barrier, PEERS - 1)

    def outgoing(peer, which):
        head = head_columns(owned_head(peer, core))
        source = (keys, fresh, values)[which].at[pl.ds(0, LIVE), :, head]
        target = (kbuf, qbuf, vbuf)[which].at[pl.ds(me * LIVE, LIVE)]
        return pltpu.make_async_remote_copy(
            src_ref=source,
            dst_ref=target,
            send_sem=send_sem.at[peer, which],
            recv_sem=(k_sem, q_sem, v_sem)[which],
            device_id=(image, peer),
            device_id_type=MESH,
        )

    def each_owner(action):
        def body(k, carry):
            peer = partner(me, k)

            @pl.when(owner_rank(peer, core) < 3)
            def _():
                action(peer)

            return carry

        lax.fori_loop(1, PEERS, body, 0)

    def send_keys_queries(peer):
        outgoing(peer, 0).start()
        outgoing(peer, 1).start()

    def send_values(peer):
        outgoing(peer, 2).start()

    each_owner(send_keys_queries)
    each_owner(send_values)

    @pl.when(is_owner)
    def _():
        for copy in text_copies() + own_copies():
            copy.start()

    for copy in scalars:
        copy.wait()
    n = counts[0, image]
    length = counts[1, image]

    @pl.when(is_owner)
    def _():
        shape = (KBLOCKS, BLK, HDIM)
        block = lax.broadcasted_iota(jnp.int32, shape, 0)
        row = lax.broadcasted_iota(jnp.int32, shape, 1)
        lane = lax.broadcasted_iota(jnp.int32, shape, 2)
        slot = block - 3 * ((block * 171) >> 9)
        dead = jnp.where(block < BLOCKS, slot - n, (block - BLOCKS) * BLK + row - length) >= 0
        hit = ((lane == block) & (block < BLOCKS)) | ((lane == HDIM - 1) & dead)
        kmask[...] = jnp.where(hit, MASKED, 0.0).astype(BF16)
        shape = (BLOCKS, BLK, HDIM)
        block = lax.broadcasted_iota(jnp.int32, shape, 0)
        lane = lax.broadcasted_iota(jnp.int32, shape, 2)
        qmask[...] = jnp.where((lane == block) | (lane == HDIM - 1), 1.0, 0.0).astype(BF16)

    mine.wait()
    diagonal = (
        lax.broadcasted_iota(jnp.int32, (ROWS, ROWS), 0) // BLK
        == lax.broadcasted_iota(jnp.int32, (ROWS, ROWS), 1) // BLK
    )
    for head in range(HEADS):
        parts = [
            own[:, :, third * HD + head * HDIM : third * HD + (head + 1) * HDIM].reshape(ROWS, HDIM)
            for third in range(3)
        ]
        scores = jnp.where(diagonal, nt(parts[0], parts[1]), MASKED)
        top = jnp.max(scores, axis=1, keepdims=True)
        weights = jnp.exp2((scores - top) * SCALE)
        total = jnp.sum(weights, axis=1, keepdims=True)
        attended = jnp.dot(weights.astype(BF16), parts[2], preferred_element_type=F32)
        ownout[head] = attended / total
        ownlse[head] = jnp.broadcast_to(top * SCALE + jnp.log2(total), (ROWS, HDIM))

    def returning(peer, which):
        source = (osend.at[pl.ds(peer * LIVE, LIVE)], lsend.at[peer])[which]
        target = (orecv.at[my_head], lrecv.at[my_head])[which]
        return pltpu.make_async_remote_copy(
            src_ref=source,
            dst_ref=target,
            send_sem=back_sem.at[peer, which],
            recv_sem=(o_sem, l_sem)[which].at[my_head],
            device_id=(image, peer),
            device_id_type=MESH,
        )

    def staying(which):
        source = (osend.at[pl.ds(me * LIVE, LIVE)], lsend.at[me])[which]
        target = (orecv.at[my_head], lrecv.at[my_head])[which]
        return pltpu.make_async_copy(source, target, (o_sem, l_sem)[which].at[my_head])

    def send_back(first, count, which):
        def body(peer, carry):
            @pl.when(peer != me)
            def _():
                returning(peer, which).start()

            @pl.when(peer == me)
            def _():
                staying(which).start()

            return carry

        lax.fori_loop(first, first + count, body, 0)

    @pl.when(is_owner)
    def _():
        pltpu.make_async_copy(kbuf, kbuf, k_sem).wait()
        pltpu.make_async_copy(qbuf, qbuf, q_sem).wait()
        lane = lax.broadcasted_iota(jnp.int32, (ROWS, HDIM), 1)

        def score(chunk, stats):
            blocks = pl.ds(chunk * CBLOCKS, CBLOCKS)
            q = jnp.concatenate([qbuf[blocks].reshape(CROWS, HDIM), qmask[blocks].reshape(CROWS, HDIM)], axis=1)
            k = jnp.concatenate(
                [kbuf[...].reshape(KBLOCKS * BLK, HDIM), kmask[...].reshape(KBLOCKS * BLK, HDIM)], axis=1
            )
            scores = nt(q, k)
            top = jnp.max(scores, axis=1, keepdims=True)
            weights = jnp.exp2((scores - top) * SCALE)
            total = jnp.sum(weights, axis=1, keepdims=True)
            pbuf[chunk] = weights.astype(BF16)
            linv[chunk] = jnp.broadcast_to(1.0 / total, (CROWS, HDIM))
            lse = jnp.broadcast_to(top * SCALE + jnp.log2(total), (CROWS, HDIM))
            for i in range(CPEERS):
                stats = jnp.where(lane == chunk * CPEERS + i, lse[i * ROWS : (i + 1) * ROWS], stats)
            return stats

        stats = lax.fori_loop(0, CHUNKS, score, jnp.zeros((ROWS, HDIM), F32))
        turned = jnp.concatenate([stats, jnp.zeros((HDIM - ROWS, HDIM), F32)], axis=0).T
        for peer in range(PEERS):
            lsend[peer] = turned[peer : peer + 1]
        send_back(0, PEERS, 1)

        pltpu.make_async_copy(vbuf, vbuf, v_sem).wait()

        def attend(chunk, carry):
            v = vbuf[...].reshape(KBLOCKS * BLK, HDIM)
            attended = jnp.dot(pbuf[chunk], v, preferred_element_type=F32) * linv[chunk]
            osend[pl.ds(chunk * CBLOCKS, CBLOCKS)] = attended.astype(BF16).reshape(CBLOCKS, BLK, HDIM)
            send_back(chunk * CPEERS, CPEERS, 0)
            return carry

        lax.fori_loop(0, CHUNKS, attend, 0)

    def finish_sends(peer):
        for which in range(3):
            outgoing(peer, which).wait_send()

    each_owner(finish_sends)

    for head in range(HEADS):
        pltpu.make_async_copy(lrecv.at[head], lrecv.at[head], l_sem.at[head]).wait()
    stacked = jnp.concatenate([lrecv[head] for head in range(HEADS)] + [jnp.zeros((HDIM - HEADS, HDIM), F32)], axis=0)
    columns = stacked.T
    live = lax.broadcasted_iota(jnp.int32, (LIVE, BLK, HDIM), 0) < n
    for head in range(HEADS):
        sibling = jnp.broadcast_to(columns[:ROWS, head : head + 1], (ROWS, HDIM))
        local = ownlse[head]
        top = jnp.maximum(sibling, local)
        a = jnp.exp2(sibling - top)
        b = jnp.exp2(local - top)
        inverse = 1.0 / (a + b)
        coef[head] = a * inverse
        ownout[head] = ownout[head] * (b * inverse)
    for head in range(HEADS):
        pltpu.make_async_copy(orecv.at[head], orecv.at[head], o_sem.at[head]).wait()
        merged = orecv[head].reshape(ROWS, HDIM).astype(F32) * coef[head] + ownout[head]
        merged = jnp.where(live, merged.reshape(LIVE, BLK, HDIM), 0.0)
        out[:, :, head * HDIM : (head + 1) * HDIM] = merged.astype(BF16)

    @pl.when(is_owner)
    def _():
        def body(k, carry):
            peer = partner(me, k)
            returning(peer, 0).wait_send()
            returning(peer, 1).wait_send()
            return carry

        lax.fori_loop(1, PEERS, body, 0)


def attention(fresh, keys, values, text, slots, lengths):
    anywhere = pl.BlockSpec(memory_space=pl.ANY)
    return pl.pallas_call(
        kernel,
        out_shape=jax.ShapeDtypeStruct((LIVE, BLK, HD), BF16),
        in_specs=[anywhere] * 6,
        out_specs=pl.BlockSpec(memory_space=pltpu.VMEM),
        scratch_shapes=[
            pltpu.VMEM((LIVE, BLK, 3 * HD), BF16),
            pltpu.VMEM((BLOCKS, BLK, HDIM), BF16),
            pltpu.VMEM((KBLOCKS, BLK, HDIM), BF16),
            pltpu.VMEM((KBLOCKS, BLK, HDIM), BF16),
            pltpu.VMEM((BLOCKS, BLK, HDIM), BF16),
            pltpu.VMEM((KBLOCKS, BLK, HDIM), BF16),
            pltpu.VMEM((CHUNKS, CROWS, KBLOCKS * BLK), BF16),
            pltpu.VMEM((CHUNKS, CROWS, HDIM), F32),
            pltpu.VMEM((BLOCKS, BLK, HDIM), BF16),
            pltpu.VMEM((PEERS, 1, HDIM), F32),
            pltpu.VMEM((HEADS, LIVE, BLK, HDIM), BF16),
            pltpu.VMEM((HEADS, 1, HDIM), F32),
            pltpu.VMEM((HEADS, ROWS, HDIM), F32),
            pltpu.VMEM((HEADS, ROWS, HDIM), F32),
            pltpu.VMEM((HEADS, ROWS, HDIM), F32),
            pltpu.SMEM((2, IMAGES), jnp.int32),
            pltpu.SemaphoreType.DMA((2,)),
            pltpu.SemaphoreType.DMA,
            pltpu.SemaphoreType.DMA,
            pltpu.SemaphoreType.DMA,
            pltpu.SemaphoreType.DMA,
            pltpu.SemaphoreType.DMA((HEADS,)),
            pltpu.SemaphoreType.DMA((HEADS,)),
            pltpu.SemaphoreType.DMA((PEERS, 3)),
            pltpu.SemaphoreType.DMA((PEERS, 2)),
        ],
        compiler_params=pltpu.CompilerParams(
            collective_id=0, has_side_effects=True, vmem_limit_bytes=24 * 1024 * 1024
        ),
    )(*[pltpu.with_memory_space_constraint(x, pltpu.HBM) for x in (fresh, keys, values, text, slots, lengths)])


def body(fresh, stale_keys, stale_values, text_kv, group_slots, text_len):
    slot_count = fresh.shape[2]
    text = text_kv[0].reshape(TBLOCKS, BLK, 2 * HD)
    merged = attention(fresh[0, 0], stale_keys[0, 0], stale_values[0, 0], text, group_slots, text_len)
    return jnp.pad(merged, ((0, slot_count - LIVE), (0, 0), (0, 0)))[None, None]


def solution(mesh):
    placed = (
        P("img", "patch", None, None, None),
        P("img", "patch", None, None, None),
        P("img", "patch", None, None, None),
        P("img", None, None),
        P(),
        P(),
    )
    return jax.shard_map(
        body,
        mesh=mesh,
        in_specs=placed,
        out_specs=P("img", "patch", None, None, None),
        check_vma=False,
    )
```

```python
import functools

import jax
import jax.numpy as jnp
from jax import lax
from jax.experimental import pallas as pl
from jax.experimental.pallas import tpu as pltpu
from jax.sharding import PartitionSpec as P

MESH = pl.DeviceIdType.MESH
F32 = jnp.float32
BF16 = jnp.bfloat16

HDIM = 128
HEADS = 12
HD = HDIM * HEADS
BLK = 16
LIVE = 3
TXT = 128
PEERS = 16
IMAGES = 32
ROWS = LIVE * BLK
BLOCKS = PEERS * LIVE
TBLOCKS = TXT // BLK
KBLOCKS = BLOCKS + TBLOCKS
CHUNKS = 4
CPEERS = PEERS // CHUNKS
CBLOCKS = BLOCKS // CHUNKS
CROWS = CBLOCKS * BLK
SCALE = 1.4426950408889634 / HDIM**0.5
MASKED = -1e30


def nt(a, b):
    return lax.dot_general(a, b, (((1,), (1,)), ((), ())), preferred_element_type=F32)


def owner_rank(peer, core):
    z, x = peer // 2, peer % 2
    return lax.rem(z + 15 - 2 * core - x, 4)


def owned_head(peer, core):
    z, x = peer // 2, peer % 2
    return (z // 4) * 6 + x * 3 + owner_rank(peer, core)


def partner(me, k):
    half = k // 2
    odd = lax.rem(k, 2)
    offset = PEERS // 2 + odd * half - (1 - odd) * half
    return lax.rem(me + offset, PEERS)


def kernel(
    fresh, keys, values, text, slots_in, lengths_in, out,
    own, qbuf, kbuf, vbuf, qmask, kmask, pbuf, linv, osend, lsend, orecv, lrecv, ownout, ownlse, coef,
    counts, count_sem, own_sem, q_sem, k_sem, v_sem, o_sem, l_sem, send_sem, back_sem,
):
    image = lax.axis_index("img")
    me = lax.axis_index("patch")
    core = lax.rem(image, 2)
    my_rank = owner_rank(me, core)
    is_owner = my_rank < 3
    my_head = owned_head(me, core)

    barrier = pltpu.get_barrier_semaphore()

    def greet(k, carry):
        pl.semaphore_signal(barrier, inc=1, device_id=(image, partner(me, k)), device_id_type=MESH)
        return carry

    lax.fori_loop(1, PEERS, greet, 0)

    scalars = [
        pltpu.make_async_copy(source, counts.at[i], count_sem.at[i]) for i, source in enumerate((slots_in, lengths_in))
    ]
    for copy in scalars:
        copy.start()
    mine = pltpu.make_async_copy(fresh.at[pl.ds(0, LIVE)], own, own_sem)
    mine.start()

    def head_columns(head, third=0):
        return pl.ds(pl.multiple_of(third * HD + head * HDIM, HDIM), HDIM)

    def text_copies():
        where = pl.ds(BLOCKS, TBLOCKS)
        return (
            pltpu.make_async_copy(text.at[:, :, head_columns(my_head)], kbuf.at[where], k_sem),
            pltpu.make_async_copy(text.at[:, :, head_columns(my_head, 1)], vbuf.at[where], v_sem),
        )

    def own_copies():
        where = pl.ds(me * LIVE, LIVE)
        head = head_columns(my_head)
        return (
            pltpu.make_async_copy(keys.at[pl.ds(0, LIVE), :, head], kbuf.at[where], k_sem),
            pltpu.make_async_copy(fresh.at[pl.ds(0, LIVE), :, head], qbuf.at[where], q_sem),
            pltpu.make_async_copy(values.at[pl.ds(0, LIVE), :, head], vbuf.at[where], v_sem),
        )

    pl.semaphore_wait(barrier, PEERS - 1)

    def outgoing(peer, which):
        head = head_columns(owned_head(peer, core))
        source = (keys, fresh, values)[which].at[pl.ds(0, LIVE), :, head]
        target = (kbuf, qbuf, vbuf)[which].at[pl.ds(me * LIVE, LIVE)]
        return pltpu.make_async_remote_copy(
            src_ref=source,
            dst_ref=target,
            send_sem=send_sem.at[peer, which],
            recv_sem=(k_sem, q_sem, v_sem)[which],
            device_id=(image, peer),
            device_id_type=MESH,
        )

    def each_owner(action):
        def body(k, carry):
            peer = partner(me, k)

            @pl.when(owner_rank(peer, core) < 3)
            def _():
                action(peer)

            return carry

        lax.fori_loop(1, PEERS, body, 0)

    def send_keys_queries(peer):
        outgoing(peer, 0).start()
        outgoing(peer, 1).start()

    def send_values(peer):
        outgoing(peer, 2).start()

    each_owner(send_keys_queries)
    each_owner(send_values)

    @pl.when(is_owner)
    def _():
        for copy in text_copies() + own_copies():
            copy.start()

    for copy in scalars:
        copy.wait()
    n = counts[0, image]
    length = counts[1, image]

    @pl.when(is_owner)
    def _():
        shape = (KBLOCKS, BLK, HDIM)
        block = lax.broadcasted_iota(jnp.int32, shape, 0)
        row = lax.broadcasted_iota(jnp.int32, shape, 1)
        lane = lax.broadcasted_iota(jnp.int32, shape, 2)
        slot = block - 3 * ((block * 171) >> 9)
        dead = jnp.where(block < BLOCKS, slot - n, (block - BLOCKS) * BLK + row - length) >= 0
        hit = ((lane == block) & (block < BLOCKS)) | ((lane == HDIM - 1) & dead)
        kmask[...] = jnp.where(hit, MASKED, 0.0).astype(BF16)
        shape = (BLOCKS, BLK, HDIM)
        block = lax.broadcasted_iota(jnp.int32, shape, 0)
        lane = lax.broadcasted_iota(jnp.int32, shape, 2)
        qmask[...] = jnp.where((lane == block) | (lane == HDIM - 1), 1.0, 0.0).astype(BF16)

    mine.wait()
    diagonal = (
        lax.broadcasted_iota(jnp.int32, (ROWS, ROWS), 0) // BLK
        == lax.broadcasted_iota(jnp.int32, (ROWS, ROWS), 1) // BLK
    )
    for head in range(HEADS):
        parts = [
            own[:, :, third * HD + head * HDIM : third * HD + (head + 1) * HDIM].reshape(ROWS, HDIM)
            for third in range(3)
        ]
        scores = jnp.where(diagonal, nt(parts[0], parts[1]), MASKED)
        top = jnp.max(scores, axis=1, keepdims=True)
        weights = jnp.exp2((scores - top) * SCALE)
        total = jnp.sum(weights, axis=1, keepdims=True)
        attended = jnp.dot(weights.astype(BF16), parts[2], preferred_element_type=F32)
        ownout[head] = attended / total
        ownlse[head] = jnp.broadcast_to(top * SCALE + jnp.log2(total), (ROWS, HDIM))

    def returning(peer, which):
        source = (osend.at[pl.ds(peer * LIVE, LIVE)], lsend.at[peer])[which]
        target = (orecv.at[my_head], lrecv.at[my_head])[which]
        return pltpu.make_async_remote_copy(
            src_ref=source,
            dst_ref=target,
            send_sem=back_sem.at[peer, which],
            recv_sem=(o_sem, l_sem)[which].at[my_head],
            device_id=(image, peer),
            device_id_type=MESH,
        )

    def staying(which):
        source = (osend.at[pl.ds(me * LIVE, LIVE)], lsend.at[me])[which]
        target = (orecv.at[my_head], lrecv.at[my_head])[which]
        return pltpu.make_async_copy(source, target, (o_sem, l_sem)[which].at[my_head])

    def send_back(first, count, which):
        def body(peer, carry):
            @pl.when(peer != me)
            def _():
                returning(peer, which).start()

            @pl.when(peer == me)
            def _():
                staying(which).start()

            return carry

        lax.fori_loop(first, first + count, body, 0)

    @pl.when(is_owner)
    def _():
        pltpu.make_async_copy(kbuf, kbuf, k_sem).wait()
        pltpu.make_async_copy(qbuf, qbuf, q_sem).wait()
        lane = lax.broadcasted_iota(jnp.int32, (ROWS, HDIM), 1)

        def score(chunk, stats):
            blocks = pl.ds(chunk * CBLOCKS, CBLOCKS)
            q = jnp.concatenate([qbuf[blocks].reshape(CROWS, HDIM), qmask[blocks].reshape(CROWS, HDIM)], axis=1)
            k = jnp.concatenate(
                [kbuf[...].reshape(KBLOCKS * BLK, HDIM), kmask[...].reshape(KBLOCKS * BLK, HDIM)], axis=1
            )
            scores = nt(q, k)
            top = jnp.max(scores, axis=1, keepdims=True)
            weights = jnp.exp2((scores - top) * SCALE)
            total = jnp.sum(weights, axis=1, keepdims=True)
            pbuf[chunk] = weights.astype(BF16)
            linv[chunk] = jnp.broadcast_to(1.0 / total, (CROWS, HDIM))
            lse = jnp.broadcast_to(top * SCALE + jnp.log2(total), (CROWS, HDIM))
            for i in range(CPEERS):
                stats = jnp.where(lane == chunk * CPEERS + i, lse[i * ROWS : (i + 1) * ROWS], stats)
            return stats

        stats = lax.fori_loop(0, CHUNKS, score, jnp.zeros((ROWS, HDIM), F32))
        turned = jnp.concatenate([stats, jnp.zeros((HDIM - ROWS, HDIM), F32)], axis=0).T
        for peer in range(PEERS):
            lsend[peer] = turned[peer : peer + 1]
        send_back(0, PEERS, 1)

        pltpu.make_async_copy(vbuf, vbuf, v_sem).wait()

        def attend(chunk, carry):
            v = vbuf[...].reshape(KBLOCKS * BLK, HDIM)
            attended = jnp.dot(pbuf[chunk], v, preferred_element_type=F32) * linv[chunk]
            osend[pl.ds(chunk * CBLOCKS, CBLOCKS)] = attended.astype(BF16).reshape(CBLOCKS, BLK, HDIM)
            send_back(chunk * CPEERS, CPEERS, 0)
            return carry

        lax.fori_loop(0, CHUNKS, attend, 0)

    def finish_sends(peer):
        for which in range(3):
            outgoing(peer, which).wait_send()

    each_owner(finish_sends)

    for head in range(HEADS):
        pltpu.make_async_copy(lrecv.at[head], lrecv.at[head], l_sem.at[head]).wait()
    stacked = jnp.concatenate([lrecv[head] for head in range(HEADS)] + [jnp.zeros((HDIM - HEADS, HDIM), F32)], axis=0)
    columns = stacked.T
    live = lax.broadcasted_iota(jnp.int32, (LIVE, BLK, HDIM), 0) < n
    for head in range(HEADS):
        sibling = jnp.broadcast_to(columns[:ROWS, head : head + 1], (ROWS, HDIM))
        local = ownlse[head]
        top = jnp.maximum(sibling, local)
        a = jnp.exp2(sibling - top)
        b = jnp.exp2(local - top)
        inverse = 1.0 / (a + b)
        coef[head] = a * inverse
        ownout[head] = ownout[head] * (b * inverse)
    for head in range(HEADS):
        pltpu.make_async_copy(orecv.at[head], orecv.at[head], o_sem.at[head]).wait()
        merged = orecv[head].reshape(ROWS, HDIM).astype(F32) * coef[head] + ownout[head]
        merged = jnp.where(live, merged.reshape(LIVE, BLK, HDIM), 0.0)
        out[:, :, head * HDIM : (head + 1) * HDIM] = merged.astype(BF16)

    @pl.when(is_owner)
    def _():
        def body(k, carry):
            peer = partner(me, k)
            returning(peer, 0).wait_send()
            returning(peer, 1).wait_send()
            return carry

        lax.fori_loop(1, PEERS, body, 0)


def attention(fresh, keys, values, text, slots, lengths):
    anywhere = pl.BlockSpec(memory_space=pl.ANY)
    return pl.pallas_call(
        kernel,
        out_shape=jax.ShapeDtypeStruct((LIVE, BLK, HD), BF16),
        in_specs=[anywhere] * 6,
        out_specs=pl.BlockSpec(memory_space=pltpu.VMEM),
        scratch_shapes=[
            pltpu.VMEM((LIVE, BLK, 3 * HD), BF16),
            pltpu.VMEM((BLOCKS, BLK, HDIM), BF16),
            pltpu.VMEM((KBLOCKS, BLK, HDIM), BF16),
            pltpu.VMEM((KBLOCKS, BLK, HDIM), BF16),
            pltpu.VMEM((BLOCKS, BLK, HDIM), BF16),
            pltpu.VMEM((KBLOCKS, BLK, HDIM), BF16),
            pltpu.VMEM((CHUNKS, CROWS, KBLOCKS * BLK), BF16),
            pltpu.VMEM((CHUNKS, CROWS, HDIM), F32),
            pltpu.VMEM((BLOCKS, BLK, HDIM), BF16),
            pltpu.VMEM((PEERS, 1, HDIM), F32),
            pltpu.VMEM((HEADS, LIVE, BLK, HDIM), BF16),
            pltpu.VMEM((HEADS, 1, HDIM), F32),
            pltpu.VMEM((HEADS, ROWS, HDIM), F32),
            pltpu.VMEM((HEADS, ROWS, HDIM), F32),
            pltpu.VMEM((HEADS, ROWS, HDIM), F32),
            pltpu.SMEM((2, IMAGES), jnp.int32),
            pltpu.SemaphoreType.DMA((2,)),
            pltpu.SemaphoreType.DMA,
            pltpu.SemaphoreType.DMA,
            pltpu.SemaphoreType.DMA,
            pltpu.SemaphoreType.DMA,
            pltpu.SemaphoreType.DMA((HEADS,)),
            pltpu.SemaphoreType.DMA((HEADS,)),
            pltpu.SemaphoreType.DMA((PEERS, 3)),
            pltpu.SemaphoreType.DMA((PEERS, 2)),
        ],
        compiler_params=pltpu.CompilerParams(
            collective_id=0, has_side_effects=True, vmem_limit_bytes=24 * 1024 * 1024
        ),
    )(*[pltpu.with_memory_space_constraint(x, pltpu.HBM) for x in (fresh, keys, values, text, slots, lengths)])


def body(fresh, stale_keys, stale_values, text_kv, group_slots, text_len):
    slot_count = fresh.shape[2]
    text = text_kv[0].reshape(TBLOCKS, BLK, 2 * HD)
    merged = attention(fresh[0, 0], stale_keys[0, 0], stale_values[0, 0], text, group_slots, text_len)
    return jnp.pad(merged, ((0, slot_count - LIVE), (0, 0), (0, 0)))[None, None]


def solution(mesh):
    placed = (
        P("img", "patch", None, None, None),
        P("img", "patch", None, None, None),
        P("img", "patch", None, None, None),
        P("img", None, None),
        P(),
        P(),
    )
    return jax.shard_map(
        body,
        mesh=mesh,
        in_specs=placed,
        out_specs=P("img", "patch", None, None, None),
        check_vma=False,
    )
```

```python
import functools

import jax
import jax.numpy as jnp
from jax import lax
from jax.experimental import pallas as pl
from jax.experimental.pallas import tpu as pltpu
from jax.sharding import PartitionSpec as P

MESH = pl.DeviceIdType.MESH
F32 = jnp.float32
BF16 = jnp.bfloat16

HDIM = 128
HEADS = 12
HD = HDIM * HEADS
BLK = 16
LIVE = 3
TXT = 128
PEERS = 16
IMAGES = 32
ROWS = LIVE * BLK
BLOCKS = PEERS * LIVE
TBLOCKS = TXT // BLK
KBLOCKS = BLOCKS + TBLOCKS
CHUNKS = 4
CPEERS = PEERS // CHUNKS
CBLOCKS = BLOCKS // CHUNKS
CROWS = CBLOCKS * BLK
SCALE = 1.4426950408889634 / HDIM**0.5
MASKED = -1e30


def nt(a, b):
    return lax.dot_general(a, b, (((1,), (1,)), ((), ())), preferred_element_type=F32)


def owner_rank(peer, core):
    z, x = peer // 2, peer % 2
    return lax.rem(z + 15 - 2 * core - x, 4)


def owned_head(peer, core):
    z, x = peer // 2, peer % 2
    return (z // 4) * 6 + x * 3 + owner_rank(peer, core)


def partner(me, k):
    half = k // 2
    odd = lax.rem(k, 2)
    offset = PEERS // 2 + odd * half - (1 - odd) * half
    return lax.rem(me + offset, PEERS)


def kernel(
    fresh, keys, values, text, slots_in, lengths_in, out,
    own, stale, chunks, inbox, tkeys, tvalues, qmask, kmask, pbuf, linv,
    osend, lsend, orecv, lrecv, ownout, ownlse, coef, counts,
    local_sem, text_sem, kq_sem, v_sem, o_sem, l_sem, kq_sent, v_sent, o_sent, l_sent,
):
    image = lax.axis_index("img")
    me = lax.axis_index("patch")
    core = lax.rem(image, 2)
    is_owner = owner_rank(me, core) < 3
    my_head = owned_head(me, core)

    barrier = pltpu.get_barrier_semaphore()

    def greet(k, carry):
        pl.semaphore_signal(barrier, inc=1, device_id=(image, partner(me, k)), device_id_type=MESH)
        return carry

    lax.fori_loop(1, PEERS, greet, 0)

    live = pl.ds(0, LIVE)
    local = [
        pltpu.make_async_copy(keys.at[live], stale.at[0], local_sem.at[0]),
        pltpu.make_async_copy(fresh.at[live], own, local_sem.at[1]),
        pltpu.make_async_copy(values.at[live], stale.at[1], local_sem.at[2]),
        pltpu.make_async_copy(slots_in, counts.at[0], local_sem.at[3]),
        pltpu.make_async_copy(lengths_in, counts.at[1], local_sem.at[4]),
    ]
    for copy in local:
        copy.start()

    def text_copy(third, target):
        columns = pl.ds(pl.multiple_of(third * HD + my_head * HDIM, HDIM), HDIM)
        return pltpu.make_async_copy(text.at[:, :, columns], target, text_sem.at[third])

    texts = [text_copy(0, tkeys), text_copy(1, tvalues)]

    @pl.when(is_owner)
    def _():
        for copy in texts:
            copy.start()

    def stage(part, source):
        for head in range(HEADS):
            chunks[head, part] = source[:, :, head * HDIM : (head + 1) * HDIM]

    local[0].wait()
    stage(0, stale.at[0])
    local[1].wait()
    stage(1, own)
    local[2].wait()
    stage(2, stale.at[1])

    pl.semaphore_wait(barrier, PEERS - 1)

    keys_queries = pl.ds(0, 2)
    only_values = pl.ds(2, 1)

    def send(peer, parts, sent, received):
        pltpu.make_async_remote_copy(
            src_ref=chunks.at[owned_head(peer, core), parts],
            dst_ref=inbox.at[me, parts],
            send_sem=sent,
            recv_sem=received,
            device_id=(image, peer),
            device_id_type=MESH,
        ).start()

    def send_all(parts, sent, received):
        def step(k, carry):
            peer = partner(me, k)

            @pl.when(owner_rank(peer, core) < 3)
            def _():
                send(peer, parts, sent, received)

            return carry

        lax.fori_loop(1, PEERS, step, 0)

        @pl.when(is_owner)
        def _():
            pltpu.make_async_copy(chunks.at[my_head, parts], inbox.at[me, parts], received).start()

    send_all(keys_queries, kq_sent, kq_sem)
    send_all(only_values, v_sent, v_sem)

    def wait_for(ref, sem):
        pltpu.make_async_copy(ref, ref, sem).wait()

    local[3].wait()
    local[4].wait()
    n = counts[0, image]
    length = counts[1, image]

    @pl.when(is_owner)
    def _():
        shape = (KBLOCKS, BLK, HDIM)
        block = lax.broadcasted_iota(jnp.int32, shape, 0)
        row = lax.broadcasted_iota(jnp.int32, shape, 1)
        lane = lax.broadcasted_iota(jnp.int32, shape, 2)
        slot = block - 3 * ((block * 171) >> 9)
        dead = jnp.where(block < BLOCKS, slot - n, (block - BLOCKS) * BLK + row - length) >= 0
        hit = ((lane == block) & (block < BLOCKS)) | ((lane == HDIM - 1) & dead)
        kmask[...] = jnp.where(hit, MASKED, 0.0).astype(BF16)
        shape = (BLOCKS, BLK, HDIM)
        block = lax.broadcasted_iota(jnp.int32, shape, 0)
        lane = lax.broadcasted_iota(jnp.int32, shape, 2)
        qmask[...] = jnp.where((lane == block) | (lane == HDIM - 1), 1.0, 0.0).astype(BF16)

    def attend_own(first, count):
        heads = range(first, first + count)
        diagonal = (
            lax.broadcasted_iota(jnp.int32, (ROWS, ROWS), 0) // BLK
            == lax.broadcasted_iota(jnp.int32, (ROWS, ROWS), 1) // BLK
        )

        def third(which, head):
            at = which * HD + head * HDIM
            return own[:, :, at : at + HDIM].reshape(ROWS, HDIM)

        scores = [jnp.where(diagonal, nt(third(0, head), third(1, head)), MASKED) for head in heads]
        tops = [jnp.max(x, axis=1, keepdims=True) for x in scores]
        weights = [jnp.exp2((x - top) * SCALE) for x, top in zip(scores, tops)]
        totals = [jnp.sum(x, axis=1, keepdims=True) for x in weights]
        sums = [
            jnp.dot(x.astype(BF16), third(2, head), preferred_element_type=F32) for x, head in zip(weights, heads)
        ]
        for i, head in enumerate(heads):
            ownout[head] = sums[i] / totals[i]
            ownlse[head] = jnp.broadcast_to(tops[i] * SCALE + jnp.log2(totals[i]), (ROWS, HDIM))

    attend_own(0, HEADS // 2)

    def send_back(first, count, source_of, target, sent, received):
        def step(peer, carry):
            @pl.when(peer != me)
            def _():
                pltpu.make_async_remote_copy(
                    src_ref=source_of(peer),
                    dst_ref=target,
                    send_sem=sent,
                    recv_sem=received,
                    device_id=(image, peer),
                    device_id_type=MESH,
                ).start()

            @pl.when(peer == me)
            def _():
                pltpu.make_async_copy(source_of(peer), target, received).start()

            return carry

        lax.fori_loop(first, first + count, step, 0)

    @pl.when(is_owner)
    def _():
        for copy in texts:
            copy.wait()
        wait_for(inbox.at[:, keys_queries], kq_sem)
        lane = lax.broadcasted_iota(jnp.int32, (ROWS, HDIM), 1)
        stats = jnp.zeros((ROWS, HDIM), F32)
        k = jnp.concatenate([inbox[:, 0].reshape(BLOCKS * BLK, HDIM), tkeys[...].reshape(TXT, HDIM)], axis=0)
        k = jnp.concatenate([k, kmask[...].reshape(KBLOCKS * BLK, HDIM)], axis=1)
        for chunk in range(CHUNKS):
            peers = slice(chunk * CPEERS, (chunk + 1) * CPEERS)
            blocks = slice(chunk * CBLOCKS, (chunk + 1) * CBLOCKS)
            q = jnp.concatenate(
                [inbox[peers, 1].reshape(CROWS, HDIM), qmask[blocks].reshape(CROWS, HDIM)], axis=1
            )
            scores = nt(q, k)
            top = jnp.max(scores, axis=1, keepdims=True)
            weights = jnp.exp2((scores - top) * SCALE)
            total = jnp.sum(weights, axis=1, keepdims=True)
            pbuf[chunk] = weights.astype(BF16)
            linv[chunk] = jnp.broadcast_to(1.0 / total, (CROWS, HDIM))
            lse = jnp.broadcast_to(top * SCALE + jnp.log2(total), (CROWS, HDIM))
            for i in range(CPEERS):
                stats = jnp.where(lane == chunk * CPEERS + i, lse[i * ROWS : (i + 1) * ROWS], stats)
        turned = jnp.concatenate([stats, jnp.zeros((HDIM - ROWS, HDIM), F32)], axis=0).T
        for peer in range(PEERS):
            lsend[peer] = turned[peer : peer + 1]
        send_back(0, PEERS, lambda peer: lsend.at[peer], lrecv.at[my_head], l_sent, l_sem)

        wait_for(inbox.at[:, only_values], v_sem)
        v = jnp.concatenate([inbox[:, 2].reshape(BLOCKS * BLK, HDIM), tvalues[...].reshape(TXT, HDIM)], axis=0)
        for chunk in range(CHUNKS):
            attended = jnp.dot(pbuf[chunk], v, preferred_element_type=F32) * linv[chunk]
            peers = slice(chunk * CPEERS, (chunk + 1) * CPEERS)
            osend[peers] = attended.astype(BF16).reshape(CPEERS, LIVE, BLK, HDIM)
            send_back(chunk * CPEERS, CPEERS, lambda peer: osend.at[peer], orecv.at[my_head], o_sent, o_sem)

    attend_own(HEADS // 2, HEADS // 2)

    @pl.when(is_owner)
    def _():
        wait_for(inbox.at[pl.ds(0, HEADS - 1), keys_queries], kq_sent)
        wait_for(inbox.at[pl.ds(0, HEADS - 1), only_values], v_sent)

    @pl.when(jnp.logical_not(is_owner))
    def _():
        wait_for(inbox.at[pl.ds(0, HEADS), keys_queries], kq_sent)
        wait_for(inbox.at[pl.ds(0, HEADS), only_values], v_sent)

    wait_for(lrecv, l_sem)
    stacked = jnp.concatenate([lrecv[head] for head in range(HEADS)] + [jnp.zeros((HDIM - HEADS, HDIM), F32)], axis=0)
    columns = stacked.T
    shown = lax.broadcasted_iota(jnp.int32, (LIVE, BLK, HDIM), 0) < n
    for head in range(HEADS):
        sibling = jnp.broadcast_to(columns[:ROWS, head : head + 1], (ROWS, HDIM))
        within = ownlse[head]
        top = jnp.maximum(sibling, within)
        a = jnp.exp2(sibling - top)
        b = jnp.exp2(within - top)
        inverse = 1.0 / (a + b)
        coef[head] = a * inverse
        ownout[head] = ownout[head] * (b * inverse)
    wait_for(orecv, o_sem)
    for head in range(HEADS):
        merged = orecv[head].reshape(ROWS, HDIM).astype(F32) * coef[head] + ownout[head]
        merged = jnp.where(shown, merged.reshape(LIVE, BLK, HDIM), 0.0)
        out[:, :, head * HDIM : (head + 1) * HDIM] = merged.astype(BF16)

    @pl.when(is_owner)
    def _():
        wait_for(lsend.at[pl.ds(0, PEERS - 1)], l_sent)
        wait_for(osend.at[pl.ds(0, PEERS - 1)], o_sent)


def attention(fresh, keys, values, text, slots, lengths):
    anywhere = pl.BlockSpec(memory_space=pl.ANY)
    semaphore = pltpu.SemaphoreType.DMA
    return pl.pallas_call(
        kernel,
        out_shape=jax.ShapeDtypeStruct((LIVE, BLK, HD), BF16),
        in_specs=[anywhere] * 6,
        out_specs=pl.BlockSpec(memory_space=pltpu.VMEM),
        scratch_shapes=[
            pltpu.VMEM((LIVE, BLK, 3 * HD), BF16),
            pltpu.VMEM((2, LIVE, BLK, HD), BF16),
            pltpu.VMEM((HEADS, 3, LIVE, BLK, HDIM), BF16),
            pltpu.VMEM((PEERS, 3, LIVE, BLK, HDIM), BF16),
            pltpu.VMEM((TBLOCKS, BLK, HDIM), BF16),
            pltpu.VMEM((TBLOCKS, BLK, HDIM), BF16),
            pltpu.VMEM((BLOCKS, BLK, HDIM), BF16),
            pltpu.VMEM((KBLOCKS, BLK, HDIM), BF16),
            pltpu.VMEM((CHUNKS, CROWS, KBLOCKS * BLK), BF16),
            pltpu.VMEM((CHUNKS, CROWS, HDIM), F32),
            pltpu.VMEM((PEERS, LIVE, BLK, HDIM), BF16),
            pltpu.VMEM((PEERS, 1, HDIM), F32),
            pltpu.VMEM((HEADS, LIVE, BLK, HDIM), BF16),
            pltpu.VMEM((HEADS, 1, HDIM), F32),
            pltpu.VMEM((HEADS, ROWS, HDIM), F32),
            pltpu.VMEM((HEADS, ROWS, HDIM), F32),
            pltpu.VMEM((HEADS, ROWS, HDIM), F32),
            pltpu.SMEM((2, IMAGES), jnp.int32),
            semaphore((5,)),
            semaphore((2,)),
        ]
        + [semaphore] * 8,
        compiler_params=pltpu.CompilerParams(
            collective_id=0, has_side_effects=True, vmem_limit_bytes=24 * 1024 * 1024
        ),
    )(*[pltpu.with_memory_space_constraint(x, pltpu.HBM) for x in (fresh, keys, values, text, slots, lengths)])


def body(fresh, stale_keys, stale_values, text_kv, group_slots, text_len):
    slot_count = fresh.shape[2]
    text = text_kv[0].reshape(TBLOCKS, BLK, 2 * HD)
    merged = attention(fresh[0, 0], stale_keys[0, 0], stale_values[0, 0], text, group_slots, text_len)
    return jnp.pad(merged, ((0, slot_count - LIVE), (0, 0), (0, 0)))[None, None]


def solution(mesh):
    placed = (
        P("img", "patch", None, None, None),
        P("img", "patch", None, None, None),
        P("img", "patch", None, None, None),
        P("img", None, None),
        P(),
        P(),
    )
    return jax.shard_map(
        body,
        mesh=mesh,
        in_specs=placed,
        out_specs=P("img", "patch", None, None, None),
        check_vma=False,
    )
```

```python
import functools

import jax
import jax.numpy as jnp
from jax import lax
from jax.experimental import pallas as pl
from jax.experimental.pallas import tpu as pltpu
from jax.sharding import PartitionSpec as P

MESH = pl.DeviceIdType.MESH
F32 = jnp.float32
BF16 = jnp.bfloat16

HDIM = 128
HEADS = 12
HD = HDIM * HEADS
BLK = 16
LIVE = 3
TXT = 128
PEERS = 16
IMAGES = 32
ROWS = LIVE * BLK
BLOCKS = PEERS * LIVE
TBLOCKS = TXT // BLK
KBLOCKS = BLOCKS + TBLOCKS
CHUNKS = 4
CPEERS = PEERS // CHUNKS
CBLOCKS = BLOCKS // CHUNKS
CROWS = CBLOCKS * BLK
SCALE = 1.4426950408889634 / HDIM**0.5
MASKED = -1e30


def nt(a, b):
    return lax.dot_general(a, b, (((1,), (1,)), ((), ())), preferred_element_type=F32)


def owner_rank(peer, core):
    z, x = peer // 2, peer % 2
    return lax.rem(z + 15 - 2 * core - x, 4)


def owned_head(peer, core):
    z, x = peer // 2, peer % 2
    return (z // 4) * 6 + x * 3 + owner_rank(peer, core)


def partner(me, k):
    half = k // 2
    odd = lax.rem(k, 2)
    offset = PEERS // 2 + odd * half - (1 - odd) * half
    return lax.rem(me + offset, PEERS)


def kernel(
    fresh, keys, values, text, slots_in, lengths_in, out,
    own, stale, chunks, inbox, passing, tkeys, tvalues, qmask, kmask, pbuf, linv,
    osend, lsend, orecv, lrecv, ownout, ownlse, coef, counts,
    local_sem, text_sem, kq_sem, v_sem, o_sem, l_sem, kq_sent, v_sent, o_sent, l_sent,
    relay_sem, pass_sent,
):
    image = lax.axis_index("img")
    me = lax.axis_index("patch")
    core = lax.rem(image, 2)
    is_owner = owner_rank(me, core) < 3
    my_head = owned_head(me, core)

    barrier = pltpu.get_barrier_semaphore()

    def greet(k, carry):
        pl.semaphore_signal(barrier, inc=1, device_id=(image, partner(me, k)), device_id_type=MESH)
        return carry

    lax.fori_loop(1, PEERS, greet, 0)

    live = pl.ds(0, LIVE)
    local = [
        pltpu.make_async_copy(keys.at[live], stale.at[0], local_sem.at[0]),
        pltpu.make_async_copy(fresh.at[live], own, local_sem.at[1]),
        pltpu.make_async_copy(values.at[live], stale.at[1], local_sem.at[2]),
        pltpu.make_async_copy(slots_in, counts.at[0], local_sem.at[3]),
        pltpu.make_async_copy(lengths_in, counts.at[1], local_sem.at[4]),
    ]
    for copy in local:
        copy.start()

    def text_copy(third, target):
        columns = pl.ds(pl.multiple_of(third * HD + my_head * HDIM, HDIM), HDIM)
        return pltpu.make_async_copy(text.at[:, :, columns], target, text_sem.at[third])

    texts = [text_copy(0, tkeys), text_copy(1, tvalues)]

    @pl.when(is_owner)
    def _():
        for copy in texts:
            copy.start()

    def stage(part, source):
        for head in range(HEADS):
            chunks[head, part] = source[:, :, head * HDIM : (head + 1) * HDIM]

    local[0].wait()
    stage(0, stale.at[0])
    local[1].wait()
    stage(1, own)
    local[2].wait()
    stage(2, stale.at[1])

    pl.semaphore_wait(barrier, PEERS - 1)

    keys_queries = pl.ds(0, 2)
    only_values = pl.ds(2, 1)

    def remote(source, target, sent, received, peer):
        return pltpu.make_async_remote_copy(
            src_ref=source,
            dst_ref=target,
            send_sem=sent,
            recv_sem=received,
            device_id=(image, peer),
            device_id_type=MESH,
        )

    z, x = me // 2, lax.rem(me, 2)
    opposite = lax.rem(z + 4, 8)
    downwards = 1 - lax.rem(z, 2)
    relay = 2 * lax.rem(z + 2 + 4 * downwards, 8) + x
    origin = lax.rem(z + 6 + 4 * downwards, 8)
    goal = lax.rem(origin + 4, 8)

    def send_to_relay(parts, which, sent):
        for side in range(2):
            peer = 2 * opposite + side

            @pl.when(owner_rank(peer, core) < 3)
            def _():
                source = chunks.at[owned_head(peer, core), parts]
                remote(source, passing.at[side, parts], sent, relay_sem.at[side, which], relay).start()

    def forward(parts, which, received, act):
        for side in range(2):
            peer = 2 * goal + side

            @pl.when(owner_rank(peer, core) < 3)
            def _():
                held = passing.at[side, parts]
                act(remote(held, inbox.at[2 * origin + x, parts], pass_sent.at[side, which], received, peer), side)

    def pass_on(parts, which, received):
        def act(copy, side):
            held = passing.at[side, parts]
            pltpu.make_async_copy(held, held, relay_sem.at[side, which]).wait()
            copy.start()

        forward(parts, which, received, act)

    def passed_on(parts, which, received):
        forward(parts, which, received, lambda copy, side: copy.wait_send())

    def send_all(parts, sent, received):
        def step(k, carry):
            peer = partner(me, k)

            @pl.when(jnp.logical_and(owner_rank(peer, core) < 3, peer // 2 != opposite))
            def _():
                remote(chunks.at[owned_head(peer, core), parts], inbox.at[me, parts], sent, received, peer).start()

            return carry

        lax.fori_loop(1, PEERS, step, 0)

        @pl.when(is_owner)
        def _():
            pltpu.make_async_copy(chunks.at[my_head, parts], inbox.at[me, parts], received).start()

    send_to_relay(keys_queries, 0, kq_sent)
    send_to_relay(only_values, 1, v_sent)
    send_all(keys_queries, kq_sent, kq_sem)
    pass_on(keys_queries, 0, kq_sem)
    send_all(only_values, v_sent, v_sem)
    pass_on(only_values, 1, v_sem)

    def wait_for(ref, sem):
        pltpu.make_async_copy(ref, ref, sem).wait()

    local[3].wait()
    local[4].wait()
    n = counts[0, image]
    length = counts[1, image]

    @pl.when(is_owner)
    def _():
        shape = (KBLOCKS, BLK, HDIM)
        block = lax.broadcasted_iota(jnp.int32, shape, 0)
        row = lax.broadcasted_iota(jnp.int32, shape, 1)
        lane = lax.broadcasted_iota(jnp.int32, shape, 2)
        slot = block - 3 * ((block * 171) >> 9)
        dead = jnp.where(block < BLOCKS, slot - n, (block - BLOCKS) * BLK + row - length) >= 0
        hit = ((lane == block) & (block < BLOCKS)) | ((lane == HDIM - 1) & dead)
        kmask[...] = jnp.where(hit, MASKED, 0.0).astype(BF16)
        shape = (BLOCKS, BLK, HDIM)
        block = lax.broadcasted_iota(jnp.int32, shape, 0)
        lane = lax.broadcasted_iota(jnp.int32, shape, 2)
        qmask[...] = jnp.where((lane == block) | (lane == HDIM - 1), 1.0, 0.0).astype(BF16)

    def attend_own(first, count):
        heads = range(first, first + count)
        diagonal = (
            lax.broadcasted_iota(jnp.int32, (ROWS, ROWS), 0) // BLK
            == lax.broadcasted_iota(jnp.int32, (ROWS, ROWS), 1) // BLK
        )

        def third(which, head):
            at = which * HD + head * HDIM
            return own[:, :, at : at + HDIM].reshape(ROWS, HDIM)

        scores = [jnp.where(diagonal, nt(third(0, head), third(1, head)), MASKED) for head in heads]
        tops = [jnp.max(x, axis=1, keepdims=True) for x in scores]
        weights = [jnp.exp2((x - top) * SCALE) for x, top in zip(scores, tops)]
        totals = [jnp.sum(x, axis=1, keepdims=True) for x in weights]
        sums = [
            jnp.dot(x.astype(BF16), third(2, head), preferred_element_type=F32) for x, head in zip(weights, heads)
        ]
        for i, head in enumerate(heads):
            ownout[head] = sums[i] / totals[i]
            ownlse[head] = jnp.broadcast_to(tops[i] * SCALE + jnp.log2(totals[i]), (ROWS, HDIM))

    attend_own(0, HEADS // 2)

    def send_back(first, count, source_of, target, sent, received):
        def step(peer, carry):
            @pl.when(peer != me)
            def _():
                remote(source_of(peer), target, sent, received, peer).start()

            @pl.when(peer == me)
            def _():
                pltpu.make_async_copy(source_of(peer), target, received).start()

            return carry

        lax.fori_loop(first, first + count, step, 0)

    @pl.when(is_owner)
    def _():
        for copy in texts:
            copy.wait()
        wait_for(inbox.at[:, keys_queries], kq_sem)
        lane = lax.broadcasted_iota(jnp.int32, (ROWS, HDIM), 1)
        stats = jnp.zeros((ROWS, HDIM), F32)
        k = jnp.concatenate([inbox[:, 0].reshape(BLOCKS * BLK, HDIM), tkeys[...].reshape(TXT, HDIM)], axis=0)
        k = jnp.concatenate([k, kmask[...].reshape(KBLOCKS * BLK, HDIM)], axis=1)
        for chunk in range(CHUNKS):
            peers = slice(chunk * CPEERS, (chunk + 1) * CPEERS)
            blocks = slice(chunk * CBLOCKS, (chunk + 1) * CBLOCKS)
            q = jnp.concatenate(
                [inbox[peers, 1].reshape(CROWS, HDIM), qmask[blocks].reshape(CROWS, HDIM)], axis=1
            )
            scores = nt(q, k)
            top = jnp.max(scores, axis=1, keepdims=True)
            weights = jnp.exp2((scores - top) * SCALE)
            total = jnp.sum(weights, axis=1, keepdims=True)
            pbuf[chunk] = weights.astype(BF16)
            linv[chunk] = jnp.broadcast_to(1.0 / total, (CROWS, HDIM))
            lse = jnp.broadcast_to(top * SCALE + jnp.log2(total), (CROWS, HDIM))
            for i in range(CPEERS):
                stats = jnp.where(lane == chunk * CPEERS + i, lse[i * ROWS : (i + 1) * ROWS], stats)
        turned = jnp.concatenate([stats, jnp.zeros((HDIM - ROWS, HDIM), F32)], axis=0).T
        for peer in range(PEERS):
            lsend[peer] = turned[peer : peer + 1]
        send_back(0, PEERS, lambda peer: lsend.at[peer], lrecv.at[my_head], l_sent, l_sem)

        wait_for(inbox.at[:, only_values], v_sem)
        v = jnp.concatenate([inbox[:, 2].reshape(BLOCKS * BLK, HDIM), tvalues[...].reshape(TXT, HDIM)], axis=0)
        for chunk in range(CHUNKS):
            attended = jnp.dot(pbuf[chunk], v, preferred_element_type=F32) * linv[chunk]
            peers = slice(chunk * CPEERS, (chunk + 1) * CPEERS)
            osend[peers] = attended.astype(BF16).reshape(CPEERS, LIVE, BLK, HDIM)
            send_back(chunk * CPEERS, CPEERS, lambda peer: osend.at[peer], orecv.at[my_head], o_sent, o_sem)

    attend_own(HEADS // 2, HEADS // 2)

    @pl.when(is_owner)
    def _():
        wait_for(inbox.at[pl.ds(0, HEADS - 1), keys_queries], kq_sent)
        wait_for(inbox.at[pl.ds(0, HEADS - 1), only_values], v_sent)

    @pl.when(jnp.logical_not(is_owner))
    def _():
        wait_for(inbox.at[pl.ds(0, HEADS), keys_queries], kq_sent)
        wait_for(inbox.at[pl.ds(0, HEADS), only_values], v_sent)

    passed_on(keys_queries, 0, kq_sem)
    passed_on(only_values, 1, v_sem)

    wait_for(lrecv, l_sem)
    stacked = jnp.concatenate([lrecv[head] for head in range(HEADS)] + [jnp.zeros((HDIM - HEADS, HDIM), F32)], axis=0)
    columns = stacked.T
    shown = lax.broadcasted_iota(jnp.int32, (LIVE, BLK, HDIM), 0) < n
    for head in range(HEADS):
        sibling = jnp.broadcast_to(columns[:ROWS, head : head + 1], (ROWS, HDIM))
        within = ownlse[head]
        top = jnp.maximum(sibling, within)
        a = jnp.exp2(sibling - top)
        b = jnp.exp2(within - top)
        inverse = 1.0 / (a + b)
        coef[head] = a * inverse
        ownout[head] = ownout[head] * (b * inverse)
    wait_for(orecv, o_sem)
    for head in range(HEADS):
        merged = orecv[head].reshape(ROWS, HDIM).astype(F32) * coef[head] + ownout[head]
        merged = jnp.where(shown, merged.reshape(LIVE, BLK, HDIM), 0.0)
        out[:, :, head * HDIM : (head + 1) * HDIM] = merged.astype(BF16)

    @pl.when(is_owner)
    def _():
        wait_for(lsend.at[pl.ds(0, PEERS - 1)], l_sent)
        wait_for(osend.at[pl.ds(0, PEERS - 1)], o_sent)


def attention(fresh, keys, values, text, slots, lengths):
    anywhere = pl.BlockSpec(memory_space=pl.ANY)
    semaphore = pltpu.SemaphoreType.DMA
    return pl.pallas_call(
        kernel,
        out_shape=jax.ShapeDtypeStruct((LIVE, BLK, HD), BF16),
        in_specs=[anywhere] * 6,
        out_specs=pl.BlockSpec(memory_space=pltpu.VMEM),
        scratch_shapes=[
            pltpu.VMEM((LIVE, BLK, 3 * HD), BF16),
            pltpu.VMEM((2, LIVE, BLK, HD), BF16),
            pltpu.VMEM((HEADS, 3, LIVE, BLK, HDIM), BF16),
            pltpu.VMEM((PEERS, 3, LIVE, BLK, HDIM), BF16),
            pltpu.VMEM((2, 3, LIVE, BLK, HDIM), BF16),
            pltpu.VMEM((TBLOCKS, BLK, HDIM), BF16),
            pltpu.VMEM((TBLOCKS, BLK, HDIM), BF16),
            pltpu.VMEM((BLOCKS, BLK, HDIM), BF16),
            pltpu.VMEM((KBLOCKS, BLK, HDIM), BF16),
            pltpu.VMEM((CHUNKS, CROWS, KBLOCKS * BLK), BF16),
            pltpu.VMEM((CHUNKS, CROWS, HDIM), F32),
            pltpu.VMEM((PEERS, LIVE, BLK, HDIM), BF16),
            pltpu.VMEM((PEERS, 1, HDIM), F32),
            pltpu.VMEM((HEADS, LIVE, BLK, HDIM), BF16),
            pltpu.VMEM((HEADS, 1, HDIM), F32),
            pltpu.VMEM((HEADS, ROWS, HDIM), F32),
            pltpu.VMEM((HEADS, ROWS, HDIM), F32),
            pltpu.VMEM((HEADS, ROWS, HDIM), F32),
            pltpu.SMEM((2, IMAGES), jnp.int32),
            semaphore((5,)),
            semaphore((2,)),
        ]
        + [semaphore] * 8
        + [semaphore((2, 2))] * 2,
        compiler_params=pltpu.CompilerParams(
            collective_id=0, has_side_effects=True, vmem_limit_bytes=24 * 1024 * 1024
        ),
    )(*[pltpu.with_memory_space_constraint(x, pltpu.HBM) for x in (fresh, keys, values, text, slots, lengths)])


def body(fresh, stale_keys, stale_values, text_kv, group_slots, text_len):
    slot_count = fresh.shape[2]
    text = text_kv[0].reshape(TBLOCKS, BLK, 2 * HD)
    merged = attention(fresh[0, 0], stale_keys[0, 0], stale_values[0, 0], text, group_slots, text_len)
    return jnp.pad(merged, ((0, slot_count - LIVE), (0, 0), (0, 0)))[None, None]


def solution(mesh):
    placed = (
        P("img", "patch", None, None, None),
        P("img", "patch", None, None, None),
        P("img", "patch", None, None, None),
        P("img", None, None),
        P(),
        P(),
    )
    return jax.shard_map(
        body,
        mesh=mesh,
        in_specs=placed,
        out_specs=P("img", "patch", None, None, None),
        check_vma=False,
    )
```

```python
import functools

import jax
import jax.numpy as jnp
from jax import lax
from jax.experimental import pallas as pl
from jax.experimental.pallas import tpu as pltpu
from jax.sharding import PartitionSpec as P

MESH = pl.DeviceIdType.MESH
F32 = jnp.float32
BF16 = jnp.bfloat16

HDIM = 128
HEADS = 12
HD = HDIM * HEADS
BLK = 16
LIVE = 3
TXT = 128
PEERS = 16
IMAGES = 32
ROWS = LIVE * BLK
BLOCKS = PEERS * LIVE
TBLOCKS = TXT // BLK
KBLOCKS = BLOCKS + TBLOCKS
CHUNKS = 4
CPEERS = PEERS // CHUNKS
CBLOCKS = BLOCKS // CHUNKS
CROWS = CBLOCKS * BLK
SCALE = 1.4426950408889634 / HDIM**0.5
MASKED = -1e30


def nt(a, b):
    return lax.dot_general(a, b, (((1,), (1,)), ((), ())), preferred_element_type=F32)


def owner_rank(peer, core):
    z, x = peer // 2, peer % 2
    return lax.rem(z + 15 - 2 * core - x, 4)


def owned_head(peer, core):
    z, x = peer // 2, peer % 2
    return (z // 4) * 6 + x * 3 + owner_rank(peer, core)


def offset_of(k):
    half = k // 2
    odd = lax.rem(k, 2)
    return lax.rem(PEERS // 2 + odd * half + (1 - odd) * (PEERS - half), PEERS)


def partner(me, k):
    return lax.rem(me + offset_of(k), PEERS)


def kernel(
    fresh, keys, values, text, slots_in, lengths_in, out,
    own, stale, chunks, inbox, tkeys, tvalues, qmask, kmask,
    osend, lsend, orecv, lrecv, ownout, ownlse, coef, counts,
    local_sem, text_sem, q_sem, kv_sem, o_sem, l_sem, kv_sent, q_sent, o_sent, l_sent,
):
    image = lax.axis_index("img")
    me = lax.axis_index("patch")
    core = lax.rem(image, 2)
    is_owner = owner_rank(me, core) < 3
    my_head = owned_head(me, core)

    barrier = pltpu.get_barrier_semaphore()

    def greet(k, carry):
        pl.semaphore_signal(barrier, inc=1, device_id=(image, partner(me, k)), device_id_type=MESH)
        return carry

    lax.fori_loop(1, PEERS, greet, 0)

    live = pl.ds(0, LIVE)
    local = [
        pltpu.make_async_copy(keys.at[live], stale.at[0], local_sem.at[0]),
        pltpu.make_async_copy(values.at[live], stale.at[1], local_sem.at[1]),
        pltpu.make_async_copy(fresh.at[live], own, local_sem.at[2]),
        pltpu.make_async_copy(slots_in, counts.at[0], local_sem.at[3]),
        pltpu.make_async_copy(lengths_in, counts.at[1], local_sem.at[4]),
    ]
    for copy in local:
        copy.start()

    def text_copy(third, target):
        columns = pl.ds(pl.multiple_of(third * HD + my_head * HDIM, HDIM), HDIM)
        return pltpu.make_async_copy(text.at[:, :, columns], target, text_sem.at[third])

    texts = [text_copy(0, tkeys), text_copy(1, tvalues)]

    @pl.when(is_owner)
    def _():
        for copy in texts:
            copy.start()

    def stage(part, source):
        for head in range(HEADS):
            chunks[head, part] = source[:, :, head * HDIM : (head + 1) * HDIM]

    local[0].wait()
    stage(0, stale.at[0])
    local[1].wait()
    stage(1, stale.at[1])
    local[2].wait()
    stage(2, own)

    pl.semaphore_wait(barrier, PEERS - 1)

    keys_values = pl.ds(0, 2)
    queries = pl.ds(2, 1)

    def remote(source, target, sent, received, peer):
        return pltpu.make_async_remote_copy(
            src_ref=source,
            dst_ref=target,
            send_sem=sent,
            recv_sem=received,
            device_id=(image, peer),
            device_id_type=MESH,
        )

    def send(parts, sent, received_of):
        def step(k, carry):
            peer = partner(me, k)

            @pl.when(owner_rank(peer, core) < 3)
            def _():
                source = chunks.at[owned_head(peer, core), parts]
                remote(source, inbox.at[me, parts], sent, received_of(k), peer).start()

            return carry

        lax.fori_loop(1, PEERS, step, 0)

        @pl.when(is_owner)
        def _():
            source = chunks.at[my_head, parts]
            pltpu.make_async_copy(source, inbox.at[me, parts], received_of(PEERS)).start()

    send(keys_values, kv_sent, lambda k: kv_sem)
    send(queries, q_sent, lambda k: q_sem.at[(k - 1) // CPEERS])

    def wait_for(ref, sem):
        pltpu.make_async_copy(ref, ref, sem).wait()

    local[3].wait()
    local[4].wait()
    n = counts[0, image]
    length = counts[1, image]

    @pl.when(is_owner)
    def _():
        shape = (KBLOCKS, BLK, HDIM)
        block = lax.broadcasted_iota(jnp.int32, shape, 0)
        row = lax.broadcasted_iota(jnp.int32, shape, 1)
        lane = lax.broadcasted_iota(jnp.int32, shape, 2)
        slot = block - 3 * ((block * 171) >> 9)
        dead = jnp.where(block < BLOCKS, slot - n, (block - BLOCKS) * BLK + row - length) >= 0
        hit = ((lane == block) & (block < BLOCKS)) | ((lane == HDIM - 1) & dead)
        kmask[...] = jnp.where(hit, MASKED, 0.0).astype(BF16)
        shape = (BLOCKS, BLK, HDIM)
        block = lax.broadcasted_iota(jnp.int32, shape, 0)
        lane = lax.broadcasted_iota(jnp.int32, shape, 2)
        qmask[...] = jnp.where((lane == block) | (lane == HDIM - 1), 1.0, 0.0).astype(BF16)

    def attend_own(first, count):
        heads = range(first, first + count)
        diagonal = (
            lax.broadcasted_iota(jnp.int32, (ROWS, ROWS), 0) // BLK
            == lax.broadcasted_iota(jnp.int32, (ROWS, ROWS), 1) // BLK
        )

        def third(which, head):
            at = which * HD + head * HDIM
            return own[:, :, at : at + HDIM].reshape(ROWS, HDIM)

        scores = [jnp.where(diagonal, nt(third(0, head), third(1, head)), MASKED) for head in heads]
        tops = [jnp.max(x, axis=1, keepdims=True) for x in scores]
        weights = [jnp.exp2((x - top) * SCALE) for x, top in zip(scores, tops)]
        totals = [jnp.sum(x, axis=1, keepdims=True) for x in weights]
        sums = [
            jnp.dot(x.astype(BF16), third(2, head), preferred_element_type=F32) for x, head in zip(weights, heads)
        ]
        for i, head in enumerate(heads):
            ownout[head] = sums[i] / totals[i]
            ownlse[head] = jnp.broadcast_to(tops[i] * SCALE + jnp.log2(totals[i]), (ROWS, HDIM))

    attend_own(0, HEADS)

    def send_back(group, source_of, target, sent, received):
        def step(k, carry):
            peer = lax.rem(me + PEERS - offset_of(k), PEERS)

            @pl.when(peer != me)
            def _():
                remote(source_of(peer), target, sent, received, peer).start()

            @pl.when(peer == me)
            def _():
                pltpu.make_async_copy(source_of(peer), target, received).start()

            return carry

        lax.fori_loop(group * CPEERS + 1, (group + 1) * CPEERS + 1, step, 0)

    @pl.when(is_owner)
    def _():
        for copy in texts:
            copy.wait()
        wait_for(inbox.at[:, keys_values], kv_sem)
        lane = lax.broadcasted_iota(jnp.int32, (ROWS, HDIM), 1)
        k = jnp.concatenate([inbox[:, 0].reshape(BLOCKS * BLK, HDIM), tkeys[...].reshape(TXT, HDIM)], axis=0)
        k = jnp.concatenate([k, kmask[...].reshape(KBLOCKS * BLK, HDIM)], axis=1)
        v = jnp.concatenate([inbox[:, 1].reshape(BLOCKS * BLK, HDIM), tvalues[...].reshape(TXT, HDIM)], axis=0)
        for group in range(CHUNKS):
            wait_for(inbox.at[pl.ds(0, CPEERS), queries], q_sem.at[group])
            peers = [lax.rem(me + PEERS - offset_of(group * CPEERS + i + 1), PEERS) for i in range(CPEERS)]
            q = jnp.concatenate(
                [
                    jnp.concatenate(
                        [inbox[peer, 2].reshape(ROWS, HDIM), qmask[pl.ds(peer * LIVE, LIVE)].reshape(ROWS, HDIM)],
                        axis=1,
                    )
                    for peer in peers
                ],
                axis=0,
            )
            scores = nt(q, k)
            top = jnp.max(scores, axis=1, keepdims=True)
            weights = jnp.exp2((scores - top) * SCALE)
            total = jnp.sum(weights, axis=1, keepdims=True)
            attended = jnp.dot(weights.astype(BF16), v, preferred_element_type=F32) * (1.0 / total)
            attended = attended.astype(BF16).reshape(CPEERS, LIVE, BLK, HDIM)
            for i, peer in enumerate(peers):
                osend[peer] = attended[i]
            send_back(group, lambda peer: osend.at[peer], orecv.at[my_head], o_sent, o_sem)
            lse = jnp.broadcast_to(top * SCALE + jnp.log2(total), (CROWS, HDIM))
            stats = jnp.zeros((ROWS, HDIM), F32)
            for i in range(CPEERS):
                stats = jnp.where(lane == i, lse[i * ROWS : (i + 1) * ROWS], stats)
            turned = jnp.concatenate([stats, jnp.zeros((HDIM - ROWS, HDIM), F32)], axis=0).T
            for i, peer in enumerate(peers):
                lsend[peer] = turned[i : i + 1]
            send_back(group, lambda peer: lsend.at[peer], lrecv.at[my_head], l_sent, l_sem)

    @pl.when(is_owner)
    def _():
        wait_for(inbox.at[pl.ds(0, HEADS - 1), keys_values], kv_sent)
        wait_for(inbox.at[pl.ds(0, HEADS - 1), queries], q_sent)

    @pl.when(jnp.logical_not(is_owner))
    def _():
        wait_for(inbox.at[pl.ds(0, HEADS), keys_values], kv_sent)
        wait_for(inbox.at[pl.ds(0, HEADS), queries], q_sent)

    wait_for(lrecv, l_sem)
    stacked = jnp.concatenate([lrecv[head] for head in range(HEADS)] + [jnp.zeros((HDIM - HEADS, HDIM), F32)], axis=0)
    columns = stacked.T
    shown = lax.broadcasted_iota(jnp.int32, (LIVE, BLK, HDIM), 0) < n
    for head in range(HEADS):
        sibling = jnp.broadcast_to(columns[:ROWS, head : head + 1], (ROWS, HDIM))
        within = ownlse[head]
        top = jnp.maximum(sibling, within)
        a = jnp.exp2(sibling - top)
        b = jnp.exp2(within - top)
        inverse = 1.0 / (a + b)
        coef[head] = a * inverse
        ownout[head] = ownout[head] * (b * inverse)
    wait_for(orecv, o_sem)
    for head in range(HEADS):
        merged = orecv[head].reshape(ROWS, HDIM).astype(F32) * coef[head] + ownout[head]
        merged = jnp.where(shown, merged.reshape(LIVE, BLK, HDIM), 0.0)
        out[:, :, head * HDIM : (head + 1) * HDIM] = merged.astype(BF16)

    @pl.when(is_owner)
    def _():
        wait_for(lsend.at[pl.ds(0, PEERS - 1)], l_sent)
        wait_for(osend.at[pl.ds(0, PEERS - 1)], o_sent)


def attention(fresh, keys, values, text, slots, lengths):
    anywhere = pl.BlockSpec(memory_space=pl.ANY)
    semaphore = pltpu.SemaphoreType.DMA
    return pl.pallas_call(
        kernel,
        out_shape=jax.ShapeDtypeStruct((LIVE, BLK, HD), BF16),
        in_specs=[anywhere] * 6,
        out_specs=pl.BlockSpec(memory_space=pltpu.VMEM),
        scratch_shapes=[
            pltpu.VMEM((LIVE, BLK, 3 * HD), BF16),
            pltpu.VMEM((2, LIVE, BLK, HD), BF16),
            pltpu.VMEM((HEADS, 3, LIVE, BLK, HDIM), BF16),
            pltpu.VMEM((PEERS, 3, LIVE, BLK, HDIM), BF16),
            pltpu.VMEM((TBLOCKS, BLK, HDIM), BF16),
            pltpu.VMEM((TBLOCKS, BLK, HDIM), BF16),
            pltpu.VMEM((BLOCKS, BLK, HDIM), BF16),
            pltpu.VMEM((KBLOCKS, BLK, HDIM), BF16),
            pltpu.VMEM((PEERS, LIVE, BLK, HDIM), BF16),
            pltpu.VMEM((PEERS, 1, HDIM), F32),
            pltpu.VMEM((HEADS, LIVE, BLK, HDIM), BF16),
            pltpu.VMEM((HEADS, 1, HDIM), F32),
            pltpu.VMEM((HEADS, ROWS, HDIM), F32),
            pltpu.VMEM((HEADS, ROWS, HDIM), F32),
            pltpu.VMEM((HEADS, ROWS, HDIM), F32),
            pltpu.SMEM((2, IMAGES), jnp.int32),
            semaphore((5,)),
            semaphore((2,)),
            semaphore((CHUNKS,)),
        ]
        + [semaphore] * 7,
        compiler_params=pltpu.CompilerParams(
            collective_id=0, has_side_effects=True, vmem_limit_bytes=24 * 1024 * 1024
        ),
    )(*[pltpu.with_memory_space_constraint(x, pltpu.HBM) for x in (fresh, keys, values, text, slots, lengths)])


def body(fresh, stale_keys, stale_values, text_kv, group_slots, text_len):
    slot_count = fresh.shape[2]
    text = text_kv[0].reshape(TBLOCKS, BLK, 2 * HD)
    merged = attention(fresh[0, 0], stale_keys[0, 0], stale_values[0, 0], text, group_slots, text_len)
    return jnp.pad(merged, ((0, slot_count - LIVE), (0, 0), (0, 0)))[None, None]


def solution(mesh):
    placed = (
        P("img", "patch", None, None, None),
        P("img", "patch", None, None, None),
        P("img", "patch", None, None, None),
        P("img", None, None),
        P(),
        P(),
    )
    return jax.shard_map(
        body,
        mesh=mesh,
        in_specs=placed,
        out_specs=P("img", "patch", None, None, None),
        check_vma=False,
    )
```

```python
import functools

import jax
import jax.numpy as jnp
from jax import lax
from jax.experimental import pallas as pl
from jax.experimental.pallas import tpu as pltpu
from jax.sharding import PartitionSpec as P

MESH = pl.DeviceIdType.MESH
F32 = jnp.float32
BF16 = jnp.bfloat16

HDIM = 128
HEADS = 12
HD = HDIM * HEADS
BLK = 16
LIVE = 3
TXT = 128
PEERS = 16
IMAGES = 32
ROWS = LIVE * BLK
BLOCKS = PEERS * LIVE
TBLOCKS = TXT // BLK
KEYS = BLOCKS * BLK + TXT
CHUNKS = 2
CPEERS = PEERS // CHUNKS
CROWS = CPEERS * ROWS
SCALE = 1.4426950408889634 / HDIM**0.5
MASKED = -1e30


def nt(a, b):
    return lax.dot_general(a, b, (((1,), (1,)), ((), ())), preferred_element_type=F32)


def owner_rank(peer, core):
    z, x = peer // 2, peer % 2
    return lax.rem(z + 15 - 2 * core - x, 4)


def owned_head(peer, core):
    z, x = peer // 2, peer % 2
    return (z // 4) * 6 + x * 3 + owner_rank(peer, core)


def partner(me, k):
    half = k // 2
    odd = lax.rem(k, 2)
    offset = PEERS // 2 + odd * half - (1 - odd) * half
    return lax.rem(me + offset, PEERS)


def kernel(
    fresh, keys, values, text, slots_in, lengths_in, out,
    own, stale, chunks, inbox, tkeys, tvalues, qmask, turned_keys, sbuf, pbuf, linv,
    osend, lsend, orecv, lrecv, ownout, ownlse, coef, counts,
    local_sem, text_sem, kq_sem, v_sem, o_sem, l_sem, kq_sent, v_sent, o_sent, l_sent,
):
    image = lax.axis_index("img")
    me = lax.axis_index("patch")
    core = lax.rem(image, 2)
    is_owner = owner_rank(me, core) < 3
    my_head = owned_head(me, core)

    barrier = pltpu.get_barrier_semaphore()

    def greet(k, carry):
        pl.semaphore_signal(barrier, inc=1, device_id=(image, partner(me, k)), device_id_type=MESH)
        return carry

    lax.fori_loop(1, PEERS, greet, 0)

    live = pl.ds(0, LIVE)
    local = [
        pltpu.make_async_copy(keys.at[live], stale.at[0], local_sem.at[0]),
        pltpu.make_async_copy(fresh.at[live], own, local_sem.at[1]),
        pltpu.make_async_copy(values.at[live], stale.at[1], local_sem.at[2]),
        pltpu.make_async_copy(slots_in, counts.at[0], local_sem.at[3]),
        pltpu.make_async_copy(lengths_in, counts.at[1], local_sem.at[4]),
    ]
    for copy in local:
        copy.start()

    def text_copy(third, target):
        columns = pl.ds(pl.multiple_of(third * HD + my_head * HDIM, HDIM), HDIM)
        return pltpu.make_async_copy(text.at[:, :, columns], target, text_sem.at[third])

    texts = [text_copy(0, tkeys), text_copy(1, tvalues)]

    @pl.when(is_owner)
    def _():
        for copy in texts:
            copy.start()

    def stage(part, source):
        for head in range(HEADS):
            chunks[head, part] = source[:, :, head * HDIM : (head + 1) * HDIM]

    local[0].wait()
    stage(0, stale.at[0])
    local[1].wait()
    stage(1, own)
    local[2].wait()
    stage(2, stale.at[1])

    pl.semaphore_wait(barrier, PEERS - 1)

    keys_queries = pl.ds(0, 2)
    only_values = pl.ds(2, 1)

    def send(peer, parts, sent, received):
        pltpu.make_async_remote_copy(
            src_ref=chunks.at[owned_head(peer, core), parts],
            dst_ref=inbox.at[me, parts],
            send_sem=sent,
            recv_sem=received,
            device_id=(image, peer),
            device_id_type=MESH,
        ).start()

    def send_all(parts, sent, received):
        def step(k, carry):
            peer = partner(me, k)

            @pl.when(owner_rank(peer, core) < 3)
            def _():
                send(peer, parts, sent, received)

            return carry

        lax.fori_loop(1, PEERS, step, 0)

        @pl.when(is_owner)
        def _():
            pltpu.make_async_copy(chunks.at[my_head, parts], inbox.at[me, parts], received).start()

    send_all(keys_queries, kq_sent, kq_sem)
    send_all(only_values, v_sent, v_sem)

    def wait_for(ref, sem):
        pltpu.make_async_copy(ref, ref, sem).wait()

    local[3].wait()
    local[4].wait()
    n = counts[0, image]
    length = counts[1, image]

    @pl.when(is_owner)
    def _():
        key = lax.broadcasted_iota(jnp.int32, (1, KEYS), 1)
        block = (key >> 4) + jnp.where(key < BLOCKS * BLK, 0, HDIM)
        slot = block - 3 * ((block * 171) >> 9)
        past = jnp.where(key < BLOCKS * BLK, slot - n, key - BLOCKS * BLK - length)
        mark = jnp.where(past >= 0, HDIM - 1, -1)
        row = lax.broadcasted_iota(jnp.int32, (HDIM, KEYS), 0)
        turned_keys[HDIM:] = jnp.where((row == block) | (row == mark), MASKED, 0.0).astype(BF16)
        shape = (BLOCKS, BLK, HDIM)
        block = lax.broadcasted_iota(jnp.int32, shape, 0)
        lane = lax.broadcasted_iota(jnp.int32, shape, 2)
        qmask[...] = jnp.where((lane == block) | (lane == HDIM - 1), 1.0, 0.0).astype(BF16)

    def attend_own(first, count):
        heads = range(first, first + count)
        diagonal = (
            lax.broadcasted_iota(jnp.int32, (ROWS, ROWS), 0) // BLK
            == lax.broadcasted_iota(jnp.int32, (ROWS, ROWS), 1) // BLK
        )

        def third(which, head):
            at = which * HD + head * HDIM
            return own[:, :, at : at + HDIM].reshape(ROWS, HDIM)

        scores = [jnp.where(diagonal, nt(third(0, head), third(1, head)), MASKED) for head in heads]
        tops = [jnp.max(x, axis=1, keepdims=True) for x in scores]
        weights = [jnp.exp2((x - top) * SCALE) for x, top in zip(scores, tops)]
        totals = [jnp.sum(x, axis=1, keepdims=True) for x in weights]
        sums = [
            jnp.dot(x.astype(BF16), third(2, head), preferred_element_type=F32) for x, head in zip(weights, heads)
        ]
        for i, head in enumerate(heads):
            ownout[head] = sums[i] / totals[i]
            ownlse[head] = jnp.broadcast_to(tops[i] * SCALE + jnp.log2(totals[i]), (ROWS, HDIM))

    attend_own(0, HEADS // 2)

    def send_back(first, count, source_of, target, sent, received):
        def step(peer, carry):
            @pl.when(peer != me)
            def _():
                pltpu.make_async_remote_copy(
                    src_ref=source_of(peer),
                    dst_ref=target,
                    send_sem=sent,
                    recv_sem=received,
                    device_id=(image, peer),
                    device_id_type=MESH,
                ).start()

            @pl.when(peer == me)
            def _():
                pltpu.make_async_copy(source_of(peer), target, received).start()

            return carry

        lax.fori_loop(first, first + count, step, 0)

    @pl.when(is_owner)
    def _():
        for copy in texts:
            copy.wait()
        wait_for(inbox.at[:, keys_queries], kq_sem)
        k = jnp.concatenate([inbox[:, 0].reshape(BLOCKS * BLK, HDIM), tkeys[...].reshape(TXT, HDIM)], axis=0)
        turned_keys[:HDIM] = k.T
        q = jnp.concatenate(
            [inbox[:, 1].reshape(BLOCKS * BLK, HDIM), qmask[...].reshape(BLOCKS * BLK, HDIM)], axis=1
        )
        sbuf[...] = jnp.dot(q, turned_keys[...], preferred_element_type=F32)
        lane = lax.broadcasted_iota(jnp.int32, (ROWS, HDIM), 1)
        stats = jnp.zeros((ROWS, HDIM), F32)
        for peer in range(PEERS):
            rows = slice(peer * ROWS, (peer + 1) * ROWS)
            scores = sbuf[rows]
            top = jnp.max(scores, axis=1, keepdims=True)
            weights = jnp.exp2((scores - top) * SCALE)
            total = jnp.sum(weights, axis=1, keepdims=True)
            pbuf[rows] = weights.astype(BF16)
            linv[rows] = jnp.broadcast_to(1.0 / total, (ROWS, HDIM))
            stats = jnp.where(lane == peer, top * SCALE + jnp.log2(total), stats)
        turned = jnp.concatenate([stats, jnp.zeros((HDIM - ROWS, HDIM), F32)], axis=0).T
        for peer in range(PEERS):
            lsend[peer] = turned[peer : peer + 1]
        send_back(0, PEERS, lambda peer: lsend.at[peer], lrecv.at[my_head], l_sent, l_sem)

        wait_for(inbox.at[:, only_values], v_sem)
        v = jnp.concatenate([inbox[:, 2].reshape(BLOCKS * BLK, HDIM), tvalues[...].reshape(TXT, HDIM)], axis=0)
        for chunk in range(CHUNKS):
            rows = slice(chunk * CROWS, (chunk + 1) * CROWS)
            attended = jnp.dot(pbuf[rows], v, preferred_element_type=F32) * linv[rows]
            peers = slice(chunk * CPEERS, (chunk + 1) * CPEERS)
            osend[peers] = attended.astype(BF16).reshape(CPEERS, LIVE, BLK, HDIM)
            send_back(chunk * CPEERS, CPEERS, lambda peer: osend.at[peer], orecv.at[my_head], o_sent, o_sem)

    attend_own(HEADS // 2, HEADS // 2)

    @pl.when(is_owner)
    def _():
        wait_for(inbox.at[pl.ds(0, HEADS - 1), keys_queries], kq_sent)
        wait_for(inbox.at[pl.ds(0, HEADS - 1), only_values], v_sent)

    @pl.when(jnp.logical_not(is_owner))
    def _():
        wait_for(inbox.at[pl.ds(0, HEADS), keys_queries], kq_sent)
        wait_for(inbox.at[pl.ds(0, HEADS), only_values], v_sent)

    wait_for(lrecv, l_sem)
    stacked = jnp.concatenate([lrecv[head] for head in range(HEADS)] + [jnp.zeros((HDIM - HEADS, HDIM), F32)], axis=0)
    columns = stacked.T
    shown = lax.broadcasted_iota(jnp.int32, (LIVE, BLK, HDIM), 0) < n
    for head in range(HEADS):
        sibling = jnp.broadcast_to(columns[:ROWS, head : head + 1], (ROWS, HDIM))
        within = ownlse[head]
        top = jnp.maximum(sibling, within)
        a = jnp.exp2(sibling - top)
        b = jnp.exp2(within - top)
        inverse = 1.0 / (a + b)
        coef[head] = a * inverse
        ownout[head] = ownout[head] * (b * inverse)
    wait_for(orecv, o_sem)
    for head in range(HEADS):
        merged = orecv[head].reshape(ROWS, HDIM).astype(F32) * coef[head] + ownout[head]
        merged = jnp.where(shown, merged.reshape(LIVE, BLK, HDIM), 0.0)
        out[:, :, head * HDIM : (head + 1) * HDIM] = merged.astype(BF16)

    @pl.when(is_owner)
    def _():
        wait_for(lsend.at[pl.ds(0, PEERS - 1)], l_sent)
        wait_for(osend.at[pl.ds(0, PEERS - 1)], o_sent)


def attention(fresh, keys, values, text, slots, lengths):
    anywhere = pl.BlockSpec(memory_space=pl.ANY)
    semaphore = pltpu.SemaphoreType.DMA
    return pl.pallas_call(
        kernel,
        out_shape=jax.ShapeDtypeStruct((LIVE, BLK, HD), BF16),
        in_specs=[anywhere] * 6,
        out_specs=pl.BlockSpec(memory_space=pltpu.VMEM),
        scratch_shapes=[
            pltpu.VMEM((LIVE, BLK, 3 * HD), BF16),
            pltpu.VMEM((2, LIVE, BLK, HD), BF16),
            pltpu.VMEM((HEADS, 3, LIVE, BLK, HDIM), BF16),
            pltpu.VMEM((PEERS, 3, LIVE, BLK, HDIM), BF16),
            pltpu.VMEM((TBLOCKS, BLK, HDIM), BF16),
            pltpu.VMEM((TBLOCKS, BLK, HDIM), BF16),
            pltpu.VMEM((BLOCKS, BLK, HDIM), BF16),
            pltpu.VMEM((2 * HDIM, KEYS), BF16),
            pltpu.VMEM((BLOCKS * BLK, KEYS), F32),
            pltpu.VMEM((BLOCKS * BLK, KEYS), BF16),
            pltpu.VMEM((BLOCKS * BLK, HDIM), F32),
            pltpu.VMEM((PEERS, LIVE, BLK, HDIM), BF16),
            pltpu.VMEM((PEERS, 1, HDIM), F32),
            pltpu.VMEM((HEADS, LIVE, BLK, HDIM), BF16),
            pltpu.VMEM((HEADS, 1, HDIM), F32),
            pltpu.VMEM((HEADS, ROWS, HDIM), F32),
            pltpu.VMEM((HEADS, ROWS, HDIM), F32),
            pltpu.VMEM((HEADS, ROWS, HDIM), F32),
            pltpu.SMEM((2, IMAGES), jnp.int32),
            semaphore((5,)),
            semaphore((2,)),
        ]
        + [semaphore] * 8,
        compiler_params=pltpu.CompilerParams(
            collective_id=0, has_side_effects=True, vmem_limit_bytes=24 * 1024 * 1024
        ),
    )(*[pltpu.with_memory_space_constraint(x, pltpu.HBM) for x in (fresh, keys, values, text, slots, lengths)])


def body(fresh, stale_keys, stale_values, text_kv, group_slots, text_len):
    slot_count = fresh.shape[2]
    text = text_kv[0].reshape(TBLOCKS, BLK, 2 * HD)
    merged = attention(fresh[0, 0], stale_keys[0, 0], stale_values[0, 0], text, group_slots, text_len)
    return jnp.pad(merged, ((0, slot_count - LIVE), (0, 0), (0, 0)))[None, None]


def solution(mesh):
    placed = (
        P("img", "patch", None, None, None),
        P("img", "patch", None, None, None),
        P("img", "patch", None, None, None),
        P("img", None, None),
        P(),
        P(),
    )
    return jax.shard_map(
        body,
        mesh=mesh,
        in_specs=placed,
        out_specs=P("img", "patch", None, None, None),
        check_vma=False,
    )
```

```python
import functools

import jax
import jax.numpy as jnp
from jax import lax
from jax.experimental import pallas as pl
from jax.experimental.pallas import tpu as pltpu
from jax.sharding import PartitionSpec as P

MESH = pl.DeviceIdType.MESH
F32 = jnp.float32
BF16 = jnp.bfloat16

HDIM = 128
HEADS = 12
HD = HDIM * HEADS
BLK = 16
LIVE = 3
TXT = 128
PEERS = 16
IMAGES = 32
ROWS = LIVE * BLK
BLOCKS = PEERS * LIVE
TBLOCKS = TXT // BLK
KEYS = BLOCKS * BLK + TXT
CHUNKS = 2
CPEERS = PEERS // CHUNKS
CROWS = CPEERS * ROWS
SCALE = 1.4426950408889634 / HDIM**0.5
MASKED = -1e30


def nt(a, b):
    return lax.dot_general(a, b, (((1,), (1,)), ((), ())), preferred_element_type=F32)


def owner_rank(peer, core):
    z, x = peer // 2, peer % 2
    return lax.rem(z + 15 - 2 * core - x, 4)


def owned_head(peer, core):
    z, x = peer // 2, peer % 2
    return (z // 4) * 6 + x * 3 + owner_rank(peer, core)


def offset_of(k):
    half = k // 2
    odd = lax.rem(k, 2)
    return lax.rem(PEERS // 2 + odd * half + (1 - odd) * (PEERS - half), PEERS)


def partner(me, k):
    return lax.rem(me + offset_of(k), PEERS)


def kernel(
    fresh, keys, values, text, slots_in, lengths_in, out,
    own, stale, chunks, inbox, tkeys, tvalues, qmask, turned_keys, sbuf, pbuf, linv,
    osend, lsend, orecv, lrecv, ownout, ownlse, coef, counts,
    local_sem, text_sem, kq_sem, v_sem, o_sem, l_sem, kq_sent, v_sent, o_sent, l_sent,
):
    image = lax.axis_index("img")
    me = lax.axis_index("patch")
    core = lax.rem(image, 2)
    is_owner = owner_rank(me, core) < 3
    my_head = owned_head(me, core)

    barrier = pltpu.get_barrier_semaphore()

    def greet(k, carry):
        pl.semaphore_signal(barrier, inc=1, device_id=(image, partner(me, k)), device_id_type=MESH)
        return carry

    lax.fori_loop(1, PEERS, greet, 0)

    live = pl.ds(0, LIVE)
    local = [
        pltpu.make_async_copy(keys.at[live], stale.at[0], local_sem.at[0]),
        pltpu.make_async_copy(fresh.at[live], own, local_sem.at[1]),
        pltpu.make_async_copy(values.at[live], stale.at[1], local_sem.at[2]),
        pltpu.make_async_copy(slots_in, counts.at[0], local_sem.at[3]),
        pltpu.make_async_copy(lengths_in, counts.at[1], local_sem.at[4]),
    ]
    for copy in local:
        copy.start()

    def text_copy(third, target):
        columns = pl.ds(pl.multiple_of(third * HD + my_head * HDIM, HDIM), HDIM)
        return pltpu.make_async_copy(text.at[:, :, columns], target, text_sem.at[third])

    texts = [text_copy(0, tkeys), text_copy(1, tvalues)]

    @pl.when(is_owner)
    def _():
        for copy in texts:
            copy.start()

    def stage(part, source):
        for head in range(HEADS):
            chunks[head, part] = source[:, :, head * HDIM : (head + 1) * HDIM]

    local[0].wait()
    stage(0, stale.at[0])
    local[1].wait()
    stage(1, own)
    local[2].wait()
    stage(2, stale.at[1])

    pl.semaphore_wait(barrier, PEERS - 1)

    keys_queries = pl.ds(0, 2)
    only_values = pl.ds(2, 1)

    def send(peer, parts, sent, received):
        pltpu.make_async_remote_copy(
            src_ref=chunks.at[owned_head(peer, core), parts],
            dst_ref=inbox.at[me, parts],
            send_sem=sent,
            recv_sem=received,
            device_id=(image, peer),
            device_id_type=MESH,
        ).start()

    def send_all(parts, sent, received):
        def step(k, carry):
            peer = partner(me, k)

            @pl.when(owner_rank(peer, core) < 3)
            def _():
                send(peer, parts, sent, received)

            return carry

        lax.fori_loop(1, PEERS, step, 0)

        @pl.when(is_owner)
        def _():
            pltpu.make_async_copy(chunks.at[my_head, parts], inbox.at[me, parts], received).start()

    send_all(keys_queries, kq_sent, kq_sem)
    send_all(only_values, v_sent, v_sem)

    def wait_for(ref, sem):
        pltpu.make_async_copy(ref, ref, sem).wait()

    local[3].wait()
    local[4].wait()
    n = counts[0, image]
    length = counts[1, image]

    @pl.when(is_owner)
    def _():
        key = lax.broadcasted_iota(jnp.int32, (1, KEYS), 1)
        block = (key >> 4) + jnp.where(key < BLOCKS * BLK, 0, HDIM)
        slot = block - 3 * ((block * 171) >> 9)
        past = jnp.where(key < BLOCKS * BLK, slot - n, key - BLOCKS * BLK - length)
        mark = jnp.where(past >= 0, HDIM - 1, -1)
        row = lax.broadcasted_iota(jnp.int32, (HDIM, KEYS), 0)
        turned_keys[HDIM:] = jnp.where((row == block) | (row == mark), MASKED, 0.0).astype(BF16)
        shape = (BLOCKS, BLK, HDIM)
        block = lax.broadcasted_iota(jnp.int32, shape, 0)
        lane = lax.broadcasted_iota(jnp.int32, shape, 2)
        qmask[...] = jnp.where((lane == block) | (lane == HDIM - 1), 1.0, 0.0).astype(BF16)

    def attend_own(first, count):
        heads = range(first, first + count)
        diagonal = (
            lax.broadcasted_iota(jnp.int32, (ROWS, ROWS), 0) // BLK
            == lax.broadcasted_iota(jnp.int32, (ROWS, ROWS), 1) // BLK
        )

        def third(which, head):
            at = which * HD + head * HDIM
            return own[:, :, at : at + HDIM].reshape(ROWS, HDIM)

        scores = [jnp.where(diagonal, nt(third(0, head), third(1, head)), MASKED) for head in heads]
        tops = [jnp.max(x, axis=1, keepdims=True) for x in scores]
        weights = [jnp.exp2((x - top) * SCALE) for x, top in zip(scores, tops)]
        totals = [jnp.sum(x, axis=1, keepdims=True) for x in weights]
        sums = [
            jnp.dot(x.astype(BF16), third(2, head), preferred_element_type=F32) for x, head in zip(weights, heads)
        ]
        for i, head in enumerate(heads):
            ownout[head] = sums[i] / totals[i]
            ownlse[head] = jnp.broadcast_to(tops[i] * SCALE + jnp.log2(totals[i]), (ROWS, HDIM))

    attend_own(0, HEADS // 2)

    def send_back(first, count, source, target, sent, received):
        def step(k, carry):
            peer = partner(me, k)

            @pl.when(peer != me)
            def _():
                pltpu.make_async_remote_copy(
                    src_ref=source.at[peer],
                    dst_ref=target,
                    send_sem=sent,
                    recv_sem=received,
                    device_id=(image, peer),
                    device_id_type=MESH,
                ).start()

            @pl.when(peer == me)
            def _():
                pltpu.make_async_copy(source.at[peer], target, received).start()

            return carry

        lax.fori_loop(first, first + count, step, 0)

    @pl.when(is_owner)
    def _():
        for copy in texts:
            copy.wait()
        wait_for(inbox.at[:, keys_queries], kq_sem)
        k = jnp.concatenate([inbox[:, 0].reshape(BLOCKS * BLK, HDIM), tkeys[...].reshape(TXT, HDIM)], axis=0)
        turned_keys[:HDIM] = k.T
        q = jnp.concatenate(
            [inbox[:, 1].reshape(BLOCKS * BLK, HDIM), qmask[...].reshape(BLOCKS * BLK, HDIM)], axis=1
        )
        sbuf[...] = jnp.dot(q, turned_keys[...], preferred_element_type=F32)
        lane = lax.broadcasted_iota(jnp.int32, (ROWS, HDIM), 1)
        stats = jnp.zeros((ROWS, HDIM), F32)
        for peer in range(PEERS):
            rows = slice(peer * ROWS, (peer + 1) * ROWS)
            scores = sbuf[rows]
            top = jnp.max(scores, axis=1, keepdims=True)
            weights = jnp.exp2((scores - top) * SCALE)
            total = jnp.sum(weights, axis=1, keepdims=True)
            pbuf[peer] = weights.astype(BF16)
            linv[peer] = jnp.broadcast_to(1.0 / total, (ROWS, HDIM))
            stats = jnp.where(lane == peer, top * SCALE + jnp.log2(total), stats)
        turned = jnp.concatenate([stats, jnp.zeros((HDIM - ROWS, HDIM), F32)], axis=0).T
        for peer in range(PEERS):
            lsend[peer] = turned[peer : peer + 1]
        send_back(1, PEERS, lsend, lrecv.at[my_head], l_sent, l_sem)

        wait_for(inbox.at[:, only_values], v_sem)
        v = jnp.concatenate([inbox[:, 2].reshape(BLOCKS * BLK, HDIM), tvalues[...].reshape(TXT, HDIM)], axis=0)
        for chunk in range(CHUNKS):
            peers = [partner(me, chunk * CPEERS + i + 1) for i in range(CPEERS)]
            weights = jnp.concatenate([pbuf[peer] for peer in peers], axis=0)
            attended = jnp.dot(weights, v, preferred_element_type=F32)
            for i, peer in enumerate(peers):
                scaled = attended[i * ROWS : (i + 1) * ROWS] * linv[peer]
                osend[peer] = scaled.astype(BF16).reshape(LIVE, BLK, HDIM)
            send_back(chunk * CPEERS + 1, CPEERS, osend, orecv.at[my_head], o_sent, o_sem)

    attend_own(HEADS // 2, HEADS // 2)

    @pl.when(is_owner)
    def _():
        wait_for(inbox.at[pl.ds(0, HEADS - 1), keys_queries], kq_sent)
        wait_for(inbox.at[pl.ds(0, HEADS - 1), only_values], v_sent)

    @pl.when(jnp.logical_not(is_owner))
    def _():
        wait_for(inbox.at[pl.ds(0, HEADS), keys_queries], kq_sent)
        wait_for(inbox.at[pl.ds(0, HEADS), only_values], v_sent)

    wait_for(lrecv, l_sem)
    stacked = jnp.concatenate([lrecv[head] for head in range(HEADS)] + [jnp.zeros((HDIM - HEADS, HDIM), F32)], axis=0)
    columns = stacked.T
    shown = lax.broadcasted_iota(jnp.int32, (LIVE, BLK, HDIM), 0) < n
    for head in range(HEADS):
        sibling = jnp.broadcast_to(columns[:ROWS, head : head + 1], (ROWS, HDIM))
        within = ownlse[head]
        top = jnp.maximum(sibling, within)
        a = jnp.exp2(sibling - top)
        b = jnp.exp2(within - top)
        inverse = 1.0 / (a + b)
        coef[head] = a * inverse
        ownout[head] = ownout[head] * (b * inverse)
    wait_for(orecv, o_sem)
    for head in range(HEADS):
        merged = orecv[head].reshape(ROWS, HDIM).astype(F32) * coef[head] + ownout[head]
        merged = jnp.where(shown, merged.reshape(LIVE, BLK, HDIM), 0.0)
        out[:, :, head * HDIM : (head + 1) * HDIM] = merged.astype(BF16)

    @pl.when(is_owner)
    def _():
        wait_for(lsend.at[pl.ds(0, PEERS - 1)], l_sent)
        wait_for(osend.at[pl.ds(0, PEERS - 1)], o_sent)


def attention(fresh, keys, values, text, slots, lengths):
    anywhere = pl.BlockSpec(memory_space=pl.ANY)
    semaphore = pltpu.SemaphoreType.DMA
    return pl.pallas_call(
        kernel,
        out_shape=jax.ShapeDtypeStruct((LIVE, BLK, HD), BF16),
        in_specs=[anywhere] * 6,
        out_specs=pl.BlockSpec(memory_space=pltpu.VMEM),
        scratch_shapes=[
            pltpu.VMEM((LIVE, BLK, 3 * HD), BF16),
            pltpu.VMEM((2, LIVE, BLK, HD), BF16),
            pltpu.VMEM((HEADS, 3, LIVE, BLK, HDIM), BF16),
            pltpu.VMEM((PEERS, 3, LIVE, BLK, HDIM), BF16),
            pltpu.VMEM((TBLOCKS, BLK, HDIM), BF16),
            pltpu.VMEM((TBLOCKS, BLK, HDIM), BF16),
            pltpu.VMEM((BLOCKS, BLK, HDIM), BF16),
            pltpu.VMEM((2 * HDIM, KEYS), BF16),
            pltpu.VMEM((BLOCKS * BLK, KEYS), F32),
            pltpu.VMEM((PEERS, ROWS, KEYS), BF16),
            pltpu.VMEM((PEERS, ROWS, HDIM), F32),
            pltpu.VMEM((PEERS, LIVE, BLK, HDIM), BF16),
            pltpu.VMEM((PEERS, 1, HDIM), F32),
            pltpu.VMEM((HEADS, LIVE, BLK, HDIM), BF16),
            pltpu.VMEM((HEADS, 1, HDIM), F32),
            pltpu.VMEM((HEADS, ROWS, HDIM), F32),
            pltpu.VMEM((HEADS, ROWS, HDIM), F32),
            pltpu.VMEM((HEADS, ROWS, HDIM), F32),
            pltpu.SMEM((2, IMAGES), jnp.int32),
            semaphore((5,)),
            semaphore((2,)),
        ]
        + [semaphore] * 8,
        compiler_params=pltpu.CompilerParams(
            collective_id=0, has_side_effects=True, vmem_limit_bytes=24 * 1024 * 1024
        ),
    )(*[pltpu.with_memory_space_constraint(x, pltpu.HBM) for x in (fresh, keys, values, text, slots, lengths)])


def body(fresh, stale_keys, stale_values, text_kv, group_slots, text_len):
    slot_count = fresh.shape[2]
    text = text_kv[0].reshape(TBLOCKS, BLK, 2 * HD)
    merged = attention(fresh[0, 0], stale_keys[0, 0], stale_values[0, 0], text, group_slots, text_len)
    return jnp.pad(merged, ((0, slot_count - LIVE), (0, 0), (0, 0)))[None, None]


def solution(mesh):
    placed = (
        P("img", "patch", None, None, None),
        P("img", "patch", None, None, None),
        P("img", "patch", None, None, None),
        P("img", None, None),
        P(),
        P(),
    )
    return jax.shard_map(
        body,
        mesh=mesh,
        in_specs=placed,
        out_specs=P("img", "patch", None, None, None),
        check_vma=False,
    )
```

```python
import functools

import jax
import jax.numpy as jnp
from jax import lax
from jax.experimental import pallas as pl
from jax.experimental.pallas import tpu as pltpu
from jax.sharding import PartitionSpec as P

MESH = pl.DeviceIdType.MESH
F32 = jnp.float32
BF16 = jnp.bfloat16

HDIM = 128
HEADS = 12
HD = HDIM * HEADS
BLK = 16
LIVE = 3
TXT = 128
PEERS = 16
IMAGES = 32
ROWS = LIVE * BLK
BLOCKS = PEERS * LIVE
TBLOCKS = TXT // BLK
KEYS = BLOCKS * BLK + TXT
GROUPS = 2
CPEERS = PEERS // GROUPS
CROWS = CPEERS * ROWS
SCALE = 1.4426950408889634 / HDIM**0.5
MASKED = -1e30


def nt(a, b):
    return lax.dot_general(a, b, (((1,), (1,)), ((), ())), preferred_element_type=F32)


def owner_rank(peer, core):
    z, x = peer // 2, peer % 2
    return lax.rem(z + 15 - 2 * core - x, 4)


def owned_head(peer, core):
    z, x = peer // 2, peer % 2
    return (z // 4) * 6 + x * 3 + owner_rank(peer, core)


def offset_of(k):
    half = k // 2
    odd = lax.rem(k, 2)
    return lax.rem(PEERS // 2 + odd * half + (1 - odd) * (PEERS - half), PEERS)


def partner(me, k):
    return lax.rem(me + offset_of(k), PEERS)


def origin(me, k):
    return lax.rem(me + PEERS - offset_of(k), PEERS)


def kernel(
    fresh, keys, values, text, slots_in, lengths_in, out,
    own, stale, chunks, inbox, tkeys, tvalues, qmask, turned_keys, sbuf, pbuf, linv,
    osend, lsend, orecv, lrecv, ownout, ownlse, coef, counts,
    local_sem, text_sem, q_sem, kv_sem, o_sem, l_sem, kv_sent, q_sent, o_sent, l_sent,
):
    image = lax.axis_index("img")
    me = lax.axis_index("patch")
    core = lax.rem(image, 2)
    is_owner = owner_rank(me, core) < 3
    my_head = owned_head(me, core)

    barrier = pltpu.get_barrier_semaphore()

    def greet(k, carry):
        pl.semaphore_signal(barrier, inc=1, device_id=(image, partner(me, k)), device_id_type=MESH)
        return carry

    lax.fori_loop(1, PEERS, greet, 0)

    live = pl.ds(0, LIVE)
    local = [
        pltpu.make_async_copy(keys.at[live], stale.at[0], local_sem.at[0]),
        pltpu.make_async_copy(values.at[live], stale.at[1], local_sem.at[1]),
        pltpu.make_async_copy(fresh.at[live], own, local_sem.at[2]),
        pltpu.make_async_copy(slots_in, counts.at[0], local_sem.at[3]),
        pltpu.make_async_copy(lengths_in, counts.at[1], local_sem.at[4]),
    ]
    for copy in local:
        copy.start()

    def text_copy(third, target):
        columns = pl.ds(pl.multiple_of(third * HD + my_head * HDIM, HDIM), HDIM)
        return pltpu.make_async_copy(text.at[:, :, columns], target, text_sem.at[third])

    texts = [text_copy(0, tkeys), text_copy(1, tvalues)]

    @pl.when(is_owner)
    def _():
        for copy in texts:
            copy.start()

    def stage(part, source):
        for head in range(HEADS):
            chunks[head, part] = source[:, :, head * HDIM : (head + 1) * HDIM]

    local[0].wait()
    stage(0, stale.at[0])
    local[1].wait()
    stage(1, stale.at[1])
    local[2].wait()
    stage(2, own)

    pl.semaphore_wait(barrier, PEERS - 1)

    keys_values = pl.ds(0, 2)
    queries = pl.ds(2, 1)

    def remote(source, target, sent, received, peer):
        return pltpu.make_async_remote_copy(
            src_ref=source,
            dst_ref=target,
            send_sem=sent,
            recv_sem=received,
            device_id=(image, peer),
            device_id_type=MESH,
        )

    def send(parts, sent, received_of):
        def step(k, carry):
            peer = partner(me, k)

            @pl.when(owner_rank(peer, core) < 3)
            def _():
                source = chunks.at[owned_head(peer, core), parts]
                remote(source, inbox.at[me, parts], sent, received_of(k), peer).start()

            return carry

        lax.fori_loop(1, PEERS, step, 0)

        @pl.when(is_owner)
        def _():
            source = chunks.at[my_head, parts]
            pltpu.make_async_copy(source, inbox.at[me, parts], received_of(PEERS)).start()

    send(keys_values, kv_sent, lambda k: kv_sem)
    send(queries, q_sent, lambda k: q_sem.at[(k - 1) // CPEERS])

    def wait_for(ref, sem):
        pltpu.make_async_copy(ref, ref, sem).wait()

    local[3].wait()
    local[4].wait()
    n = counts[0, image]
    length = counts[1, image]

    @pl.when(is_owner)
    def _():
        key = lax.broadcasted_iota(jnp.int32, (1, KEYS), 1)
        block = (key >> 4) + jnp.where(key < BLOCKS * BLK, 0, HDIM)
        slot = block - 3 * ((block * 171) >> 9)
        past = jnp.where(key < BLOCKS * BLK, slot - n, key - BLOCKS * BLK - length)
        mark = jnp.where(past >= 0, HDIM - 1, -1)
        row = lax.broadcasted_iota(jnp.int32, (HDIM, KEYS), 0)
        turned_keys[HDIM:] = jnp.where((row == block) | (row == mark), MASKED, 0.0).astype(BF16)
        shape = (BLOCKS, BLK, HDIM)
        block = lax.broadcasted_iota(jnp.int32, shape, 0)
        lane = lax.broadcasted_iota(jnp.int32, shape, 2)
        qmask[...] = jnp.where((lane == block) | (lane == HDIM - 1), 1.0, 0.0).astype(BF16)

    def attend_own(first, count):
        heads = range(first, first + count)
        diagonal = (
            lax.broadcasted_iota(jnp.int32, (ROWS, ROWS), 0) // BLK
            == lax.broadcasted_iota(jnp.int32, (ROWS, ROWS), 1) // BLK
        )

        def third(which, head):
            at = which * HD + head * HDIM
            return own[:, :, at : at + HDIM].reshape(ROWS, HDIM)

        scores = [jnp.where(diagonal, nt(third(0, head), third(1, head)), MASKED) for head in heads]
        tops = [jnp.max(x, axis=1, keepdims=True) for x in scores]
        weights = [jnp.exp2((x - top) * SCALE) for x, top in zip(scores, tops)]
        totals = [jnp.sum(x, axis=1, keepdims=True) for x in weights]
        sums = [
            jnp.dot(x.astype(BF16), third(2, head), preferred_element_type=F32) for x, head in zip(weights, heads)
        ]
        for i, head in enumerate(heads):
            ownout[head] = sums[i] / totals[i]
            ownlse[head] = jnp.broadcast_to(tops[i] * SCALE + jnp.log2(totals[i]), (ROWS, HDIM))

    attend_own(0, HEADS)

    def send_back(group, source, target, sent, received):
        def step(k, carry):
            peer = origin(me, k)

            @pl.when(peer != me)
            def _():
                remote(source.at[peer], target, sent, received, peer).start()

            @pl.when(peer == me)
            def _():
                pltpu.make_async_copy(source.at[peer], target, received).start()

            return carry

        lax.fori_loop(group * CPEERS + 1, (group + 1) * CPEERS + 1, step, 0)

    @pl.when(is_owner)
    def _():
        for copy in texts:
            copy.wait()
        wait_for(inbox.at[:, keys_values], kv_sem)
        k = jnp.concatenate([inbox[:, 0].reshape(BLOCKS * BLK, HDIM), tkeys[...].reshape(TXT, HDIM)], axis=0)
        turned_keys[:HDIM] = k.T
        v = jnp.concatenate([inbox[:, 1].reshape(BLOCKS * BLK, HDIM), tvalues[...].reshape(TXT, HDIM)], axis=0)
        lane = lax.broadcasted_iota(jnp.int32, (ROWS, HDIM), 1)
        for group in range(GROUPS):
            wait_for(inbox.at[pl.ds(0, CPEERS), queries], q_sem.at[group])
            peers = [origin(me, group * CPEERS + i + 1) for i in range(CPEERS)]
            q = jnp.concatenate([inbox[peer, 2].reshape(ROWS, HDIM) for peer in peers], axis=0)
            marks = jnp.concatenate([qmask[pl.ds(peer * LIVE, LIVE)].reshape(ROWS, HDIM) for peer in peers], axis=0)
            sbuf[group] = jnp.dot(
                jnp.concatenate([q, marks], axis=1), turned_keys[...], preferred_element_type=F32
            )
            stats = jnp.zeros((ROWS, HDIM), F32)
            for i in range(CPEERS):
                rows = slice(i * ROWS, (i + 1) * ROWS)
                scores = sbuf[group, rows]
                top = jnp.max(scores, axis=1, keepdims=True)
                weights = jnp.exp2((scores - top) * SCALE)
                total = jnp.sum(weights, axis=1, keepdims=True)
                pbuf[group, rows] = weights.astype(BF16)
                linv[group, rows] = jnp.broadcast_to(1.0 / total, (ROWS, HDIM))
                stats = jnp.where(lane == i, top * SCALE + jnp.log2(total), stats)
            turned = jnp.concatenate([stats, jnp.zeros((HDIM - ROWS, HDIM), F32)], axis=0).T
            attended = jnp.dot(pbuf[group], v, preferred_element_type=F32) * linv[group]
            attended = attended.astype(BF16).reshape(CPEERS, LIVE, BLK, HDIM)
            for i, peer in enumerate(peers):
                osend[peer] = attended[i]
                lsend[peer] = turned[i : i + 1]
            send_back(group, lsend, lrecv.at[my_head], l_sent, l_sem)
            send_back(group, osend, orecv.at[my_head], o_sent, o_sem)

    @pl.when(is_owner)
    def _():
        wait_for(inbox.at[pl.ds(0, HEADS - 1), keys_values], kv_sent)
        wait_for(inbox.at[pl.ds(0, HEADS - 1), queries], q_sent)

    @pl.when(jnp.logical_not(is_owner))
    def _():
        wait_for(inbox.at[pl.ds(0, HEADS), keys_values], kv_sent)
        wait_for(inbox.at[pl.ds(0, HEADS), queries], q_sent)

    wait_for(lrecv, l_sem)
    stacked = jnp.concatenate([lrecv[head] for head in range(HEADS)] + [jnp.zeros((HDIM - HEADS, HDIM), F32)], axis=0)
    columns = stacked.T
    shown = lax.broadcasted_iota(jnp.int32, (LIVE, BLK, HDIM), 0) < n
    for head in range(HEADS):
        sibling = jnp.broadcast_to(columns[:ROWS, head : head + 1], (ROWS, HDIM))
        within = ownlse[head]
        top = jnp.maximum(sibling, within)
        a = jnp.exp2(sibling - top)
        b = jnp.exp2(within - top)
        inverse = 1.0 / (a + b)
        coef[head] = a * inverse
        ownout[head] = ownout[head] * (b * inverse)
    wait_for(orecv, o_sem)
    for head in range(HEADS):
        merged = orecv[head].reshape(ROWS, HDIM).astype(F32) * coef[head] + ownout[head]
        merged = jnp.where(shown, merged.reshape(LIVE, BLK, HDIM), 0.0)
        out[:, :, head * HDIM : (head + 1) * HDIM] = merged.astype(BF16)

    @pl.when(is_owner)
    def _():
        wait_for(lsend.at[pl.ds(0, PEERS - 1)], l_sent)
        wait_for(osend.at[pl.ds(0, PEERS - 1)], o_sent)


def attention(fresh, keys, values, text, slots, lengths):
    anywhere = pl.BlockSpec(memory_space=pl.ANY)
    semaphore = pltpu.SemaphoreType.DMA
    return pl.pallas_call(
        kernel,
        out_shape=jax.ShapeDtypeStruct((LIVE, BLK, HD), BF16),
        in_specs=[anywhere] * 6,
        out_specs=pl.BlockSpec(memory_space=pltpu.VMEM),
        scratch_shapes=[
            pltpu.VMEM((LIVE, BLK, 3 * HD), BF16),
            pltpu.VMEM((2, LIVE, BLK, HD), BF16),
            pltpu.VMEM((HEADS, 3, LIVE, BLK, HDIM), BF16),
            pltpu.VMEM((PEERS, 3, LIVE, BLK, HDIM), BF16),
            pltpu.VMEM((TBLOCKS, BLK, HDIM), BF16),
            pltpu.VMEM((TBLOCKS, BLK, HDIM), BF16),
            pltpu.VMEM((BLOCKS, BLK, HDIM), BF16),
            pltpu.VMEM((2 * HDIM, KEYS), BF16),
            pltpu.VMEM((GROUPS, CROWS, KEYS), F32),
            pltpu.VMEM((GROUPS, CROWS, KEYS), BF16),
            pltpu.VMEM((GROUPS, CROWS, HDIM), F32),
            pltpu.VMEM((PEERS, LIVE, BLK, HDIM), BF16),
            pltpu.VMEM((PEERS, 1, HDIM), F32),
            pltpu.VMEM((HEADS, LIVE, BLK, HDIM), BF16),
            pltpu.VMEM((HEADS, 1, HDIM), F32),
            pltpu.VMEM((HEADS, ROWS, HDIM), F32),
            pltpu.VMEM((HEADS, ROWS, HDIM), F32),
            pltpu.VMEM((HEADS, ROWS, HDIM), F32),
            pltpu.SMEM((2, IMAGES), jnp.int32),
            semaphore((5,)),
            semaphore((2,)),
            semaphore((GROUPS,)),
        ]
        + [semaphore] * 7,
        compiler_params=pltpu.CompilerParams(
            collective_id=0, has_side_effects=True, vmem_limit_bytes=24 * 1024 * 1024
        ),
    )(*[pltpu.with_memory_space_constraint(x, pltpu.HBM) for x in (fresh, keys, values, text, slots, lengths)])


def body(fresh, stale_keys, stale_values, text_kv, group_slots, text_len):
    slot_count = fresh.shape[2]
    text = text_kv[0].reshape(TBLOCKS, BLK, 2 * HD)
    merged = attention(fresh[0, 0], stale_keys[0, 0], stale_values[0, 0], text, group_slots, text_len)
    return jnp.pad(merged, ((0, slot_count - LIVE), (0, 0), (0, 0)))[None, None]


def solution(mesh):
    placed = (
        P("img", "patch", None, None, None),
        P("img", "patch", None, None, None),
        P("img", "patch", None, None, None),
        P("img", None, None),
        P(),
        P(),
    )
    return jax.shard_map(
        body,
        mesh=mesh,
        in_specs=placed,
        out_specs=P("img", "patch", None, None, None),
        check_vma=False,
    )
```

```python
import functools

import jax
import jax.numpy as jnp
from jax import lax
from jax.experimental import pallas as pl
from jax.experimental.pallas import tpu as pltpu
from jax.sharding import PartitionSpec as P

MESH = pl.DeviceIdType.MESH
F32 = jnp.float32
BF16 = jnp.bfloat16

HDIM = 128
HEADS = 12
HD = HDIM * HEADS
BLK = 16
LIVE = 3
TXT = 128
PEERS = 16
IMAGES = 32
ROWS = LIVE * BLK
BLOCKS = PEERS * LIVE
TBLOCKS = TXT // BLK
KEYS = BLOCKS * BLK + TXT
CHUNKS = 2
CPEERS = PEERS // CHUNKS
CROWS = CPEERS * ROWS
SCALE = 1.4426950408889634 / HDIM**0.5
MASKED = -1e30


def nt(a, b):
    return lax.dot_general(a, b, (((1,), (1,)), ((), ())), preferred_element_type=F32)


def owner_rank(peer, core):
    z, x = peer // 2, peer % 2
    return lax.rem(z + 15 - 2 * core - x, 4)


def owned_head(peer, core):
    z, x = peer // 2, peer % 2
    return (z // 4) * 6 + x * 3 + owner_rank(peer, core)


def offset_of(k):
    half = k // 2
    odd = lax.rem(k, 2)
    return lax.rem(PEERS // 2 + odd * half + (1 - odd) * (PEERS - half), PEERS)


def partner(me, k):
    return lax.rem(me + offset_of(k), PEERS)


def kernel(
    fresh, keys, values, text, slots_in, lengths_in, out,
    own, stale, chunks, inbox, tkeys, tvalues, qmask, turned_keys, sbuf, pbuf, linv,
    osend, lsend, orecv, lrecv, ownout, ownlse, coef, counts,
    local_sem, text_sem, kq_sem, v_sem, o_sem, l_sem, kq_sent, v_sent, o_sent, l_sent,
):
    image = lax.axis_index("img")
    me = lax.axis_index("patch")
    core = lax.rem(image, 2)
    is_owner = owner_rank(me, core) < 3
    my_head = owned_head(me, core)

    barrier = pltpu.get_barrier_semaphore()

    def greet(k, carry):
        pl.semaphore_signal(barrier, inc=1, device_id=(image, partner(me, k)), device_id_type=MESH)
        return carry

    lax.fori_loop(1, PEERS, greet, 0)

    live = pl.ds(0, LIVE)
    local = [
        pltpu.make_async_copy(keys.at[live], stale.at[0], local_sem.at[0]),
        pltpu.make_async_copy(fresh.at[live], own, local_sem.at[1]),
        pltpu.make_async_copy(values.at[live], stale.at[1], local_sem.at[2]),
        pltpu.make_async_copy(slots_in, counts.at[0], local_sem.at[3]),
        pltpu.make_async_copy(lengths_in, counts.at[1], local_sem.at[4]),
    ]
    for copy in local:
        copy.start()

    def text_copy(third, target):
        columns = pl.ds(pl.multiple_of(third * HD + my_head * HDIM, HDIM), HDIM)
        return pltpu.make_async_copy(text.at[:, :, columns], target, text_sem.at[third])

    texts = [text_copy(0, tkeys), text_copy(1, tvalues)]

    @pl.when(is_owner)
    def _():
        for copy in texts:
            copy.start()

    def stage(part, source):
        for head in range(HEADS):
            chunks[head, part] = source[:, :, head * HDIM : (head + 1) * HDIM]

    local[0].wait()
    stage(0, stale.at[0])
    local[1].wait()
    stage(1, own)
    local[2].wait()
    stage(2, stale.at[1])

    pl.semaphore_wait(barrier, PEERS - 1)

    keys_queries = pl.ds(0, 2)
    only_values = pl.ds(2, 1)

    def send(peer, parts, sent, received):
        pltpu.make_async_remote_copy(
            src_ref=chunks.at[owned_head(peer, core), parts],
            dst_ref=inbox.at[me, parts],
            send_sem=sent,
            recv_sem=received,
            device_id=(image, peer),
            device_id_type=MESH,
        ).start()

    def send_all(parts, sent, received):
        def step(k, carry):
            peer = partner(me, k)

            @pl.when(owner_rank(peer, core) < 3)
            def _():
                send(peer, parts, sent, received)

            return carry

        lax.fori_loop(1, PEERS, step, 0)

        @pl.when(is_owner)
        def _():
            pltpu.make_async_copy(chunks.at[my_head, parts], inbox.at[me, parts], received).start()

    send_all(keys_queries, kq_sent, kq_sem)
    send_all(only_values, v_sent, v_sem)

    def wait_for(ref, sem):
        pltpu.make_async_copy(ref, ref, sem).wait()

    local[3].wait()
    local[4].wait()
    n = counts[0, image]
    length = counts[1, image]

    @pl.when(is_owner)
    def _():
        key = lax.broadcasted_iota(jnp.int32, (1, KEYS), 1)
        block = (key >> 4) + jnp.where(key < BLOCKS * BLK, 0, HDIM)
        slot = block - 3 * ((block * 171) >> 9)
        past = jnp.where(key < BLOCKS * BLK, slot - n, key - BLOCKS * BLK - length)
        mark = jnp.where(past >= 0, HDIM - 1, -1)
        row = lax.broadcasted_iota(jnp.int32, (HDIM, KEYS), 0)
        turned_keys[HDIM:] = jnp.where((row == block) | (row == mark), MASKED, 0.0).astype(BF16)
        shape = (BLOCKS, BLK, HDIM)
        block = lax.broadcasted_iota(jnp.int32, shape, 0)
        lane = lax.broadcasted_iota(jnp.int32, shape, 2)
        qmask[...] = jnp.where((lane == block) | (lane == HDIM - 1), 1.0, 0.0).astype(BF16)

    def attend_own(first, count):
        heads = range(first, first + count)
        diagonal = (
            lax.broadcasted_iota(jnp.int32, (ROWS, ROWS), 0) // BLK
            == lax.broadcasted_iota(jnp.int32, (ROWS, ROWS), 1) // BLK
        )

        def third(which, head):
            at = which * HD + head * HDIM
            return own[:, :, at : at + HDIM].reshape(ROWS, HDIM)

        scores = [jnp.where(diagonal, nt(third(0, head), third(1, head)), MASKED) for head in heads]
        tops = [jnp.max(x, axis=1, keepdims=True) for x in scores]
        weights = [jnp.exp2((x - top) * SCALE) for x, top in zip(scores, tops)]
        totals = [jnp.sum(x, axis=1, keepdims=True) for x in weights]
        sums = [
            jnp.dot(x.astype(BF16), third(2, head), preferred_element_type=F32) for x, head in zip(weights, heads)
        ]
        for i, head in enumerate(heads):
            ownout[head] = sums[i] / totals[i]
            ownlse[head] = jnp.broadcast_to(tops[i] * SCALE + jnp.log2(totals[i]), (ROWS, HDIM))

    def send_back(first, count, source, target, sent, received):
        def step(k, carry):
            peer = partner(me, k)

            @pl.when(peer != me)
            def _():
                pltpu.make_async_remote_copy(
                    src_ref=source.at[peer],
                    dst_ref=target,
                    send_sem=sent,
                    recv_sem=received,
                    device_id=(image, peer),
                    device_id_type=MESH,
                ).start()

            @pl.when(peer == me)
            def _():
                pltpu.make_async_copy(source.at[peer], target, received).start()

            return carry

        lax.fori_loop(first, first + count, step, 0)

    @pl.when(is_owner)
    def _():
        for copy in texts:
            copy.wait()
        wait_for(inbox.at[:, keys_queries], kq_sem)
        k = jnp.concatenate([inbox[:, 0].reshape(BLOCKS * BLK, HDIM), tkeys[...].reshape(TXT, HDIM)], axis=0)
        turned_keys[:HDIM] = k.T
        q = jnp.concatenate(
            [inbox[:, 1].reshape(BLOCKS * BLK, HDIM), qmask[...].reshape(BLOCKS * BLK, HDIM)], axis=1
        )
        sbuf[...] = jnp.dot(q, turned_keys[...], preferred_element_type=F32)
        lane = lax.broadcasted_iota(jnp.int32, (ROWS, HDIM), 1)
        stats = jnp.zeros((ROWS, HDIM), F32)
        for peer in range(PEERS):
            rows = slice(peer * ROWS, (peer + 1) * ROWS)
            scores = sbuf[rows]
            top = jnp.max(scores, axis=1, keepdims=True)
            weights = jnp.exp2((scores - top) * SCALE)
            total = jnp.sum(weights, axis=1, keepdims=True)
            pbuf[peer] = weights.astype(BF16)
            linv[peer] = jnp.broadcast_to(1.0 / total, (ROWS, HDIM))
            stats = jnp.where(lane == peer, top * SCALE + jnp.log2(total), stats)
        turned = jnp.concatenate([stats, jnp.zeros((HDIM - ROWS, HDIM), F32)], axis=0).T
        for peer in range(PEERS):
            lsend[peer] = turned[peer : peer + 1]
        send_back(1, PEERS, lsend, lrecv.at[my_head], l_sent, l_sem)

        wait_for(inbox.at[:, only_values], v_sem)
        v = jnp.concatenate([inbox[:, 2].reshape(BLOCKS * BLK, HDIM), tvalues[...].reshape(TXT, HDIM)], axis=0)
        for chunk in range(CHUNKS):
            peers = [partner(me, chunk * CPEERS + i + 1) for i in range(CPEERS)]
            weights = jnp.concatenate([pbuf[peer] for peer in peers], axis=0)
            attended = jnp.dot(weights, v, preferred_element_type=F32)
            for i, peer in enumerate(peers):
                scaled = attended[i * ROWS : (i + 1) * ROWS] * linv[peer]
                osend[peer] = scaled.astype(BF16).reshape(LIVE, BLK, HDIM)
            send_back(chunk * CPEERS + 1, CPEERS, osend, orecv.at[my_head], o_sent, o_sem)

    attend_own(0, HEADS)

    @pl.when(is_owner)
    def _():
        wait_for(inbox.at[pl.ds(0, HEADS - 1), keys_queries], kq_sent)
        wait_for(inbox.at[pl.ds(0, HEADS - 1), only_values], v_sent)

    @pl.when(jnp.logical_not(is_owner))
    def _():
        wait_for(inbox.at[pl.ds(0, HEADS), keys_queries], kq_sent)
        wait_for(inbox.at[pl.ds(0, HEADS), only_values], v_sent)

    wait_for(lrecv, l_sem)
    stacked = jnp.concatenate([lrecv[head] for head in range(HEADS)] + [jnp.zeros((HDIM - HEADS, HDIM), F32)], axis=0)
    columns = stacked.T
    shown = lax.broadcasted_iota(jnp.int32, (LIVE, BLK, HDIM), 0) < n
    for head in range(HEADS):
        sibling = jnp.broadcast_to(columns[:ROWS, head : head + 1], (ROWS, HDIM))
        within = ownlse[head]
        top = jnp.maximum(sibling, within)
        a = jnp.exp2(sibling - top)
        b = jnp.exp2(within - top)
        inverse = 1.0 / (a + b)
        coef[head] = a * inverse
        ownout[head] = ownout[head] * (b * inverse)
    wait_for(orecv, o_sem)
    for head in range(HEADS):
        merged = orecv[head].reshape(ROWS, HDIM).astype(F32) * coef[head] + ownout[head]
        merged = jnp.where(shown, merged.reshape(LIVE, BLK, HDIM), 0.0)
        out[:, :, head * HDIM : (head + 1) * HDIM] = merged.astype(BF16)

    @pl.when(is_owner)
    def _():
        wait_for(lsend.at[pl.ds(0, PEERS - 1)], l_sent)
        wait_for(osend.at[pl.ds(0, PEERS - 1)], o_sent)


def attention(fresh, keys, values, text, slots, lengths):
    anywhere = pl.BlockSpec(memory_space=pl.ANY)
    semaphore = pltpu.SemaphoreType.DMA
    return pl.pallas_call(
        kernel,
        out_shape=jax.ShapeDtypeStruct((LIVE, BLK, HD), BF16),
        in_specs=[anywhere] * 6,
        out_specs=pl.BlockSpec(memory_space=pltpu.VMEM),
        scratch_shapes=[
            pltpu.VMEM((LIVE, BLK, 3 * HD), BF16),
            pltpu.VMEM((2, LIVE, BLK, HD), BF16),
            pltpu.VMEM((HEADS, 3, LIVE, BLK, HDIM), BF16),
            pltpu.VMEM((PEERS, 3, LIVE, BLK, HDIM), BF16),
            pltpu.VMEM((TBLOCKS, BLK, HDIM), BF16),
            pltpu.VMEM((TBLOCKS, BLK, HDIM), BF16),
            pltpu.VMEM((BLOCKS, BLK, HDIM), BF16),
            pltpu.VMEM((2 * HDIM, KEYS), BF16),
            pltpu.VMEM((BLOCKS * BLK, KEYS), F32),
            pltpu.VMEM((PEERS, ROWS, KEYS), BF16),
            pltpu.VMEM((PEERS, ROWS, HDIM), F32),
            pltpu.VMEM((PEERS, LIVE, BLK, HDIM), BF16),
            pltpu.VMEM((PEERS, 1, HDIM), F32),
            pltpu.VMEM((HEADS, LIVE, BLK, HDIM), BF16),
            pltpu.VMEM((HEADS, 1, HDIM), F32),
            pltpu.VMEM((HEADS, ROWS, HDIM), F32),
            pltpu.VMEM((HEADS, ROWS, HDIM), F32),
            pltpu.VMEM((HEADS, ROWS, HDIM), F32),
            pltpu.SMEM((2, IMAGES), jnp.int32),
            semaphore((5,)),
            semaphore((2,)),
        ]
        + [semaphore] * 8,
        compiler_params=pltpu.CompilerParams(
            collective_id=0, has_side_effects=True, vmem_limit_bytes=24 * 1024 * 1024
        ),
    )(*[pltpu.with_memory_space_constraint(x, pltpu.HBM) for x in (fresh, keys, values, text, slots, lengths)])


def body(fresh, stale_keys, stale_values, text_kv, group_slots, text_len):
    slot_count = fresh.shape[2]
    text = text_kv[0].reshape(TBLOCKS, BLK, 2 * HD)
    merged = attention(fresh[0, 0], stale_keys[0, 0], stale_values[0, 0], text, group_slots, text_len)
    return jnp.pad(merged, ((0, slot_count - LIVE), (0, 0), (0, 0)))[None, None]


def solution(mesh):
    placed = (
        P("img", "patch", None, None, None),
        P("img", "patch", None, None, None),
        P("img", "patch", None, None, None),
        P("img", None, None),
        P(),
        P(),
    )
    return jax.shard_map(
        body,
        mesh=mesh,
        in_specs=placed,
        out_specs=P("img", "patch", None, None, None),
        check_vma=False,
    )
```

```python
import functools

import jax
import jax.numpy as jnp
from jax import lax
from jax.experimental import pallas as pl
from jax.experimental.pallas import tpu as pltpu
from jax.sharding import PartitionSpec as P

MESH = pl.DeviceIdType.MESH
F32 = jnp.float32
BF16 = jnp.bfloat16

HDIM = 128
HEADS = 12
HD = HDIM * HEADS
BLK = 16
LIVE = 3
TXT = 128
PEERS = 16
IMAGES = 32
ROWS = LIVE * BLK
BLOCKS = PEERS * LIVE
TBLOCKS = TXT // BLK
KEYS = BLOCKS * BLK + TXT
GROUPS = 4
CPEERS = PEERS // GROUPS
CROWS = CPEERS * ROWS
SCALE = 1.4426950408889634 / HDIM**0.5
MASKED = -1e30


def nt(a, b):
    return lax.dot_general(a, b, (((1,), (1,)), ((), ())), preferred_element_type=F32)


def owner_rank(peer, core):
    z, x = peer // 2, peer % 2
    return lax.rem(z + 15 - 2 * core - x, 4)


def owned_head(peer, core):
    z, x = peer // 2, peer % 2
    return (z // 4) * 6 + x * 3 + owner_rank(peer, core)


def offset_of(k):
    half = k // 2
    odd = lax.rem(k, 2)
    return lax.rem(PEERS // 2 + odd * half + (1 - odd) * (PEERS - half), PEERS)


def partner(me, k):
    return lax.rem(me + offset_of(k), PEERS)


def origin(me, k):
    return lax.rem(me + PEERS - offset_of(k), PEERS)


def kernel(
    fresh, keys, values, text, slots_in, lengths_in, out,
    own, stale, chunks, inbox, tkeys, tvalues, qmask, turned_keys, sbuf, pbuf, linv,
    osend, lsend, orecv, lrecv, ownout, ownlse, coef, counts,
    local_sem, text_sem, sent_sem, q_sem, k_sem, v_sem, o_sem, l_sem, o_sent, l_sent,
):
    image = lax.axis_index("img")
    me = lax.axis_index("patch")
    core = lax.rem(image, 2)
    is_owner = owner_rank(me, core) < 3
    my_head = owned_head(me, core)

    barrier = pltpu.get_barrier_semaphore()

    def greet(k, carry):
        pl.semaphore_signal(barrier, inc=1, device_id=(image, partner(me, k)), device_id_type=MESH)
        return carry

    lax.fori_loop(1, PEERS, greet, 0)

    live = pl.ds(0, LIVE)
    local = [
        pltpu.make_async_copy(keys.at[live], stale.at[0], local_sem.at[0]),
        pltpu.make_async_copy(fresh.at[live], own, local_sem.at[1]),
        pltpu.make_async_copy(values.at[live], stale.at[1], local_sem.at[2]),
        pltpu.make_async_copy(slots_in, counts.at[0], local_sem.at[3]),
        pltpu.make_async_copy(lengths_in, counts.at[1], local_sem.at[4]),
    ]
    for copy in local:
        copy.start()

    def text_copy(third, target):
        columns = pl.ds(pl.multiple_of(third * HD + my_head * HDIM, HDIM), HDIM)
        return pltpu.make_async_copy(text.at[:, :, columns], target, text_sem.at[third])

    texts = [text_copy(0, tkeys), text_copy(1, tvalues)]

    @pl.when(is_owner)
    def _():
        for copy in texts:
            copy.start()

    def stage(part, source):
        for head in range(HEADS):
            chunks[head, part] = source[:, :, head * HDIM : (head + 1) * HDIM]

    local[0].wait()
    stage(0, stale.at[0])
    local[1].wait()
    stage(1, own)
    local[2].wait()
    stage(2, stale.at[1])

    pl.semaphore_wait(barrier, PEERS - 1)

    def remote(source, target, sent, received, peer):
        return pltpu.make_async_remote_copy(
            src_ref=source,
            dst_ref=target,
            send_sem=sent,
            recv_sem=received,
            device_id=(image, peer),
            device_id_type=MESH,
        )

    def send(part, received_of):
        def step(k, carry):
            peer = partner(me, k)

            @pl.when(owner_rank(peer, core) < 3)
            def _():
                source = chunks.at[owned_head(peer, core), part]
                remote(source, inbox.at[me, part], sent_sem.at[part], received_of(k), peer).start()

            return carry

        lax.fori_loop(1, PEERS, step, 0)

        @pl.when(is_owner)
        def _():
            pltpu.make_async_copy(chunks.at[my_head, part], inbox.at[me, part], received_of(PEERS)).start()

    send(0, lambda k: k_sem)
    send(1, lambda k: q_sem.at[(k - 1) // CPEERS])
    send(2, lambda k: v_sem)

    def wait_for(ref, sem):
        pltpu.make_async_copy(ref, ref, sem).wait()

    local[3].wait()
    local[4].wait()
    n = counts[0, image]
    length = counts[1, image]

    @pl.when(is_owner)
    def _():
        key = lax.broadcasted_iota(jnp.int32, (1, KEYS), 1)
        block = (key >> 4) + jnp.where(key < BLOCKS * BLK, 0, HDIM)
        slot = block - 3 * ((block * 171) >> 9)
        past = jnp.where(key < BLOCKS * BLK, slot - n, key - BLOCKS * BLK - length)
        mark = jnp.where(past >= 0, HDIM - 1, -1)
        row = lax.broadcasted_iota(jnp.int32, (HDIM, KEYS), 0)
        turned_keys[HDIM:] = jnp.where((row == block) | (row == mark), MASKED, 0.0).astype(BF16)
        shape = (BLOCKS, BLK, HDIM)
        block = lax.broadcasted_iota(jnp.int32, shape, 0)
        lane = lax.broadcasted_iota(jnp.int32, shape, 2)
        qmask[...] = jnp.where((lane == block) | (lane == HDIM - 1), 1.0, 0.0).astype(BF16)

    def attend_own(first, count):
        heads = range(first, first + count)
        diagonal = (
            lax.broadcasted_iota(jnp.int32, (ROWS, ROWS), 0) // BLK
            == lax.broadcasted_iota(jnp.int32, (ROWS, ROWS), 1) // BLK
        )

        def third(which, head):
            at = which * HD + head * HDIM
            return own[:, :, at : at + HDIM].reshape(ROWS, HDIM)

        scores = [jnp.where(diagonal, nt(third(0, head), third(1, head)), MASKED) for head in heads]
        tops = [jnp.max(x, axis=1, keepdims=True) for x in scores]
        weights = [jnp.exp2((x - top) * SCALE) for x, top in zip(scores, tops)]
        totals = [jnp.sum(x, axis=1, keepdims=True) for x in weights]
        sums = [
            jnp.dot(x.astype(BF16), third(2, head), preferred_element_type=F32) for x, head in zip(weights, heads)
        ]
        for i, head in enumerate(heads):
            ownout[head] = sums[i] / totals[i]
            ownlse[head] = jnp.broadcast_to(tops[i] * SCALE + jnp.log2(totals[i]), (ROWS, HDIM))

    def send_back(first, count, source, target, sent, received):
        def step(k, carry):
            peer = origin(me, k)

            @pl.when(peer != me)
            def _():
                remote(source.at[peer], target, sent, received, peer).start()

            @pl.when(peer == me)
            def _():
                pltpu.make_async_copy(source.at[peer], target, received).start()

            return carry

        lax.fori_loop(first + 1, first + count + 1, step, 0)

    @pl.when(is_owner)
    def _():
        for copy in texts:
            copy.wait()
        wait_for(inbox.at[:, 0], k_sem)
        k = jnp.concatenate([inbox[:, 0].reshape(BLOCKS * BLK, HDIM), tkeys[...].reshape(TXT, HDIM)], axis=0)
        turned_keys[:HDIM] = k.T
        lane = lax.broadcasted_iota(jnp.int32, (ROWS, HDIM), 1)
        stats = jnp.zeros((ROWS, HDIM), F32)
        for group in range(GROUPS):
            wait_for(inbox.at[pl.ds(0, CPEERS), 1], q_sem.at[group])
            peers = [origin(me, group * CPEERS + i + 1) for i in range(CPEERS)]
            q = jnp.concatenate([inbox[peer, 1].reshape(ROWS, HDIM) for peer in peers], axis=0)
            marks = jnp.concatenate([qmask[pl.ds(peer * LIVE, LIVE)].reshape(ROWS, HDIM) for peer in peers], axis=0)
            sbuf[group] = jnp.dot(
                jnp.concatenate([q, marks], axis=1), turned_keys[...], preferred_element_type=F32
            )
            for i in range(CPEERS):
                rows = slice(i * ROWS, (i + 1) * ROWS)
                scores = sbuf[group, rows]
                top = jnp.max(scores, axis=1, keepdims=True)
                weights = jnp.exp2((scores - top) * SCALE)
                total = jnp.sum(weights, axis=1, keepdims=True)
                pbuf[group, rows] = weights.astype(BF16)
                linv[group, rows] = jnp.broadcast_to(1.0 / total, (ROWS, HDIM))
                stats = jnp.where(lane == group * CPEERS + i, top * SCALE + jnp.log2(total), stats)
        turned = jnp.concatenate([stats, jnp.zeros((HDIM - ROWS, HDIM), F32)], axis=0).T
        for k in range(PEERS):
            lsend[origin(me, k + 1)] = turned[k : k + 1]
        send_back(0, PEERS, lsend, lrecv.at[my_head], l_sent, l_sem)

        wait_for(inbox.at[:, 2], v_sem)
        v = jnp.concatenate([inbox[:, 2].reshape(BLOCKS * BLK, HDIM), tvalues[...].reshape(TXT, HDIM)], axis=0)
        for half in range(2):
            groups = slice(half * GROUPS // 2, (half + 1) * GROUPS // 2)
            weights = pbuf[groups].reshape(PEERS // 2 * ROWS, KEYS)
            attended = jnp.dot(weights, v, preferred_element_type=F32)
            attended = attended * linv[groups].reshape(PEERS // 2 * ROWS, HDIM)
            attended = attended.astype(BF16).reshape(PEERS // 2, LIVE, BLK, HDIM)
            for i in range(PEERS // 2):
                osend[origin(me, half * PEERS // 2 + i + 1)] = attended[i]
            send_back(half * PEERS // 2, PEERS // 2, osend, orecv.at[my_head], o_sent, o_sem)

    attend_own(0, HEADS)

    @pl.when(is_owner)
    def _():
        for part in range(3):
            wait_for(inbox.at[pl.ds(0, HEADS - 1), part], sent_sem.at[part])

    @pl.when(jnp.logical_not(is_owner))
    def _():
        for part in range(3):
            wait_for(inbox.at[pl.ds(0, HEADS), part], sent_sem.at[part])

    wait_for(lrecv, l_sem)
    stacked = jnp.concatenate([lrecv[head] for head in range(HEADS)] + [jnp.zeros((HDIM - HEADS, HDIM), F32)], axis=0)
    columns = stacked.T
    shown = lax.broadcasted_iota(jnp.int32, (LIVE, BLK, HDIM), 0) < n
    for head in range(HEADS):
        sibling = jnp.broadcast_to(columns[:ROWS, head : head + 1], (ROWS, HDIM))
        within = ownlse[head]
        top = jnp.maximum(sibling, within)
        a = jnp.exp2(sibling - top)
        b = jnp.exp2(within - top)
        inverse = 1.0 / (a + b)
        coef[head] = a * inverse
        ownout[head] = ownout[head] * (b * inverse)
    wait_for(orecv, o_sem)
    for head in range(HEADS):
        merged = orecv[head].reshape(ROWS, HDIM).astype(F32) * coef[head] + ownout[head]
        merged = jnp.where(shown, merged.reshape(LIVE, BLK, HDIM), 0.0)
        out[:, :, head * HDIM : (head + 1) * HDIM] = merged.astype(BF16)

    @pl.when(is_owner)
    def _():
        wait_for(lsend.at[pl.ds(0, PEERS - 1)], l_sent)
        wait_for(osend.at[pl.ds(0, PEERS - 1)], o_sent)


def attention(fresh, keys, values, text, slots, lengths):
    anywhere = pl.BlockSpec(memory_space=pl.ANY)
    semaphore = pltpu.SemaphoreType.DMA
    return pl.pallas_call(
        kernel,
        out_shape=jax.ShapeDtypeStruct((LIVE, BLK, HD), BF16),
        in_specs=[anywhere] * 6,
        out_specs=pl.BlockSpec(memory_space=pltpu.VMEM),
        scratch_shapes=[
            pltpu.VMEM((LIVE, BLK, 3 * HD), BF16),
            pltpu.VMEM((2, LIVE, BLK, HD), BF16),
            pltpu.VMEM((HEADS, 3, LIVE, BLK, HDIM), BF16),
            pltpu.VMEM((PEERS, 3, LIVE, BLK, HDIM), BF16),
            pltpu.VMEM((TBLOCKS, BLK, HDIM), BF16),
            pltpu.VMEM((TBLOCKS, BLK, HDIM), BF16),
            pltpu.VMEM((BLOCKS, BLK, HDIM), BF16),
            pltpu.VMEM((2 * HDIM, KEYS), BF16),
            pltpu.VMEM((GROUPS, CROWS, KEYS), F32),
            pltpu.VMEM((GROUPS, CROWS, KEYS), BF16),
            pltpu.VMEM((GROUPS, CROWS, HDIM), F32),
            pltpu.VMEM((PEERS, LIVE, BLK, HDIM), BF16),
            pltpu.VMEM((PEERS, 1, HDIM), F32),
            pltpu.VMEM((HEADS, LIVE, BLK, HDIM), BF16),
            pltpu.VMEM((HEADS, 1, HDIM), F32),
            pltpu.VMEM((HEADS, ROWS, HDIM), F32),
            pltpu.VMEM((HEADS, ROWS, HDIM), F32),
            pltpu.VMEM((HEADS, ROWS, HDIM), F32),
            pltpu.SMEM((2, IMAGES), jnp.int32),
            semaphore((5,)),
            semaphore((2,)),
            semaphore((3,)),
            semaphore((GROUPS,)),
        ]
        + [semaphore] * 6,
        compiler_params=pltpu.CompilerParams(
            collective_id=0, has_side_effects=True, vmem_limit_bytes=24 * 1024 * 1024
        ),
    )(*[pltpu.with_memory_space_constraint(x, pltpu.HBM) for x in (fresh, keys, values, text, slots, lengths)])


def body(fresh, stale_keys, stale_values, text_kv, group_slots, text_len):
    slot_count = fresh.shape[2]
    text = text_kv[0].reshape(TBLOCKS, BLK, 2 * HD)
    merged = attention(fresh[0, 0], stale_keys[0, 0], stale_values[0, 0], text, group_slots, text_len)
    return jnp.pad(merged, ((0, slot_count - LIVE), (0, 0), (0, 0)))[None, None]


def solution(mesh):
    placed = (
        P("img", "patch", None, None, None),
        P("img", "patch", None, None, None),
        P("img", "patch", None, None, None),
        P("img", None, None),
        P(),
        P(),
    )
    return jax.shard_map(
        body,
        mesh=mesh,
        in_specs=placed,
        out_specs=P("img", "patch", None, None, None),
        check_vma=False,
    )
```

```python
import functools

import jax
import jax.numpy as jnp
from jax import lax
from jax.experimental import pallas as pl
from jax.experimental.pallas import tpu as pltpu
from jax.sharding import PartitionSpec as P

MESH = pl.DeviceIdType.MESH
F32 = jnp.float32
BF16 = jnp.bfloat16

HDIM = 128
HEADS = 12
HD = HDIM * HEADS
BLK = 16
LIVE = 3
TXT = 128
PEERS = 16
IMAGES = 32
ROWS = LIVE * BLK
BLOCKS = PEERS * LIVE
PAIRED = PEERS * (LIVE - 1)
TBLOCKS = TXT // BLK
KEYS = BLOCKS * BLK + TXT
GROUPS = 4
CPEERS = PEERS // GROUPS
CROWS = CPEERS * ROWS
SCALE = 1.4426950408889634 / HDIM**0.5
MASKED = -1e30


def nt(a, b):
    return lax.dot_general(a, b, (((1,), (1,)), ((), ())), preferred_element_type=F32)


def owner_rank(peer):
    z, x = peer // 2, lax.rem(peer, 2)
    return lax.rem(z + 7 - 2 * x, 4)


def owned_head(peer):
    z, x = peer // 2, lax.rem(peer, 2)
    return (z // 4) * 6 + x * 3 + owner_rank(peer)


def offset_of(k):
    half = k // 2
    odd = lax.rem(k, 2)
    return lax.rem(PEERS // 2 + odd * half + (1 - odd) * (PEERS - half), PEERS)


def partner(me, k):
    return lax.rem(me + offset_of(k), PEERS)


def origin(me, k):
    return lax.rem(me + PEERS - offset_of(k), PEERS)


def kernel(
    fresh, keys, values, text, slots_in, lengths_in, out,
    own, stale, chunks, third, theirs, shared, inbox, xbox, tkeys, tvalues, qmask, turned_keys, sbuf, pbuf, linv,
    osend, lsend, orecv, lrecv, ownout, ownlse, coef, counts,
    local_sem, text_sem, sent_sem, q_sem, k_sem, v_sem, x_sem, theirs_sem, o_sem, l_sem,
    o_sent, l_sent, x_sent, theirs_sent, pass_sent,
):
    image = lax.axis_index("img")
    me = lax.axis_index("patch")
    core = lax.rem(image, 2)
    is_owner = owner_rank(me) < 3
    my_head = owned_head(me)
    sibling = image + 1 - 2 * core

    barrier = pltpu.get_barrier_semaphore()

    def greet(k, carry):
        pl.semaphore_signal(barrier, inc=1, device_id=(image, partner(me, k)), device_id_type=MESH)
        return carry

    pl.semaphore_signal(barrier, inc=1, device_id=(sibling, me), device_id_type=MESH)
    lax.fori_loop(1, PEERS, greet, 0)

    live = pl.ds(0, LIVE)
    local = [
        pltpu.make_async_copy(keys.at[live], stale.at[0], local_sem.at[0]),
        pltpu.make_async_copy(fresh.at[live], own, local_sem.at[1]),
        pltpu.make_async_copy(values.at[live], stale.at[1], local_sem.at[2]),
        pltpu.make_async_copy(slots_in, counts.at[0], local_sem.at[3]),
        pltpu.make_async_copy(lengths_in, counts.at[1], local_sem.at[4]),
    ]
    for copy in local:
        copy.start()

    def text_copy(third, target):
        columns = pl.ds(pl.multiple_of(third * HD + my_head * HDIM, HDIM), HDIM)
        return pltpu.make_async_copy(text.at[:, :, columns], target, text_sem.at[third])

    texts = [text_copy(0, tkeys), text_copy(1, tvalues)]

    @pl.when(is_owner)
    def _():
        for copy in texts:
            copy.start()

    def stage(part, source):
        for head in range(HEADS):
            columns = slice(head * HDIM, (head + 1) * HDIM)
            chunks[head, part] = source[: LIVE - 1, :, columns]
            third[head, part] = source[LIVE - 1, :, columns]

    local[0].wait()
    stage(0, stale.at[0])
    local[1].wait()
    stage(1, own)
    local[2].wait()
    stage(2, stale.at[1])

    pl.semaphore_wait(barrier, PEERS)

    def remote(source, target, sent, received, peer, group=image):
        return pltpu.make_async_remote_copy(
            src_ref=source,
            dst_ref=target,
            send_sem=sent,
            recv_sem=received,
            device_id=(group, peer),
            device_id_type=MESH,
        )

    half = HEADS // 2
    exchange = remote(third.at[pl.ds(half * (1 - core), half)], theirs, theirs_sent, theirs_sem, me, sibling)
    exchange.start()

    def send(part, received_of):
        def step(k, carry):
            peer = partner(me, k)

            @pl.when(owner_rank(peer) < 3)
            def _():
                source = chunks.at[owned_head(peer), part]
                remote(source, inbox.at[me, part], sent_sem.at[part], received_of(k), peer).start()

            return carry

        lax.fori_loop(1, PEERS, step, 0)

        @pl.when(is_owner)
        def _():
            pltpu.make_async_copy(chunks.at[my_head, part], inbox.at[me, part], received_of(PEERS)).start()

    send(0, lambda k: k_sem)

    local[3].wait()
    local[4].wait()
    n = counts[0, image]
    length = counts[1, image]
    exchange.wait()
    mine = third[pl.ds(half * core, half)]
    shared[...] = jnp.where(n == LIVE, mine, theirs[...])

    def send_shared(k, carry):
        peer = partner(me, k)
        head = owned_head(peer)

        @pl.when(jnp.logical_and(owner_rank(peer) < 3, head // half == core))
        def _():
            remote(shared.at[head - half * core], xbox.at[me], x_sent, x_sem, peer).start()

        return carry

    lax.fori_loop(1, PEERS, send_shared, 0)
    is_first = jnp.logical_and(is_owner, my_head // half == core)

    @pl.when(is_first)
    def _():
        pltpu.make_async_copy(shared.at[my_head - half * core], xbox.at[me], x_sem).start()

    send(1, lambda k: q_sem.at[(k - 1) // CPEERS])
    send(2, lambda k: v_sem)

    def wait_for(ref, sem):
        pltpu.make_async_copy(ref, ref, sem).wait()

    @pl.when(is_owner)
    def _():
        key = lax.broadcasted_iota(jnp.int32, (1, KEYS), 1)
        block = (key >> 4) + jnp.where(key < BLOCKS * BLK, 0, HDIM)
        slot = jnp.where(block < PAIRED, block & 1, LIVE - 1)
        past = jnp.where(key < BLOCKS * BLK, slot - n, key - BLOCKS * BLK - length)
        mark = jnp.where(past >= 0, HDIM - 1, -1)
        row = lax.broadcasted_iota(jnp.int32, (HDIM, KEYS), 0)
        turned_keys[HDIM:] = jnp.where((row == block) | (row == mark), MASKED, 0.0).astype(BF16)
        shape = (PEERS, LIVE, BLK, HDIM)
        peer = lax.broadcasted_iota(jnp.int32, shape, 0)
        slot = lax.broadcasted_iota(jnp.int32, shape, 1)
        lane = lax.broadcasted_iota(jnp.int32, shape, 3)
        block = jnp.where(slot < LIVE - 1, peer * (LIVE - 1) + slot, PAIRED + peer)
        qmask[...] = jnp.where((lane == block) | (lane == HDIM - 1), 1.0, 0.0).astype(BF16)

    def attend_own(first, count):
        heads = range(first, first + count)
        diagonal = (
            lax.broadcasted_iota(jnp.int32, (ROWS, ROWS), 0) // BLK
            == lax.broadcasted_iota(jnp.int32, (ROWS, ROWS), 1) // BLK
        )

        def third(which, head):
            at = which * HD + head * HDIM
            return own[:, :, at : at + HDIM].reshape(ROWS, HDIM)

        scores = [jnp.where(diagonal, nt(third(0, head), third(1, head)), MASKED) for head in heads]
        tops = [jnp.max(x, axis=1, keepdims=True) for x in scores]
        weights = [jnp.exp2((x - top) * SCALE) for x, top in zip(scores, tops)]
        totals = [jnp.sum(x, axis=1, keepdims=True) for x in weights]
        sums = [
            jnp.dot(x.astype(BF16), third(2, head), preferred_element_type=F32) for x, head in zip(weights, heads)
        ]
        for i, head in enumerate(heads):
            ownout[head] = sums[i] / totals[i]
            ownlse[head] = jnp.broadcast_to(tops[i] * SCALE + jnp.log2(totals[i]), (ROWS, HDIM))

    def send_back(first, count, source, target, sent, received):
        def step(k, carry):
            peer = origin(me, k)

            @pl.when(peer != me)
            def _():
                remote(source.at[peer], target, sent, received, peer).start()

            @pl.when(peer == me)
            def _():
                pltpu.make_async_copy(source.at[peer], target, received).start()

            return carry

        lax.fori_loop(first + 1, first + count + 1, step, 0)

    @pl.when(is_owner)
    def _():
        for copy in texts:
            copy.wait()
        wait_for(inbox.at[:, 0], k_sem)

        def gather(part, texts):
            return jnp.concatenate(
                [
                    inbox[:, part].reshape(PAIRED * BLK, HDIM),
                    xbox[:, part].reshape(PEERS * BLK, HDIM),
                    texts[...].reshape(TXT, HDIM),
                ],
                axis=0,
            )

        wait_for(xbox, x_sem)

        @pl.when(is_first)
        def _():
            remote(xbox, xbox, pass_sent, x_sem, me, sibling).start()

        k = gather(0, tkeys)
        turned_keys[:HDIM] = k.T
        lane = lax.broadcasted_iota(jnp.int32, (ROWS, HDIM), 1)
        stats = jnp.zeros((ROWS, HDIM), F32)
        for group in range(GROUPS):
            wait_for(inbox.at[pl.ds(0, CPEERS), 1], q_sem.at[group])
            peers = [origin(me, group * CPEERS + i + 1) for i in range(CPEERS)]
            q = jnp.concatenate(
                [
                    part
                    for peer in peers
                    for part in (inbox[peer, 1].reshape(ROWS - BLK, HDIM), xbox[peer, 1])
                ],
                axis=0,
            )
            marks = jnp.concatenate([qmask[peer].reshape(ROWS, HDIM) for peer in peers], axis=0)
            sbuf[group] = jnp.dot(
                jnp.concatenate([q, marks], axis=1), turned_keys[...], preferred_element_type=F32
            )
            for i in range(CPEERS):
                rows = slice(i * ROWS, (i + 1) * ROWS)
                scores = sbuf[group, rows]
                top = jnp.max(scores, axis=1, keepdims=True)
                weights = jnp.exp2((scores - top) * SCALE)
                total = jnp.sum(weights, axis=1, keepdims=True)
                pbuf[group, rows] = weights.astype(BF16)
                linv[group, rows] = jnp.broadcast_to(1.0 / total, (ROWS, HDIM))
                stats = jnp.where(lane == group * CPEERS + i, top * SCALE + jnp.log2(total), stats)
        turned = jnp.concatenate([stats, jnp.zeros((HDIM - ROWS, HDIM), F32)], axis=0).T
        for k in range(PEERS):
            lsend[origin(me, k + 1)] = turned[k : k + 1]
        send_back(0, PEERS, lsend, lrecv.at[my_head], l_sent, l_sem)

        wait_for(inbox.at[:, 2], v_sem)
        v = gather(2, tvalues)
        for side in range(2):
            groups = slice(side * GROUPS // 2, (side + 1) * GROUPS // 2)
            weights = pbuf[groups].reshape(PEERS // 2 * ROWS, KEYS)
            attended = jnp.dot(weights, v, preferred_element_type=F32)
            attended = attended * linv[groups].reshape(PEERS // 2 * ROWS, HDIM)
            attended = attended.astype(BF16).reshape(PEERS // 2, LIVE, BLK, HDIM)
            for i in range(PEERS // 2):
                osend[origin(me, side * PEERS // 2 + i + 1)] = attended[i]
            send_back(side * PEERS // 2, PEERS // 2, osend, orecv.at[my_head], o_sent, o_sem)

    attend_own(0, HEADS)

    @pl.when(is_owner)
    def _():
        for part in range(3):
            wait_for(inbox.at[pl.ds(0, HEADS - 1), part], sent_sem.at[part])

    @pl.when(jnp.logical_not(is_owner))
    def _():
        for part in range(3):
            wait_for(inbox.at[pl.ds(0, HEADS), part], sent_sem.at[part])

    @pl.when(is_first)
    def _():
        wait_for(xbox.at[pl.ds(0, half - 1)], x_sent)
        wait_for(xbox, pass_sent)

    @pl.when(jnp.logical_not(is_first))
    def _():
        wait_for(xbox.at[pl.ds(0, half)], x_sent)

    wait_for(lrecv, l_sem)
    stacked = jnp.concatenate([lrecv[head] for head in range(HEADS)] + [jnp.zeros((HDIM - HEADS, HDIM), F32)], axis=0)
    columns = stacked.T
    shown = lax.broadcasted_iota(jnp.int32, (LIVE, BLK, HDIM), 0) < n
    for head in range(HEADS):
        others = jnp.broadcast_to(columns[:ROWS, head : head + 1], (ROWS, HDIM))
        within = ownlse[head]
        top = jnp.maximum(others, within)
        a = jnp.exp2(others - top)
        b = jnp.exp2(within - top)
        inverse = 1.0 / (a + b)
        coef[head] = a * inverse
        ownout[head] = ownout[head] * (b * inverse)
    wait_for(orecv, o_sem)
    for head in range(HEADS):
        merged = orecv[head].reshape(ROWS, HDIM).astype(F32) * coef[head] + ownout[head]
        merged = jnp.where(shown, merged.reshape(LIVE, BLK, HDIM), 0.0)
        out[:, :, head * HDIM : (head + 1) * HDIM] = merged.astype(BF16)

    @pl.when(is_owner)
    def _():
        wait_for(lsend.at[pl.ds(0, PEERS - 1)], l_sent)
        wait_for(osend.at[pl.ds(0, PEERS - 1)], o_sent)


def attention(fresh, keys, values, text, slots, lengths):
    anywhere = pl.BlockSpec(memory_space=pl.ANY)
    semaphore = pltpu.SemaphoreType.DMA
    return pl.pallas_call(
        kernel,
        out_shape=jax.ShapeDtypeStruct((LIVE, BLK, HD), BF16),
        in_specs=[anywhere] * 6,
        out_specs=pl.BlockSpec(memory_space=pltpu.VMEM),
        scratch_shapes=[
            pltpu.VMEM((LIVE, BLK, 3 * HD), BF16),
            pltpu.VMEM((2, LIVE, BLK, HD), BF16),
            pltpu.VMEM((HEADS, 3, LIVE - 1, BLK, HDIM), BF16),
            pltpu.VMEM((HEADS, 3, BLK, HDIM), BF16),
            pltpu.VMEM((HEADS // 2, 3, BLK, HDIM), BF16),
            pltpu.VMEM((HEADS // 2, 3, BLK, HDIM), BF16),
            pltpu.VMEM((PEERS, 3, LIVE - 1, BLK, HDIM), BF16),
            pltpu.VMEM((PEERS, 3, BLK, HDIM), BF16),
            pltpu.VMEM((TBLOCKS, BLK, HDIM), BF16),
            pltpu.VMEM((TBLOCKS, BLK, HDIM), BF16),
            pltpu.VMEM((PEERS, LIVE, BLK, HDIM), BF16),
            pltpu.VMEM((2 * HDIM, KEYS), BF16),
            pltpu.VMEM((GROUPS, CROWS, KEYS), F32),
            pltpu.VMEM((GROUPS, CROWS, KEYS), BF16),
            pltpu.VMEM((GROUPS, CROWS, HDIM), F32),
            pltpu.VMEM((PEERS, LIVE, BLK, HDIM), BF16),
            pltpu.VMEM((PEERS, 1, HDIM), F32),
            pltpu.VMEM((HEADS, LIVE, BLK, HDIM), BF16),
            pltpu.VMEM((HEADS, 1, HDIM), F32),
            pltpu.VMEM((HEADS, ROWS, HDIM), F32),
            pltpu.VMEM((HEADS, ROWS, HDIM), F32),
            pltpu.VMEM((HEADS, ROWS, HDIM), F32),
            pltpu.SMEM((2, IMAGES), jnp.int32),
            semaphore((5,)),
            semaphore((2,)),
            semaphore((3,)),
            semaphore((GROUPS,)),
        ]
        + [semaphore] * 11,
        compiler_params=pltpu.CompilerParams(
            collective_id=0, has_side_effects=True, vmem_limit_bytes=24 * 1024 * 1024
        ),
    )(*[pltpu.with_memory_space_constraint(x, pltpu.HBM) for x in (fresh, keys, values, text, slots, lengths)])


def body(fresh, stale_keys, stale_values, text_kv, group_slots, text_len):
    slot_count = fresh.shape[2]
    text = text_kv[0].reshape(TBLOCKS, BLK, 2 * HD)
    merged = attention(fresh[0, 0], stale_keys[0, 0], stale_values[0, 0], text, group_slots, text_len)
    return jnp.pad(merged, ((0, slot_count - LIVE), (0, 0), (0, 0)))[None, None]


def solution(mesh):
    placed = (
        P("img", "patch", None, None, None),
        P("img", "patch", None, None, None),
        P("img", "patch", None, None, None),
        P("img", None, None),
        P(),
        P(),
    )
    return jax.shard_map(
        body,
        mesh=mesh,
        in_specs=placed,
        out_specs=P("img", "patch", None, None, None),
        check_vma=False,
    )
```

```python
import functools

import jax
import jax.numpy as jnp
from jax import lax
from jax.experimental import pallas as pl
from jax.experimental.pallas import tpu as pltpu
from jax.sharding import PartitionSpec as P

MESH = pl.DeviceIdType.MESH
F32 = jnp.float32
BF16 = jnp.bfloat16

HDIM = 128
HEADS = 12
HD = HDIM * HEADS
BLK = 16
LIVE = 3
TXT = 128
PEERS = 16
IMAGES = 32
ROWS = LIVE * BLK
BLOCKS = PEERS * LIVE
TBLOCKS = TXT // BLK
KEYS = BLOCKS * BLK + TXT
GROUPS = 2
CPEERS = PEERS // GROUPS
CROWS = CPEERS * ROWS
SCALE = 1.4426950408889634 / HDIM**0.5
MASKED = -1e30


def nt(a, b):
    return lax.dot_general(a, b, (((1,), (1,)), ((), ())), preferred_element_type=F32)


def owner_rank(peer, core):
    z, x = peer // 2, peer % 2
    return lax.rem(z + 15 - 2 * core - x, 4)


def owned_head(peer, core):
    z, x = peer // 2, peer % 2
    return (z // 4) * 6 + x * 3 + owner_rank(peer, core)


def offset_of(k):
    half = k // 2
    odd = lax.rem(k, 2)
    return lax.rem(PEERS // 2 + odd * half + (1 - odd) * (PEERS - half), PEERS)


def partner(me, k):
    return lax.rem(me + offset_of(k), PEERS)


def origin(me, k):
    return lax.rem(me + PEERS - offset_of(k), PEERS)


def kernel(
    fresh, keys, values, text, slots_in, lengths_in, out,
    own, stale, chunks, inbox, tkeys, tvalues, qmask, kmask, turned_values, sbuf, pbuf,
    osend, lsend, orecv, lrecv, ownout, ownlse, coef, counts,
    local_sem, text_sem, q_sem, kv_sem, o_sem, l_sem, kv_sent, q_sent, o_sent, l_sent,
):
    image = lax.axis_index("img")
    me = lax.axis_index("patch")
    core = lax.rem(image, 2)
    is_owner = owner_rank(me, core) < 3
    my_head = owned_head(me, core)

    barrier = pltpu.get_barrier_semaphore()

    def greet(k, carry):
        pl.semaphore_signal(barrier, inc=1, device_id=(image, partner(me, k)), device_id_type=MESH)
        return carry

    lax.fori_loop(1, PEERS, greet, 0)

    live = pl.ds(0, LIVE)
    local = [
        pltpu.make_async_copy(keys.at[live], stale.at[0], local_sem.at[0]),
        pltpu.make_async_copy(values.at[live], stale.at[1], local_sem.at[1]),
        pltpu.make_async_copy(fresh.at[live], own, local_sem.at[2]),
        pltpu.make_async_copy(slots_in, counts.at[0], local_sem.at[3]),
        pltpu.make_async_copy(lengths_in, counts.at[1], local_sem.at[4]),
    ]
    for copy in local:
        copy.start()

    def text_copy(third, target):
        columns = pl.ds(pl.multiple_of(third * HD + my_head * HDIM, HDIM), HDIM)
        return pltpu.make_async_copy(text.at[:, :, columns], target, text_sem.at[third])

    texts = [text_copy(0, tkeys), text_copy(1, tvalues)]

    @pl.when(is_owner)
    def _():
        for copy in texts:
            copy.start()

    def stage(part, source):
        for head in range(HEADS):
            chunks[head, part] = source[:, :, head * HDIM : (head + 1) * HDIM]

    local[0].wait()
    stage(0, stale.at[0])
    local[1].wait()
    stage(1, stale.at[1])
    local[2].wait()
    stage(2, own)

    pl.semaphore_wait(barrier, PEERS - 1)

    keys_values = pl.ds(0, 2)
    queries = pl.ds(2, 1)

    def remote(source, target, sent, received, peer):
        return pltpu.make_async_remote_copy(
            src_ref=source,
            dst_ref=target,
            send_sem=sent,
            recv_sem=received,
            device_id=(image, peer),
            device_id_type=MESH,
        )

    def send(parts, sent, received_of):
        def step(k, carry):
            peer = partner(me, k)

            @pl.when(owner_rank(peer, core) < 3)
            def _():
                source = chunks.at[owned_head(peer, core), parts]
                remote(source, inbox.at[me, parts], sent, received_of(k), peer).start()

            return carry

        lax.fori_loop(1, PEERS, step, 0)

        @pl.when(is_owner)
        def _():
            source = chunks.at[my_head, parts]
            pltpu.make_async_copy(source, inbox.at[me, parts], received_of(PEERS)).start()

    send(keys_values, kv_sent, lambda k: kv_sem)
    send(queries, q_sent, lambda k: q_sem.at[(k - 1) // CPEERS])

    def wait_for(ref, sem):
        pltpu.make_async_copy(ref, ref, sem).wait()

    local[3].wait()
    local[4].wait()
    n = counts[0, image]
    length = counts[1, image]

    @pl.when(is_owner)
    def _():
        shape = (KEYS // BLK, BLK, HDIM)
        block = lax.broadcasted_iota(jnp.int32, shape, 0)
        row = lax.broadcasted_iota(jnp.int32, shape, 1)
        lane = lax.broadcasted_iota(jnp.int32, shape, 2)
        slot = block - 3 * ((block * 171) >> 9)
        past = jnp.where(block < BLOCKS, slot - n, (block - BLOCKS) * BLK + row - length)
        mark = jnp.where(past >= 0, HDIM - 1, -1)
        own_mark = jnp.where(block < BLOCKS, block, -1)
        kmask[...] = jnp.where((lane == own_mark) | (lane == mark), MASKED, 0.0).astype(BF16)
        shape = (BLOCKS, BLK, HDIM)
        block = lax.broadcasted_iota(jnp.int32, shape, 0)
        lane = lax.broadcasted_iota(jnp.int32, shape, 2)
        qmask[...] = jnp.where((lane == block) | (lane == HDIM - 1), 1.0, 0.0).astype(BF16)

    def attend_own(first, count):
        heads = range(first, first + count)
        diagonal = (
            lax.broadcasted_iota(jnp.int32, (ROWS, ROWS), 0) // BLK
            == lax.broadcasted_iota(jnp.int32, (ROWS, ROWS), 1) // BLK
        )

        def third(which, head):
            at = which * HD + head * HDIM
            return own[:, :, at : at + HDIM].reshape(ROWS, HDIM)

        scores = [jnp.where(diagonal, nt(third(0, head), third(1, head)), MASKED) for head in heads]
        tops = [jnp.max(x, axis=1, keepdims=True) for x in scores]
        weights = [jnp.exp2((x - top) * SCALE) for x, top in zip(scores, tops)]
        totals = [jnp.sum(x, axis=1, keepdims=True) for x in weights]
        sums = [
            jnp.dot(x.astype(BF16), third(2, head), preferred_element_type=F32) for x, head in zip(weights, heads)
        ]
        for i, head in enumerate(heads):
            ownout[head] = sums[i] / totals[i]
            ownlse[head] = jnp.broadcast_to(tops[i] * SCALE + jnp.log2(totals[i]), (ROWS, HDIM))

    def send_back(group, source, target, sent, received):
        def step(k, carry):
            peer = origin(me, k)

            @pl.when(peer != me)
            def _():
                remote(source.at[peer], target, sent, received, peer).start()

            @pl.when(peer == me)
            def _():
                pltpu.make_async_copy(source.at[peer], target, received).start()

            return carry

        lax.fori_loop(group * CPEERS + 1, (group + 1) * CPEERS + 1, step, 0)

    @pl.when(is_owner)
    def _():
        for copy in texts:
            copy.wait()
        wait_for(inbox.at[:, keys_values], kv_sem)
        k = jnp.concatenate([inbox[:, 0].reshape(BLOCKS * BLK, HDIM), tkeys[...].reshape(TXT, HDIM)], axis=0)
        k = jnp.concatenate([k, kmask[...].reshape(KEYS, HDIM)], axis=1)
        v = jnp.concatenate([inbox[:, 1].reshape(BLOCKS * BLK, HDIM), tvalues[...].reshape(TXT, HDIM)], axis=0)
        turned_values[...] = v.T
        for group in range(GROUPS):
            wait_for(inbox.at[pl.ds(0, CPEERS), queries], q_sem.at[group])
            peers = [origin(me, group * CPEERS + i + 1) for i in range(CPEERS)]
            q = jnp.concatenate([inbox[peer, 2].reshape(ROWS, HDIM) for peer in peers], axis=0)
            marks = jnp.concatenate([qmask[pl.ds(peer * LIVE, LIVE)].reshape(ROWS, HDIM) for peer in peers], axis=0)
            sbuf[group] = nt(k, jnp.concatenate([q, marks], axis=1))
            inverses, lses = [], []
            for at in range(0, CROWS, HDIM):
                columns = slice(at, at + HDIM)
                top = jnp.max(sbuf[group, :, columns], axis=0, keepdims=True)
                sums = jnp.zeros((8, HDIM), F32)
                for row in range(0, KEYS, HDIM):
                    rows = slice(row, row + HDIM)
                    weights = jnp.exp2((sbuf[group, rows, columns] - top) * SCALE)
                    sums = sums + jnp.sum(weights.reshape(HDIM // 8, 8, HDIM), axis=0)
                    pbuf[group, rows, columns] = weights.astype(BF16)
                total = jnp.sum(sums, axis=0, keepdims=True)
                inverses.append(1.0 / total)
                lses.append(top * SCALE + jnp.log2(total))
            lse = jnp.concatenate(lses, axis=1)
            for i, peer in enumerate(peers):
                row = lse[:, i * ROWS : (i + 1) * ROWS]
                lsend[peer] = jnp.concatenate([row, jnp.zeros((1, HDIM - ROWS), F32)], axis=1)
            send_back(group, lsend, lrecv.at[my_head], l_sent, l_sem)
            attended = jnp.dot(turned_values[...], pbuf[group], preferred_element_type=F32)
            attended = (attended * jnp.concatenate(inverses, axis=1)).T.astype(BF16)
            attended = attended.reshape(CPEERS, LIVE, BLK, HDIM)
            for i, peer in enumerate(peers):
                osend[peer] = attended[i]
            send_back(group, osend, orecv.at[my_head], o_sent, o_sem)

    attend_own(0, HEADS)

    @pl.when(is_owner)
    def _():
        wait_for(inbox.at[pl.ds(0, HEADS - 1), keys_values], kv_sent)
        wait_for(inbox.at[pl.ds(0, HEADS - 1), queries], q_sent)

    @pl.when(jnp.logical_not(is_owner))
    def _():
        wait_for(inbox.at[pl.ds(0, HEADS), keys_values], kv_sent)
        wait_for(inbox.at[pl.ds(0, HEADS), queries], q_sent)

    wait_for(lrecv, l_sem)
    stacked = jnp.concatenate([lrecv[head] for head in range(HEADS)] + [jnp.zeros((HDIM - HEADS, HDIM), F32)], axis=0)
    columns = stacked.T
    shown = lax.broadcasted_iota(jnp.int32, (LIVE, BLK, HDIM), 0) < n
    for head in range(HEADS):
        sibling = jnp.broadcast_to(columns[:ROWS, head : head + 1], (ROWS, HDIM))
        within = ownlse[head]
        top = jnp.maximum(sibling, within)
        a = jnp.exp2(sibling - top)
        b = jnp.exp2(within - top)
        inverse = 1.0 / (a + b)
        coef[head] = a * inverse
        ownout[head] = ownout[head] * (b * inverse)
    wait_for(orecv, o_sem)
    for head in range(HEADS):
        merged = orecv[head].reshape(ROWS, HDIM).astype(F32) * coef[head] + ownout[head]
        merged = jnp.where(shown, merged.reshape(LIVE, BLK, HDIM), 0.0)
        out[:, :, head * HDIM : (head + 1) * HDIM] = merged.astype(BF16)

    @pl.when(is_owner)
    def _():
        wait_for(lsend.at[pl.ds(0, PEERS - 1)], l_sent)
        wait_for(osend.at[pl.ds(0, PEERS - 1)], o_sent)


def attention(fresh, keys, values, text, slots, lengths):
    anywhere = pl.BlockSpec(memory_space=pl.ANY)
    semaphore = pltpu.SemaphoreType.DMA
    return pl.pallas_call(
        kernel,
        out_shape=jax.ShapeDtypeStruct((LIVE, BLK, HD), BF16),
        in_specs=[anywhere] * 6,
        out_specs=pl.BlockSpec(memory_space=pltpu.VMEM),
        scratch_shapes=[
            pltpu.VMEM((LIVE, BLK, 3 * HD), BF16),
            pltpu.VMEM((2, LIVE, BLK, HD), BF16),
            pltpu.VMEM((HEADS, 3, LIVE, BLK, HDIM), BF16),
            pltpu.VMEM((PEERS, 3, LIVE, BLK, HDIM), BF16),
            pltpu.VMEM((TBLOCKS, BLK, HDIM), BF16),
            pltpu.VMEM((TBLOCKS, BLK, HDIM), BF16),
            pltpu.VMEM((BLOCKS, BLK, HDIM), BF16),
            pltpu.VMEM((KEYS // BLK, BLK, HDIM), BF16),
            pltpu.VMEM((HDIM, KEYS), BF16),
            pltpu.VMEM((GROUPS, KEYS, CROWS), F32),
            pltpu.VMEM((GROUPS, KEYS, CROWS), BF16),
            pltpu.VMEM((PEERS, LIVE, BLK, HDIM), BF16),
            pltpu.VMEM((PEERS, 1, HDIM), F32),
            pltpu.VMEM((HEADS, LIVE, BLK, HDIM), BF16),
            pltpu.VMEM((HEADS, 1, HDIM), F32),
            pltpu.VMEM((HEADS, ROWS, HDIM), F32),
            pltpu.VMEM((HEADS, ROWS, HDIM), F32),
            pltpu.VMEM((HEADS, ROWS, HDIM), F32),
            pltpu.SMEM((2, IMAGES), jnp.int32),
            semaphore((5,)),
            semaphore((2,)),
            semaphore((GROUPS,)),
        ]
        + [semaphore] * 7,
        compiler_params=pltpu.CompilerParams(
            collective_id=0, has_side_effects=True, vmem_limit_bytes=24 * 1024 * 1024
        ),
    )(*[pltpu.with_memory_space_constraint(x, pltpu.HBM) for x in (fresh, keys, values, text, slots, lengths)])


def body(fresh, stale_keys, stale_values, text_kv, group_slots, text_len):
    slot_count = fresh.shape[2]
    text = text_kv[0].reshape(TBLOCKS, BLK, 2 * HD)
    merged = attention(fresh[0, 0], stale_keys[0, 0], stale_values[0, 0], text, group_slots, text_len)
    return jnp.pad(merged, ((0, slot_count - LIVE), (0, 0), (0, 0)))[None, None]


def solution(mesh):
    placed = (
        P("img", "patch", None, None, None),
        P("img", "patch", None, None, None),
        P("img", "patch", None, None, None),
        P("img", None, None),
        P(),
        P(),
    )
    return jax.shard_map(
        body,
        mesh=mesh,
        in_specs=placed,
        out_specs=P("img", "patch", None, None, None),
        check_vma=False,
    )
```

```python
import functools

import jax
import jax.numpy as jnp
from jax import lax
from jax.experimental import pallas as pl
from jax.experimental.pallas import tpu as pltpu
from jax.sharding import PartitionSpec as P

MESH = pl.DeviceIdType.MESH
F32 = jnp.float32
BF16 = jnp.bfloat16

HDIM = 128
HEADS = 12
HD = HDIM * HEADS
BLK = 16
LIVE = 3
TXT = 128
PEERS = 16
IMAGES = 32
ROWS = LIVE * BLK
BLOCKS = PEERS * LIVE
TBLOCKS = TXT // BLK
KEYS = BLOCKS * BLK + TXT
CHUNKS = 2
CPEERS = PEERS // CHUNKS
CROWS = CPEERS * ROWS
SCALE = 1.4426950408889634 / HDIM**0.5
MASKED = -1e30


def nt(a, b):
    return lax.dot_general(a, b, (((1,), (1,)), ((), ())), preferred_element_type=F32)


def owner_rank(peer, core):
    z, x = peer // 2, peer % 2
    return lax.rem(z + 15 - 2 * core - x, 4)


def owned_head(peer, core):
    z, x = peer // 2, peer % 2
    return (z // 4) * 6 + x * 3 + owner_rank(peer, core)


def offset_of(k):
    half = k // 2
    odd = lax.rem(k, 2)
    return lax.rem(PEERS // 2 + odd * half + (1 - odd) * (PEERS - half), PEERS)


def partner(me, k):
    return lax.rem(me + offset_of(k), PEERS)


def kernel(
    fresh, keys, values, text, slots_in, lengths_in, out,
    own, stale, chunks, inbox, tkeys, tvalues, qmask, turned_keys, sbuf, pbuf, linv,
    osend, lsend, orecv, lrecv, ownout, ownlse, coef, counts,
    local_sem, text_sem, kq_sem, v_sem, o_sem, l_sem, kq_sent, v_sent, o_sent, l_sent, here,
):
    image = lax.axis_index("img")
    me = lax.axis_index("patch")
    core = lax.rem(image, 2)
    is_owner = owner_rank(me, core) < 3
    my_head = owned_head(me, core)

    barrier = pltpu.get_barrier_semaphore()

    def greet(peer, carry):
        pl.semaphore_signal(barrier, inc=1, device_id=(image, peer), device_id_type=MESH)
        return carry

    lax.fori_loop(me + 1, PEERS, greet, 0)

    live = pl.ds(0, LIVE)
    local = [
        pltpu.make_async_copy(keys.at[live], stale.at[0], local_sem.at[0]),
        pltpu.make_async_copy(fresh.at[live], own, local_sem.at[1]),
        pltpu.make_async_copy(values.at[live], stale.at[1], local_sem.at[2]),
        pltpu.make_async_copy(slots_in, counts.at[0], local_sem.at[3]),
        pltpu.make_async_copy(lengths_in, counts.at[1], local_sem.at[4]),
    ]
    for copy in local:
        copy.start()

    def text_copy(third, target):
        columns = pl.ds(pl.multiple_of(third * HD + my_head * HDIM, HDIM), HDIM)
        return pltpu.make_async_copy(text.at[:, :, columns], target, text_sem.at[third])

    texts = [text_copy(0, tkeys), text_copy(1, tvalues)]

    @pl.when(is_owner)
    def _():
        for copy in texts:
            copy.start()

    def stage(part, source):
        for head in range(HEADS):
            chunks[head, part] = source[:, :, head * HDIM : (head + 1) * HDIM]

    local[0].wait()
    stage(0, stale.at[0])
    local[1].wait()
    stage(1, own)
    local[2].wait()
    stage(2, stale.at[1])

    @pl.when(me > 0)
    def _():
        pl.semaphore_wait(barrier, me)

    def tell(peer, carry):
        pl.semaphore_signal(here.at[me], inc=1, device_id=(image, peer), device_id_type=MESH)
        return carry

    lax.fori_loop(0, me, tell, 0)

    keys_queries = pl.ds(0, 2)
    only_values = pl.ds(2, 1)

    def send(peer, parts, sent, received):
        pltpu.make_async_remote_copy(
            src_ref=chunks.at[owned_head(peer, core), parts],
            dst_ref=inbox.at[me, parts],
            send_sem=sent,
            recv_sem=received,
            device_id=(image, peer),
            device_id_type=MESH,
        ).start()

    def send_before(parts, sent, received):
        def step(k, carry):
            peer = partner(me, k)

            @pl.when(jnp.logical_and(peer < me, owner_rank(peer, core) < 3))
            def _():
                send(peer, parts, sent, received)

            return carry

        lax.fori_loop(1, PEERS, step, 0)

    send_before(keys_queries, kq_sent, kq_sem)
    send_before(only_values, v_sent, v_sem)

    @pl.when(is_owner)
    def _():
        for parts, received in ((keys_queries, kq_sem), (only_values, v_sem)):
            pltpu.make_async_copy(chunks.at[my_head, parts], inbox.at[me, parts], received).start()

    def send_after(peer, carry):
        pl.semaphore_wait(here.at[peer], 1)

        @pl.when(owner_rank(peer, core) < 3)
        def _():
            send(peer, keys_queries, kq_sent, kq_sem)
            send(peer, only_values, v_sent, v_sem)

        return carry

    lax.fori_loop(me + 1, PEERS, send_after, 0)

    def wait_for(ref, sem):
        pltpu.make_async_copy(ref, ref, sem).wait()

    local[3].wait()
    local[4].wait()
    n = counts[0, image]
    length = counts[1, image]

    @pl.when(is_owner)
    def _():
        key = lax.broadcasted_iota(jnp.int32, (1, KEYS), 1)
        block = (key >> 4) + jnp.where(key < BLOCKS * BLK, 0, HDIM)
        slot = block - 3 * ((block * 171) >> 9)
        past = jnp.where(key < BLOCKS * BLK, slot - n, key - BLOCKS * BLK - length)
        mark = jnp.where(past >= 0, HDIM - 1, -1)
        row = lax.broadcasted_iota(jnp.int32, (HDIM, KEYS), 0)
        turned_keys[HDIM:] = jnp.where((row == block) | (row == mark), MASKED, 0.0).astype(BF16)
        shape = (BLOCKS, BLK, HDIM)
        block = lax.broadcasted_iota(jnp.int32, shape, 0)
        lane = lax.broadcasted_iota(jnp.int32, shape, 2)
        qmask[...] = jnp.where((lane == block) | (lane == HDIM - 1), 1.0, 0.0).astype(BF16)

    def attend_own(first, count):
        heads = range(first, first + count)
        diagonal = (
            lax.broadcasted_iota(jnp.int32, (ROWS, ROWS), 0) // BLK
            == lax.broadcasted_iota(jnp.int32, (ROWS, ROWS), 1) // BLK
        )

        def third(which, head):
            at = which * HD + head * HDIM
            return own[:, :, at : at + HDIM].reshape(ROWS, HDIM)

        scores = [jnp.where(diagonal, nt(third(0, head), third(1, head)), MASKED) for head in heads]
        tops = [jnp.max(x, axis=1, keepdims=True) for x in scores]
        weights = [jnp.exp2((x - top) * SCALE) for x, top in zip(scores, tops)]
        totals = [jnp.sum(x, axis=1, keepdims=True) for x in weights]
        sums = [
            jnp.dot(x.astype(BF16), third(2, head), preferred_element_type=F32) for x, head in zip(weights, heads)
        ]
        for i, head in enumerate(heads):
            ownout[head] = sums[i] / totals[i]
            ownlse[head] = jnp.broadcast_to(tops[i] * SCALE + jnp.log2(totals[i]), (ROWS, HDIM))

    def send_back(first, count, source, target, sent, received):
        def step(k, carry):
            peer = partner(me, k)

            @pl.when(peer != me)
            def _():
                pltpu.make_async_remote_copy(
                    src_ref=source.at[peer],
                    dst_ref=target,
                    send_sem=sent,
                    recv_sem=received,
                    device_id=(image, peer),
                    device_id_type=MESH,
                ).start()

            @pl.when(peer == me)
            def _():
                pltpu.make_async_copy(source.at[peer], target, received).start()

            return carry

        lax.fori_loop(first, first + count, step, 0)

    @pl.when(is_owner)
    def _():
        for copy in texts:
            copy.wait()
        wait_for(inbox.at[:, keys_queries], kq_sem)
        k = jnp.concatenate([inbox[:, 0].reshape(BLOCKS * BLK, HDIM), tkeys[...].reshape(TXT, HDIM)], axis=0)
        turned_keys[:HDIM] = k.T
        q = jnp.concatenate(
            [inbox[:, 1].reshape(BLOCKS * BLK, HDIM), qmask[...].reshape(BLOCKS * BLK, HDIM)], axis=1
        )
        sbuf[...] = jnp.dot(q, turned_keys[...], preferred_element_type=F32)
        lane = lax.broadcasted_iota(jnp.int32, (ROWS, HDIM), 1)
        stats = jnp.zeros((ROWS, HDIM), F32)
        for peer in range(PEERS):
            rows = slice(peer * ROWS, (peer + 1) * ROWS)
            scores = sbuf[rows]
            top = jnp.max(scores, axis=1, keepdims=True)
            weights = jnp.exp2((scores - top) * SCALE)
            total = jnp.sum(weights, axis=1, keepdims=True)
            pbuf[peer] = weights.astype(BF16)
            linv[peer] = jnp.broadcast_to(1.0 / total, (ROWS, HDIM))
            stats = jnp.where(lane == peer, top * SCALE + jnp.log2(total), stats)
        turned = jnp.concatenate([stats, jnp.zeros((HDIM - ROWS, HDIM), F32)], axis=0).T
        for peer in range(PEERS):
            lsend[peer] = turned[peer : peer + 1]
        send_back(1, PEERS, lsend, lrecv.at[my_head], l_sent, l_sem)

        wait_for(inbox.at[:, only_values], v_sem)
        v = jnp.concatenate([inbox[:, 2].reshape(BLOCKS * BLK, HDIM), tvalues[...].reshape(TXT, HDIM)], axis=0)
        for chunk in range(CHUNKS):
            peers = [partner(me, chunk * CPEERS + i + 1) for i in range(CPEERS)]
            weights = jnp.concatenate([pbuf[peer] for peer in peers], axis=0)
            attended = jnp.dot(weights, v, preferred_element_type=F32)
            for i, peer in enumerate(peers):
                scaled = attended[i * ROWS : (i + 1) * ROWS] * linv[peer]
                osend[peer] = scaled.astype(BF16).reshape(LIVE, BLK, HDIM)
            send_back(chunk * CPEERS + 1, CPEERS, osend, orecv.at[my_head], o_sent, o_sem)

    attend_own(0, HEADS)

    @pl.when(is_owner)
    def _():
        wait_for(inbox.at[pl.ds(0, HEADS - 1), keys_queries], kq_sent)
        wait_for(inbox.at[pl.ds(0, HEADS - 1), only_values], v_sent)

    @pl.when(jnp.logical_not(is_owner))
    def _():
        wait_for(inbox.at[pl.ds(0, HEADS), keys_queries], kq_sent)
        wait_for(inbox.at[pl.ds(0, HEADS), only_values], v_sent)

    wait_for(lrecv, l_sem)
    stacked = jnp.concatenate([lrecv[head] for head in range(HEADS)] + [jnp.zeros((HDIM - HEADS, HDIM), F32)], axis=0)
    columns = stacked.T
    shown = lax.broadcasted_iota(jnp.int32, (LIVE, BLK, HDIM), 0) < n
    for head in range(HEADS):
        sibling = jnp.broadcast_to(columns[:ROWS, head : head + 1], (ROWS, HDIM))
        within = ownlse[head]
        top = jnp.maximum(sibling, within)
        a = jnp.exp2(sibling - top)
        b = jnp.exp2(within - top)
        inverse = 1.0 / (a + b)
        coef[head] = a * inverse
        ownout[head] = ownout[head] * (b * inverse)
    wait_for(orecv, o_sem)
    for head in range(HEADS):
        merged = orecv[head].reshape(ROWS, HDIM).astype(F32) * coef[head] + ownout[head]
        merged = jnp.where(shown, merged.reshape(LIVE, BLK, HDIM), 0.0)
        out[:, :, head * HDIM : (head + 1) * HDIM] = merged.astype(BF16)

    @pl.when(is_owner)
    def _():
        wait_for(lsend.at[pl.ds(0, PEERS - 1)], l_sent)
        wait_for(osend.at[pl.ds(0, PEERS - 1)], o_sent)


def attention(fresh, keys, values, text, slots, lengths):
    anywhere = pl.BlockSpec(memory_space=pl.ANY)
    semaphore = pltpu.SemaphoreType.DMA
    return pl.pallas_call(
        kernel,
        out_shape=jax.ShapeDtypeStruct((LIVE, BLK, HD), BF16),
        in_specs=[anywhere] * 6,
        out_specs=pl.BlockSpec(memory_space=pltpu.VMEM),
        scratch_shapes=[
            pltpu.VMEM((LIVE, BLK, 3 * HD), BF16),
            pltpu.VMEM((2, LIVE, BLK, HD), BF16),
            pltpu.VMEM((HEADS, 3, LIVE, BLK, HDIM), BF16),
            pltpu.VMEM((PEERS, 3, LIVE, BLK, HDIM), BF16),
            pltpu.VMEM((TBLOCKS, BLK, HDIM), BF16),
            pltpu.VMEM((TBLOCKS, BLK, HDIM), BF16),
            pltpu.VMEM((BLOCKS, BLK, HDIM), BF16),
            pltpu.VMEM((2 * HDIM, KEYS), BF16),
            pltpu.VMEM((BLOCKS * BLK, KEYS), F32),
            pltpu.VMEM((PEERS, ROWS, KEYS), BF16),
            pltpu.VMEM((PEERS, ROWS, HDIM), F32),
            pltpu.VMEM((PEERS, LIVE, BLK, HDIM), BF16),
            pltpu.VMEM((PEERS, 1, HDIM), F32),
            pltpu.VMEM((HEADS, LIVE, BLK, HDIM), BF16),
            pltpu.VMEM((HEADS, 1, HDIM), F32),
            pltpu.VMEM((HEADS, ROWS, HDIM), F32),
            pltpu.VMEM((HEADS, ROWS, HDIM), F32),
            pltpu.VMEM((HEADS, ROWS, HDIM), F32),
            pltpu.SMEM((2, IMAGES), jnp.int32),
            semaphore((5,)),
            semaphore((2,)),
        ]
        + [semaphore] * 8
        + [pltpu.SemaphoreType.REGULAR((PEERS,))],
        compiler_params=pltpu.CompilerParams(
            collective_id=0, has_side_effects=True, vmem_limit_bytes=24 * 1024 * 1024
        ),
    )(*[pltpu.with_memory_space_constraint(x, pltpu.HBM) for x in (fresh, keys, values, text, slots, lengths)])


def body(fresh, stale_keys, stale_values, text_kv, group_slots, text_len):
    slot_count = fresh.shape[2]
    text = text_kv[0].reshape(TBLOCKS, BLK, 2 * HD)
    merged = attention(fresh[0, 0], stale_keys[0, 0], stale_values[0, 0], text, group_slots, text_len)
    return jnp.pad(merged, ((0, slot_count - LIVE), (0, 0), (0, 0)))[None, None]


def solution(mesh):
    placed = (
        P("img", "patch", None, None, None),
        P("img", "patch", None, None, None),
        P("img", "patch", None, None, None),
        P("img", None, None),
        P(),
        P(),
    )
    return jax.shard_map(
        body,
        mesh=mesh,
        in_specs=placed,
        out_specs=P("img", "patch", None, None, None),
        check_vma=False,
    )
```

```python
import functools

import jax
import jax.numpy as jnp
from jax import lax
from jax.experimental import pallas as pl
from jax.experimental.pallas import tpu as pltpu
from jax.sharding import PartitionSpec as P

MESH = pl.DeviceIdType.MESH
F32 = jnp.float32
BF16 = jnp.bfloat16

HDIM = 128
HEADS = 12
HD = HDIM * HEADS
BLK = 16
LIVE = 3
TXT = 128
PEERS = 16
IMAGES = 32
ROWS = LIVE * BLK
BLOCKS = PEERS * LIVE
TBLOCKS = TXT // BLK
KEYS = BLOCKS * BLK + TXT
CHUNKS = 2
CPEERS = PEERS // CHUNKS
CROWS = CPEERS * ROWS
SCALE = 1.4426950408889634 / HDIM**0.5
MASKED = -1e30


def nt(a, b):
    return lax.dot_general(a, b, (((1,), (1,)), ((), ())), preferred_element_type=F32)


def owner_rank(peer, core):
    z, x = peer // 2, peer % 2
    return lax.rem(z + 15 - 2 * core - x, 4)


def owned_head(peer, core):
    z, x = peer // 2, peer % 2
    return (z // 4) * 6 + x * 3 + owner_rank(peer, core)


def partner(me, core, k):
    half = k // 2
    up = lax.rem(k + core, 2)
    return lax.rem(me + PEERS // 2 + up * half + (1 - up) * (PEERS - half), PEERS)


def kernel(
    fresh, keys, values, text, slots_in, lengths_in, out,
    own, stale, chunks, inbox, tkeys, tvalues, qmask, turned_keys, sbuf, pbuf, linv,
    osend, lsend, orecv, lrecv, ownout, ownlse, coef, counts,
    local_sem, text_sem, kq_sem, v_sem, o_sem, l_sem, kq_sent, v_sent, o_sent, l_sent, here,
):
    image = lax.axis_index("img")
    me = lax.axis_index("patch")
    core = lax.rem(image, 2)
    is_owner = owner_rank(me, core) < 3
    my_head = owned_head(me, core)

    barrier = pltpu.get_barrier_semaphore()

    def greet(peer, carry):
        pl.semaphore_signal(barrier, inc=1, device_id=(image, peer), device_id_type=MESH)
        return carry

    lax.fori_loop(me + 1, PEERS, greet, 0)

    live = pl.ds(0, LIVE)
    local = [
        pltpu.make_async_copy(keys.at[live], stale.at[0], local_sem.at[0]),
        pltpu.make_async_copy(fresh.at[live], own, local_sem.at[1]),
        pltpu.make_async_copy(values.at[live], stale.at[1], local_sem.at[2]),
        pltpu.make_async_copy(slots_in, counts.at[0], local_sem.at[3]),
        pltpu.make_async_copy(lengths_in, counts.at[1], local_sem.at[4]),
    ]
    for copy in local:
        copy.start()

    def text_copy(third, target):
        columns = pl.ds(pl.multiple_of(third * HD + my_head * HDIM, HDIM), HDIM)
        return pltpu.make_async_copy(text.at[:, :, columns], target, text_sem.at[third])

    texts = [text_copy(0, tkeys), text_copy(1, tvalues)]

    @pl.when(is_owner)
    def _():
        for copy in texts:
            copy.start()

    def stage(part, source):
        for head in range(HEADS):
            chunks[head, part] = source[:, :, head * HDIM : (head + 1) * HDIM]

    local[0].wait()
    stage(0, stale.at[0])
    local[1].wait()
    stage(1, own)
    local[2].wait()
    stage(2, stale.at[1])

    @pl.when(me > 0)
    def _():
        pl.semaphore_wait(barrier, me)

    def tell(peer, carry):
        pl.semaphore_signal(here.at[me], inc=1, device_id=(image, peer), device_id_type=MESH)
        return carry

    lax.fori_loop(0, me, tell, 0)

    keys_queries = pl.ds(0, 2)
    only_values = pl.ds(2, 1)

    def send(peer, parts, sent, received):
        pltpu.make_async_remote_copy(
            src_ref=chunks.at[owned_head(peer, core), parts],
            dst_ref=inbox.at[me, parts],
            send_sem=sent,
            recv_sem=received,
            device_id=(image, peer),
            device_id_type=MESH,
        ).start()

    def send_before(parts, sent, received):
        def step(k, carry):
            peer = partner(me, core, k)

            @pl.when(jnp.logical_and(peer < me, owner_rank(peer, core) < 3))
            def _():
                send(peer, parts, sent, received)

            return carry

        lax.fori_loop(1, PEERS, step, 0)

    send_before(keys_queries, kq_sent, kq_sem)
    send_before(only_values, v_sent, v_sem)

    @pl.when(is_owner)
    def _():
        for parts, received in ((keys_queries, kq_sem), (only_values, v_sem)):
            pltpu.make_async_copy(chunks.at[my_head, parts], inbox.at[me, parts], received).start()

    def send_after(peer, carry):
        pl.semaphore_wait(here.at[peer], 1)

        @pl.when(owner_rank(peer, core) < 3)
        def _():
            send(peer, keys_queries, kq_sent, kq_sem)
            send(peer, only_values, v_sent, v_sem)

        return carry

    lax.fori_loop(me + 1, PEERS, send_after, 0)

    def wait_for(ref, sem):
        pltpu.make_async_copy(ref, ref, sem).wait()

    local[3].wait()
    local[4].wait()
    n = counts[0, image]
    length = counts[1, image]

    @pl.when(is_owner)
    def _():
        key = lax.broadcasted_iota(jnp.int32, (1, KEYS), 1)
        block = (key >> 4) + jnp.where(key < BLOCKS * BLK, 0, HDIM)
        slot = block - 3 * ((block * 171) >> 9)
        past = jnp.where(key < BLOCKS * BLK, slot - n, key - BLOCKS * BLK - length)
        mark = jnp.where(past >= 0, HDIM - 1, -1)
        row = lax.broadcasted_iota(jnp.int32, (HDIM, KEYS), 0)
        turned_keys[HDIM:] = jnp.where((row == block) | (row == mark), MASKED, 0.0).astype(BF16)
        shape = (BLOCKS, BLK, HDIM)
        block = lax.broadcasted_iota(jnp.int32, shape, 0)
        lane = lax.broadcasted_iota(jnp.int32, shape, 2)
        qmask[...] = jnp.where((lane == block) | (lane == HDIM - 1), 1.0, 0.0).astype(BF16)

    def attend_own(first, count):
        heads = range(first, first + count)
        diagonal = (
            lax.broadcasted_iota(jnp.int32, (ROWS, ROWS), 0) // BLK
            == lax.broadcasted_iota(jnp.int32, (ROWS, ROWS), 1) // BLK
        )

        def third(which, head):
            at = which * HD + head * HDIM
            return own[:, :, at : at + HDIM].reshape(ROWS, HDIM)

        scores = [jnp.where(diagonal, nt(third(0, head), third(1, head)), MASKED) for head in heads]
        tops = [jnp.max(x, axis=1, keepdims=True) for x in scores]
        weights = [jnp.exp2((x - top) * SCALE) for x, top in zip(scores, tops)]
        totals = [jnp.sum(x, axis=1, keepdims=True) for x in weights]
        sums = [
            jnp.dot(x.astype(BF16), third(2, head), preferred_element_type=F32) for x, head in zip(weights, heads)
        ]
        for i, head in enumerate(heads):
            ownout[head] = sums[i] / totals[i]
            ownlse[head] = jnp.broadcast_to(tops[i] * SCALE + jnp.log2(totals[i]), (ROWS, HDIM))

    def send_back(first, count, source, target, sent, received):
        def step(k, carry):
            peer = partner(me, core, k)

            @pl.when(peer != me)
            def _():
                pltpu.make_async_remote_copy(
                    src_ref=source.at[peer],
                    dst_ref=target,
                    send_sem=sent,
                    recv_sem=received,
                    device_id=(image, peer),
                    device_id_type=MESH,
                ).start()

            @pl.when(peer == me)
            def _():
                pltpu.make_async_copy(source.at[peer], target, received).start()

            return carry

        lax.fori_loop(first, first + count, step, 0)

    @pl.when(is_owner)
    def _():
        for copy in texts:
            copy.wait()
        wait_for(inbox.at[:, keys_queries], kq_sem)
        k = jnp.concatenate([inbox[:, 0].reshape(BLOCKS * BLK, HDIM), tkeys[...].reshape(TXT, HDIM)], axis=0)
        turned_keys[:HDIM] = k.T
        q = jnp.concatenate(
            [inbox[:, 1].reshape(BLOCKS * BLK, HDIM), qmask[...].reshape(BLOCKS * BLK, HDIM)], axis=1
        )
        sbuf[...] = jnp.dot(q, turned_keys[...], preferred_element_type=F32)
        lane = lax.broadcasted_iota(jnp.int32, (ROWS, HDIM), 1)
        stats = jnp.zeros((ROWS, HDIM), F32)
        for peer in range(PEERS):
            rows = slice(peer * ROWS, (peer + 1) * ROWS)
            scores = sbuf[rows]
            top = jnp.max(scores, axis=1, keepdims=True)
            weights = jnp.exp2((scores - top) * SCALE)
            total = jnp.sum(weights, axis=1, keepdims=True)
            pbuf[peer] = weights.astype(BF16)
            linv[peer] = jnp.broadcast_to(1.0 / total, (ROWS, HDIM))
            stats = jnp.where(lane == peer, top * SCALE + jnp.log2(total), stats)
        turned = jnp.concatenate([stats, jnp.zeros((HDIM - ROWS, HDIM), F32)], axis=0).T
        for peer in range(PEERS):
            lsend[peer] = turned[peer : peer + 1]
        send_back(1, PEERS, lsend, lrecv.at[my_head], l_sent, l_sem)

        wait_for(inbox.at[:, only_values], v_sem)
        v = jnp.concatenate([inbox[:, 2].reshape(BLOCKS * BLK, HDIM), tvalues[...].reshape(TXT, HDIM)], axis=0)
        for chunk in range(CHUNKS):
            peers = [partner(me, core, chunk * CPEERS + i + 1) for i in range(CPEERS)]
            weights = jnp.concatenate([pbuf[peer] for peer in peers], axis=0)
            attended = jnp.dot(weights, v, preferred_element_type=F32)
            for i, peer in enumerate(peers):
                scaled = attended[i * ROWS : (i + 1) * ROWS] * linv[peer]
                osend[peer] = scaled.astype(BF16).reshape(LIVE, BLK, HDIM)
            send_back(chunk * CPEERS + 1, CPEERS, osend, orecv.at[my_head], o_sent, o_sem)

    attend_own(0, HEADS)

    @pl.when(is_owner)
    def _():
        wait_for(inbox.at[pl.ds(0, HEADS - 1), keys_queries], kq_sent)
        wait_for(inbox.at[pl.ds(0, HEADS - 1), only_values], v_sent)

    @pl.when(jnp.logical_not(is_owner))
    def _():
        wait_for(inbox.at[pl.ds(0, HEADS), keys_queries], kq_sent)
        wait_for(inbox.at[pl.ds(0, HEADS), only_values], v_sent)

    wait_for(lrecv, l_sem)
    stacked = jnp.concatenate([lrecv[head] for head in range(HEADS)] + [jnp.zeros((HDIM - HEADS, HDIM), F32)], axis=0)
    columns = stacked.T
    shown = lax.broadcasted_iota(jnp.int32, (LIVE, BLK, HDIM), 0) < n
    for head in range(HEADS):
        sibling = jnp.broadcast_to(columns[:ROWS, head : head + 1], (ROWS, HDIM))
        within = ownlse[head]
        top = jnp.maximum(sibling, within)
        a = jnp.exp2(sibling - top)
        b = jnp.exp2(within - top)
        inverse = 1.0 / (a + b)
        coef[head] = a * inverse
        ownout[head] = ownout[head] * (b * inverse)
    wait_for(orecv, o_sem)
    for head in range(HEADS):
        merged = orecv[head].reshape(ROWS, HDIM).astype(F32) * coef[head] + ownout[head]
        merged = jnp.where(shown, merged.reshape(LIVE, BLK, HDIM), 0.0)
        out[:, :, head * HDIM : (head + 1) * HDIM] = merged.astype(BF16)

    @pl.when(is_owner)
    def _():
        wait_for(lsend.at[pl.ds(0, PEERS - 1)], l_sent)
        wait_for(osend.at[pl.ds(0, PEERS - 1)], o_sent)


def attention(fresh, keys, values, text, slots, lengths):
    anywhere = pl.BlockSpec(memory_space=pl.ANY)
    semaphore = pltpu.SemaphoreType.DMA
    return pl.pallas_call(
        kernel,
        out_shape=jax.ShapeDtypeStruct((LIVE, BLK, HD), BF16),
        in_specs=[anywhere] * 6,
        out_specs=pl.BlockSpec(memory_space=pltpu.VMEM),
        scratch_shapes=[
            pltpu.VMEM((LIVE, BLK, 3 * HD), BF16),
            pltpu.VMEM((2, LIVE, BLK, HD), BF16),
            pltpu.VMEM((HEADS, 3, LIVE, BLK, HDIM), BF16),
            pltpu.VMEM((PEERS, 3, LIVE, BLK, HDIM), BF16),
            pltpu.VMEM((TBLOCKS, BLK, HDIM), BF16),
            pltpu.VMEM((TBLOCKS, BLK, HDIM), BF16),
            pltpu.VMEM((BLOCKS, BLK, HDIM), BF16),
            pltpu.VMEM((2 * HDIM, KEYS), BF16),
            pltpu.VMEM((BLOCKS * BLK, KEYS), F32),
            pltpu.VMEM((PEERS, ROWS, KEYS), BF16),
            pltpu.VMEM((PEERS, ROWS, HDIM), F32),
            pltpu.VMEM((PEERS, LIVE, BLK, HDIM), BF16),
            pltpu.VMEM((PEERS, 1, HDIM), F32),
            pltpu.VMEM((HEADS, LIVE, BLK, HDIM), BF16),
            pltpu.VMEM((HEADS, 1, HDIM), F32),
            pltpu.VMEM((HEADS, ROWS, HDIM), F32),
            pltpu.VMEM((HEADS, ROWS, HDIM), F32),
            pltpu.VMEM((HEADS, ROWS, HDIM), F32),
            pltpu.SMEM((2, IMAGES), jnp.int32),
            semaphore((5,)),
            semaphore((2,)),
        ]
        + [semaphore] * 8
        + [pltpu.SemaphoreType.REGULAR((PEERS,))],
        compiler_params=pltpu.CompilerParams(
            collective_id=0, has_side_effects=True, vmem_limit_bytes=24 * 1024 * 1024
        ),
    )(*[pltpu.with_memory_space_constraint(x, pltpu.HBM) for x in (fresh, keys, values, text, slots, lengths)])


def body(fresh, stale_keys, stale_values, text_kv, group_slots, text_len):
    slot_count = fresh.shape[2]
    text = text_kv[0].reshape(TBLOCKS, BLK, 2 * HD)
    merged = attention(fresh[0, 0], stale_keys[0, 0], stale_values[0, 0], text, group_slots, text_len)
    return jnp.pad(merged, ((0, slot_count - LIVE), (0, 0), (0, 0)))[None, None]


def solution(mesh):
    placed = (
        P("img", "patch", None, None, None),
        P("img", "patch", None, None, None),
        P("img", "patch", None, None, None),
        P("img", None, None),
        P(),
        P(),
    )
    return jax.shard_map(
        body,
        mesh=mesh,
        in_specs=placed,
        out_specs=P("img", "patch", None, None, None),
        check_vma=False,
    )
```

```python
import functools

import jax
import jax.numpy as jnp
from jax import lax
from jax.experimental import pallas as pl
from jax.experimental.pallas import tpu as pltpu
from jax.sharding import PartitionSpec as P

MESH = pl.DeviceIdType.MESH
F32 = jnp.float32
BF16 = jnp.bfloat16

HDIM = 128
HEADS = 12
HD = HDIM * HEADS
BLK = 16
LIVE = 3
TXT = 128
PEERS = 16
IMAGES = 32
ROWS = LIVE * BLK
BLOCKS = PEERS * LIVE
TBLOCKS = TXT // BLK
KEYS = BLOCKS * BLK + TXT
CHUNKS = 2
CPEERS = PEERS // CHUNKS
CROWS = CPEERS * ROWS
SCALE = 1.4426950408889634 / HDIM**0.5
MASKED = -1e30


def nt(a, b):
    return lax.dot_general(a, b, (((1,), (1,)), ((), ())), preferred_element_type=F32)


def owner_rank(peer, core):
    return ((peer >> 1) + 15 - 2 * core - (peer & 1)) & 3


def owned_head(peer, core):
    return (peer >> 3) * 6 + (peer & 1) * 3 + owner_rank(peer, core)


def partner(me, core, k):
    reach = k // 2 if k % 2 else -(k // 2)
    return (me + PEERS // 2 + reach * (1 - 2 * core)) & (PEERS - 1)


def kernel(
    fresh, keys, values, text, slots_in, lengths_in, out,
    own, stale, chunks, inbox, tkeys, tvalues, qmask, turned_keys, sbuf, pbuf, linv,
    osend, lsend, orecv, lrecv, ownout, ownlse, coef, counts,
    local_sem, text_sem, kq_sem, v_sem, o_sem, l_sem, kq_sent, v_sent, o_sent, l_sent, here,
):
    image = lax.axis_index("img")
    me = lax.axis_index("patch")
    core = image & 1
    is_owner = owner_rank(me, core) < 3
    my_head = owned_head(me, core)

    barrier = pltpu.get_barrier_semaphore()

    live = pl.ds(0, LIVE)
    local = [
        pltpu.make_async_copy(keys.at[live], stale.at[0], local_sem.at[0]),
        pltpu.make_async_copy(fresh.at[live], own, local_sem.at[1]),
        pltpu.make_async_copy(values.at[live], stale.at[1], local_sem.at[2]),
        pltpu.make_async_copy(slots_in, counts.at[0], local_sem.at[3]),
        pltpu.make_async_copy(lengths_in, counts.at[1], local_sem.at[4]),
    ]
    for copy in local:
        copy.start()

    def greet(peer, carry):
        pl.semaphore_signal(barrier, inc=1, device_id=(image, peer), device_id_type=MESH)
        return carry

    lax.fori_loop(me + 1, PEERS, greet, 0)

    @pl.when(me > 0)
    def _():
        pl.semaphore_wait(barrier, me)

    def tell(peer, carry):
        pl.semaphore_signal(here.at[me], inc=1, device_id=(image, peer), device_id_type=MESH)
        return carry

    lax.fori_loop(0, me, tell, 0)

    def text_copy(third, target):
        columns = pl.ds(pl.multiple_of(third * HD + my_head * HDIM, HDIM), HDIM)
        return pltpu.make_async_copy(text.at[:, :, columns], target, text_sem.at[third])

    texts = [text_copy(0, tkeys), text_copy(1, tvalues)]

    @pl.when(is_owner)
    def _():
        for copy in texts:
            copy.start()

    def stage(part, source):
        for head in range(HEADS):
            chunks[head, part] = source[:, :, head * HDIM : (head + 1) * HDIM]

    local[0].wait()
    stage(0, stale.at[0])
    local[1].wait()
    stage(1, own)
    local[2].wait()
    stage(2, stale.at[1])

    keys_queries = pl.ds(0, 2)
    only_values = pl.ds(2, 1)

    def send(peer, parts, sent, received):
        pltpu.make_async_remote_copy(
            src_ref=chunks.at[owned_head(peer, core), parts],
            dst_ref=inbox.at[me, parts],
            send_sem=sent,
            recv_sem=received,
            device_id=(image, peer),
            device_id_type=MESH,
        ).start()

    def send_before(parts, sent, received):
        for k in range(1, PEERS):
            peer = partner(me, core, k)

            @pl.when(jnp.logical_and(peer < me, owner_rank(peer, core) < 3))
            def _(peer=peer):
                send(peer, parts, sent, received)

    send_before(keys_queries, kq_sent, kq_sem)
    send_before(only_values, v_sent, v_sem)

    @pl.when(is_owner)
    def _():
        for parts, received in ((keys_queries, kq_sem), (only_values, v_sem)):
            pltpu.make_async_copy(chunks.at[my_head, parts], inbox.at[me, parts], received).start()

    def send_after(peer, carry):
        pl.semaphore_wait(here.at[peer], 1)

        @pl.when(owner_rank(peer, core) < 3)
        def _():
            send(peer, keys_queries, kq_sent, kq_sem)
            send(peer, only_values, v_sent, v_sem)

        return carry

    lax.fori_loop(me + 1, PEERS, send_after, 0)

    def wait_for(ref, sem):
        pltpu.make_async_copy(ref, ref, sem).wait()

    local[3].wait()
    local[4].wait()
    n = counts[0, image]
    length = counts[1, image]

    @pl.when(is_owner)
    def _():
        key = lax.broadcasted_iota(jnp.int32, (1, KEYS), 1)
        block = (key >> 4) + jnp.where(key < BLOCKS * BLK, 0, HDIM)
        slot = block - 3 * ((block * 171) >> 9)
        past = jnp.where(key < BLOCKS * BLK, slot - n, key - BLOCKS * BLK - length)
        mark = jnp.where(past >= 0, HDIM - 1, -1)
        row = lax.broadcasted_iota(jnp.int32, (HDIM, KEYS), 0)
        turned_keys[HDIM:] = jnp.where((row == block) | (row == mark), MASKED, 0.0).astype(BF16)
        shape = (BLOCKS, BLK, HDIM)
        block = lax.broadcasted_iota(jnp.int32, shape, 0)
        lane = lax.broadcasted_iota(jnp.int32, shape, 2)
        qmask[...] = jnp.where((lane == block) | (lane == HDIM - 1), 1.0, 0.0).astype(BF16)

    def attend_own(first, count):
        heads = range(first, first + count)
        diagonal = (
            lax.broadcasted_iota(jnp.int32, (ROWS, ROWS), 0) // BLK
            == lax.broadcasted_iota(jnp.int32, (ROWS, ROWS), 1) // BLK
        )

        def third(which, head):
            at = which * HD + head * HDIM
            return own[:, :, at : at + HDIM].reshape(ROWS, HDIM)

        scores = [jnp.where(diagonal, nt(third(0, head), third(1, head)), MASKED) for head in heads]
        tops = [jnp.max(x, axis=1, keepdims=True) for x in scores]
        weights = [jnp.exp2((x - top) * SCALE) for x, top in zip(scores, tops)]
        totals = [jnp.sum(x, axis=1, keepdims=True) for x in weights]
        sums = [
            jnp.dot(x.astype(BF16), third(2, head), preferred_element_type=F32) for x, head in zip(weights, heads)
        ]
        for i, head in enumerate(heads):
            ownout[head] = sums[i] / totals[i]
            ownlse[head] = jnp.broadcast_to(tops[i] * SCALE + jnp.log2(totals[i]), (ROWS, HDIM))

    def send_back(first, count, source, target, sent, received):
        for k in range(first, first + count):
            peer = partner(me, core, k)
            if k == PEERS:
                pltpu.make_async_copy(source.at[me], target, received).start()
            else:
                pltpu.make_async_remote_copy(
                    src_ref=source.at[peer],
                    dst_ref=target,
                    send_sem=sent,
                    recv_sem=received,
                    device_id=(image, peer),
                    device_id_type=MESH,
                ).start()

    @pl.when(is_owner)
    def _():
        for copy in texts:
            copy.wait()
        wait_for(inbox.at[:, keys_queries], kq_sem)
        k = jnp.concatenate([inbox[:, 0].reshape(BLOCKS * BLK, HDIM), tkeys[...].reshape(TXT, HDIM)], axis=0)
        turned_keys[:HDIM] = k.T
        q = jnp.concatenate(
            [inbox[:, 1].reshape(BLOCKS * BLK, HDIM), qmask[...].reshape(BLOCKS * BLK, HDIM)], axis=1
        )
        sbuf[...] = jnp.dot(q, turned_keys[...], preferred_element_type=F32)
        lane = lax.broadcasted_iota(jnp.int32, (ROWS, HDIM), 1)
        stats = jnp.zeros((ROWS, HDIM), F32)
        for peer in range(PEERS):
            rows = slice(peer * ROWS, (peer + 1) * ROWS)
            scores = sbuf[rows]
            top = jnp.max(scores, axis=1, keepdims=True)
            weights = jnp.exp2((scores - top) * SCALE)
            total = jnp.sum(weights, axis=1, keepdims=True)
            pbuf[peer] = weights.astype(BF16)
            linv[peer] = jnp.broadcast_to(1.0 / total, (ROWS, HDIM))
            stats = jnp.where(lane == peer, top * SCALE + jnp.log2(total), stats)
        turned = jnp.concatenate([stats, jnp.zeros((HDIM - ROWS, HDIM), F32)], axis=0).T
        for peer in range(PEERS):
            lsend[peer] = turned[peer : peer + 1]
        send_back(1, PEERS, lsend, lrecv.at[my_head], l_sent, l_sem)

        wait_for(inbox.at[:, only_values], v_sem)
        v = jnp.concatenate([inbox[:, 2].reshape(BLOCKS * BLK, HDIM), tvalues[...].reshape(TXT, HDIM)], axis=0)
        for chunk in range(CHUNKS):
            peers = [partner(me, core, chunk * CPEERS + i + 1) for i in range(CPEERS)]
            weights = jnp.concatenate([pbuf[peer] for peer in peers], axis=0)
            attended = jnp.dot(weights, v, preferred_element_type=F32)
            for i, peer in enumerate(peers):
                scaled = attended[i * ROWS : (i + 1) * ROWS] * linv[peer]
                osend[peer] = scaled.astype(BF16).reshape(LIVE, BLK, HDIM)
            send_back(chunk * CPEERS + 1, CPEERS, osend, orecv.at[my_head], o_sent, o_sem)

    attend_own(0, HEADS)

    @pl.when(is_owner)
    def _():
        wait_for(inbox.at[pl.ds(0, HEADS - 1), keys_queries], kq_sent)
        wait_for(inbox.at[pl.ds(0, HEADS - 1), only_values], v_sent)

    @pl.when(jnp.logical_not(is_owner))
    def _():
        wait_for(inbox.at[pl.ds(0, HEADS), keys_queries], kq_sent)
        wait_for(inbox.at[pl.ds(0, HEADS), only_values], v_sent)

    wait_for(lrecv, l_sem)
    stacked = jnp.concatenate([lrecv[head] for head in range(HEADS)] + [jnp.zeros((HDIM - HEADS, HDIM), F32)], axis=0)
    columns = stacked.T
    shown = lax.broadcasted_iota(jnp.int32, (LIVE, BLK, HDIM), 0) < n
    for head in range(HEADS):
        sibling = jnp.broadcast_to(columns[:ROWS, head : head + 1], (ROWS, HDIM))
        within = ownlse[head]
        top = jnp.maximum(sibling, within)
        a = jnp.exp2(sibling - top)
        b = jnp.exp2(within - top)
        inverse = 1.0 / (a + b)
        coef[head] = a * inverse
        ownout[head] = ownout[head] * (b * inverse)
    wait_for(orecv, o_sem)
    for head in range(HEADS):
        merged = orecv[head].reshape(ROWS, HDIM).astype(F32) * coef[head] + ownout[head]
        merged = jnp.where(shown, merged.reshape(LIVE, BLK, HDIM), 0.0)
        out[:, :, head * HDIM : (head + 1) * HDIM] = merged.astype(BF16)

    @pl.when(is_owner)
    def _():
        wait_for(lsend.at[pl.ds(0, PEERS - 1)], l_sent)
        wait_for(osend.at[pl.ds(0, PEERS - 1)], o_sent)


def attention(fresh, keys, values, text, slots, lengths):
    anywhere = pl.BlockSpec(memory_space=pl.ANY)
    semaphore = pltpu.SemaphoreType.DMA
    return pl.pallas_call(
        kernel,
        out_shape=jax.ShapeDtypeStruct((LIVE, BLK, HD), BF16),
        in_specs=[anywhere] * 6,
        out_specs=pl.BlockSpec(memory_space=pltpu.VMEM),
        scratch_shapes=[
            pltpu.VMEM((LIVE, BLK, 3 * HD), BF16),
            pltpu.VMEM((2, LIVE, BLK, HD), BF16),
            pltpu.VMEM((HEADS, 3, LIVE, BLK, HDIM), BF16),
            pltpu.VMEM((PEERS, 3, LIVE, BLK, HDIM), BF16),
            pltpu.VMEM((TBLOCKS, BLK, HDIM), BF16),
            pltpu.VMEM((TBLOCKS, BLK, HDIM), BF16),
            pltpu.VMEM((BLOCKS, BLK, HDIM), BF16),
            pltpu.VMEM((2 * HDIM, KEYS), BF16),
            pltpu.VMEM((BLOCKS * BLK, KEYS), F32),
            pltpu.VMEM((PEERS, ROWS, KEYS), BF16),
            pltpu.VMEM((PEERS, ROWS, HDIM), F32),
            pltpu.VMEM((PEERS, LIVE, BLK, HDIM), BF16),
            pltpu.VMEM((PEERS, 1, HDIM), F32),
            pltpu.VMEM((HEADS, LIVE, BLK, HDIM), BF16),
            pltpu.VMEM((HEADS, 1, HDIM), F32),
            pltpu.VMEM((HEADS, ROWS, HDIM), F32),
            pltpu.VMEM((HEADS, ROWS, HDIM), F32),
            pltpu.VMEM((HEADS, ROWS, HDIM), F32),
            pltpu.SMEM((2, IMAGES), jnp.int32),
            semaphore((5,)),
            semaphore((2,)),
        ]
        + [semaphore] * 8
        + [pltpu.SemaphoreType.REGULAR((PEERS,))],
        compiler_params=pltpu.CompilerParams(
            collective_id=0, has_side_effects=True, vmem_limit_bytes=24 * 1024 * 1024
        ),
    )(*[pltpu.with_memory_space_constraint(x, pltpu.HBM) for x in (fresh, keys, values, text, slots, lengths)])


def body(fresh, stale_keys, stale_values, text_kv, group_slots, text_len):
    slot_count = fresh.shape[2]
    text = text_kv[0].reshape(TBLOCKS, BLK, 2 * HD)
    merged = attention(fresh[0, 0], stale_keys[0, 0], stale_values[0, 0], text, group_slots, text_len)
    return jnp.pad(merged, ((0, slot_count - LIVE), (0, 0), (0, 0)))[None, None]


def solution(mesh):
    placed = (
        P("img", "patch", None, None, None),
        P("img", "patch", None, None, None),
        P("img", "patch", None, None, None),
        P("img", None, None),
        P(),
        P(),
    )
    return jax.shard_map(
        body,
        mesh=mesh,
        in_specs=placed,
        out_specs=P("img", "patch", None, None, None),
        check_vma=False,
    )
```

```python
import functools

import jax
import jax.numpy as jnp
from jax import lax
from jax.experimental import pallas as pl
from jax.experimental.pallas import tpu as pltpu
from jax.sharding import PartitionSpec as P

MESH = pl.DeviceIdType.MESH
F32 = jnp.float32
BF16 = jnp.bfloat16

HDIM = 128
HEADS = 12
HD = HDIM * HEADS
BLK = 16
LIVE = 3
TXT = 128
PEERS = 16
IMAGES = 32
ROWS = LIVE * BLK
BLOCKS = PEERS * LIVE
TBLOCKS = TXT // BLK
KEYS = BLOCKS * BLK + TXT
CHUNKS = 2
CPEERS = PEERS // CHUNKS
CROWS = CPEERS * ROWS
SCALE = 1.4426950408889634 / HDIM**0.5
MASKED = -1e30


def nt(a, b):
    return lax.dot_general(a, b, (((1,), (1,)), ((), ())), preferred_element_type=F32)


def owner_rank(peer):
    return ((peer >> 1) + 13 - (peer & 1)) & 3


def owned_head(peer):
    return (peer >> 3) * 6 + (peer & 1) * 3 + owner_rank(peer)


def partner(me, core, k):
    reach = k // 2 if k % 2 else -(k // 2)
    return (me + PEERS // 2 + reach * (1 - 2 * core)) & (PEERS - 1)


def kernel(
    fresh, keys, values, text, slots_in, lengths_in, out,
    own, stale, chunks, inbox, tkeys, tvalues, qmask, turned_keys, sbuf, pbuf, linv,
    osend, lsend, orecv, lrecv, ownout, ownlse, coef, counts,
    local_sem, text_sem, kq_sem, v_sem, o_sem, l_sem, kq_sent, v_sent, o_sent, l_sent, here,
):
    image = lax.axis_index("img")
    me = lax.axis_index("patch")
    core = image & 1
    is_owner = owner_rank(me) < 3
    my_head = owned_head(me)

    barrier = pltpu.get_barrier_semaphore()

    live = pl.ds(0, LIVE)
    local = [
        pltpu.make_async_copy(keys.at[live], stale.at[0], local_sem.at[0]),
        pltpu.make_async_copy(fresh.at[live], own, local_sem.at[1]),
        pltpu.make_async_copy(values.at[live], stale.at[1], local_sem.at[2]),
        pltpu.make_async_copy(slots_in, counts.at[0], local_sem.at[3]),
        pltpu.make_async_copy(lengths_in, counts.at[1], local_sem.at[4]),
    ]
    for copy in local:
        copy.start()

    def greet(peer, carry):
        pl.semaphore_signal(barrier, inc=1, device_id=(image, peer), device_id_type=MESH)
        return carry

    lax.fori_loop(me + 1, PEERS, greet, 0)

    @pl.when(me > 0)
    def _():
        pl.semaphore_wait(barrier, me)

    def tell(peer, carry):
        pl.semaphore_signal(here.at[me], inc=1, device_id=(image, peer), device_id_type=MESH)
        return carry

    lax.fori_loop(0, me, tell, 0)

    def text_copy(third, target):
        columns = pl.ds(pl.multiple_of(third * HD + my_head * HDIM, HDIM), HDIM)
        return pltpu.make_async_copy(text.at[:, :, columns], target, text_sem.at[third])

    texts = [text_copy(0, tkeys), text_copy(1, tvalues)]

    @pl.when(is_owner)
    def _():
        for copy in texts:
            copy.start()

    def stage(part, source):
        for head in range(HEADS):
            chunks[head, part] = source[:, :, head * HDIM : (head + 1) * HDIM]

    local[0].wait()
    stage(0, stale.at[0])
    local[1].wait()
    stage(1, own)
    local[2].wait()
    stage(2, stale.at[1])

    keys_queries = pl.ds(0, 2)
    only_values = pl.ds(2, 1)

    def send(peer, parts, sent, received):
        pltpu.make_async_remote_copy(
            src_ref=chunks.at[owned_head(peer), parts],
            dst_ref=inbox.at[me, parts],
            send_sem=sent,
            recv_sem=received,
            device_id=(image, peer),
            device_id_type=MESH,
        ).start()

    def send_before(parts, sent, received):
        for k in range(1, PEERS):
            peer = partner(me, core, k)

            @pl.when(jnp.logical_and(peer < me, owner_rank(peer) < 3))
            def _(peer=peer):
                send(peer, parts, sent, received)

    send_before(keys_queries, kq_sent, kq_sem)
    send_before(only_values, v_sent, v_sem)

    @pl.when(is_owner)
    def _():
        for parts, received in ((keys_queries, kq_sem), (only_values, v_sem)):
            pltpu.make_async_copy(chunks.at[my_head, parts], inbox.at[me, parts], received).start()

    def send_after(peer, carry):
        pl.semaphore_wait(here.at[peer], 1)

        @pl.when(owner_rank(peer) < 3)
        def _():
            send(peer, keys_queries, kq_sent, kq_sem)
            send(peer, only_values, v_sent, v_sem)

        return carry

    lax.fori_loop(me + 1, PEERS, send_after, 0)

    def wait_for(ref, sem):
        pltpu.make_async_copy(ref, ref, sem).wait()

    local[3].wait()
    local[4].wait()
    n = counts[0, image]
    length = counts[1, image]

    @pl.when(is_owner)
    def _():
        key = lax.broadcasted_iota(jnp.int32, (1, KEYS), 1)
        block = (key >> 4) + jnp.where(key < BLOCKS * BLK, 0, HDIM)
        slot = block - 3 * ((block * 171) >> 9)
        past = jnp.where(key < BLOCKS * BLK, slot - n, key - BLOCKS * BLK - length)
        mark = jnp.where(past >= 0, HDIM - 1, -1)
        row = lax.broadcasted_iota(jnp.int32, (HDIM, KEYS), 0)
        turned_keys[HDIM:] = jnp.where((row == block) | (row == mark), MASKED, 0.0).astype(BF16)
        shape = (BLOCKS, BLK, HDIM)
        block = lax.broadcasted_iota(jnp.int32, shape, 0)
        lane = lax.broadcasted_iota(jnp.int32, shape, 2)
        qmask[...] = jnp.where((lane == block) | (lane == HDIM - 1), 1.0, 0.0).astype(BF16)

    def attend_own(first, count):
        heads = range(first, first + count)
        diagonal = (
            lax.broadcasted_iota(jnp.int32, (ROWS, ROWS), 0) // BLK
            == lax.broadcasted_iota(jnp.int32, (ROWS, ROWS), 1) // BLK
        )

        def third(which, head):
            at = which * HD + head * HDIM
            return own[:, :, at : at + HDIM].reshape(ROWS, HDIM)

        scores = [jnp.where(diagonal, nt(third(0, head), third(1, head)), MASKED) for head in heads]
        tops = [jnp.max(x, axis=1, keepdims=True) for x in scores]
        weights = [jnp.exp2((x - top) * SCALE) for x, top in zip(scores, tops)]
        totals = [jnp.sum(x, axis=1, keepdims=True) for x in weights]
        sums = [
            jnp.dot(x.astype(BF16), third(2, head), preferred_element_type=F32) for x, head in zip(weights, heads)
        ]
        for i, head in enumerate(heads):
            ownout[head] = sums[i] / totals[i]
            ownlse[head] = jnp.broadcast_to(tops[i] * SCALE + jnp.log2(totals[i]), (ROWS, HDIM))

    def send_back(first, count, source, target, sent, received):
        for k in range(first, first + count):
            peer = partner(me, core, k)
            if k == PEERS:
                pltpu.make_async_copy(source.at[me], target, received).start()
            else:
                pltpu.make_async_remote_copy(
                    src_ref=source.at[peer],
                    dst_ref=target,
                    send_sem=sent,
                    recv_sem=received,
                    device_id=(image, peer),
                    device_id_type=MESH,
                ).start()

    @pl.when(is_owner)
    def _():
        for copy in texts:
            copy.wait()
        wait_for(inbox.at[:, keys_queries], kq_sem)
        k = jnp.concatenate([inbox[:, 0].reshape(BLOCKS * BLK, HDIM), tkeys[...].reshape(TXT, HDIM)], axis=0)
        turned_keys[:HDIM] = k.T
        q = jnp.concatenate(
            [inbox[:, 1].reshape(BLOCKS * BLK, HDIM), qmask[...].reshape(BLOCKS * BLK, HDIM)], axis=1
        )
        sbuf[...] = jnp.dot(q, turned_keys[...], preferred_element_type=F32)
        lane = lax.broadcasted_iota(jnp.int32, (ROWS, HDIM), 1)
        stats = jnp.zeros((ROWS, HDIM), F32)
        for peer in range(PEERS):
            rows = slice(peer * ROWS, (peer + 1) * ROWS)
            scores = sbuf[rows]
            top = jnp.max(scores, axis=1, keepdims=True)
            weights = jnp.exp2((scores - top) * SCALE)
            total = jnp.sum(weights, axis=1, keepdims=True)
            pbuf[peer] = weights.astype(BF16)
            linv[peer] = jnp.broadcast_to(1.0 / total, (ROWS, HDIM))
            stats = jnp.where(lane == peer, top * SCALE + jnp.log2(total), stats)
        turned = jnp.concatenate([stats, jnp.zeros((HDIM - ROWS, HDIM), F32)], axis=0).T
        for peer in range(PEERS):
            lsend[peer] = turned[peer : peer + 1]
        send_back(1, PEERS, lsend, lrecv.at[my_head], l_sent, l_sem)

        wait_for(inbox.at[:, only_values], v_sem)
        v = jnp.concatenate([inbox[:, 2].reshape(BLOCKS * BLK, HDIM), tvalues[...].reshape(TXT, HDIM)], axis=0)
        for chunk in range(CHUNKS):
            peers = [partner(me, core, chunk * CPEERS + i + 1) for i in range(CPEERS)]
            weights = jnp.concatenate([pbuf[peer] for peer in peers], axis=0)
            attended = jnp.dot(weights, v, preferred_element_type=F32)
            for i, peer in enumerate(peers):
                scaled = attended[i * ROWS : (i + 1) * ROWS] * linv[peer]
                osend[peer] = scaled.astype(BF16).reshape(LIVE, BLK, HDIM)
            send_back(chunk * CPEERS + 1, CPEERS, osend, orecv.at[my_head], o_sent, o_sem)

    attend_own(0, HEADS)

    @pl.when(is_owner)
    def _():
        wait_for(inbox.at[pl.ds(0, HEADS - 1), keys_queries], kq_sent)
        wait_for(inbox.at[pl.ds(0, HEADS - 1), only_values], v_sent)

    @pl.when(jnp.logical_not(is_owner))
    def _():
        wait_for(inbox.at[pl.ds(0, HEADS), keys_queries], kq_sent)
        wait_for(inbox.at[pl.ds(0, HEADS), only_values], v_sent)

    wait_for(lrecv, l_sem)
    stacked = jnp.concatenate([lrecv[head] for head in range(HEADS)] + [jnp.zeros((HDIM - HEADS, HDIM), F32)], axis=0)
    columns = stacked.T
    shown = lax.broadcasted_iota(jnp.int32, (LIVE, BLK, HDIM), 0) < n
    for head in range(HEADS):
        sibling = jnp.broadcast_to(columns[:ROWS, head : head + 1], (ROWS, HDIM))
        within = ownlse[head]
        top = jnp.maximum(sibling, within)
        a = jnp.exp2(sibling - top)
        b = jnp.exp2(within - top)
        inverse = 1.0 / (a + b)
        coef[head] = a * inverse
        ownout[head] = ownout[head] * (b * inverse)
    wait_for(orecv, o_sem)
    for head in range(HEADS):
        merged = orecv[head].reshape(ROWS, HDIM).astype(F32) * coef[head] + ownout[head]
        merged = jnp.where(shown, merged.reshape(LIVE, BLK, HDIM), 0.0)
        out[:, :, head * HDIM : (head + 1) * HDIM] = merged.astype(BF16)

    @pl.when(is_owner)
    def _():
        wait_for(lsend.at[pl.ds(0, PEERS - 1)], l_sent)
        wait_for(osend.at[pl.ds(0, PEERS - 1)], o_sent)


def attention(fresh, keys, values, text, slots, lengths):
    anywhere = pl.BlockSpec(memory_space=pl.ANY)
    semaphore = pltpu.SemaphoreType.DMA
    return pl.pallas_call(
        kernel,
        out_shape=jax.ShapeDtypeStruct((LIVE, BLK, HD), BF16),
        in_specs=[anywhere] * 6,
        out_specs=pl.BlockSpec(memory_space=pltpu.VMEM),
        scratch_shapes=[
            pltpu.VMEM((LIVE, BLK, 3 * HD), BF16),
            pltpu.VMEM((2, LIVE, BLK, HD), BF16),
            pltpu.VMEM((HEADS, 3, LIVE, BLK, HDIM), BF16),
            pltpu.VMEM((PEERS, 3, LIVE, BLK, HDIM), BF16),
            pltpu.VMEM((TBLOCKS, BLK, HDIM), BF16),
            pltpu.VMEM((TBLOCKS, BLK, HDIM), BF16),
            pltpu.VMEM((BLOCKS, BLK, HDIM), BF16),
            pltpu.VMEM((2 * HDIM, KEYS), BF16),
            pltpu.VMEM((BLOCKS * BLK, KEYS), F32),
            pltpu.VMEM((PEERS, ROWS, KEYS), BF16),
            pltpu.VMEM((PEERS, ROWS, HDIM), F32),
            pltpu.VMEM((PEERS, LIVE, BLK, HDIM), BF16),
            pltpu.VMEM((PEERS, 1, HDIM), F32),
            pltpu.VMEM((HEADS, LIVE, BLK, HDIM), BF16),
            pltpu.VMEM((HEADS, 1, HDIM), F32),
            pltpu.VMEM((HEADS, ROWS, HDIM), F32),
            pltpu.VMEM((HEADS, ROWS, HDIM), F32),
            pltpu.VMEM((HEADS, ROWS, HDIM), F32),
            pltpu.SMEM((2, IMAGES), jnp.int32),
            semaphore((5,)),
            semaphore((2,)),
        ]
        + [semaphore] * 8
        + [pltpu.SemaphoreType.REGULAR((PEERS,))],
        compiler_params=pltpu.CompilerParams(
            collective_id=0, has_side_effects=True, vmem_limit_bytes=24 * 1024 * 1024
        ),
    )(*[pltpu.with_memory_space_constraint(x, pltpu.HBM) for x in (fresh, keys, values, text, slots, lengths)])


def body(fresh, stale_keys, stale_values, text_kv, group_slots, text_len):
    slot_count = fresh.shape[2]
    text = text_kv[0].reshape(TBLOCKS, BLK, 2 * HD)
    merged = attention(fresh[0, 0], stale_keys[0, 0], stale_values[0, 0], text, group_slots, text_len)
    return jnp.pad(merged, ((0, slot_count - LIVE), (0, 0), (0, 0)))[None, None]


def solution(mesh):
    placed = (
        P("img", "patch", None, None, None),
        P("img", "patch", None, None, None),
        P("img", "patch", None, None, None),
        P("img", None, None),
        P(),
        P(),
    )
    return jax.shard_map(
        body,
        mesh=mesh,
        in_specs=placed,
        out_specs=P("img", "patch", None, None, None),
        check_vma=False,
    )
```

```python
import functools

import jax
import jax.numpy as jnp
from jax import lax
from jax.experimental import pallas as pl
from jax.experimental.pallas import tpu as pltpu
from jax.sharding import PartitionSpec as P

MESH = pl.DeviceIdType.MESH
F32 = jnp.float32
BF16 = jnp.bfloat16

HDIM = 128
HEADS = 12
HD = HDIM * HEADS
BLK = 16
LIVE = 3
TXT = 128
PEERS = 16
IMAGES = 32
ROWS = LIVE * BLK
BLOCKS = PEERS * LIVE
TBLOCKS = TXT // BLK
KEYS = BLOCKS * BLK + TXT
EARLY = 12
LATE = PEERS - EARLY
SCALE = 1.4426950408889634 / HDIM**0.5
MASKED = -1e30


def nt(a, b):
    return lax.dot_general(a, b, (((1,), (1,)), ((), ())), preferred_element_type=F32)


def owner_rank(peer, core):
    return ((peer >> 1) + 15 - 2 * core - (peer & 1)) & 3


def owned_head(peer, core):
    return (peer >> 3) * 6 + (peer & 1) * 3 + owner_rank(peer, core)


def partner(me, core, k):
    reach = k // 2 if k % 2 else -(k // 2)
    return (me + PEERS // 2 + reach * (1 - 2 * core)) & (PEERS - 1)


def kernel(
    fresh, keys, values, text, slots_in, lengths_in, out,
    own, stale, chunks, inbox, tkeys, tvalues, qmask, early_keys, late_keys,
    first_scores, late_scores, last_scores, first_weights, late_weights, last_weights, tops, totals, sums, linv,
    osend, lsend, orecv, lrecv, ownout, ownlse, coef, counts,
    local_sem, text_sem, kq_sem, v_sem, o_sem, l_sem, kq_sent, v_sent, o_sent, l_sent, here,
):
    image = lax.axis_index("img")
    me = lax.axis_index("patch")
    core = image & 1
    is_owner = owner_rank(me, core) < 3
    my_head = owned_head(me, core)

    barrier = pltpu.get_barrier_semaphore()

    live = pl.ds(0, LIVE)
    local = [
        pltpu.make_async_copy(keys.at[live], stale.at[0], local_sem.at[0]),
        pltpu.make_async_copy(fresh.at[live], own, local_sem.at[1]),
        pltpu.make_async_copy(values.at[live], stale.at[1], local_sem.at[2]),
        pltpu.make_async_copy(slots_in, counts.at[0], local_sem.at[3]),
        pltpu.make_async_copy(lengths_in, counts.at[1], local_sem.at[4]),
    ]
    for copy in local:
        copy.start()

    def greet(peer, carry):
        pl.semaphore_signal(barrier, inc=1, device_id=(image, peer), device_id_type=MESH)
        return carry

    lax.fori_loop(me + 1, PEERS, greet, 0)

    @pl.when(me > 0)
    def _():
        pl.semaphore_wait(barrier, me)

    def tell(peer, carry):
        pl.semaphore_signal(here.at[me], inc=1, device_id=(image, peer), device_id_type=MESH)
        return carry

    lax.fori_loop(0, me, tell, 0)

    def text_copy(third, target):
        columns = pl.ds(pl.multiple_of(third * HD + my_head * HDIM, HDIM), HDIM)
        return pltpu.make_async_copy(text.at[:, :, columns], target, text_sem.at[third])

    texts = [text_copy(0, tkeys), text_copy(1, tvalues)]

    @pl.when(is_owner)
    def _():
        for copy in texts:
            copy.start()

    def stage(part, source):
        for head in range(HEADS):
            chunks[head, part] = source[:, :, head * HDIM : (head + 1) * HDIM]

    local[0].wait()
    stage(0, stale.at[0])
    local[1].wait()
    stage(1, own)

    wave = (me + PEERS - EARLY) >> 4
    keys_queries = pl.ds(0, 2)
    only_values = pl.ds(2, 1)

    def send(peer, parts, sent, received):
        pltpu.make_async_remote_copy(
            src_ref=chunks.at[owned_head(peer, core), parts],
            dst_ref=inbox.at[me, parts],
            send_sem=sent,
            recv_sem=received,
            device_id=(image, peer),
            device_id_type=MESH,
        ).start()

    def send_before(parts, sent, received):
        for k in range(1, PEERS):
            peer = partner(me, core, k)

            @pl.when(jnp.logical_and(peer < me, owner_rank(peer, core) < 3))
            def _(peer=peer):
                send(peer, parts, sent, received)

    send_before(keys_queries, kq_sent, kq_sem.at[wave])
    local[2].wait()
    stage(2, stale.at[1])
    send_before(only_values, v_sent, v_sem.at[wave])

    @pl.when(is_owner)
    def _():
        for parts, received in ((keys_queries, kq_sem.at[wave]), (only_values, v_sem.at[wave])):
            pltpu.make_async_copy(chunks.at[my_head, parts], inbox.at[me, parts], received).start()

    def send_after(peer, carry):
        pl.semaphore_wait(here.at[peer], 1)

        @pl.when(owner_rank(peer, core) < 3)
        def _():
            send(peer, keys_queries, kq_sent, kq_sem.at[wave])
            send(peer, only_values, v_sent, v_sem.at[wave])

        return carry

    lax.fori_loop(me + 1, PEERS, send_after, 0)

    def wait_for(ref, sem):
        pltpu.make_async_copy(ref, ref, sem).wait()

    local[3].wait()
    local[4].wait()
    n = counts[0, image]
    length = counts[1, image]

    @pl.when(is_owner)
    def _():
        def mark_keys(target, first, tokens):
            key = lax.broadcasted_iota(jnp.int32, (1, target.shape[1]), 1)
            is_text = key >= tokens
            block = jnp.where(is_text, HDIM, (key >> 4) + first)
            slot = block - 3 * ((block * 171) >> 9)
            past = jnp.where(is_text, key - tokens - length, slot - n)
            mark = jnp.where(past >= 0, HDIM - 1, -1)
            row = lax.broadcasted_iota(jnp.int32, (HDIM, target.shape[1]), 0)
            target[HDIM:] = jnp.where((row == block) | (row == mark), MASKED, 0.0).astype(BF16)

        mark_keys(early_keys, 0, EARLY * ROWS)
        mark_keys(late_keys, EARLY * LIVE, LATE * ROWS)
        shape = (BLOCKS, BLK, HDIM)
        block = lax.broadcasted_iota(jnp.int32, shape, 0)
        lane = lax.broadcasted_iota(jnp.int32, shape, 2)
        qmask[...] = jnp.where((lane == block) | (lane == HDIM - 1), 1.0, 0.0).astype(BF16)

    def attend_own(first, count):
        heads = range(first, first + count)
        diagonal = (
            lax.broadcasted_iota(jnp.int32, (ROWS, ROWS), 0) // BLK
            == lax.broadcasted_iota(jnp.int32, (ROWS, ROWS), 1) // BLK
        )

        def third(which, head):
            at = which * HD + head * HDIM
            return own[:, :, at : at + HDIM].reshape(ROWS, HDIM)

        scores = [jnp.where(diagonal, nt(third(0, head), third(1, head)), MASKED) for head in heads]
        tops = [jnp.max(x, axis=1, keepdims=True) for x in scores]
        weights = [jnp.exp2((x - top) * SCALE) for x, top in zip(scores, tops)]
        totals = [jnp.sum(x, axis=1, keepdims=True) for x in weights]
        sums = [
            jnp.dot(x.astype(BF16), third(2, head), preferred_element_type=F32) for x, head in zip(weights, heads)
        ]
        for i, head in enumerate(heads):
            ownout[head] = sums[i] / totals[i]
            ownlse[head] = jnp.broadcast_to(tops[i] * SCALE + jnp.log2(totals[i]), (ROWS, HDIM))

    def send_back(first, count, source, target, sent, received):
        for k in range(first, first + count):
            peer = partner(me, core, k)
            if k == PEERS:
                pltpu.make_async_copy(source.at[me], target, received).start()
            else:
                pltpu.make_async_remote_copy(
                    src_ref=source.at[peer],
                    dst_ref=target,
                    send_sem=sent,
                    recv_sem=received,
                    device_id=(image, peer),
                    device_id_type=MESH,
                ).start()

    @pl.when(is_owner)
    def _():
        for copy in texts:
            copy.wait()
        early, late = slice(0, EARLY), slice(EARLY, PEERS)

        def rows_of(part, peers):
            return inbox[peers, part].reshape(-1, HDIM)

        def marked_queries(peers):
            blocks = slice(peers.start * LIVE, peers.stop * LIVE)
            return jnp.concatenate([rows_of(1, peers), qmask[blocks].reshape(-1, HDIM)], axis=1)

        def arrived(peers, parts, received):
            wait_for(inbox.at[pl.ds(peers.start, peers.stop - peers.start), parts], received)

        def rows(peer):
            return slice(peer * ROWS, (peer + 1) * ROWS)

        arrived(early, keys_queries, kq_sem.at[0])
        early_keys[:HDIM] = jnp.concatenate([rows_of(0, early), tkeys[...].reshape(TXT, HDIM)], axis=0).T
        first_scores[...] = jnp.dot(marked_queries(early), early_keys[...], preferred_element_type=F32)
        for peer in range(EARLY):
            scores = first_scores[rows(peer)]
            top = jnp.max(scores, axis=1, keepdims=True)
            weights = jnp.exp2((scores - top) * SCALE)
            first_weights[rows(peer)] = weights.astype(BF16)
            tops[rows(peer)] = jnp.broadcast_to(top, (ROWS, HDIM))
            totals[rows(peer)] = jnp.broadcast_to(jnp.sum(weights, axis=1, keepdims=True), (ROWS, HDIM))
        arrived(early, only_values, v_sem.at[0])
        early_values = jnp.concatenate([rows_of(2, early), tvalues[...].reshape(TXT, HDIM)], axis=0)
        sums[...] = jnp.dot(first_weights[...], early_values, preferred_element_type=F32)

        arrived(late, keys_queries, kq_sem.at[1])
        late_keys[:HDIM] = rows_of(0, late).T
        late_scores[: EARLY * ROWS] = jnp.dot(marked_queries(early), late_keys[...], preferred_element_type=F32)
        late_scores[EARLY * ROWS :] = jnp.dot(marked_queries(late), late_keys[...], preferred_element_type=F32)
        last_scores[...] = jnp.dot(marked_queries(late), early_keys[...], preferred_element_type=F32)
        lane = lax.broadcasted_iota(jnp.int32, (ROWS, HDIM), 1)
        stats = jnp.zeros((ROWS, HDIM), F32)
        for peer in range(PEERS):
            scores = late_scores[rows(peer)]
            top = jnp.max(scores, axis=1, keepdims=True)
            if peer < EARLY:
                before = tops[rows(peer)]
                top = jnp.maximum(top, before[:, :1])
                share = jnp.exp2((before - top) * SCALE)
                total = share * totals[rows(peer)]
            else:
                others = last_scores[rows(peer - EARLY)]
                top = jnp.maximum(top, jnp.max(others, axis=1, keepdims=True))
                weights = jnp.exp2((others - top) * SCALE)
                last_weights[rows(peer - EARLY)] = weights.astype(BF16)
                total = jnp.sum(weights, axis=1, keepdims=True)
            weights = jnp.exp2((scores - top) * SCALE)
            late_weights[rows(peer)] = weights.astype(BF16)
            total = jnp.broadcast_to(total + jnp.sum(weights, axis=1, keepdims=True), (ROWS, HDIM))
            inverse = 1.0 / total
            linv[rows(peer)] = inverse
            if peer < EARLY:
                sums[rows(peer)] = sums[rows(peer)] * (share * inverse)
            stats = jnp.where(lane == peer, top * SCALE + jnp.log2(total), stats)
        turned = jnp.concatenate([stats, jnp.zeros((HDIM - ROWS, HDIM), F32)], axis=0).T
        for peer in range(PEERS):
            lsend[peer] = turned[peer : peer + 1]
        send_back(1, PEERS, lsend, lrecv.at[my_head], l_sent, l_sem)

        arrived(late, only_values, v_sem.at[1])
        split = EARLY * ROWS
        attended = sums[...] + jnp.dot(late_weights[:split], rows_of(2, late), preferred_element_type=F32) * linv[:split]
        osend[early] = attended.astype(BF16).reshape(EARLY, LIVE, BLK, HDIM)
        attended = jnp.dot(last_weights[...], early_values, preferred_element_type=F32)
        attended = attended + jnp.dot(late_weights[split:], rows_of(2, late), preferred_element_type=F32)
        osend[late] = (attended * linv[split:]).astype(BF16).reshape(LATE, LIVE, BLK, HDIM)
        send_back(1, PEERS, osend, orecv.at[my_head], o_sent, o_sem)

    attend_own(0, HEADS)

    @pl.when(is_owner)
    def _():
        wait_for(inbox.at[pl.ds(0, HEADS - 1), keys_queries], kq_sent)
        wait_for(inbox.at[pl.ds(0, HEADS - 1), only_values], v_sent)

    @pl.when(jnp.logical_not(is_owner))
    def _():
        wait_for(inbox.at[pl.ds(0, HEADS), keys_queries], kq_sent)
        wait_for(inbox.at[pl.ds(0, HEADS), only_values], v_sent)

    wait_for(lrecv, l_sem)
    stacked = jnp.concatenate([lrecv[head] for head in range(HEADS)] + [jnp.zeros((HDIM - HEADS, HDIM), F32)], axis=0)
    columns = stacked.T
    shown = lax.broadcasted_iota(jnp.int32, (LIVE, BLK, HDIM), 0) < n
    for head in range(HEADS):
        sibling = jnp.broadcast_to(columns[:ROWS, head : head + 1], (ROWS, HDIM))
        within = ownlse[head]
        top = jnp.maximum(sibling, within)
        a = jnp.exp2(sibling - top)
        b = jnp.exp2(within - top)
        inverse = 1.0 / (a + b)
        coef[head] = a * inverse
        ownout[head] = ownout[head] * (b * inverse)
    wait_for(orecv, o_sem)
    for head in range(HEADS):
        merged = orecv[head].reshape(ROWS, HDIM).astype(F32) * coef[head] + ownout[head]
        merged = jnp.where(shown, merged.reshape(LIVE, BLK, HDIM), 0.0)
        out[:, :, head * HDIM : (head + 1) * HDIM] = merged.astype(BF16)

    @pl.when(is_owner)
    def _():
        wait_for(lsend.at[pl.ds(0, PEERS - 1)], l_sent)
        wait_for(osend.at[pl.ds(0, PEERS - 1)], o_sent)


def attention(fresh, keys, values, text, slots, lengths):
    anywhere = pl.BlockSpec(memory_space=pl.ANY)
    semaphore = pltpu.SemaphoreType.DMA
    return pl.pallas_call(
        kernel,
        out_shape=jax.ShapeDtypeStruct((LIVE, BLK, HD), BF16),
        in_specs=[anywhere] * 6,
        out_specs=pl.BlockSpec(memory_space=pltpu.VMEM),
        scratch_shapes=[
            pltpu.VMEM((LIVE, BLK, 3 * HD), BF16),
            pltpu.VMEM((2, LIVE, BLK, HD), BF16),
            pltpu.VMEM((HEADS, 3, LIVE, BLK, HDIM), BF16),
            pltpu.VMEM((PEERS, 3, LIVE, BLK, HDIM), BF16),
            pltpu.VMEM((TBLOCKS, BLK, HDIM), BF16),
            pltpu.VMEM((TBLOCKS, BLK, HDIM), BF16),
            pltpu.VMEM((BLOCKS, BLK, HDIM), BF16),
            pltpu.VMEM((2 * HDIM, EARLY * ROWS + TXT), BF16),
            pltpu.VMEM((2 * HDIM, LATE * ROWS), BF16),
            pltpu.VMEM((EARLY * ROWS, EARLY * ROWS + TXT), F32),
            pltpu.VMEM((PEERS * ROWS, LATE * ROWS), F32),
            pltpu.VMEM((LATE * ROWS, EARLY * ROWS + TXT), F32),
            pltpu.VMEM((EARLY * ROWS, EARLY * ROWS + TXT), BF16),
            pltpu.VMEM((PEERS * ROWS, LATE * ROWS), BF16),
            pltpu.VMEM((LATE * ROWS, EARLY * ROWS + TXT), BF16),
            pltpu.VMEM((EARLY * ROWS, HDIM), F32),
            pltpu.VMEM((EARLY * ROWS, HDIM), F32),
            pltpu.VMEM((EARLY * ROWS, HDIM), F32),
            pltpu.VMEM((PEERS * ROWS, HDIM), F32),
            pltpu.VMEM((PEERS, LIVE, BLK, HDIM), BF16),
            pltpu.VMEM((PEERS, 1, HDIM), F32),
            pltpu.VMEM((HEADS, LIVE, BLK, HDIM), BF16),
            pltpu.VMEM((HEADS, 1, HDIM), F32),
            pltpu.VMEM((HEADS, ROWS, HDIM), F32),
            pltpu.VMEM((HEADS, ROWS, HDIM), F32),
            pltpu.VMEM((HEADS, ROWS, HDIM), F32),
            pltpu.SMEM((2, IMAGES), jnp.int32),
            semaphore((5,)),
            semaphore((2,)),
            semaphore((2,)),
            semaphore((2,)),
        ]
        + [semaphore] * 6
        + [pltpu.SemaphoreType.REGULAR((PEERS,))],
        compiler_params=pltpu.CompilerParams(
            collective_id=0, has_side_effects=True, vmem_limit_bytes=24 * 1024 * 1024
        ),
    )(*[pltpu.with_memory_space_constraint(x, pltpu.HBM) for x in (fresh, keys, values, text, slots, lengths)])


def body(fresh, stale_keys, stale_values, text_kv, group_slots, text_len):
    slot_count = fresh.shape[2]
    text = text_kv[0].reshape(TBLOCKS, BLK, 2 * HD)
    merged = attention(fresh[0, 0], stale_keys[0, 0], stale_values[0, 0], text, group_slots, text_len)
    return jnp.pad(merged, ((0, slot_count - LIVE), (0, 0), (0, 0)))[None, None]


def solution(mesh):
    placed = (
        P("img", "patch", None, None, None),
        P("img", "patch", None, None, None),
        P("img", "patch", None, None, None),
        P("img", None, None),
        P(),
        P(),
    )
    return jax.shard_map(
        body,
        mesh=mesh,
        in_specs=placed,
        out_specs=P("img", "patch", None, None, None),
        check_vma=False,
    )
```

```python
import functools

import jax
import jax.numpy as jnp
from jax import lax
from jax.experimental import pallas as pl
from jax.experimental.pallas import tpu as pltpu
from jax.sharding import PartitionSpec as P

MESH = pl.DeviceIdType.MESH
F32 = jnp.float32
BF16 = jnp.bfloat16

HDIM = 128
HEADS = 12
HD = HDIM * HEADS
BLK = 16
LIVE = 3
TXT = 128
PEERS = 16
IMAGES = 32
ROWS = LIVE * BLK
BLOCKS = PEERS * LIVE
TBLOCKS = TXT // BLK
KEYS = BLOCKS * BLK + TXT
CHUNKS = 2
CPEERS = PEERS // CHUNKS
CROWS = CPEERS * ROWS
SCALE = 1.4426950408889634 / HDIM**0.5
MASKED = -1e30


def nt(a, b):
    return lax.dot_general(a, b, (((1,), (1,)), ((), ())), preferred_element_type=F32)


def owner_rank(peer, core):
    return ((peer >> 1) + 15 - 2 * core - (peer & 1)) & 3


def owned_head(peer, core):
    return (peer >> 3) * 6 + (peer & 1) * 3 + owner_rank(peer, core)


def partner(me, core, k):
    reach = k // 2 if k % 2 else -(k // 2)
    return (me + PEERS // 2 + reach * (1 - 2 * core)) & (PEERS - 1)


def kernel(
    fresh, keys, values, text, slots_in, lengths_in, out,
    own, inbox, tkeys, tvalues, qmask, turned_keys, sbuf, pbuf, linv,
    osend, lsend, orecv, lrecv, ownout, ownlse, coef, counts,
    local_sem, text_sem, part_sem, sent_sem, o_sem, l_sem, o_sent, l_sent, here,
):
    image = lax.axis_index("img")
    me = lax.axis_index("patch")
    core = image & 1
    is_owner = owner_rank(me, core) < 3
    my_head = owned_head(me, core)

    barrier = pltpu.get_barrier_semaphore()

    live = pl.ds(0, LIVE)
    local = [
        pltpu.make_async_copy(fresh.at[live], own, local_sem.at[0]),
        pltpu.make_async_copy(slots_in, counts.at[0], local_sem.at[1]),
        pltpu.make_async_copy(lengths_in, counts.at[1], local_sem.at[2]),
    ]
    def greet(peer, carry):
        pl.semaphore_signal(barrier, inc=1, device_id=(image, peer), device_id_type=MESH)
        return carry

    lax.fori_loop(me + 1, PEERS, greet, 0)

    @pl.when(me > 0)
    def _():
        pl.semaphore_wait(barrier, me)

    def tell(peer, carry):
        pl.semaphore_signal(here.at[me], inc=1, device_id=(image, peer), device_id_type=MESH)
        return carry

    lax.fori_loop(0, me, tell, 0)

    def text_copy(third, target):
        columns = pl.ds(pl.multiple_of(third * HD + my_head * HDIM, HDIM), HDIM)
        return pltpu.make_async_copy(text.at[:, :, columns], target, text_sem.at[third])

    texts = [text_copy(0, tkeys), text_copy(1, tvalues)]

    def piece(part, head):
        columns = pl.ds(pl.multiple_of(head * HDIM, HDIM), HDIM)
        return (keys, fresh, values)[part].at[live, :, columns]

    def send(peer, part):
        pltpu.make_async_remote_copy(
            src_ref=piece(part, owned_head(peer, core)),
            dst_ref=inbox.at[me, part],
            send_sem=sent_sem.at[part],
            recv_sem=part_sem.at[part],
            device_id=(image, peer),
            device_id_type=MESH,
        ).start()

    for part in range(3):
        for k in range(1, PEERS):
            peer = partner(me, core, k)

            @pl.when(jnp.logical_and(peer < me, owner_rank(peer, core) < 3))
            def _(peer=peer, part=part):
                send(peer, part)

    @pl.when(is_owner)
    def _():
        for part in range(3):
            pltpu.make_async_copy(piece(part, my_head), inbox.at[me, part], part_sem.at[part]).start()
        for copy in texts:
            copy.start()

    for copy in local:
        copy.start()

    def send_after(peer, carry):
        pl.semaphore_wait(here.at[peer], 1)

        @pl.when(owner_rank(peer, core) < 3)
        def _():
            for part in range(3):
                send(peer, part)

        return carry

    lax.fori_loop(me + 1, PEERS, send_after, 0)

    def wait_for(ref, sem):
        pltpu.make_async_copy(ref, ref, sem).wait()

    for copy in local:
        copy.wait()
    n = counts[0, image]
    length = counts[1, image]

    @pl.when(is_owner)
    def _():
        key = lax.broadcasted_iota(jnp.int32, (1, KEYS), 1)
        block = (key >> 4) + jnp.where(key < BLOCKS * BLK, 0, HDIM)
        slot = block - 3 * ((block * 171) >> 9)
        past = jnp.where(key < BLOCKS * BLK, slot - n, key - BLOCKS * BLK - length)
        mark = jnp.where(past >= 0, HDIM - 1, -1)
        row = lax.broadcasted_iota(jnp.int32, (HDIM, KEYS), 0)
        turned_keys[HDIM:] = jnp.where((row == block) | (row == mark), MASKED, 0.0).astype(BF16)
        shape = (BLOCKS, BLK, HDIM)
        block = lax.broadcasted_iota(jnp.int32, shape, 0)
        lane = lax.broadcasted_iota(jnp.int32, shape, 2)
        qmask[...] = jnp.where((lane == block) | (lane == HDIM - 1), 1.0, 0.0).astype(BF16)

    def attend_own(first, count):
        heads = range(first, first + count)
        diagonal = (
            lax.broadcasted_iota(jnp.int32, (ROWS, ROWS), 0) // BLK
            == lax.broadcasted_iota(jnp.int32, (ROWS, ROWS), 1) // BLK
        )

        def third(which, head):
            at = which * HD + head * HDIM
            return own[:, :, at : at + HDIM].reshape(ROWS, HDIM)

        scores = [jnp.where(diagonal, nt(third(0, head), third(1, head)), MASKED) for head in heads]
        tops = [jnp.max(x, axis=1, keepdims=True) for x in scores]
        weights = [jnp.exp2((x - top) * SCALE) for x, top in zip(scores, tops)]
        totals = [jnp.sum(x, axis=1, keepdims=True) for x in weights]
        sums = [
            jnp.dot(x.astype(BF16), third(2, head), preferred_element_type=F32) for x, head in zip(weights, heads)
        ]
        for i, head in enumerate(heads):
            ownout[head] = sums[i] / totals[i]
            ownlse[head] = jnp.broadcast_to(tops[i] * SCALE + jnp.log2(totals[i]), (ROWS, HDIM))

    def send_back(first, count, source, target, sent, received):
        for k in range(first, first + count):
            peer = partner(me, core, k)
            if k == PEERS:
                pltpu.make_async_copy(source.at[me], target, received).start()
            else:
                pltpu.make_async_remote_copy(
                    src_ref=source.at[peer],
                    dst_ref=target,
                    send_sem=sent,
                    recv_sem=received,
                    device_id=(image, peer),
                    device_id_type=MESH,
                ).start()

    @pl.when(is_owner)
    def _():
        for copy in texts:
            copy.wait()
        wait_for(inbox.at[:, 0], part_sem.at[0])
        k = jnp.concatenate([inbox[:, 0].reshape(BLOCKS * BLK, HDIM), tkeys[...].reshape(TXT, HDIM)], axis=0)
        turned_keys[:HDIM] = k.T
        wait_for(inbox.at[:, 1], part_sem.at[1])
        q = jnp.concatenate(
            [inbox[:, 1].reshape(BLOCKS * BLK, HDIM), qmask[...].reshape(BLOCKS * BLK, HDIM)], axis=1
        )
        sbuf[...] = jnp.dot(q, turned_keys[...], preferred_element_type=F32)
        lane = lax.broadcasted_iota(jnp.int32, (ROWS, HDIM), 1)
        stats = jnp.zeros((ROWS, HDIM), F32)
        for peer in range(PEERS):
            rows = slice(peer * ROWS, (peer + 1) * ROWS)
            scores = sbuf[rows]
            top = jnp.max(scores, axis=1, keepdims=True)
            weights = jnp.exp2((scores - top) * SCALE)
            total = jnp.sum(weights, axis=1, keepdims=True)
            pbuf[peer] = weights.astype(BF16)
            linv[peer] = jnp.broadcast_to(1.0 / total, (ROWS, HDIM))
            stats = jnp.where(lane == peer, top * SCALE + jnp.log2(total), stats)
        turned = jnp.concatenate([stats, jnp.zeros((HDIM - ROWS, HDIM), F32)], axis=0).T
        for peer in range(PEERS):
            lsend[peer] = turned[peer : peer + 1]
        send_back(1, PEERS, lsend, lrecv.at[my_head], l_sent, l_sem)

        wait_for(inbox.at[:, 2], part_sem.at[2])
        v = jnp.concatenate([inbox[:, 2].reshape(BLOCKS * BLK, HDIM), tvalues[...].reshape(TXT, HDIM)], axis=0)
        for chunk in range(CHUNKS):
            peers = [partner(me, core, chunk * CPEERS + i + 1) for i in range(CPEERS)]
            weights = jnp.concatenate([pbuf[peer] for peer in peers], axis=0)
            attended = jnp.dot(weights, v, preferred_element_type=F32)
            for i, peer in enumerate(peers):
                scaled = attended[i * ROWS : (i + 1) * ROWS] * linv[peer]
                osend[peer] = scaled.astype(BF16).reshape(LIVE, BLK, HDIM)
            send_back(chunk * CPEERS + 1, CPEERS, osend, orecv.at[my_head], o_sent, o_sem)

    attend_own(0, HEADS)

    @pl.when(is_owner)
    def _():
        for part in range(3):
            wait_for(inbox.at[pl.ds(0, HEADS - 1), part], sent_sem.at[part])

    @pl.when(jnp.logical_not(is_owner))
    def _():
        for part in range(3):
            wait_for(inbox.at[pl.ds(0, HEADS), part], sent_sem.at[part])

    wait_for(lrecv, l_sem)
    stacked = jnp.concatenate([lrecv[head] for head in range(HEADS)] + [jnp.zeros((HDIM - HEADS, HDIM), F32)], axis=0)
    columns = stacked.T
    shown = lax.broadcasted_iota(jnp.int32, (LIVE, BLK, HDIM), 0) < n
    for head in range(HEADS):
        sibling = jnp.broadcast_to(columns[:ROWS, head : head + 1], (ROWS, HDIM))
        within = ownlse[head]
        top = jnp.maximum(sibling, within)
        a = jnp.exp2(sibling - top)
        b = jnp.exp2(within - top)
        inverse = 1.0 / (a + b)
        coef[head] = a * inverse
        ownout[head] = ownout[head] * (b * inverse)
    wait_for(orecv, o_sem)
    for head in range(HEADS):
        merged = orecv[head].reshape(ROWS, HDIM).astype(F32) * coef[head] + ownout[head]
        merged = jnp.where(shown, merged.reshape(LIVE, BLK, HDIM), 0.0)
        out[:, :, head * HDIM : (head + 1) * HDIM] = merged.astype(BF16)

    @pl.when(is_owner)
    def _():
        wait_for(lsend.at[pl.ds(0, PEERS - 1)], l_sent)
        wait_for(osend.at[pl.ds(0, PEERS - 1)], o_sent)


def attention(fresh, keys, values, text, slots, lengths):
    anywhere = pl.BlockSpec(memory_space=pl.ANY)
    semaphore = pltpu.SemaphoreType.DMA
    return pl.pallas_call(
        kernel,
        out_shape=jax.ShapeDtypeStruct((LIVE, BLK, HD), BF16),
        in_specs=[anywhere] * 6,
        out_specs=pl.BlockSpec(memory_space=pltpu.VMEM),
        scratch_shapes=[
            pltpu.VMEM((LIVE, BLK, 3 * HD), BF16),
            pltpu.VMEM((PEERS, 3, LIVE, BLK, HDIM), BF16),
            pltpu.VMEM((TBLOCKS, BLK, HDIM), BF16),
            pltpu.VMEM((TBLOCKS, BLK, HDIM), BF16),
            pltpu.VMEM((BLOCKS, BLK, HDIM), BF16),
            pltpu.VMEM((2 * HDIM, KEYS), BF16),
            pltpu.VMEM((BLOCKS * BLK, KEYS), F32),
            pltpu.VMEM((PEERS, ROWS, KEYS), BF16),
            pltpu.VMEM((PEERS, ROWS, HDIM), F32),
            pltpu.VMEM((PEERS, LIVE, BLK, HDIM), BF16),
            pltpu.VMEM((PEERS, 1, HDIM), F32),
            pltpu.VMEM((HEADS, LIVE, BLK, HDIM), BF16),
            pltpu.VMEM((HEADS, 1, HDIM), F32),
            pltpu.VMEM((HEADS, ROWS, HDIM), F32),
            pltpu.VMEM((HEADS, ROWS, HDIM), F32),
            pltpu.VMEM((HEADS, ROWS, HDIM), F32),
            pltpu.SMEM((2, IMAGES), jnp.int32),
            semaphore((3,)),
            semaphore((2,)),
            semaphore((3,)),
            semaphore((3,)),
        ]
        + [semaphore] * 4
        + [pltpu.SemaphoreType.REGULAR((PEERS,))],
        compiler_params=pltpu.CompilerParams(
            collective_id=0, has_side_effects=True, vmem_limit_bytes=24 * 1024 * 1024
        ),
    )(*[pltpu.with_memory_space_constraint(x, pltpu.HBM) for x in (fresh, keys, values, text, slots, lengths)])


def body(fresh, stale_keys, stale_values, text_kv, group_slots, text_len):
    slot_count = fresh.shape[2]
    text = text_kv[0].reshape(TBLOCKS, BLK, 2 * HD)
    merged = attention(fresh[0, 0], stale_keys[0, 0], stale_values[0, 0], text, group_slots, text_len)
    return jnp.pad(merged, ((0, slot_count - LIVE), (0, 0), (0, 0)))[None, None]


def solution(mesh):
    placed = (
        P("img", "patch", None, None, None),
        P("img", "patch", None, None, None),
        P("img", "patch", None, None, None),
        P("img", None, None),
        P(),
        P(),
    )
    return jax.shard_map(
        body,
        mesh=mesh,
        in_specs=placed,
        out_specs=P("img", "patch", None, None, None),
        check_vma=False,
    )
```

```python
import functools

import jax
import jax.numpy as jnp
from jax import lax
from jax.experimental import pallas as pl
from jax.experimental.pallas import tpu as pltpu
from jax.sharding import PartitionSpec as P

MESH = pl.DeviceIdType.MESH
F32 = jnp.float32
BF16 = jnp.bfloat16

HDIM = 128
HEADS = 12
HD = HDIM * HEADS
BLK = 16
LIVE = 3
TXT = 128
PEERS = 16
IMAGES = 32
ROWS = LIVE * BLK
BLOCKS = PEERS * LIVE
TBLOCKS = TXT // BLK
KEYS = BLOCKS * BLK + TXT
CHUNKS = 2
CPEERS = PEERS // CHUNKS
CROWS = CPEERS * ROWS
SCALE = 1.4426950408889634 / HDIM**0.5
MASKED = -1e30


def nt(a, b):
    return lax.dot_general(a, b, (((1,), (1,)), ((), ())), preferred_element_type=F32)


def owner_rank(peer, core):
    return ((peer >> 1) + 15 - 2 * core - (peer & 1)) & 3


def owned_head(peer, core):
    return (peer >> 3) * 6 + (peer & 1) * 3 + owner_rank(peer, core)


def partner(me, core, k):
    reach = k // 2 if k % 2 else -(k // 2)
    return (me + PEERS // 2 + reach * (1 - 2 * core)) & (PEERS - 1)


def kernel(
    fresh, keys, values, text, slots_in, lengths_in, out,
    own, stale, chunks, inbox, tkeys, tvalues, qmask, turned_keys, sbuf, pbuf, linv,
    osend, lsend, orecv, lrecv, ownout, ownlse, coef, counts,
    local_sem, text_sem, kq_sem, v_sem, o_sem, l_sem, kq_sent, v_sent, o_sent, l_sent, here,
):
    image = lax.axis_index("img")
    me = lax.axis_index("patch")
    core = image & 1
    is_owner = owner_rank(me, core) < 3
    my_head = owned_head(me, core)

    barrier = pltpu.get_barrier_semaphore()

    live = pl.ds(0, LIVE)
    local = [
        pltpu.make_async_copy(keys.at[live], stale.at[0], local_sem.at[0]),
        pltpu.make_async_copy(fresh.at[live], own, local_sem.at[1]),
        pltpu.make_async_copy(values.at[live], stale.at[1], local_sem.at[2]),
        pltpu.make_async_copy(slots_in, counts.at[0], local_sem.at[3]),
        pltpu.make_async_copy(lengths_in, counts.at[1], local_sem.at[4]),
    ]
    for copy in local:
        copy.start()

    def greet(peer, carry):
        pl.semaphore_signal(barrier, inc=1, device_id=(image, peer), device_id_type=MESH)
        return carry

    lax.fori_loop(me + 1, PEERS, greet, 0)

    @pl.when(me > 0)
    def _():
        pl.semaphore_wait(barrier, me)

    def tell(peer, carry):
        pl.semaphore_signal(here.at[me], inc=1, device_id=(image, peer), device_id_type=MESH)
        return carry

    lax.fori_loop(0, me, tell, 0)

    def text_copy(third, target):
        columns = pl.ds(pl.multiple_of(third * HD + my_head * HDIM, HDIM), HDIM)
        return pltpu.make_async_copy(text.at[:, :, columns], target, text_sem.at[third])

    texts = [text_copy(0, tkeys), text_copy(1, tvalues)]

    @pl.when(is_owner)
    def _():
        for copy in texts:
            copy.start()

    def stage(part, source):
        for head in range(HEADS):
            chunks[head, part] = source[:, :, head * HDIM : (head + 1) * HDIM]

    local[0].wait()
    stage(0, stale.at[0])
    local[1].wait()
    stage(1, own)
    local[2].wait()
    stage(2, stale.at[1])

    keys_queries = pl.ds(0, 2)
    only_values = pl.ds(2, 1)

    def send(peer, parts, sent, received):
        pltpu.make_async_remote_copy(
            src_ref=chunks.at[owned_head(peer, core), parts],
            dst_ref=inbox.at[me, parts],
            send_sem=sent,
            recv_sem=received,
            device_id=(image, peer),
            device_id_type=MESH,
        ).start()

    def send_before(parts, sent, received):
        for k in range(1, PEERS):
            peer = partner(me, core, k)

            @pl.when(jnp.logical_and(peer < me, owner_rank(peer, core) < 3))
            def _(peer=peer):
                send(peer, parts, sent, received)

    def attend_own(first, count):
        heads = range(first, first + count)
        diagonal = (
            lax.broadcasted_iota(jnp.int32, (ROWS, ROWS), 0) // BLK
            == lax.broadcasted_iota(jnp.int32, (ROWS, ROWS), 1) // BLK
        )

        def third(which, head):
            at = which * HD + head * HDIM
            return own[:, :, at : at + HDIM].reshape(ROWS, HDIM)

        scores = [jnp.where(diagonal, nt(third(0, head), third(1, head)), MASKED) for head in heads]
        tops = [jnp.max(x, axis=1, keepdims=True) for x in scores]
        weights = [jnp.exp2((x - top) * SCALE) for x, top in zip(scores, tops)]
        totals = [jnp.sum(x, axis=1, keepdims=True) for x in weights]
        sums = [
            jnp.dot(x.astype(BF16), third(2, head), preferred_element_type=F32) for x, head in zip(weights, heads)
        ]
        for i, head in enumerate(heads):
            ownout[head] = sums[i] / totals[i]
            ownlse[head] = jnp.broadcast_to(tops[i] * SCALE + jnp.log2(totals[i]), (ROWS, HDIM))

    send_before(keys_queries, kq_sent, kq_sem)

    @pl.when(core == 1)
    def _():
        attend_own(0, HEADS)

    send_before(only_values, v_sent, v_sem)

    @pl.when(is_owner)
    def _():
        for parts, received in ((keys_queries, kq_sem), (only_values, v_sem)):
            pltpu.make_async_copy(chunks.at[my_head, parts], inbox.at[me, parts], received).start()

    def send_after(peer, carry):
        pl.semaphore_wait(here.at[peer], 1)

        @pl.when(owner_rank(peer, core) < 3)
        def _():
            send(peer, keys_queries, kq_sent, kq_sem)
            send(peer, only_values, v_sent, v_sem)

        return carry

    lax.fori_loop(me + 1, PEERS, send_after, 0)

    def wait_for(ref, sem):
        pltpu.make_async_copy(ref, ref, sem).wait()

    local[3].wait()
    local[4].wait()
    n = counts[0, image]
    length = counts[1, image]

    @pl.when(is_owner)
    def _():
        key = lax.broadcasted_iota(jnp.int32, (1, KEYS), 1)
        block = (key >> 4) + jnp.where(key < BLOCKS * BLK, 0, HDIM)
        slot = block - 3 * ((block * 171) >> 9)
        past = jnp.where(key < BLOCKS * BLK, slot - n, key - BLOCKS * BLK - length)
        mark = jnp.where(past >= 0, HDIM - 1, -1)
        row = lax.broadcasted_iota(jnp.int32, (HDIM, KEYS), 0)
        turned_keys[HDIM:] = jnp.where((row == block) | (row == mark), MASKED, 0.0).astype(BF16)
        shape = (BLOCKS, BLK, HDIM)
        block = lax.broadcasted_iota(jnp.int32, shape, 0)
        lane = lax.broadcasted_iota(jnp.int32, shape, 2)
        qmask[...] = jnp.where((lane == block) | (lane == HDIM - 1), 1.0, 0.0).astype(BF16)

    def send_back(first, count, source, target, sent, received):
        for k in range(first, first + count):
            peer = partner(me, core, k)
            if k == PEERS:
                pltpu.make_async_copy(source.at[me], target, received).start()
            else:
                pltpu.make_async_remote_copy(
                    src_ref=source.at[peer],
                    dst_ref=target,
                    send_sem=sent,
                    recv_sem=received,
                    device_id=(image, peer),
                    device_id_type=MESH,
                ).start()

    @pl.when(is_owner)
    def _():
        for copy in texts:
            copy.wait()
        wait_for(inbox.at[:, keys_queries], kq_sem)
        k = jnp.concatenate([inbox[:, 0].reshape(BLOCKS * BLK, HDIM), tkeys[...].reshape(TXT, HDIM)], axis=0)
        turned_keys[:HDIM] = k.T
        q = jnp.concatenate(
            [inbox[:, 1].reshape(BLOCKS * BLK, HDIM), qmask[...].reshape(BLOCKS * BLK, HDIM)], axis=1
        )
        sbuf[...] = jnp.dot(q, turned_keys[...], preferred_element_type=F32)
        lane = lax.broadcasted_iota(jnp.int32, (ROWS, HDIM), 1)
        stats = jnp.zeros((ROWS, HDIM), F32)
        for peer in range(PEERS):
            rows = slice(peer * ROWS, (peer + 1) * ROWS)
            scores = sbuf[rows]
            top = jnp.max(scores, axis=1, keepdims=True)
            weights = jnp.exp2((scores - top) * SCALE)
            total = jnp.sum(weights, axis=1, keepdims=True)
            pbuf[peer] = weights.astype(BF16)
            linv[peer] = jnp.broadcast_to(1.0 / total, (ROWS, HDIM))
            stats = jnp.where(lane == peer, top * SCALE + jnp.log2(total), stats)
        turned = jnp.concatenate([stats, jnp.zeros((HDIM - ROWS, HDIM), F32)], axis=0).T
        for peer in range(PEERS):
            lsend[peer] = turned[peer : peer + 1]
        send_back(1, PEERS, lsend, lrecv.at[my_head], l_sent, l_sem)

        wait_for(inbox.at[:, only_values], v_sem)
        v = jnp.concatenate([inbox[:, 2].reshape(BLOCKS * BLK, HDIM), tvalues[...].reshape(TXT, HDIM)], axis=0)
        for chunk in range(CHUNKS):
            peers = [partner(me, core, chunk * CPEERS + i + 1) for i in range(CPEERS)]
            weights = jnp.concatenate([pbuf[peer] for peer in peers], axis=0)
            attended = jnp.dot(weights, v, preferred_element_type=F32)
            for i, peer in enumerate(peers):
                scaled = attended[i * ROWS : (i + 1) * ROWS] * linv[peer]
                osend[peer] = scaled.astype(BF16).reshape(LIVE, BLK, HDIM)
            send_back(chunk * CPEERS + 1, CPEERS, osend, orecv.at[my_head], o_sent, o_sem)

    @pl.when(core == 0)
    def _():
        attend_own(0, HEADS)

    @pl.when(is_owner)
    def _():
        wait_for(inbox.at[pl.ds(0, HEADS - 1), keys_queries], kq_sent)
        wait_for(inbox.at[pl.ds(0, HEADS - 1), only_values], v_sent)

    @pl.when(jnp.logical_not(is_owner))
    def _():
        wait_for(inbox.at[pl.ds(0, HEADS), keys_queries], kq_sent)
        wait_for(inbox.at[pl.ds(0, HEADS), only_values], v_sent)

    wait_for(lrecv, l_sem)
    stacked = jnp.concatenate([lrecv[head] for head in range(HEADS)] + [jnp.zeros((HDIM - HEADS, HDIM), F32)], axis=0)
    columns = stacked.T
    shown = lax.broadcasted_iota(jnp.int32, (LIVE, BLK, HDIM), 0) < n
    for head in range(HEADS):
        sibling = jnp.broadcast_to(columns[:ROWS, head : head + 1], (ROWS, HDIM))
        within = ownlse[head]
        top = jnp.maximum(sibling, within)
        a = jnp.exp2(sibling - top)
        b = jnp.exp2(within - top)
        inverse = 1.0 / (a + b)
        coef[head] = a * inverse
        ownout[head] = ownout[head] * (b * inverse)
    wait_for(orecv, o_sem)
    for head in range(HEADS):
        merged = orecv[head].reshape(ROWS, HDIM).astype(F32) * coef[head] + ownout[head]
        merged = jnp.where(shown, merged.reshape(LIVE, BLK, HDIM), 0.0)
        out[:, :, head * HDIM : (head + 1) * HDIM] = merged.astype(BF16)

    @pl.when(is_owner)
    def _():
        wait_for(lsend.at[pl.ds(0, PEERS - 1)], l_sent)
        wait_for(osend.at[pl.ds(0, PEERS - 1)], o_sent)


def attention(fresh, keys, values, text, slots, lengths):
    anywhere = pl.BlockSpec(memory_space=pl.ANY)
    semaphore = pltpu.SemaphoreType.DMA
    return pl.pallas_call(
        kernel,
        out_shape=jax.ShapeDtypeStruct((LIVE, BLK, HD), BF16),
        in_specs=[anywhere] * 6,
        out_specs=pl.BlockSpec(memory_space=pltpu.VMEM),
        scratch_shapes=[
            pltpu.VMEM((LIVE, BLK, 3 * HD), BF16),
            pltpu.VMEM((2, LIVE, BLK, HD), BF16),
            pltpu.VMEM((HEADS, 3, LIVE, BLK, HDIM), BF16),
            pltpu.VMEM((PEERS, 3, LIVE, BLK, HDIM), BF16),
            pltpu.VMEM((TBLOCKS, BLK, HDIM), BF16),
            pltpu.VMEM((TBLOCKS, BLK, HDIM), BF16),
            pltpu.VMEM((BLOCKS, BLK, HDIM), BF16),
            pltpu.VMEM((2 * HDIM, KEYS), BF16),
            pltpu.VMEM((BLOCKS * BLK, KEYS), F32),
            pltpu.VMEM((PEERS, ROWS, KEYS), BF16),
            pltpu.VMEM((PEERS, ROWS, HDIM), F32),
            pltpu.VMEM((PEERS, LIVE, BLK, HDIM), BF16),
            pltpu.VMEM((PEERS, 1, HDIM), F32),
            pltpu.VMEM((HEADS, LIVE, BLK, HDIM), BF16),
            pltpu.VMEM((HEADS, 1, HDIM), F32),
            pltpu.VMEM((HEADS, ROWS, HDIM), F32),
            pltpu.VMEM((HEADS, ROWS, HDIM), F32),
            pltpu.VMEM((HEADS, ROWS, HDIM), F32),
            pltpu.SMEM((2, IMAGES), jnp.int32),
            semaphore((5,)),
            semaphore((2,)),
        ]
        + [semaphore] * 8
        + [pltpu.SemaphoreType.REGULAR((PEERS,))],
        compiler_params=pltpu.CompilerParams(
            collective_id=0, has_side_effects=True, vmem_limit_bytes=24 * 1024 * 1024
        ),
    )(*[pltpu.with_memory_space_constraint(x, pltpu.HBM) for x in (fresh, keys, values, text, slots, lengths)])


def body(fresh, stale_keys, stale_values, text_kv, group_slots, text_len):
    slot_count = fresh.shape[2]
    text = text_kv[0].reshape(TBLOCKS, BLK, 2 * HD)
    merged = attention(fresh[0, 0], stale_keys[0, 0], stale_values[0, 0], text, group_slots, text_len)
    return jnp.pad(merged, ((0, slot_count - LIVE), (0, 0), (0, 0)))[None, None]


def solution(mesh):
    placed = (
        P("img", "patch", None, None, None),
        P("img", "patch", None, None, None),
        P("img", "patch", None, None, None),
        P("img", None, None),
        P(),
        P(),
    )
    return jax.shard_map(
        body,
        mesh=mesh,
        in_specs=placed,
        out_specs=P("img", "patch", None, None, None),
        check_vma=False,
    )
```

```python
import functools

import jax
import jax.numpy as jnp
from jax import lax
from jax.experimental import pallas as pl
from jax.experimental.pallas import tpu as pltpu
from jax.sharding import PartitionSpec as P

MESH = pl.DeviceIdType.MESH
F32 = jnp.float32
BF16 = jnp.bfloat16

HDIM = 128
HEADS = 12
HD = HDIM * HEADS
BLK = 16
LIVE = 3
TXT = 128
PEERS = 16
IMAGES = 32
ROWS = LIVE * BLK
BLOCKS = PEERS * LIVE
TBLOCKS = TXT // BLK
KEYS = BLOCKS * BLK + TXT
CHUNKS = 2
CPEERS = PEERS // CHUNKS
CROWS = CPEERS * ROWS
SCALE = 1.4426950408889634 / HDIM**0.5
MASKED = -1e30


def nt(a, b):
    return lax.dot_general(a, b, (((1,), (1,)), ((), ())), preferred_element_type=F32)


def owner_rank(peer, core):
    return ((peer >> 1) + 1 - ((peer + core + 1) & 1)) & 3


def owned_head(peer, core):
    return (peer >> 3) * 6 + (peer & 1) * 3 + owner_rank(peer, core)


def partner(me, core, k):
    reach = k // 2 if k % 2 else -(k // 2)
    return (me + PEERS // 2 + reach * (1 - 2 * core)) & (PEERS - 1)


def kernel(
    fresh, keys, values, text, slots_in, lengths_in, out,
    own, stale, chunks, inbox, tkeys, tvalues, qmask, turned_keys, sbuf, pbuf, linv,
    osend, lsend, orecv, lrecv, ownout, ownlse, coef, counts,
    local_sem, text_sem, kq_sem, v_sem, o_sem, l_sem, kq_sent, v_sent, o_sent, l_sent, here,
):
    image = lax.axis_index("img")
    me = lax.axis_index("patch")
    core = image & 1
    is_owner = owner_rank(me, core) < 3
    my_head = owned_head(me, core)

    barrier = pltpu.get_barrier_semaphore()

    live = pl.ds(0, LIVE)
    local = [
        pltpu.make_async_copy(keys.at[live], stale.at[0], local_sem.at[0]),
        pltpu.make_async_copy(fresh.at[live], own, local_sem.at[1]),
        pltpu.make_async_copy(values.at[live], stale.at[1], local_sem.at[2]),
        pltpu.make_async_copy(slots_in, counts.at[0], local_sem.at[3]),
        pltpu.make_async_copy(lengths_in, counts.at[1], local_sem.at[4]),
    ]
    for copy in local:
        copy.start()

    def greet(peer, carry):
        pl.semaphore_signal(barrier, inc=1, device_id=(image, peer), device_id_type=MESH)
        return carry

    lax.fori_loop(me + 1, PEERS, greet, 0)

    @pl.when(me > 0)
    def _():
        pl.semaphore_wait(barrier, me)

    def tell(peer, carry):
        pl.semaphore_signal(here.at[me], inc=1, device_id=(image, peer), device_id_type=MESH)
        return carry

    lax.fori_loop(0, me, tell, 0)

    def text_copy(third, target):
        columns = pl.ds(pl.multiple_of(third * HD + my_head * HDIM, HDIM), HDIM)
        return pltpu.make_async_copy(text.at[:, :, columns], target, text_sem.at[third])

    texts = [text_copy(0, tkeys), text_copy(1, tvalues)]

    @pl.when(is_owner)
    def _():
        for copy in texts:
            copy.start()

    def stage(part, source):
        for head in range(HEADS):
            chunks[head, part] = source[:, :, head * HDIM : (head + 1) * HDIM]

    local[0].wait()
    stage(0, stale.at[0])
    local[1].wait()
    stage(1, own)
    local[2].wait()
    stage(2, stale.at[1])

    keys_queries = pl.ds(0, 2)
    only_values = pl.ds(2, 1)

    def send(peer, parts, sent, received):
        pltpu.make_async_remote_copy(
            src_ref=chunks.at[owned_head(peer, core), parts],
            dst_ref=inbox.at[me, parts],
            send_sem=sent,
            recv_sem=received,
            device_id=(image, peer),
            device_id_type=MESH,
        ).start()

    def send_before(parts, sent, received):
        for k in range(1, PEERS):
            peer = partner(me, core, k)

            @pl.when(jnp.logical_and(peer < me, owner_rank(peer, core) < 3))
            def _(peer=peer):
                send(peer, parts, sent, received)

    send_before(keys_queries, kq_sent, kq_sem)
    send_before(only_values, v_sent, v_sem)

    @pl.when(is_owner)
    def _():
        for parts, received in ((keys_queries, kq_sem), (only_values, v_sem)):
            pltpu.make_async_copy(chunks.at[my_head, parts], inbox.at[me, parts], received).start()

    def send_after(peer, carry):
        pl.semaphore_wait(here.at[peer], 1)

        @pl.when(owner_rank(peer, core) < 3)
        def _():
            send(peer, keys_queries, kq_sent, kq_sem)
            send(peer, only_values, v_sent, v_sem)

        return carry

    lax.fori_loop(me + 1, PEERS, send_after, 0)

    def wait_for(ref, sem):
        pltpu.make_async_copy(ref, ref, sem).wait()

    local[3].wait()
    local[4].wait()
    n = counts[0, image]
    length = counts[1, image]

    @pl.when(is_owner)
    def _():
        key = lax.broadcasted_iota(jnp.int32, (1, KEYS), 1)
        block = (key >> 4) + jnp.where(key < BLOCKS * BLK, 0, HDIM)
        slot = block - 3 * ((block * 171) >> 9)
        past = jnp.where(key < BLOCKS * BLK, slot - n, key - BLOCKS * BLK - length)
        mark = jnp.where(past >= 0, HDIM - 1, -1)
        row = lax.broadcasted_iota(jnp.int32, (HDIM, KEYS), 0)
        turned_keys[HDIM:] = jnp.where((row == block) | (row == mark), MASKED, 0.0).astype(BF16)
        shape = (BLOCKS, BLK, HDIM)
        block = lax.broadcasted_iota(jnp.int32, shape, 0)
        lane = lax.broadcasted_iota(jnp.int32, shape, 2)
        qmask[...] = jnp.where((lane == block) | (lane == HDIM - 1), 1.0, 0.0).astype(BF16)

    def attend_own(first, count):
        heads = range(first, first + count)
        diagonal = (
            lax.broadcasted_iota(jnp.int32, (ROWS, ROWS), 0) // BLK
            == lax.broadcasted_iota(jnp.int32, (ROWS, ROWS), 1) // BLK
        )

        def third(which, head):
            at = which * HD + head * HDIM
            return own[:, :, at : at + HDIM].reshape(ROWS, HDIM)

        scores = [jnp.where(diagonal, nt(third(0, head), third(1, head)), MASKED) for head in heads]
        tops = [jnp.max(x, axis=1, keepdims=True) for x in scores]
        weights = [jnp.exp2((x - top) * SCALE) for x, top in zip(scores, tops)]
        totals = [jnp.sum(x, axis=1, keepdims=True) for x in weights]
        sums = [
            jnp.dot(x.astype(BF16), third(2, head), preferred_element_type=F32) for x, head in zip(weights, heads)
        ]
        for i, head in enumerate(heads):
            ownout[head] = sums[i] / totals[i]
            ownlse[head] = jnp.broadcast_to(tops[i] * SCALE + jnp.log2(totals[i]), (ROWS, HDIM))

    def send_back(first, count, source, target, sent, received):
        for k in range(first, first + count):
            peer = partner(me, core, k)
            if k == PEERS:
                pltpu.make_async_copy(source.at[me], target, received).start()
            else:
                pltpu.make_async_remote_copy(
                    src_ref=source.at[peer],
                    dst_ref=target,
                    send_sem=sent,
                    recv_sem=received,
                    device_id=(image, peer),
                    device_id_type=MESH,
                ).start()

    @pl.when(is_owner)
    def _():
        for copy in texts:
            copy.wait()
        wait_for(inbox.at[:, keys_queries], kq_sem)
        k = jnp.concatenate([inbox[:, 0].reshape(BLOCKS * BLK, HDIM), tkeys[...].reshape(TXT, HDIM)], axis=0)
        turned_keys[:HDIM] = k.T
        q = jnp.concatenate(
            [inbox[:, 1].reshape(BLOCKS * BLK, HDIM), qmask[...].reshape(BLOCKS * BLK, HDIM)], axis=1
        )
        sbuf[...] = jnp.dot(q, turned_keys[...], preferred_element_type=F32)
        lane = lax.broadcasted_iota(jnp.int32, (ROWS, HDIM), 1)
        stats = jnp.zeros((ROWS, HDIM), F32)
        for peer in range(PEERS):
            rows = slice(peer * ROWS, (peer + 1) * ROWS)
            scores = sbuf[rows]
            top = jnp.max(scores, axis=1, keepdims=True)
            weights = jnp.exp2((scores - top) * SCALE)
            total = jnp.sum(weights, axis=1, keepdims=True)
            pbuf[peer] = weights.astype(BF16)
            linv[peer] = jnp.broadcast_to(1.0 / total, (ROWS, HDIM))
            stats = jnp.where(lane == peer, top * SCALE + jnp.log2(total), stats)
        turned = jnp.concatenate([stats, jnp.zeros((HDIM - ROWS, HDIM), F32)], axis=0).T
        for peer in range(PEERS):
            lsend[peer] = turned[peer : peer + 1]
        send_back(1, PEERS, lsend, lrecv.at[my_head], l_sent, l_sem)

        wait_for(inbox.at[:, only_values], v_sem)
        v = jnp.concatenate([inbox[:, 2].reshape(BLOCKS * BLK, HDIM), tvalues[...].reshape(TXT, HDIM)], axis=0)
        for chunk in range(CHUNKS):
            peers = [partner(me, core, chunk * CPEERS + i + 1) for i in range(CPEERS)]
            weights = jnp.concatenate([pbuf[peer] for peer in peers], axis=0)
            attended = jnp.dot(weights, v, preferred_element_type=F32)
            for i, peer in enumerate(peers):
                scaled = attended[i * ROWS : (i + 1) * ROWS] * linv[peer]
                osend[peer] = scaled.astype(BF16).reshape(LIVE, BLK, HDIM)
            send_back(chunk * CPEERS + 1, CPEERS, osend, orecv.at[my_head], o_sent, o_sem)

    attend_own(0, HEADS)

    @pl.when(is_owner)
    def _():
        wait_for(inbox.at[pl.ds(0, HEADS - 1), keys_queries], kq_sent)
        wait_for(inbox.at[pl.ds(0, HEADS - 1), only_values], v_sent)

    @pl.when(jnp.logical_not(is_owner))
    def _():
        wait_for(inbox.at[pl.ds(0, HEADS), keys_queries], kq_sent)
        wait_for(inbox.at[pl.ds(0, HEADS), only_values], v_sent)

    wait_for(lrecv, l_sem)
    stacked = jnp.concatenate([lrecv[head] for head in range(HEADS)] + [jnp.zeros((HDIM - HEADS, HDIM), F32)], axis=0)
    columns = stacked.T
    shown = lax.broadcasted_iota(jnp.int32, (LIVE, BLK, HDIM), 0) < n
    for head in range(HEADS):
        sibling = jnp.broadcast_to(columns[:ROWS, head : head + 1], (ROWS, HDIM))
        within = ownlse[head]
        top = jnp.maximum(sibling, within)
        a = jnp.exp2(sibling - top)
        b = jnp.exp2(within - top)
        inverse = 1.0 / (a + b)
        coef[head] = a * inverse
        ownout[head] = ownout[head] * (b * inverse)
    wait_for(orecv, o_sem)
    for head in range(HEADS):
        merged = orecv[head].reshape(ROWS, HDIM).astype(F32) * coef[head] + ownout[head]
        merged = jnp.where(shown, merged.reshape(LIVE, BLK, HDIM), 0.0)
        out[:, :, head * HDIM : (head + 1) * HDIM] = merged.astype(BF16)

    @pl.when(is_owner)
    def _():
        wait_for(lsend.at[pl.ds(0, PEERS - 1)], l_sent)
        wait_for(osend.at[pl.ds(0, PEERS - 1)], o_sent)


def attention(fresh, keys, values, text, slots, lengths):
    anywhere = pl.BlockSpec(memory_space=pl.ANY)
    semaphore = pltpu.SemaphoreType.DMA
    return pl.pallas_call(
        kernel,
        out_shape=jax.ShapeDtypeStruct((LIVE, BLK, HD), BF16),
        in_specs=[anywhere] * 6,
        out_specs=pl.BlockSpec(memory_space=pltpu.VMEM),
        scratch_shapes=[
            pltpu.VMEM((LIVE, BLK, 3 * HD), BF16),
            pltpu.VMEM((2, LIVE, BLK, HD), BF16),
            pltpu.VMEM((HEADS, 3, LIVE, BLK, HDIM), BF16),
            pltpu.VMEM((PEERS, 3, LIVE, BLK, HDIM), BF16),
            pltpu.VMEM((TBLOCKS, BLK, HDIM), BF16),
            pltpu.VMEM((TBLOCKS, BLK, HDIM), BF16),
            pltpu.VMEM((BLOCKS, BLK, HDIM), BF16),
            pltpu.VMEM((2 * HDIM, KEYS), BF16),
            pltpu.VMEM((BLOCKS * BLK, KEYS), F32),
            pltpu.VMEM((PEERS, ROWS, KEYS), BF16),
            pltpu.VMEM((PEERS, ROWS, HDIM), F32),
            pltpu.VMEM((PEERS, LIVE, BLK, HDIM), BF16),
            pltpu.VMEM((PEERS, 1, HDIM), F32),
            pltpu.VMEM((HEADS, LIVE, BLK, HDIM), BF16),
            pltpu.VMEM((HEADS, 1, HDIM), F32),
            pltpu.VMEM((HEADS, ROWS, HDIM), F32),
            pltpu.VMEM((HEADS, ROWS, HDIM), F32),
            pltpu.VMEM((HEADS, ROWS, HDIM), F32),
            pltpu.SMEM((2, IMAGES), jnp.int32),
            semaphore((5,)),
            semaphore((2,)),
        ]
        + [semaphore] * 8
        + [pltpu.SemaphoreType.REGULAR((PEERS,))],
        compiler_params=pltpu.CompilerParams(
            collective_id=0, has_side_effects=True, vmem_limit_bytes=24 * 1024 * 1024
        ),
    )(*[pltpu.with_memory_space_constraint(x, pltpu.HBM) for x in (fresh, keys, values, text, slots, lengths)])


def body(fresh, stale_keys, stale_values, text_kv, group_slots, text_len):
    slot_count = fresh.shape[2]
    text = text_kv[0].reshape(TBLOCKS, BLK, 2 * HD)
    merged = attention(fresh[0, 0], stale_keys[0, 0], stale_values[0, 0], text, group_slots, text_len)
    return jnp.pad(merged, ((0, slot_count - LIVE), (0, 0), (0, 0)))[None, None]


def solution(mesh):
    placed = (
        P("img", "patch", None, None, None),
        P("img", "patch", None, None, None),
        P("img", "patch", None, None, None),
        P("img", None, None),
        P(),
        P(),
    )
    return jax.shard_map(
        body,
        mesh=mesh,
        in_specs=placed,
        out_specs=P("img", "patch", None, None, None),
        check_vma=False,
    )
```

```python
import functools

import jax
import jax.numpy as jnp
from jax import lax
from jax.experimental import pallas as pl
from jax.experimental.pallas import tpu as pltpu
from jax.sharding import PartitionSpec as P

MESH = pl.DeviceIdType.MESH
F32 = jnp.float32
BF16 = jnp.bfloat16

HDIM = 128
HEADS = 12
HD = HDIM * HEADS
BLK = 16
LIVE = 3
TXT = 128
PEERS = 16
IMAGES = 32
ROWS = LIVE * BLK
BLOCKS = PEERS * LIVE
TBLOCKS = TXT // BLK
KEYS = BLOCKS * BLK + TXT
CHUNKS = 2
CPEERS = PEERS // CHUNKS
CROWS = CPEERS * ROWS
SCALE = 1.4426950408889634 / HDIM**0.5
MASKED = -1e30


def nt(a, b):
    return lax.dot_general(a, b, (((1,), (1,)), ((), ())), preferred_element_type=F32)


def owner_rank(peer, core):
    return ((peer >> 1) + 16 - 2 * core - (peer & 1)) & 3


def owned_head(peer, core):
    return (peer >> 3) * 6 + (peer & 1) * 3 + owner_rank(peer, core)


def partner(me, core, k):
    reach = k // 2 if k % 2 else -(k // 2)
    return (me + PEERS // 2 + reach * (1 - 2 * core)) & (PEERS - 1)


def kernel(
    fresh, keys, values, text, slots_in, lengths_in, out,
    own, stale, chunks, inbox, tkeys, tvalues, qmask, turned_keys, sbuf, pbuf, linv,
    osend, lsend, orecv, lrecv, ownout, ownlse, coef, counts,
    local_sem, text_sem, kq_sem, v_sem, o_sem, l_sem, kq_sent, v_sent, o_sent, l_sent, here,
):
    image = lax.axis_index("img")
    me = lax.axis_index("patch")
    core = image & 1
    is_owner = owner_rank(me, core) < 3
    my_head = owned_head(me, core)

    barrier = pltpu.get_barrier_semaphore()

    live = pl.ds(0, LIVE)
    local = [
        pltpu.make_async_copy(keys.at[live], stale.at[0], local_sem.at[0]),
        pltpu.make_async_copy(fresh.at[live], own, local_sem.at[1]),
        pltpu.make_async_copy(values.at[live], stale.at[1], local_sem.at[2]),
        pltpu.make_async_copy(slots_in, counts.at[0], local_sem.at[3]),
        pltpu.make_async_copy(lengths_in, counts.at[1], local_sem.at[4]),
    ]
    for copy in local:
        copy.start()

    def greet(peer, carry):
        pl.semaphore_signal(barrier, inc=1, device_id=(image, peer), device_id_type=MESH)
        return carry

    lax.fori_loop(me + 1, PEERS, greet, 0)

    @pl.when(me > 0)
    def _():
        pl.semaphore_wait(barrier, me)

    def tell(peer, carry):
        pl.semaphore_signal(here.at[me], inc=1, device_id=(image, peer), device_id_type=MESH)
        return carry

    lax.fori_loop(0, me, tell, 0)

    def text_copy(third, target):
        columns = pl.ds(pl.multiple_of(third * HD + my_head * HDIM, HDIM), HDIM)
        return pltpu.make_async_copy(text.at[:, :, columns], target, text_sem.at[third])

    texts = [text_copy(0, tkeys), text_copy(1, tvalues)]

    @pl.when(is_owner)
    def _():
        for copy in texts:
            copy.start()

    def stage(part, source):
        for head in range(HEADS):
            chunks[head, part] = source[:, :, head * HDIM : (head + 1) * HDIM]

    local[0].wait()
    stage(0, stale.at[0])
    local[1].wait()
    stage(1, own)
    local[2].wait()
    stage(2, stale.at[1])

    keys_queries = pl.ds(0, 2)
    only_values = pl.ds(2, 1)

    def send(peer, parts, sent, received):
        pltpu.make_async_remote_copy(
            src_ref=chunks.at[owned_head(peer, core), parts],
            dst_ref=inbox.at[me, parts],
            send_sem=sent,
            recv_sem=received,
            device_id=(image, peer),
            device_id_type=MESH,
        ).start()

    def send_before(parts, sent, received):
        for k in range(1, PEERS):
            peer = partner(me, core, k)

            @pl.when(jnp.logical_and(peer < me, owner_rank(peer, core) < 3))
            def _(peer=peer):
                send(peer, parts, sent, received)

    send_before(keys_queries, kq_sent, kq_sem)
    send_before(only_values, v_sent, v_sem)

    @pl.when(is_owner)
    def _():
        for parts, received in ((keys_queries, kq_sem), (only_values, v_sem)):
            pltpu.make_async_copy(chunks.at[my_head, parts], inbox.at[me, parts], received).start()

    def send_after(peer, carry):
        pl.semaphore_wait(here.at[peer], 1)

        @pl.when(owner_rank(peer, core) < 3)
        def _():
            send(peer, keys_queries, kq_sent, kq_sem)
            send(peer, only_values, v_sent, v_sem)

        return carry

    lax.fori_loop(me + 1, PEERS, send_after, 0)

    def wait_for(ref, sem):
        pltpu.make_async_copy(ref, ref, sem).wait()

    local[3].wait()
    local[4].wait()
    n = counts[0, image]
    length = counts[1, image]

    @pl.when(is_owner)
    def _():
        key = lax.broadcasted_iota(jnp.int32, (1, KEYS), 1)
        block = (key >> 4) + jnp.where(key < BLOCKS * BLK, 0, HDIM)
        slot = block - 3 * ((block * 171) >> 9)
        past = jnp.where(key < BLOCKS * BLK, slot - n, key - BLOCKS * BLK - length)
        mark = jnp.where(past >= 0, HDIM - 1, -1)
        row = lax.broadcasted_iota(jnp.int32, (HDIM, KEYS), 0)
        turned_keys[HDIM:] = jnp.where((row == block) | (row == mark), MASKED, 0.0).astype(BF16)
        shape = (BLOCKS, BLK, HDIM)
        block = lax.broadcasted_iota(jnp.int32, shape, 0)
        lane = lax.broadcasted_iota(jnp.int32, shape, 2)
        qmask[...] = jnp.where((lane == block) | (lane == HDIM - 1), 1.0, 0.0).astype(BF16)

    def attend_own(first, count):
        heads = range(first, first + count)
        diagonal = (
            lax.broadcasted_iota(jnp.int32, (ROWS, ROWS), 0) // BLK
            == lax.broadcasted_iota(jnp.int32, (ROWS, ROWS), 1) // BLK
        )

        def third(which, head):
            at = which * HD + head * HDIM
            return own[:, :, at : at + HDIM].reshape(ROWS, HDIM)

        scores = [jnp.where(diagonal, nt(third(0, head), third(1, head)), MASKED) for head in heads]
        tops = [jnp.max(x, axis=1, keepdims=True) for x in scores]
        weights = [jnp.exp2((x - top) * SCALE) for x, top in zip(scores, tops)]
        totals = [jnp.sum(x, axis=1, keepdims=True) for x in weights]
        sums = [
            jnp.dot(x.astype(BF16), third(2, head), preferred_element_type=F32) for x, head in zip(weights, heads)
        ]
        for i, head in enumerate(heads):
            ownout[head] = sums[i] / totals[i]
            ownlse[head] = jnp.broadcast_to(tops[i] * SCALE + jnp.log2(totals[i]), (ROWS, HDIM))

    def send_back(first, count, source, target, sent, received):
        for k in range(first, first + count):
            peer = partner(me, core, k)
            if k == PEERS:
                pltpu.make_async_copy(source.at[me], target, received).start()
            else:
                pltpu.make_async_remote_copy(
                    src_ref=source.at[peer],
                    dst_ref=target,
                    send_sem=sent,
                    recv_sem=received,
                    device_id=(image, peer),
                    device_id_type=MESH,
                ).start()

    @pl.when(is_owner)
    def _():
        for copy in texts:
            copy.wait()
        wait_for(inbox.at[:, keys_queries], kq_sem)
        k = jnp.concatenate([inbox[:, 0].reshape(BLOCKS * BLK, HDIM), tkeys[...].reshape(TXT, HDIM)], axis=0)
        turned_keys[:HDIM] = k.T
        q = jnp.concatenate(
            [inbox[:, 1].reshape(BLOCKS * BLK, HDIM), qmask[...].reshape(BLOCKS * BLK, HDIM)], axis=1
        )
        sbuf[...] = jnp.dot(q, turned_keys[...], preferred_element_type=F32)
        lane = lax.broadcasted_iota(jnp.int32, (ROWS, HDIM), 1)
        stats = jnp.zeros((ROWS, HDIM), F32)
        for peer in range(PEERS):
            rows = slice(peer * ROWS, (peer + 1) * ROWS)
            scores = sbuf[rows]
            top = jnp.max(scores, axis=1, keepdims=True)
            weights = jnp.exp2((scores - top) * SCALE)
            total = jnp.sum(weights, axis=1, keepdims=True)
            pbuf[peer] = weights.astype(BF16)
            linv[peer] = jnp.broadcast_to(1.0 / total, (ROWS, HDIM))
            stats = jnp.where(lane == peer, top * SCALE + jnp.log2(total), stats)
        turned = jnp.concatenate([stats, jnp.zeros((HDIM - ROWS, HDIM), F32)], axis=0).T
        for peer in range(PEERS):
            lsend[peer] = turned[peer : peer + 1]
        send_back(1, PEERS, lsend, lrecv.at[my_head], l_sent, l_sem)

        wait_for(inbox.at[:, only_values], v_sem)
        v = jnp.concatenate([inbox[:, 2].reshape(BLOCKS * BLK, HDIM), tvalues[...].reshape(TXT, HDIM)], axis=0)
        for chunk in range(CHUNKS):
            peers = [partner(me, core, chunk * CPEERS + i + 1) for i in range(CPEERS)]
            weights = jnp.concatenate([pbuf[peer] for peer in peers], axis=0)
            attended = jnp.dot(weights, v, preferred_element_type=F32)
            for i, peer in enumerate(peers):
                scaled = attended[i * ROWS : (i + 1) * ROWS] * linv[peer]
                osend[peer] = scaled.astype(BF16).reshape(LIVE, BLK, HDIM)
            send_back(chunk * CPEERS + 1, CPEERS, osend, orecv.at[my_head], o_sent, o_sem)

    attend_own(0, HEADS)

    @pl.when(is_owner)
    def _():
        wait_for(inbox.at[pl.ds(0, HEADS - 1), keys_queries], kq_sent)
        wait_for(inbox.at[pl.ds(0, HEADS - 1), only_values], v_sent)

    @pl.when(jnp.logical_not(is_owner))
    def _():
        wait_for(inbox.at[pl.ds(0, HEADS), keys_queries], kq_sent)
        wait_for(inbox.at[pl.ds(0, HEADS), only_values], v_sent)

    wait_for(lrecv, l_sem)
    stacked = jnp.concatenate([lrecv[head] for head in range(HEADS)] + [jnp.zeros((HDIM - HEADS, HDIM), F32)], axis=0)
    columns = stacked.T
    shown = lax.broadcasted_iota(jnp.int32, (LIVE, BLK, HDIM), 0) < n
    for head in range(HEADS):
        sibling = jnp.broadcast_to(columns[:ROWS, head : head + 1], (ROWS, HDIM))
        within = ownlse[head]
        top = jnp.maximum(sibling, within)
        a = jnp.exp2(sibling - top)
        b = jnp.exp2(within - top)
        inverse = 1.0 / (a + b)
        coef[head] = a * inverse
        ownout[head] = ownout[head] * (b * inverse)
    wait_for(orecv, o_sem)
    for head in range(HEADS):
        merged = orecv[head].reshape(ROWS, HDIM).astype(F32) * coef[head] + ownout[head]
        merged = jnp.where(shown, merged.reshape(LIVE, BLK, HDIM), 0.0)
        out[:, :, head * HDIM : (head + 1) * HDIM] = merged.astype(BF16)

    @pl.when(is_owner)
    def _():
        wait_for(lsend.at[pl.ds(0, PEERS - 1)], l_sent)
        wait_for(osend.at[pl.ds(0, PEERS - 1)], o_sent)


def attention(fresh, keys, values, text, slots, lengths):
    anywhere = pl.BlockSpec(memory_space=pl.ANY)
    semaphore = pltpu.SemaphoreType.DMA
    return pl.pallas_call(
        kernel,
        out_shape=jax.ShapeDtypeStruct((LIVE, BLK, HD), BF16),
        in_specs=[anywhere] * 6,
        out_specs=pl.BlockSpec(memory_space=pltpu.VMEM),
        scratch_shapes=[
            pltpu.VMEM((LIVE, BLK, 3 * HD), BF16),
            pltpu.VMEM((2, LIVE, BLK, HD), BF16),
            pltpu.VMEM((HEADS, 3, LIVE, BLK, HDIM), BF16),
            pltpu.VMEM((PEERS, 3, LIVE, BLK, HDIM), BF16),
            pltpu.VMEM((TBLOCKS, BLK, HDIM), BF16),
            pltpu.VMEM((TBLOCKS, BLK, HDIM), BF16),
            pltpu.VMEM((BLOCKS, BLK, HDIM), BF16),
            pltpu.VMEM((2 * HDIM, KEYS), BF16),
            pltpu.VMEM((BLOCKS * BLK, KEYS), F32),
            pltpu.VMEM((PEERS, ROWS, KEYS), BF16),
            pltpu.VMEM((PEERS, ROWS, HDIM), F32),
            pltpu.VMEM((PEERS, LIVE, BLK, HDIM), BF16),
            pltpu.VMEM((PEERS, 1, HDIM), F32),
            pltpu.VMEM((HEADS, LIVE, BLK, HDIM), BF16),
            pltpu.VMEM((HEADS, 1, HDIM), F32),
            pltpu.VMEM((HEADS, ROWS, HDIM), F32),
            pltpu.VMEM((HEADS, ROWS, HDIM), F32),
            pltpu.VMEM((HEADS, ROWS, HDIM), F32),
            pltpu.SMEM((2, IMAGES), jnp.int32),
            semaphore((5,)),
            semaphore((2,)),
        ]
        + [semaphore] * 8
        + [pltpu.SemaphoreType.REGULAR((PEERS,))],
        compiler_params=pltpu.CompilerParams(
            collective_id=0, has_side_effects=True, vmem_limit_bytes=24 * 1024 * 1024
        ),
    )(*[pltpu.with_memory_space_constraint(x, pltpu.HBM) for x in (fresh, keys, values, text, slots, lengths)])


def body(fresh, stale_keys, stale_values, text_kv, group_slots, text_len):
    slot_count = fresh.shape[2]
    text = text_kv[0].reshape(TBLOCKS, BLK, 2 * HD)
    merged = attention(fresh[0, 0], stale_keys[0, 0], stale_values[0, 0], text, group_slots, text_len)
    return jnp.pad(merged, ((0, slot_count - LIVE), (0, 0), (0, 0)))[None, None]


def solution(mesh):
    placed = (
        P("img", "patch", None, None, None),
        P("img", "patch", None, None, None),
        P("img", "patch", None, None, None),
        P("img", None, None),
        P(),
        P(),
    )
    return jax.shard_map(
        body,
        mesh=mesh,
        in_specs=placed,
        out_specs=P("img", "patch", None, None, None),
        check_vma=False,
    )
```

```python
import functools

import jax
import jax.numpy as jnp
from jax import lax
from jax.experimental import pallas as pl
from jax.experimental.pallas import tpu as pltpu
from jax.sharding import PartitionSpec as P

MESH = pl.DeviceIdType.MESH
F32 = jnp.float32
BF16 = jnp.bfloat16

HDIM = 128
HEADS = 12
HD = HDIM * HEADS
BLK = 16
LIVE = 3
TXT = 128
PEERS = 16
IMAGES = 32
ROWS = LIVE * BLK
BLOCKS = PEERS * LIVE
TBLOCKS = TXT // BLK
KEYS = BLOCKS * BLK + TXT
CHUNKS = 2
CPEERS = PEERS // CHUNKS
CROWS = CPEERS * ROWS
SCALE = 1.4426950408889634 / HDIM**0.5
MASKED = -1e30


def nt(a, b):
    return lax.dot_general(a, b, (((1,), (1,)), ((), ())), preferred_element_type=F32)


def owner_rank(peer, core):
    return ((peer >> 1) + 15 - 2 * core - (peer & 1)) & 3


def owned_head(peer, core):
    return (peer >> 3) * 6 + (peer & 1) * 3 + owner_rank(peer, core)


def partner(me, core, k):
    reach = k // 2 if k % 2 else -(k // 2)
    return (me + PEERS // 2 + reach * (1 - 2 * core)) & (PEERS - 1)


def kernel(
    fresh, keys, values, text, slots_in, lengths_in, out,
    own, stale, chunks, inbox, tkeys, tvalues, qmask, turned_keys, sbuf, pbuf, linv,
    osend, lsend, orecv, lrecv, ownout, ownlse, coef, counts,
    local_sem, text_sem, kq_sem, v_sem, o_sem, l_sem, kq_sent, v_sent, o_sent, l_sent, here,
):
    image = lax.axis_index("img")
    me = lax.axis_index("patch")
    core = image & 1
    is_owner = owner_rank(me, core) < 3
    my_head = owned_head(me, core)

    barrier = pltpu.get_barrier_semaphore()

    live = pl.ds(0, LIVE)
    local = [
        pltpu.make_async_copy(keys.at[live], stale.at[0], local_sem.at[0]),
        pltpu.make_async_copy(fresh.at[live], own, local_sem.at[1]),
        pltpu.make_async_copy(values.at[live], stale.at[1], local_sem.at[2]),
        pltpu.make_async_copy(slots_in, counts.at[0], local_sem.at[3]),
        pltpu.make_async_copy(lengths_in, counts.at[1], local_sem.at[4]),
    ]
    for copy in local:
        copy.start()

    def greet(peer, carry):
        pl.semaphore_signal(barrier, inc=1, device_id=(image, peer), device_id_type=MESH)
        return carry

    lax.fori_loop(me + 1, PEERS, greet, 0)

    @pl.when(me > 0)
    def _():
        pl.semaphore_wait(barrier, me)

    def tell(peer, carry):
        pl.semaphore_signal(here.at[me], inc=1, device_id=(image, peer), device_id_type=MESH)
        return carry

    lax.fori_loop(0, me, tell, 0)

    def text_copy(third, target):
        columns = pl.ds(pl.multiple_of(third * HD + my_head * HDIM, HDIM), HDIM)
        return pltpu.make_async_copy(text.at[:, :, columns], target, text_sem.at[third])

    texts = [text_copy(0, tkeys), text_copy(1, tvalues)]

    @pl.when(is_owner)
    def _():
        for copy in texts:
            copy.start()

    def stage(part, source):
        for head in range(HEADS):
            chunks[head, part] = source[:, :, head * HDIM : (head + 1) * HDIM]

    local[0].wait()
    stage(0, stale.at[0])
    local[1].wait()
    stage(1, own)
    local[2].wait()
    stage(2, stale.at[1])

    keys_queries = pl.ds(0, 2)
    only_values = pl.ds(2, 1)

    def send(peer, parts, sent, received):
        pltpu.make_async_remote_copy(
            src_ref=chunks.at[owned_head(peer, core), parts],
            dst_ref=inbox.at[me, parts],
            send_sem=sent,
            recv_sem=received,
            device_id=(image, peer),
            device_id_type=MESH,
        ).start()

    def send_before(parts, sent, received):
        for k in range(1, PEERS):
            peer = partner(me, core, k)

            @pl.when(jnp.logical_and(peer < me, owner_rank(peer, core) < 3))
            def _(peer=peer):
                send(peer, parts, sent, received)

    send_before(keys_queries, kq_sent, kq_sem)
    send_before(only_values, v_sent, v_sem)

    @pl.when(is_owner)
    def _():
        for parts, received in ((keys_queries, kq_sem), (only_values, v_sem)):
            pltpu.make_async_copy(chunks.at[my_head, parts], inbox.at[me, parts], received).start()

    def send_after(peer, carry):
        pl.semaphore_wait(here.at[peer], 1)

        @pl.when(owner_rank(peer, core) < 3)
        def _():
            send(peer, keys_queries, kq_sent, kq_sem)
            send(peer, only_values, v_sent, v_sem)

        return carry

    lax.fori_loop(me + 1, PEERS, send_after, 0)

    def wait_for(ref, sem):
        pltpu.make_async_copy(ref, ref, sem).wait()

    local[3].wait()
    local[4].wait()
    n = counts[0, image]
    length = counts[1, image]

    @pl.when(is_owner)
    def _():
        key = lax.broadcasted_iota(jnp.int32, (1, KEYS), 1)
        block = (key >> 4) + jnp.where(key < BLOCKS * BLK, 0, HDIM)
        slot = block - 3 * ((block * 171) >> 9)
        past = jnp.where(key < BLOCKS * BLK, slot - n, key - BLOCKS * BLK - length)
        mark = jnp.where(past >= 0, HDIM - 1, -1)
        row = lax.broadcasted_iota(jnp.int32, (HDIM, KEYS), 0)
        turned_keys[HDIM:] = jnp.where((row == block) | (row == mark), MASKED, 0.0).astype(BF16)
        shape = (BLOCKS, BLK, HDIM)
        block = lax.broadcasted_iota(jnp.int32, shape, 0)
        lane = lax.broadcasted_iota(jnp.int32, shape, 2)
        qmask[...] = jnp.where((lane == block) | (lane == HDIM - 1), 1.0, 0.0).astype(BF16)

    def attend_own(first, count):
        heads = range(first, first + count)
        diagonal = (
            lax.broadcasted_iota(jnp.int32, (ROWS, ROWS), 0) // BLK
            == lax.broadcasted_iota(jnp.int32, (ROWS, ROWS), 1) // BLK
        )

        def third(which, head):
            at = which * HD + head * HDIM
            return own[:, :, at : at + HDIM].reshape(ROWS, HDIM)

        scores = [jnp.where(diagonal, nt(third(0, head), third(1, head)), MASKED) for head in heads]
        tops = [jnp.max(x, axis=1, keepdims=True) for x in scores]
        weights = [jnp.exp2((x - top) * SCALE) for x, top in zip(scores, tops)]
        totals = [jnp.sum(x, axis=1, keepdims=True) for x in weights]
        sums = [
            jnp.dot(x.astype(BF16), third(2, head), preferred_element_type=F32) for x, head in zip(weights, heads)
        ]
        for i, head in enumerate(heads):
            ownout[head] = sums[i] / totals[i]
            ownlse[head] = jnp.broadcast_to(tops[i] * SCALE + jnp.log2(totals[i]), (ROWS, HDIM))

    def send_back(first, count, source, target, sent, received):
        for k in range(first, first + count):
            peer = partner(me, core, k)
            if k == PEERS:
                pltpu.make_async_copy(source.at[me], target, received).start()
            else:
                pltpu.make_async_remote_copy(
                    src_ref=source.at[peer],
                    dst_ref=target,
                    send_sem=sent,
                    recv_sem=received,
                    device_id=(image, peer),
                    device_id_type=MESH,
                ).start()

    @pl.when(is_owner)
    def _():
        for copy in texts:
            copy.wait()
        wait_for(inbox.at[:, keys_queries], kq_sem)
        k = jnp.concatenate([inbox[:, 0].reshape(BLOCKS * BLK, HDIM), tkeys[...].reshape(TXT, HDIM)], axis=0)
        turned_keys[:HDIM] = k.T
        lane = lax.broadcasted_iota(jnp.int32, (ROWS, HDIM), 1)
        for chunk in range(CHUNKS):
            peers = [partner(me, core, chunk * CPEERS + i + 1) for i in range(CPEERS)]
            q = jnp.concatenate([inbox[peer, 1].reshape(ROWS, HDIM) for peer in peers], axis=0)
            marks = jnp.concatenate([qmask[pl.ds(peer * LIVE, LIVE)].reshape(ROWS, HDIM) for peer in peers], axis=0)
            sbuf[chunk] = jnp.dot(
                jnp.concatenate([q, marks], axis=1), turned_keys[...], preferred_element_type=F32
            )
            stats = jnp.zeros((ROWS, HDIM), F32)
            for i in range(CPEERS):
                rows = slice(i * ROWS, (i + 1) * ROWS)
                scores = sbuf[chunk, rows]
                top = jnp.max(scores, axis=1, keepdims=True)
                weights = jnp.exp2((scores - top) * SCALE)
                total = jnp.sum(weights, axis=1, keepdims=True)
                pbuf[chunk, rows] = weights.astype(BF16)
                linv[chunk, rows] = jnp.broadcast_to(1.0 / total, (ROWS, HDIM))
                stats = jnp.where(lane == i, top * SCALE + jnp.log2(total), stats)
            if chunk == 0:
                wait_for(inbox.at[:, only_values], v_sem)
            v = jnp.concatenate([inbox[:, 2].reshape(BLOCKS * BLK, HDIM), tvalues[...].reshape(TXT, HDIM)], axis=0)
            attended = jnp.dot(pbuf[chunk], v, preferred_element_type=F32) * linv[chunk]
            attended = attended.astype(BF16).reshape(CPEERS, LIVE, BLK, HDIM)
            for i, peer in enumerate(peers):
                osend[peer] = attended[i]
            send_back(chunk * CPEERS + 1, CPEERS, osend, orecv.at[my_head], o_sent, o_sem)
            turned = jnp.concatenate([stats, jnp.zeros((HDIM - ROWS, HDIM), F32)], axis=0).T
            for i, peer in enumerate(peers):
                lsend[peer] = turned[i : i + 1]
            send_back(chunk * CPEERS + 1, CPEERS, lsend, lrecv.at[my_head], l_sent, l_sem)

    attend_own(0, HEADS)

    @pl.when(is_owner)
    def _():
        wait_for(inbox.at[pl.ds(0, HEADS - 1), keys_queries], kq_sent)
        wait_for(inbox.at[pl.ds(0, HEADS - 1), only_values], v_sent)

    @pl.when(jnp.logical_not(is_owner))
    def _():
        wait_for(inbox.at[pl.ds(0, HEADS), keys_queries], kq_sent)
        wait_for(inbox.at[pl.ds(0, HEADS), only_values], v_sent)

    wait_for(lrecv, l_sem)
    stacked = jnp.concatenate([lrecv[head] for head in range(HEADS)] + [jnp.zeros((HDIM - HEADS, HDIM), F32)], axis=0)
    columns = stacked.T
    shown = lax.broadcasted_iota(jnp.int32, (LIVE, BLK, HDIM), 0) < n
    for head in range(HEADS):
        sibling = jnp.broadcast_to(columns[:ROWS, head : head + 1], (ROWS, HDIM))
        within = ownlse[head]
        top = jnp.maximum(sibling, within)
        a = jnp.exp2(sibling - top)
        b = jnp.exp2(within - top)
        inverse = 1.0 / (a + b)
        coef[head] = a * inverse
        ownout[head] = ownout[head] * (b * inverse)
    wait_for(orecv, o_sem)
    for head in range(HEADS):
        merged = orecv[head].reshape(ROWS, HDIM).astype(F32) * coef[head] + ownout[head]
        merged = jnp.where(shown, merged.reshape(LIVE, BLK, HDIM), 0.0)
        out[:, :, head * HDIM : (head + 1) * HDIM] = merged.astype(BF16)

    @pl.when(is_owner)
    def _():
        wait_for(lsend.at[pl.ds(0, PEERS - 1)], l_sent)
        wait_for(osend.at[pl.ds(0, PEERS - 1)], o_sent)


def attention(fresh, keys, values, text, slots, lengths):
    anywhere = pl.BlockSpec(memory_space=pl.ANY)
    semaphore = pltpu.SemaphoreType.DMA
    return pl.pallas_call(
        kernel,
        out_shape=jax.ShapeDtypeStruct((LIVE, BLK, HD), BF16),
        in_specs=[anywhere] * 6,
        out_specs=pl.BlockSpec(memory_space=pltpu.VMEM),
        scratch_shapes=[
            pltpu.VMEM((LIVE, BLK, 3 * HD), BF16),
            pltpu.VMEM((2, LIVE, BLK, HD), BF16),
            pltpu.VMEM((HEADS, 3, LIVE, BLK, HDIM), BF16),
            pltpu.VMEM((PEERS, 3, LIVE, BLK, HDIM), BF16),
            pltpu.VMEM((TBLOCKS, BLK, HDIM), BF16),
            pltpu.VMEM((TBLOCKS, BLK, HDIM), BF16),
            pltpu.VMEM((BLOCKS, BLK, HDIM), BF16),
            pltpu.VMEM((2 * HDIM, KEYS), BF16),
            pltpu.VMEM((CHUNKS, CROWS, KEYS), F32),
            pltpu.VMEM((CHUNKS, CROWS, KEYS), BF16),
            pltpu.VMEM((CHUNKS, CROWS, HDIM), F32),
            pltpu.VMEM((PEERS, LIVE, BLK, HDIM), BF16),
            pltpu.VMEM((PEERS, 1, HDIM), F32),
            pltpu.VMEM((HEADS, LIVE, BLK, HDIM), BF16),
            pltpu.VMEM((HEADS, 1, HDIM), F32),
            pltpu.VMEM((HEADS, ROWS, HDIM), F32),
            pltpu.VMEM((HEADS, ROWS, HDIM), F32),
            pltpu.VMEM((HEADS, ROWS, HDIM), F32),
            pltpu.SMEM((2, IMAGES), jnp.int32),
            semaphore((5,)),
            semaphore((2,)),
        ]
        + [semaphore] * 8
        + [pltpu.SemaphoreType.REGULAR((PEERS,))],
        compiler_params=pltpu.CompilerParams(
            collective_id=0, has_side_effects=True, vmem_limit_bytes=24 * 1024 * 1024
        ),
    )(*[pltpu.with_memory_space_constraint(x, pltpu.HBM) for x in (fresh, keys, values, text, slots, lengths)])


def body(fresh, stale_keys, stale_values, text_kv, group_slots, text_len):
    slot_count = fresh.shape[2]
    text = text_kv[0].reshape(TBLOCKS, BLK, 2 * HD)
    merged = attention(fresh[0, 0], stale_keys[0, 0], stale_values[0, 0], text, group_slots, text_len)
    return jnp.pad(merged, ((0, slot_count - LIVE), (0, 0), (0, 0)))[None, None]


def solution(mesh):
    placed = (
        P("img", "patch", None, None, None),
        P("img", "patch", None, None, None),
        P("img", "patch", None, None, None),
        P("img", None, None),
        P(),
        P(),
    )
    return jax.shard_map(
        body,
        mesh=mesh,
        in_specs=placed,
        out_specs=P("img", "patch", None, None, None),
        check_vma=False,
    )
```

```python
import functools

import jax
import jax.numpy as jnp
from jax import lax
from jax.experimental import pallas as pl
from jax.experimental.pallas import tpu as pltpu
from jax.sharding import PartitionSpec as P

MESH = pl.DeviceIdType.MESH
F32 = jnp.float32
BF16 = jnp.bfloat16

HDIM = 128
HEADS = 12
HD = HDIM * HEADS
BLK = 16
LIVE = 3
TXT = 128
PEERS = 16
IMAGES = 32
ROWS = LIVE * BLK
BLOCKS = PEERS * LIVE
TBLOCKS = TXT // BLK
KEYS = BLOCKS * BLK + TXT
CHUNKS = 2
CPEERS = PEERS // CHUNKS
CROWS = CPEERS * ROWS
SCALE = 1.4426950408889634 / HDIM**0.5
MASKED = -1e30


def nt(a, b):
    return lax.dot_general(a, b, (((1,), (1,)), ((), ())), preferred_element_type=F32)


def owner_rank(peer, core):
    return ((peer >> 1) + 15 - 2 * core - (peer & 1)) & 3


def owned_head(peer, core):
    return (peer >> 3) * 6 + (peer & 1) * 3 + owner_rank(peer, core)


def partner(me, core, k):
    reach = k // 2 if k % 2 else -(k // 2)
    return (me + PEERS // 2 + reach * (1 - 2 * core)) & (PEERS - 1)


def kernel(
    fresh, keys, values, text, slots_in, lengths_in, out,
    own, stale, chunks, inbox, tkeys, tvalues, qmask, turned_keys, sbuf, pbuf, linv,
    osend, lsend, orecv, lrecv, ownout, ownlse, coef, counts,
    local_sem, text_sem, kq_sem, v_sem, o_sem, l_sem, kq_sent, v_sent, o_sent, l_sent,
):
    image = lax.axis_index("img")
    me = lax.axis_index("patch")
    core = image & 1
    is_owner = owner_rank(me, core) < 3
    my_head = owned_head(me, core)

    barrier = pltpu.get_barrier_semaphore()

    live = pl.ds(0, LIVE)
    local = [
        pltpu.make_async_copy(keys.at[live], stale.at[0], local_sem.at[0]),
        pltpu.make_async_copy(fresh.at[live], own, local_sem.at[1]),
        pltpu.make_async_copy(values.at[live], stale.at[1], local_sem.at[2]),
        pltpu.make_async_copy(slots_in, counts.at[0], local_sem.at[3]),
        pltpu.make_async_copy(lengths_in, counts.at[1], local_sem.at[4]),
    ]
    for copy in local:
        copy.start()

    for k in range(1, PEERS):
        pl.semaphore_signal(barrier, inc=1, device_id=(image, partner(me, core, k)), device_id_type=MESH)

    def text_copy(third, target):
        columns = pl.ds(pl.multiple_of(third * HD + my_head * HDIM, HDIM), HDIM)
        return pltpu.make_async_copy(text.at[:, :, columns], target, text_sem.at[third])

    texts = [text_copy(0, tkeys), text_copy(1, tvalues)]

    @pl.when(is_owner)
    def _():
        for copy in texts:
            copy.start()

    def stage(part, source):
        for head in range(HEADS):
            chunks[head, part] = source[:, :, head * HDIM : (head + 1) * HDIM]

    local[0].wait()
    stage(0, stale.at[0])
    local[1].wait()
    stage(1, own)
    local[2].wait()
    stage(2, stale.at[1])

    pl.semaphore_wait(barrier, PEERS - 1)

    keys_queries = pl.ds(0, 2)
    only_values = pl.ds(2, 1)

    def send(peer, parts, sent, received):
        pltpu.make_async_remote_copy(
            src_ref=chunks.at[owned_head(peer, core), parts],
            dst_ref=inbox.at[me, parts],
            send_sem=sent,
            recv_sem=received,
            device_id=(image, peer),
            device_id_type=MESH,
        ).start()

    def send_all(parts, sent, received):
        for k in range(1, PEERS):
            peer = partner(me, core, k)

            @pl.when(owner_rank(peer, core) < 3)
            def _(peer=peer):
                send(peer, parts, sent, received)

    send_all(keys_queries, kq_sent, kq_sem)
    send_all(only_values, v_sent, v_sem)

    @pl.when(is_owner)
    def _():
        for parts, received in ((keys_queries, kq_sem), (only_values, v_sem)):
            pltpu.make_async_copy(chunks.at[my_head, parts], inbox.at[me, parts], received).start()

    def wait_for(ref, sem):
        pltpu.make_async_copy(ref, ref, sem).wait()

    local[3].wait()
    local[4].wait()
    n = counts[0, image]
    length = counts[1, image]

    @pl.when(is_owner)
    def _():
        key = lax.broadcasted_iota(jnp.int32, (1, KEYS), 1)
        block = (key >> 4) + jnp.where(key < BLOCKS * BLK, 0, HDIM)
        slot = block - 3 * ((block * 171) >> 9)
        past = jnp.where(key < BLOCKS * BLK, slot - n, key - BLOCKS * BLK - length)
        mark = jnp.where(past >= 0, HDIM - 1, -1)
        row = lax.broadcasted_iota(jnp.int32, (HDIM, KEYS), 0)
        turned_keys[HDIM:] = jnp.where((row == block) | (row == mark), MASKED, 0.0).astype(BF16)
        shape = (BLOCKS, BLK, HDIM)
        block = lax.broadcasted_iota(jnp.int32, shape, 0)
        lane = lax.broadcasted_iota(jnp.int32, shape, 2)
        qmask[...] = jnp.where((lane == block) | (lane == HDIM - 1), 1.0, 0.0).astype(BF16)

    def attend_own(first, count):
        heads = range(first, first + count)
        diagonal = (
            lax.broadcasted_iota(jnp.int32, (ROWS, ROWS), 0) // BLK
            == lax.broadcasted_iota(jnp.int32, (ROWS, ROWS), 1) // BLK
        )

        def third(which, head):
            at = which * HD + head * HDIM
            return own[:, :, at : at + HDIM].reshape(ROWS, HDIM)

        scores = [jnp.where(diagonal, nt(third(0, head), third(1, head)), MASKED) for head in heads]
        tops = [jnp.max(x, axis=1, keepdims=True) for x in scores]
        weights = [jnp.exp2((x - top) * SCALE) for x, top in zip(scores, tops)]
        totals = [jnp.sum(x, axis=1, keepdims=True) for x in weights]
        sums = [
            jnp.dot(x.astype(BF16), third(2, head), preferred_element_type=F32) for x, head in zip(weights, heads)
        ]
        for i, head in enumerate(heads):
            ownout[head] = sums[i] / totals[i]
            ownlse[head] = jnp.broadcast_to(tops[i] * SCALE + jnp.log2(totals[i]), (ROWS, HDIM))

    def send_back(first, count, source, target, sent, received):
        for k in range(first, first + count):
            peer = partner(me, core, k)
            if k == PEERS:
                pltpu.make_async_copy(source.at[me], target, received).start()
            else:
                pltpu.make_async_remote_copy(
                    src_ref=source.at[peer],
                    dst_ref=target,
                    send_sem=sent,
                    recv_sem=received,
                    device_id=(image, peer),
                    device_id_type=MESH,
                ).start()

    @pl.when(is_owner)
    def _():
        for copy in texts:
            copy.wait()
        wait_for(inbox.at[:, keys_queries], kq_sem)
        k = jnp.concatenate([inbox[:, 0].reshape(BLOCKS * BLK, HDIM), tkeys[...].reshape(TXT, HDIM)], axis=0)
        turned_keys[:HDIM] = k.T
        q = jnp.concatenate(
            [inbox[:, 1].reshape(BLOCKS * BLK, HDIM), qmask[...].reshape(BLOCKS * BLK, HDIM)], axis=1
        )
        sbuf[...] = jnp.dot(q, turned_keys[...], preferred_element_type=F32)
        lane = lax.broadcasted_iota(jnp.int32, (ROWS, HDIM), 1)
        stats = jnp.zeros((ROWS, HDIM), F32)
        for peer in range(PEERS):
            rows = slice(peer * ROWS, (peer + 1) * ROWS)
            scores = sbuf[rows]
            top = jnp.max(scores, axis=1, keepdims=True)
            weights = jnp.exp2((scores - top) * SCALE)
            total = jnp.sum(weights, axis=1, keepdims=True)
            pbuf[peer] = weights.astype(BF16)
            linv[peer] = jnp.broadcast_to(1.0 / total, (ROWS, HDIM))
            stats = jnp.where(lane == peer, top * SCALE + jnp.log2(total), stats)
        turned = jnp.concatenate([stats, jnp.zeros((HDIM - ROWS, HDIM), F32)], axis=0).T
        for peer in range(PEERS):
            lsend[peer] = turned[peer : peer + 1]
        send_back(1, PEERS, lsend, lrecv.at[my_head], l_sent, l_sem)

        wait_for(inbox.at[:, only_values], v_sem)
        v = jnp.concatenate([inbox[:, 2].reshape(BLOCKS * BLK, HDIM), tvalues[...].reshape(TXT, HDIM)], axis=0)
        for chunk in range(CHUNKS):
            peers = [partner(me, core, chunk * CPEERS + i + 1) for i in range(CPEERS)]
            weights = jnp.concatenate([pbuf[peer] for peer in peers], axis=0)
            attended = jnp.dot(weights, v, preferred_element_type=F32)
            for i, peer in enumerate(peers):
                scaled = attended[i * ROWS : (i + 1) * ROWS] * linv[peer]
                osend[peer] = scaled.astype(BF16).reshape(LIVE, BLK, HDIM)
            send_back(chunk * CPEERS + 1, CPEERS, osend, orecv.at[my_head], o_sent, o_sem)

    attend_own(0, HEADS)

    @pl.when(is_owner)
    def _():
        wait_for(inbox.at[pl.ds(0, HEADS - 1), keys_queries], kq_sent)
        wait_for(inbox.at[pl.ds(0, HEADS - 1), only_values], v_sent)

    @pl.when(jnp.logical_not(is_owner))
    def _():
        wait_for(inbox.at[pl.ds(0, HEADS), keys_queries], kq_sent)
        wait_for(inbox.at[pl.ds(0, HEADS), only_values], v_sent)

    wait_for(lrecv, l_sem)
    stacked = jnp.concatenate([lrecv[head] for head in range(HEADS)] + [jnp.zeros((HDIM - HEADS, HDIM), F32)], axis=0)
    columns = stacked.T
    shown = lax.broadcasted_iota(jnp.int32, (LIVE, BLK, HDIM), 0) < n
    for head in range(HEADS):
        sibling = jnp.broadcast_to(columns[:ROWS, head : head + 1], (ROWS, HDIM))
        within = ownlse[head]
        top = jnp.maximum(sibling, within)
        a = jnp.exp2(sibling - top)
        b = jnp.exp2(within - top)
        inverse = 1.0 / (a + b)
        coef[head] = a * inverse
        ownout[head] = ownout[head] * (b * inverse)
    wait_for(orecv, o_sem)
    for head in range(HEADS):
        merged = orecv[head].reshape(ROWS, HDIM).astype(F32) * coef[head] + ownout[head]
        merged = jnp.where(shown, merged.reshape(LIVE, BLK, HDIM), 0.0)
        out[:, :, head * HDIM : (head + 1) * HDIM] = merged.astype(BF16)

    @pl.when(is_owner)
    def _():
        wait_for(lsend.at[pl.ds(0, PEERS - 1)], l_sent)
        wait_for(osend.at[pl.ds(0, PEERS - 1)], o_sent)


def attention(fresh, keys, values, text, slots, lengths):
    anywhere = pl.BlockSpec(memory_space=pl.ANY)
    semaphore = pltpu.SemaphoreType.DMA
    return pl.pallas_call(
        kernel,
        out_shape=jax.ShapeDtypeStruct((LIVE, BLK, HD), BF16),
        in_specs=[anywhere] * 6,
        out_specs=pl.BlockSpec(memory_space=pltpu.VMEM),
        scratch_shapes=[
            pltpu.VMEM((LIVE, BLK, 3 * HD), BF16),
            pltpu.VMEM((2, LIVE, BLK, HD), BF16),
            pltpu.VMEM((HEADS, 3, LIVE, BLK, HDIM), BF16),
            pltpu.VMEM((PEERS, 3, LIVE, BLK, HDIM), BF16),
            pltpu.VMEM((TBLOCKS, BLK, HDIM), BF16),
            pltpu.VMEM((TBLOCKS, BLK, HDIM), BF16),
            pltpu.VMEM((BLOCKS, BLK, HDIM), BF16),
            pltpu.VMEM((2 * HDIM, KEYS), BF16),
            pltpu.VMEM((BLOCKS * BLK, KEYS), F32),
            pltpu.VMEM((PEERS, ROWS, KEYS), BF16),
            pltpu.VMEM((PEERS, ROWS, HDIM), F32),
            pltpu.VMEM((PEERS, LIVE, BLK, HDIM), BF16),
            pltpu.VMEM((PEERS, 1, HDIM), F32),
            pltpu.VMEM((HEADS, LIVE, BLK, HDIM), BF16),
            pltpu.VMEM((HEADS, 1, HDIM), F32),
            pltpu.VMEM((HEADS, ROWS, HDIM), F32),
            pltpu.VMEM((HEADS, ROWS, HDIM), F32),
            pltpu.VMEM((HEADS, ROWS, HDIM), F32),
            pltpu.SMEM((2, IMAGES), jnp.int32),
            semaphore((5,)),
            semaphore((2,)),
        ]
        + [semaphore] * 8,
        compiler_params=pltpu.CompilerParams(
            collective_id=0, has_side_effects=True, vmem_limit_bytes=24 * 1024 * 1024
        ),
    )(*[pltpu.with_memory_space_constraint(x, pltpu.HBM) for x in (fresh, keys, values, text, slots, lengths)])


def body(fresh, stale_keys, stale_values, text_kv, group_slots, text_len):
    slot_count = fresh.shape[2]
    text = text_kv[0].reshape(TBLOCKS, BLK, 2 * HD)
    merged = attention(fresh[0, 0], stale_keys[0, 0], stale_values[0, 0], text, group_slots, text_len)
    return jnp.pad(merged, ((0, slot_count - LIVE), (0, 0), (0, 0)))[None, None]


def solution(mesh):
    placed = (
        P("img", "patch", None, None, None),
        P("img", "patch", None, None, None),
        P("img", "patch", None, None, None),
        P("img", None, None),
        P(),
        P(),
    )
    return jax.shard_map(
        body,
        mesh=mesh,
        in_specs=placed,
        out_specs=P("img", "patch", None, None, None),
        check_vma=False,
    )
```

```python
import functools

import jax
import jax.numpy as jnp
from jax import lax
from jax.experimental import pallas as pl
from jax.experimental.pallas import tpu as pltpu
from jax.sharding import PartitionSpec as P

MESH = pl.DeviceIdType.MESH
F32 = jnp.float32
BF16 = jnp.bfloat16

HDIM = 128
HEADS = 12
HD = HDIM * HEADS
BLK = 16
LIVE = 3
TXT = 128
PEERS = 16
IMAGES = 32
ROWS = LIVE * BLK
BLOCKS = PEERS * LIVE
TBLOCKS = TXT // BLK
KEYS = BLOCKS * BLK + TXT
CHUNKS = 4
CPEERS = PEERS // CHUNKS
CROWS = CPEERS * ROWS
SCALE = 1.4426950408889634 / HDIM**0.5
MASKED = -1e30


def nt(a, b):
    return lax.dot_general(a, b, (((1,), (1,)), ((), ())), preferred_element_type=F32)


def owner_rank(peer, core):
    return ((peer >> 1) + 15 - 2 * core - (peer & 1)) & 3


def owned_head(peer, core):
    return (peer >> 3) * 6 + (peer & 1) * 3 + owner_rank(peer, core)


def partner(me, core, k):
    reach = k // 2 if k % 2 else -(k // 2)
    return (me + PEERS // 2 + reach * (1 - 2 * core)) & (PEERS - 1)


def kernel(
    fresh, keys, values, text, slots_in, lengths_in, out,
    own, stale, chunks, inbox, tkeys, tvalues, qmask, turned_keys, sbuf, pbuf, linv,
    osend, lsend, orecv, lrecv, ownout, ownlse, coef, counts,
    local_sem, text_sem, kq_sem, v_sem, o_sem, l_sem, kq_sent, v_sent, o_sent, l_sent, here,
):
    image = lax.axis_index("img")
    me = lax.axis_index("patch")
    core = image & 1
    is_owner = owner_rank(me, core) < 3
    my_head = owned_head(me, core)

    barrier = pltpu.get_barrier_semaphore()

    live = pl.ds(0, LIVE)
    local = [
        pltpu.make_async_copy(keys.at[live], stale.at[0], local_sem.at[0]),
        pltpu.make_async_copy(fresh.at[live], own, local_sem.at[1]),
        pltpu.make_async_copy(values.at[live], stale.at[1], local_sem.at[2]),
        pltpu.make_async_copy(slots_in, counts.at[0], local_sem.at[3]),
        pltpu.make_async_copy(lengths_in, counts.at[1], local_sem.at[4]),
    ]
    for copy in local:
        copy.start()

    def greet(peer, carry):
        pl.semaphore_signal(barrier, inc=1, device_id=(image, peer), device_id_type=MESH)
        return carry

    lax.fori_loop(me + 1, PEERS, greet, 0)

    @pl.when(me > 0)
    def _():
        pl.semaphore_wait(barrier, me)

    def tell(peer, carry):
        pl.semaphore_signal(here.at[me], inc=1, device_id=(image, peer), device_id_type=MESH)
        return carry

    lax.fori_loop(0, me, tell, 0)

    def text_copy(third, target):
        columns = pl.ds(pl.multiple_of(third * HD + my_head * HDIM, HDIM), HDIM)
        return pltpu.make_async_copy(text.at[:, :, columns], target, text_sem.at[third])

    texts = [text_copy(0, tkeys), text_copy(1, tvalues)]

    @pl.when(is_owner)
    def _():
        for copy in texts:
            copy.start()

    def stage(part, source):
        for head in range(HEADS):
            chunks[head, part] = source[:, :, head * HDIM : (head + 1) * HDIM]

    local[0].wait()
    stage(0, stale.at[0])
    local[1].wait()
    stage(1, own)
    local[2].wait()
    stage(2, stale.at[1])

    keys_queries = pl.ds(0, 2)
    only_values = pl.ds(2, 1)

    def send(peer, parts, sent, received):
        pltpu.make_async_remote_copy(
            src_ref=chunks.at[owned_head(peer, core), parts],
            dst_ref=inbox.at[me, parts],
            send_sem=sent,
            recv_sem=received,
            device_id=(image, peer),
            device_id_type=MESH,
        ).start()

    def send_before(parts, sent, received):
        for k in range(1, PEERS):
            peer = partner(me, core, k)

            @pl.when(jnp.logical_and(peer < me, owner_rank(peer, core) < 3))
            def _(peer=peer):
                send(peer, parts, sent, received)

    send_before(keys_queries, kq_sent, kq_sem)
    send_before(only_values, v_sent, v_sem)

    @pl.when(is_owner)
    def _():
        for parts, received in ((keys_queries, kq_sem), (only_values, v_sem)):
            pltpu.make_async_copy(chunks.at[my_head, parts], inbox.at[me, parts], received).start()

    def attend_own(first, count):
        heads = range(first, first + count)
        diagonal = (
            lax.broadcasted_iota(jnp.int32, (ROWS, ROWS), 0) // BLK
            == lax.broadcasted_iota(jnp.int32, (ROWS, ROWS), 1) // BLK
        )

        def third(which, head):
            at = which * HD + head * HDIM
            return own[:, :, at : at + HDIM].reshape(ROWS, HDIM)

        scores = [jnp.where(diagonal, nt(third(0, head), third(1, head)), MASKED) for head in heads]
        tops = [jnp.max(x, axis=1, keepdims=True) for x in scores]
        weights = [jnp.exp2((x - top) * SCALE) for x, top in zip(scores, tops)]
        totals = [jnp.sum(x, axis=1, keepdims=True) for x in weights]
        sums = [
            jnp.dot(x.astype(BF16), third(2, head), preferred_element_type=F32) for x, head in zip(weights, heads)
        ]
        for i, head in enumerate(heads):
            ownout[head] = sums[i] / totals[i]
            ownlse[head] = jnp.broadcast_to(tops[i] * SCALE + jnp.log2(totals[i]), (ROWS, HDIM))

    @pl.when(me < PEERS // 2)
    def _():
        attend_own(0, HEADS)

    def send_after(peer, carry):
        pl.semaphore_wait(here.at[peer], 1)

        @pl.when(owner_rank(peer, core) < 3)
        def _():
            send(peer, keys_queries, kq_sent, kq_sem)
            send(peer, only_values, v_sent, v_sem)

        return carry

    lax.fori_loop(me + 1, PEERS, send_after, 0)

    def wait_for(ref, sem):
        pltpu.make_async_copy(ref, ref, sem).wait()

    local[3].wait()
    local[4].wait()
    n = counts[0, image]
    length = counts[1, image]

    @pl.when(is_owner)
    def _():
        key = lax.broadcasted_iota(jnp.int32, (1, KEYS), 1)
        block = (key >> 4) + jnp.where(key < BLOCKS * BLK, 0, HDIM)
        slot = block - 3 * ((block * 171) >> 9)
        past = jnp.where(key < BLOCKS * BLK, slot - n, key - BLOCKS * BLK - length)
        mark = jnp.where(past >= 0, HDIM - 1, -1)
        row = lax.broadcasted_iota(jnp.int32, (HDIM, KEYS), 0)
        turned_keys[HDIM:] = jnp.where((row == block) | (row == mark), MASKED, 0.0).astype(BF16)
        shape = (BLOCKS, BLK, HDIM)
        block = lax.broadcasted_iota(jnp.int32, shape, 0)
        lane = lax.broadcasted_iota(jnp.int32, shape, 2)
        qmask[...] = jnp.where((lane == block) | (lane == HDIM - 1), 1.0, 0.0).astype(BF16)

    def send_back(peers, source, target, sent, received):
        for peer in peers:

            @pl.when(me != peer)
            def _(peer=peer):
                pltpu.make_async_remote_copy(
                    src_ref=source.at[peer],
                    dst_ref=target,
                    send_sem=sent,
                    recv_sem=received,
                    device_id=(image, peer),
                    device_id_type=MESH,
                ).start()

            @pl.when(me == peer)
            def _(peer=peer):
                pltpu.make_async_copy(source.at[peer], target, received).start()

    @pl.when(is_owner)
    def _():
        for copy in texts:
            copy.wait()
        wait_for(inbox.at[:, keys_queries], kq_sem)
        k = jnp.concatenate([inbox[:, 0].reshape(BLOCKS * BLK, HDIM), tkeys[...].reshape(TXT, HDIM)], axis=0)
        turned_keys[:HDIM] = k.T
        lane = lax.broadcasted_iota(jnp.int32, (ROWS, HDIM), 1)
        for chunk in range(CHUNKS):
            peers = range(chunk * CPEERS, (chunk + 1) * CPEERS)
            some = slice(peers.start, peers.stop)
            q = inbox[some, 1].reshape(CROWS, HDIM)
            marks = qmask[peers.start * LIVE : peers.stop * LIVE].reshape(CROWS, HDIM)
            sbuf[chunk] = jnp.dot(
                jnp.concatenate([q, marks], axis=1), turned_keys[...], preferred_element_type=F32
            )
            stats = jnp.zeros((ROWS, HDIM), F32)
            for i in range(CPEERS):
                rows = slice(i * ROWS, (i + 1) * ROWS)
                scores = sbuf[chunk, rows]
                top = jnp.max(scores, axis=1, keepdims=True)
                weights = jnp.exp2((scores - top) * SCALE)
                total = jnp.sum(weights, axis=1, keepdims=True)
                pbuf[chunk, rows] = weights.astype(BF16)
                linv[chunk, rows] = jnp.broadcast_to(1.0 / total, (ROWS, HDIM))
                stats = jnp.where(lane == i, top * SCALE + jnp.log2(total), stats)
            if chunk == 0:
                wait_for(inbox.at[:, only_values], v_sem)
            v = jnp.concatenate([inbox[:, 2].reshape(BLOCKS * BLK, HDIM), tvalues[...].reshape(TXT, HDIM)], axis=0)
            attended = jnp.dot(pbuf[chunk], v, preferred_element_type=F32) * linv[chunk]
            attended = attended.astype(BF16).reshape(CPEERS, LIVE, BLK, HDIM)
            osend[some] = attended
            send_back(peers, osend, orecv.at[my_head], o_sent, o_sem)
            turned = jnp.concatenate([stats, jnp.zeros((HDIM - ROWS, HDIM), F32)], axis=0).T
            for i, peer in enumerate(peers):
                lsend[peer] = turned[i : i + 1]
            send_back(peers, lsend, lrecv.at[my_head], l_sent, l_sem)

    @pl.when(me >= PEERS // 2)
    def _():
        attend_own(0, HEADS)

    @pl.when(is_owner)
    def _():
        wait_for(inbox.at[pl.ds(0, HEADS - 1), keys_queries], kq_sent)
        wait_for(inbox.at[pl.ds(0, HEADS - 1), only_values], v_sent)

    @pl.when(jnp.logical_not(is_owner))
    def _():
        wait_for(inbox.at[pl.ds(0, HEADS), keys_queries], kq_sent)
        wait_for(inbox.at[pl.ds(0, HEADS), only_values], v_sent)

    wait_for(lrecv, l_sem)
    stacked = jnp.concatenate([lrecv[head] for head in range(HEADS)] + [jnp.zeros((HDIM - HEADS, HDIM), F32)], axis=0)
    columns = stacked.T
    shown = lax.broadcasted_iota(jnp.int32, (LIVE, BLK, HDIM), 0) < n
    for head in range(HEADS):
        sibling = jnp.broadcast_to(columns[:ROWS, head : head + 1], (ROWS, HDIM))
        within = ownlse[head]
        top = jnp.maximum(sibling, within)
        a = jnp.exp2(sibling - top)
        b = jnp.exp2(within - top)
        inverse = 1.0 / (a + b)
        coef[head] = a * inverse
        ownout[head] = ownout[head] * (b * inverse)
    wait_for(orecv, o_sem)
    for head in range(HEADS):
        merged = orecv[head].reshape(ROWS, HDIM).astype(F32) * coef[head] + ownout[head]
        merged = jnp.where(shown, merged.reshape(LIVE, BLK, HDIM), 0.0)
        out[:, :, head * HDIM : (head + 1) * HDIM] = merged.astype(BF16)

    @pl.when(is_owner)
    def _():
        wait_for(lsend.at[pl.ds(0, PEERS - 1)], l_sent)
        wait_for(osend.at[pl.ds(0, PEERS - 1)], o_sent)


def attention(fresh, keys, values, text, slots, lengths):
    anywhere = pl.BlockSpec(memory_space=pl.ANY)
    semaphore = pltpu.SemaphoreType.DMA
    return pl.pallas_call(
        kernel,
        out_shape=jax.ShapeDtypeStruct((LIVE, BLK, HD), BF16),
        in_specs=[anywhere] * 6,
        out_specs=pl.BlockSpec(memory_space=pltpu.VMEM),
        scratch_shapes=[
            pltpu.VMEM((LIVE, BLK, 3 * HD), BF16),
            pltpu.VMEM((2, LIVE, BLK, HD), BF16),
            pltpu.VMEM((HEADS, 3, LIVE, BLK, HDIM), BF16),
            pltpu.VMEM((PEERS, 3, LIVE, BLK, HDIM), BF16),
            pltpu.VMEM((TBLOCKS, BLK, HDIM), BF16),
            pltpu.VMEM((TBLOCKS, BLK, HDIM), BF16),
            pltpu.VMEM((BLOCKS, BLK, HDIM), BF16),
            pltpu.VMEM((2 * HDIM, KEYS), BF16),
            pltpu.VMEM((CHUNKS, CROWS, KEYS), F32),
            pltpu.VMEM((CHUNKS, CROWS, KEYS), BF16),
            pltpu.VMEM((CHUNKS, CROWS, HDIM), F32),
            pltpu.VMEM((PEERS, LIVE, BLK, HDIM), BF16),
            pltpu.VMEM((PEERS, 1, HDIM), F32),
            pltpu.VMEM((HEADS, LIVE, BLK, HDIM), BF16),
            pltpu.VMEM((HEADS, 1, HDIM), F32),
            pltpu.VMEM((HEADS, ROWS, HDIM), F32),
            pltpu.VMEM((HEADS, ROWS, HDIM), F32),
            pltpu.VMEM((HEADS, ROWS, HDIM), F32),
            pltpu.SMEM((2, IMAGES), jnp.int32),
            semaphore((5,)),
            semaphore((2,)),
        ]
        + [semaphore] * 8
        + [pltpu.SemaphoreType.REGULAR((PEERS,))],
        compiler_params=pltpu.CompilerParams(
            collective_id=0, has_side_effects=True, vmem_limit_bytes=24 * 1024 * 1024
        ),
    )(*[pltpu.with_memory_space_constraint(x, pltpu.HBM) for x in (fresh, keys, values, text, slots, lengths)])


def body(fresh, stale_keys, stale_values, text_kv, group_slots, text_len):
    slot_count = fresh.shape[2]
    text = text_kv[0].reshape(TBLOCKS, BLK, 2 * HD)
    merged = attention(fresh[0, 0], stale_keys[0, 0], stale_values[0, 0], text, group_slots, text_len)
    return jnp.pad(merged, ((0, slot_count - LIVE), (0, 0), (0, 0)))[None, None]


def solution(mesh):
    placed = (
        P("img", "patch", None, None, None),
        P("img", "patch", None, None, None),
        P("img", "patch", None, None, None),
        P("img", None, None),
        P(),
        P(),
    )
    return jax.shard_map(
        body,
        mesh=mesh,
        in_specs=placed,
        out_specs=P("img", "patch", None, None, None),
        check_vma=False,
    )
```

```python
import functools

import jax
import jax.numpy as jnp
from jax import lax
from jax.experimental import pallas as pl
from jax.experimental.pallas import tpu as pltpu
from jax.sharding import PartitionSpec as P

MESH = pl.DeviceIdType.MESH
F32 = jnp.float32
BF16 = jnp.bfloat16

HDIM = 128
HEADS = 12
HD = HDIM * HEADS
BLK = 16
LIVE = 3
TXT = 128
PEERS = 16
IMAGES = 32
ROWS = LIVE * BLK
BLOCKS = PEERS * LIVE
TBLOCKS = TXT // BLK
KEYS = BLOCKS * BLK + TXT
CHUNKS = 4
CPEERS = PEERS // CHUNKS
CROWS = CPEERS * ROWS
SCALE = 1.4426950408889634 / HDIM**0.5
MASKED = -1e30


def nt(a, b):
    return lax.dot_general(a, b, (((1,), (1,)), ((), ())), preferred_element_type=F32)


def owner_rank(peer, core):
    return ((peer >> 1) + 15 - 2 * core - (peer & 1)) & 3


def owned_head(peer, core):
    return (peer >> 3) * 6 + (peer & 1) * 3 + owner_rank(peer, core)


def partner(me, core, k):
    reach = k // 2 if k % 2 else -(k // 2)
    return (me + PEERS // 2 + reach * (1 - 2 * core)) & (PEERS - 1)


def kernel(
    fresh, keys, values, text, slots_in, lengths_in, out,
    own, stale, chunks, inbox, tkeys, tvalues, qmask, turned_keys, sbuf, pbuf, linv,
    osend, lsend, orecv, lrecv, ownout, ownlse, coef, counts,
    local_sem, text_sem, sent_sem, q_sem, k_sem, v_sem, o_sem, l_sem, o_sent, l_sent, here,
):
    image = lax.axis_index("img")
    me = lax.axis_index("patch")
    core = image & 1
    is_owner = owner_rank(me, core) < 3
    my_head = owned_head(me, core)

    barrier = pltpu.get_barrier_semaphore()

    live = pl.ds(0, LIVE)
    local = [
        pltpu.make_async_copy(keys.at[live], stale.at[0], local_sem.at[0]),
        pltpu.make_async_copy(fresh.at[live], own, local_sem.at[1]),
        pltpu.make_async_copy(values.at[live], stale.at[1], local_sem.at[2]),
        pltpu.make_async_copy(slots_in, counts.at[0], local_sem.at[3]),
        pltpu.make_async_copy(lengths_in, counts.at[1], local_sem.at[4]),
    ]
    for copy in local:
        copy.start()

    def greet(peer, carry):
        pl.semaphore_signal(barrier, inc=1, device_id=(image, peer), device_id_type=MESH)
        return carry

    lax.fori_loop(me + 1, PEERS, greet, 0)

    @pl.when(me > 0)
    def _():
        pl.semaphore_wait(barrier, me)

    def tell(peer, carry):
        pl.semaphore_signal(here.at[me], inc=1, device_id=(image, peer), device_id_type=MESH)
        return carry

    lax.fori_loop(0, me, tell, 0)

    def text_copy(third, target):
        columns = pl.ds(pl.multiple_of(third * HD + my_head * HDIM, HDIM), HDIM)
        return pltpu.make_async_copy(text.at[:, :, columns], target, text_sem.at[third])

    texts = [text_copy(0, tkeys), text_copy(1, tvalues)]

    @pl.when(is_owner)
    def _():
        for copy in texts:
            copy.start()

    def stage(part, source):
        for head in range(HEADS):
            chunks[head, part] = source[:, :, head * HDIM : (head + 1) * HDIM]

    local[0].wait()
    stage(0, stale.at[0])
    local[1].wait()
    stage(2, own)
    local[2].wait()
    stage(1, stale.at[1])

    def received(part):
        return (k_sem, v_sem, q_sem.at[me >> 2])[part]

    def send(peer, part):
        pltpu.make_async_remote_copy(
            src_ref=chunks.at[owned_head(peer, core), part],
            dst_ref=inbox.at[me, part],
            send_sem=sent_sem.at[part],
            recv_sem=received(part),
            device_id=(image, peer),
            device_id_type=MESH,
        ).start()

    for part in range(3):
        for k in range(1, PEERS):
            peer = partner(me, core, k)

            @pl.when(jnp.logical_and(peer < me, owner_rank(peer, core) < 3))
            def _(peer=peer, part=part):
                send(peer, part)

    @pl.when(is_owner)
    def _():
        for part in range(3):
            pltpu.make_async_copy(chunks.at[my_head, part], inbox.at[me, part], received(part)).start()

    def attend_own(first, count):
        heads = range(first, first + count)
        diagonal = (
            lax.broadcasted_iota(jnp.int32, (ROWS, ROWS), 0) // BLK
            == lax.broadcasted_iota(jnp.int32, (ROWS, ROWS), 1) // BLK
        )

        def third(which, head):
            at = which * HD + head * HDIM
            return own[:, :, at : at + HDIM].reshape(ROWS, HDIM)

        scores = [jnp.where(diagonal, nt(third(0, head), third(1, head)), MASKED) for head in heads]
        tops = [jnp.max(x, axis=1, keepdims=True) for x in scores]
        weights = [jnp.exp2((x - top) * SCALE) for x, top in zip(scores, tops)]
        totals = [jnp.sum(x, axis=1, keepdims=True) for x in weights]
        sums = [
            jnp.dot(x.astype(BF16), third(2, head), preferred_element_type=F32) for x, head in zip(weights, heads)
        ]
        for i, head in enumerate(heads):
            ownout[head] = sums[i] / totals[i]
            ownlse[head] = jnp.broadcast_to(tops[i] * SCALE + jnp.log2(totals[i]), (ROWS, HDIM))

    @pl.when(me < PEERS // 2)
    def _():
        attend_own(0, HEADS)

    def send_after(peer, carry):
        pl.semaphore_wait(here.at[peer], 1)

        @pl.when(owner_rank(peer, core) < 3)
        def _():
            for part in range(3):
                send(peer, part)

        return carry

    lax.fori_loop(me + 1, PEERS, send_after, 0)

    def wait_for(ref, sem):
        pltpu.make_async_copy(ref, ref, sem).wait()

    local[3].wait()
    local[4].wait()
    n = counts[0, image]
    length = counts[1, image]

    @pl.when(is_owner)
    def _():
        key = lax.broadcasted_iota(jnp.int32, (1, KEYS), 1)
        block = (key >> 4) + jnp.where(key < BLOCKS * BLK, 0, HDIM)
        slot = block - 3 * ((block * 171) >> 9)
        past = jnp.where(key < BLOCKS * BLK, slot - n, key - BLOCKS * BLK - length)
        mark = jnp.where(past >= 0, HDIM - 1, -1)
        row = lax.broadcasted_iota(jnp.int32, (HDIM, KEYS), 0)
        turned_keys[HDIM:] = jnp.where((row == block) | (row == mark), MASKED, 0.0).astype(BF16)
        shape = (BLOCKS, BLK, HDIM)
        block = lax.broadcasted_iota(jnp.int32, shape, 0)
        lane = lax.broadcasted_iota(jnp.int32, shape, 2)
        qmask[...] = jnp.where((lane == block) | (lane == HDIM - 1), 1.0, 0.0).astype(BF16)

    def send_back(peers, source, target, sent, received):
        for peer in peers:

            @pl.when(me != peer)
            def _(peer=peer):
                pltpu.make_async_remote_copy(
                    src_ref=source.at[peer],
                    dst_ref=target,
                    send_sem=sent,
                    recv_sem=received,
                    device_id=(image, peer),
                    device_id_type=MESH,
                ).start()

            @pl.when(me == peer)
            def _(peer=peer):
                pltpu.make_async_copy(source.at[peer], target, received).start()

    @pl.when(is_owner)
    def _():
        for copy in texts:
            copy.wait()
        wait_for(inbox.at[:, 0], k_sem)
        k = jnp.concatenate([inbox[:, 0].reshape(BLOCKS * BLK, HDIM), tkeys[...].reshape(TXT, HDIM)], axis=0)
        turned_keys[:HDIM] = k.T
        lane = lax.broadcasted_iota(jnp.int32, (ROWS, HDIM), 1)
        for chunk in range(CHUNKS):
            peers = range(chunk * CPEERS, (chunk + 1) * CPEERS)
            some = slice(peers.start, peers.stop)
            wait_for(inbox.at[pl.ds(0, CPEERS), 2], q_sem.at[chunk])
            q = inbox[some, 2].reshape(CROWS, HDIM)
            marks = qmask[peers.start * LIVE : peers.stop * LIVE].reshape(CROWS, HDIM)
            sbuf[chunk] = jnp.dot(
                jnp.concatenate([q, marks], axis=1), turned_keys[...], preferred_element_type=F32
            )
            stats = jnp.zeros((ROWS, HDIM), F32)
            for i in range(CPEERS):
                rows = slice(i * ROWS, (i + 1) * ROWS)
                scores = sbuf[chunk, rows]
                top = jnp.max(scores, axis=1, keepdims=True)
                weights = jnp.exp2((scores - top) * SCALE)
                total = jnp.sum(weights, axis=1, keepdims=True)
                pbuf[chunk, rows] = weights.astype(BF16)
                linv[chunk, rows] = jnp.broadcast_to(1.0 / total, (ROWS, HDIM))
                stats = jnp.where(lane == i, top * SCALE + jnp.log2(total), stats)
            if chunk == 0:
                wait_for(inbox.at[:, 1], v_sem)
            v = jnp.concatenate([inbox[:, 1].reshape(BLOCKS * BLK, HDIM), tvalues[...].reshape(TXT, HDIM)], axis=0)
            attended = jnp.dot(pbuf[chunk], v, preferred_element_type=F32) * linv[chunk]
            attended = attended.astype(BF16).reshape(CPEERS, LIVE, BLK, HDIM)
            osend[some] = attended
            send_back(peers, osend, orecv.at[my_head], o_sent, o_sem)
            turned = jnp.concatenate([stats, jnp.zeros((HDIM - ROWS, HDIM), F32)], axis=0).T
            for i, peer in enumerate(peers):
                lsend[peer] = turned[i : i + 1]
            send_back(peers, lsend, lrecv.at[my_head], l_sent, l_sem)

    @pl.when(me >= PEERS // 2)
    def _():
        attend_own(0, HEADS)

    @pl.when(is_owner)
    def _():
        for part in range(3):
            wait_for(inbox.at[pl.ds(0, HEADS - 1), part], sent_sem.at[part])

    @pl.when(jnp.logical_not(is_owner))
    def _():
        for part in range(3):
            wait_for(inbox.at[pl.ds(0, HEADS), part], sent_sem.at[part])

    wait_for(lrecv, l_sem)
    stacked = jnp.concatenate([lrecv[head] for head in range(HEADS)] + [jnp.zeros((HDIM - HEADS, HDIM), F32)], axis=0)
    columns = stacked.T
    shown = lax.broadcasted_iota(jnp.int32, (LIVE, BLK, HDIM), 0) < n
    for head in range(HEADS):
        sibling = jnp.broadcast_to(columns[:ROWS, head : head + 1], (ROWS, HDIM))
        within = ownlse[head]
        top = jnp.maximum(sibling, within)
        a = jnp.exp2(sibling - top)
        b = jnp.exp2(within - top)
        inverse = 1.0 / (a + b)
        coef[head] = a * inverse
        ownout[head] = ownout[head] * (b * inverse)
    wait_for(orecv, o_sem)
    for head in range(HEADS):
        merged = orecv[head].reshape(ROWS, HDIM).astype(F32) * coef[head] + ownout[head]
        merged = jnp.where(shown, merged.reshape(LIVE, BLK, HDIM), 0.0)
        out[:, :, head * HDIM : (head + 1) * HDIM] = merged.astype(BF16)

    @pl.when(is_owner)
    def _():
        wait_for(lsend.at[pl.ds(0, PEERS - 1)], l_sent)
        wait_for(osend.at[pl.ds(0, PEERS - 1)], o_sent)


def attention(fresh, keys, values, text, slots, lengths):
    anywhere = pl.BlockSpec(memory_space=pl.ANY)
    semaphore = pltpu.SemaphoreType.DMA
    return pl.pallas_call(
        kernel,
        out_shape=jax.ShapeDtypeStruct((LIVE, BLK, HD), BF16),
        in_specs=[anywhere] * 6,
        out_specs=pl.BlockSpec(memory_space=pltpu.VMEM),
        scratch_shapes=[
            pltpu.VMEM((LIVE, BLK, 3 * HD), BF16),
            pltpu.VMEM((2, LIVE, BLK, HD), BF16),
            pltpu.VMEM((HEADS, 3, LIVE, BLK, HDIM), BF16),
            pltpu.VMEM((PEERS, 3, LIVE, BLK, HDIM), BF16),
            pltpu.VMEM((TBLOCKS, BLK, HDIM), BF16),
            pltpu.VMEM((TBLOCKS, BLK, HDIM), BF16),
            pltpu.VMEM((BLOCKS, BLK, HDIM), BF16),
            pltpu.VMEM((2 * HDIM, KEYS), BF16),
            pltpu.VMEM((CHUNKS, CROWS, KEYS), F32),
            pltpu.VMEM((CHUNKS, CROWS, KEYS), BF16),
            pltpu.VMEM((CHUNKS, CROWS, HDIM), F32),
            pltpu.VMEM((PEERS, LIVE, BLK, HDIM), BF16),
            pltpu.VMEM((PEERS, 1, HDIM), F32),
            pltpu.VMEM((HEADS, LIVE, BLK, HDIM), BF16),
            pltpu.VMEM((HEADS, 1, HDIM), F32),
            pltpu.VMEM((HEADS, ROWS, HDIM), F32),
            pltpu.VMEM((HEADS, ROWS, HDIM), F32),
            pltpu.VMEM((HEADS, ROWS, HDIM), F32),
            pltpu.SMEM((2, IMAGES), jnp.int32),
            semaphore((5,)),
            semaphore((2,)),
            semaphore((3,)),
            semaphore((CHUNKS,)),
        ]
        + [semaphore] * 6
        + [pltpu.SemaphoreType.REGULAR((PEERS,))],
        compiler_params=pltpu.CompilerParams(
            collective_id=0, has_side_effects=True, vmem_limit_bytes=24 * 1024 * 1024
        ),
    )(*[pltpu.with_memory_space_constraint(x, pltpu.HBM) for x in (fresh, keys, values, text, slots, lengths)])


def body(fresh, stale_keys, stale_values, text_kv, group_slots, text_len):
    slot_count = fresh.shape[2]
    text = text_kv[0].reshape(TBLOCKS, BLK, 2 * HD)
    merged = attention(fresh[0, 0], stale_keys[0, 0], stale_values[0, 0], text, group_slots, text_len)
    return jnp.pad(merged, ((0, slot_count - LIVE), (0, 0), (0, 0)))[None, None]


def solution(mesh):
    placed = (
        P("img", "patch", None, None, None),
        P("img", "patch", None, None, None),
        P("img", "patch", None, None, None),
        P("img", None, None),
        P(),
        P(),
    )
    return jax.shard_map(
        body,
        mesh=mesh,
        in_specs=placed,
        out_specs=P("img", "patch", None, None, None),
        check_vma=False,
    )
```

```python
import functools

import jax
import jax.numpy as jnp
from jax import lax
from jax.experimental import pallas as pl
from jax.experimental.pallas import tpu as pltpu
from jax.sharding import PartitionSpec as P

MESH = pl.DeviceIdType.MESH
F32 = jnp.float32
BF16 = jnp.bfloat16

HDIM = 128
HEADS = 12
HD = HDIM * HEADS
BLK = 16
LIVE = 3
TXT = 128
PEERS = 16
IMAGES = 32
ROWS = LIVE * BLK
BLOCKS = PEERS * LIVE
TBLOCKS = TXT // BLK
KEYS = BLOCKS * BLK + TXT
CHUNKS = 4
CPEERS = PEERS // CHUNKS
CROWS = CPEERS * ROWS
SCALE = 1.4426950408889634 / HDIM**0.5
MASKED = -1e30


def nt(a, b):
    return lax.dot_general(a, b, (((1,), (1,)), ((), ())), preferred_element_type=F32)


def owner_rank(peer, core):
    return ((peer >> 1) + 14 - 2 * core - (peer & 1)) & 3


def owned_head(peer, core):
    return (peer >> 3) * 6 + (peer & 1) * 3 + owner_rank(peer, core)


def partner(me, core, k):
    reach = k // 2 if k % 2 else -(k // 2)
    return (me + PEERS // 2 + reach * (1 - 2 * core)) & (PEERS - 1)


def kernel(
    fresh, keys, values, text, slots_in, lengths_in, out,
    own, stale, chunks, inbox, tkeys, tvalues, qmask, turned_keys, sbuf, pbuf, linv,
    osend, lsend, orecv, lrecv, ownout, ownlse, coef, counts,
    local_sem, text_sem, sent_sem, q_sem, k_sem, v_sem, o_sem, l_sem, o_sent, l_sent, here,
):
    image = lax.axis_index("img")
    me = lax.axis_index("patch")
    core = image & 1
    is_owner = owner_rank(me, core) < 3
    my_head = owned_head(me, core)

    barrier = pltpu.get_barrier_semaphore()

    live = pl.ds(0, LIVE)
    local = [
        pltpu.make_async_copy(keys.at[live], stale.at[0], local_sem.at[0]),
        pltpu.make_async_copy(fresh.at[live], own, local_sem.at[1]),
        pltpu.make_async_copy(values.at[live], stale.at[1], local_sem.at[2]),
        pltpu.make_async_copy(slots_in, counts.at[0], local_sem.at[3]),
        pltpu.make_async_copy(lengths_in, counts.at[1], local_sem.at[4]),
    ]
    for copy in local:
        copy.start()

    def greet(peer, carry):
        pl.semaphore_signal(barrier, inc=1, device_id=(image, peer), device_id_type=MESH)
        return carry

    lax.fori_loop(me + 1, PEERS, greet, 0)

    @pl.when(me > 0)
    def _():
        pl.semaphore_wait(barrier, me)

    def tell(peer, carry):
        pl.semaphore_signal(here.at[me], inc=1, device_id=(image, peer), device_id_type=MESH)
        return carry

    lax.fori_loop(0, me, tell, 0)

    def text_copy(third, target):
        columns = pl.ds(pl.multiple_of(third * HD + my_head * HDIM, HDIM), HDIM)
        return pltpu.make_async_copy(text.at[:, :, columns], target, text_sem.at[third])

    texts = [text_copy(0, tkeys), text_copy(1, tvalues)]

    @pl.when(is_owner)
    def _():
        for copy in texts:
            copy.start()

    def stage(part, source):
        for head in range(HEADS):
            chunks[head, part] = source[:, :, head * HDIM : (head + 1) * HDIM]

    local[0].wait()
    stage(0, stale.at[0])
    local[1].wait()
    stage(2, own)
    local[2].wait()
    stage(1, stale.at[1])

    def received(part):
        return (k_sem, v_sem, q_sem.at[me >> 2])[part]

    def send(peer, part):
        pltpu.make_async_remote_copy(
            src_ref=chunks.at[owned_head(peer, core), part],
            dst_ref=inbox.at[me, part],
            send_sem=sent_sem.at[part],
            recv_sem=received(part),
            device_id=(image, peer),
            device_id_type=MESH,
        ).start()

    for part in range(3):
        for k in range(1, PEERS):
            peer = partner(me, core, k)

            @pl.when(jnp.logical_and(peer < me, owner_rank(peer, core) < 3))
            def _(peer=peer, part=part):
                send(peer, part)

    @pl.when(is_owner)
    def _():
        for part in range(3):
            pltpu.make_async_copy(chunks.at[my_head, part], inbox.at[me, part], received(part)).start()

    def attend_own(first, count):
        heads = range(first, first + count)
        diagonal = (
            lax.broadcasted_iota(jnp.int32, (ROWS, ROWS), 0) // BLK
            == lax.broadcasted_iota(jnp.int32, (ROWS, ROWS), 1) // BLK
        )

        def third(which, head):
            at = which * HD + head * HDIM
            return own[:, :, at : at + HDIM].reshape(ROWS, HDIM)

        scores = [jnp.where(diagonal, nt(third(0, head), third(1, head)), MASKED) for head in heads]
        tops = [jnp.max(x, axis=1, keepdims=True) for x in scores]
        weights = [jnp.exp2((x - top) * SCALE) for x, top in zip(scores, tops)]
        totals = [jnp.sum(x, axis=1, keepdims=True) for x in weights]
        sums = [
            jnp.dot(x.astype(BF16), third(2, head), preferred_element_type=F32) for x, head in zip(weights, heads)
        ]
        for i, head in enumerate(heads):
            ownout[head] = sums[i] / totals[i]
            ownlse[head] = jnp.broadcast_to(tops[i] * SCALE + jnp.log2(totals[i]), (ROWS, HDIM))

    @pl.when(me < PEERS // 2)
    def _():
        attend_own(0, HEADS)

    def send_after(peer, carry):
        pl.semaphore_wait(here.at[peer], 1)

        @pl.when(owner_rank(peer, core) < 3)
        def _():
            for part in range(3):
                send(peer, part)

        return carry

    lax.fori_loop(me + 1, PEERS, send_after, 0)

    def wait_for(ref, sem):
        pltpu.make_async_copy(ref, ref, sem).wait()

    local[3].wait()
    local[4].wait()
    n = counts[0, image]
    length = counts[1, image]

    @pl.when(is_owner)
    def _():
        key = lax.broadcasted_iota(jnp.int32, (1, KEYS), 1)
        block = (key >> 4) + jnp.where(key < BLOCKS * BLK, 0, HDIM)
        slot = block - 3 * ((block * 171) >> 9)
        past = jnp.where(key < BLOCKS * BLK, slot - n, key - BLOCKS * BLK - length)
        mark = jnp.where(past >= 0, HDIM - 1, -1)
        row = lax.broadcasted_iota(jnp.int32, (HDIM, KEYS), 0)
        turned_keys[HDIM:] = jnp.where((row == block) | (row == mark), MASKED, 0.0).astype(BF16)
        shape = (BLOCKS, BLK, HDIM)
        block = lax.broadcasted_iota(jnp.int32, shape, 0)
        lane = lax.broadcasted_iota(jnp.int32, shape, 2)
        qmask[...] = jnp.where((lane == block) | (lane == HDIM - 1), 1.0, 0.0).astype(BF16)

    def send_back(peers, source, target, sent, received):
        for peer in peers:

            @pl.when(me != peer)
            def _(peer=peer):
                pltpu.make_async_remote_copy(
                    src_ref=source.at[peer],
                    dst_ref=target,
                    send_sem=sent,
                    recv_sem=received,
                    device_id=(image, peer),
                    device_id_type=MESH,
                ).start()

            @pl.when(me == peer)
            def _(peer=peer):
                pltpu.make_async_copy(source.at[peer], target, received).start()

    @pl.when(is_owner)
    def _():
        for copy in texts:
            copy.wait()
        wait_for(inbox.at[:, 0], k_sem)
        k = jnp.concatenate([inbox[:, 0].reshape(BLOCKS * BLK, HDIM), tkeys[...].reshape(TXT, HDIM)], axis=0)
        turned_keys[:HDIM] = k.T
        lane = lax.broadcasted_iota(jnp.int32, (ROWS, HDIM), 1)
        for chunk in range(CHUNKS):
            peers = range(chunk * CPEERS, (chunk + 1) * CPEERS)
            some = slice(peers.start, peers.stop)
            wait_for(inbox.at[pl.ds(0, CPEERS), 2], q_sem.at[chunk])
            q = inbox[some, 2].reshape(CROWS, HDIM)
            marks = qmask[peers.start * LIVE : peers.stop * LIVE].reshape(CROWS, HDIM)
            sbuf[chunk] = jnp.dot(
                jnp.concatenate([q, marks], axis=1), turned_keys[...], preferred_element_type=F32
            )
            stats = jnp.zeros((ROWS, HDIM), F32)
            for i in range(CPEERS):
                rows = slice(i * ROWS, (i + 1) * ROWS)
                scores = sbuf[chunk, rows]
                top = jnp.max(scores, axis=1, keepdims=True)
                weights = jnp.exp2((scores - top) * SCALE)
                total = jnp.sum(weights, axis=1, keepdims=True)
                pbuf[chunk, rows] = weights.astype(BF16)
                linv[chunk, rows] = jnp.broadcast_to(1.0 / total, (ROWS, HDIM))
                stats = jnp.where(lane == i, top * SCALE + jnp.log2(total), stats)
            if chunk == 0:
                wait_for(inbox.at[:, 1], v_sem)
            v = jnp.concatenate([inbox[:, 1].reshape(BLOCKS * BLK, HDIM), tvalues[...].reshape(TXT, HDIM)], axis=0)
            attended = jnp.dot(pbuf[chunk], v, preferred_element_type=F32) * linv[chunk]
            attended = attended.astype(BF16).reshape(CPEERS, LIVE, BLK, HDIM)
            osend[some] = attended
            send_back(peers, osend, orecv.at[my_head], o_sent, o_sem)
            turned = jnp.concatenate([stats, jnp.zeros((HDIM - ROWS, HDIM), F32)], axis=0).T
            for i, peer in enumerate(peers):
                lsend[peer] = turned[i : i + 1]
            send_back(peers, lsend, lrecv.at[my_head], l_sent, l_sem)

    @pl.when(me >= PEERS // 2)
    def _():
        attend_own(0, HEADS)

    @pl.when(is_owner)
    def _():
        for part in range(3):
            wait_for(inbox.at[pl.ds(0, HEADS - 1), part], sent_sem.at[part])

    @pl.when(jnp.logical_not(is_owner))
    def _():
        for part in range(3):
            wait_for(inbox.at[pl.ds(0, HEADS), part], sent_sem.at[part])

    wait_for(lrecv, l_sem)
    stacked = jnp.concatenate([lrecv[head] for head in range(HEADS)] + [jnp.zeros((HDIM - HEADS, HDIM), F32)], axis=0)
    columns = stacked.T
    shown = lax.broadcasted_iota(jnp.int32, (LIVE, BLK, HDIM), 0) < n
    for head in range(HEADS):
        sibling = jnp.broadcast_to(columns[:ROWS, head : head + 1], (ROWS, HDIM))
        within = ownlse[head]
        top = jnp.maximum(sibling, within)
        a = jnp.exp2(sibling - top)
        b = jnp.exp2(within - top)
        inverse = 1.0 / (a + b)
        coef[head] = a * inverse
        ownout[head] = ownout[head] * (b * inverse)
    wait_for(orecv, o_sem)
    for head in range(HEADS):
        merged = orecv[head].reshape(ROWS, HDIM).astype(F32) * coef[head] + ownout[head]
        merged = jnp.where(shown, merged.reshape(LIVE, BLK, HDIM), 0.0)
        out[:, :, head * HDIM : (head + 1) * HDIM] = merged.astype(BF16)

    @pl.when(is_owner)
    def _():
        wait_for(lsend.at[pl.ds(0, PEERS - 1)], l_sent)
        wait_for(osend.at[pl.ds(0, PEERS - 1)], o_sent)


def attention(fresh, keys, values, text, slots, lengths):
    anywhere = pl.BlockSpec(memory_space=pl.ANY)
    semaphore = pltpu.SemaphoreType.DMA
    return pl.pallas_call(
        kernel,
        out_shape=jax.ShapeDtypeStruct((LIVE, BLK, HD), BF16),
        in_specs=[anywhere] * 6,
        out_specs=pl.BlockSpec(memory_space=pltpu.VMEM),
        scratch_shapes=[
            pltpu.VMEM((LIVE, BLK, 3 * HD), BF16),
            pltpu.VMEM((2, LIVE, BLK, HD), BF16),
            pltpu.VMEM((HEADS, 3, LIVE, BLK, HDIM), BF16),
            pltpu.VMEM((PEERS, 3, LIVE, BLK, HDIM), BF16),
            pltpu.VMEM((TBLOCKS, BLK, HDIM), BF16),
            pltpu.VMEM((TBLOCKS, BLK, HDIM), BF16),
            pltpu.VMEM((BLOCKS, BLK, HDIM), BF16),
            pltpu.VMEM((2 * HDIM, KEYS), BF16),
            pltpu.VMEM((CHUNKS, CROWS, KEYS), F32),
            pltpu.VMEM((CHUNKS, CROWS, KEYS), BF16),
            pltpu.VMEM((CHUNKS, CROWS, HDIM), F32),
            pltpu.VMEM((PEERS, LIVE, BLK, HDIM), BF16),
            pltpu.VMEM((PEERS, 1, HDIM), F32),
            pltpu.VMEM((HEADS, LIVE, BLK, HDIM), BF16),
            pltpu.VMEM((HEADS, 1, HDIM), F32),
            pltpu.VMEM((HEADS, ROWS, HDIM), F32),
            pltpu.VMEM((HEADS, ROWS, HDIM), F32),
            pltpu.VMEM((HEADS, ROWS, HDIM), F32),
            pltpu.SMEM((2, IMAGES), jnp.int32),
            semaphore((5,)),
            semaphore((2,)),
            semaphore((3,)),
            semaphore((CHUNKS,)),
        ]
        + [semaphore] * 6
        + [pltpu.SemaphoreType.REGULAR((PEERS,))],
        compiler_params=pltpu.CompilerParams(
            collective_id=0, has_side_effects=True, vmem_limit_bytes=24 * 1024 * 1024
        ),
    )(*[pltpu.with_memory_space_constraint(x, pltpu.HBM) for x in (fresh, keys, values, text, slots, lengths)])


def body(fresh, stale_keys, stale_values, text_kv, group_slots, text_len):
    slot_count = fresh.shape[2]
    text = text_kv[0].reshape(TBLOCKS, BLK, 2 * HD)
    merged = attention(fresh[0, 0], stale_keys[0, 0], stale_values[0, 0], text, group_slots, text_len)
    return jnp.pad(merged, ((0, slot_count - LIVE), (0, 0), (0, 0)))[None, None]


def solution(mesh):
    placed = (
        P("img", "patch", None, None, None),
        P("img", "patch", None, None, None),
        P("img", "patch", None, None, None),
        P("img", None, None),
        P(),
        P(),
    )
    return jax.shard_map(
        body,
        mesh=mesh,
        in_specs=placed,
        out_specs=P("img", "patch", None, None, None),
        check_vma=False,
    )
```
